32 devices in a mesh: gx: 4 (over x, core), gy: 8 (over z, y).
Axes of the slice: x: 2, y: 2, z: 4, core: 2. Of those that a mesh axis runs over, the one named last changes fastest.
Arguments:
- parent_fields: float32 [5, 4, 192, 3072], P(None, None, 'gx', 'gy'), may hold values from -6 to 6
- parent_velocity: float32 [2, 4, 192, 3072], P(None, None, 'gx', 'gy'), may hold values from -0.3 to 0.3
- parent_mixing: float32 [4, 192, 3072], P(None, 'gx', 'gy'), may hold values from 0.01 to 0.1
- nest_fields: float32 [5, 4, 192, 3072], P(None, None, 'gx', 'gy'), may hold values from -6 to 6
- nest_velocity: float32 [2, 4, 192, 3072], P(None, None, 'gx', 'gy'), may hold values from -0.3 to 0.3
- nest_mixing: float32 [4, 192, 3072], P(None, 'gx', 'gy'), may hold values from 0.01 to 0.1
- nest_anchor: int32 [2], replicated, may hold values from 1 to 1791, as said below
Outputs:
- parent_result: float32 [5, 4, 192, 3072], P(None, None, 'gx', 'gy')
- nest_result: float32 [5, 4, 192, 3072], P(None, None, 'gx', 'gy')
The draws below stay inside these ranges and needn't reach their ends.
Inputs may be any that keep to these rules, and one draw needn't show every extreme that they name: `nest_anchor`: the row anchor is 1 to 126; the column anchor is 1537 to 1791, so the nest with a rim of one parent cell lies inside the parent grid.
All inputs are finite; a program needn't handle non-finite values.
Results may differ from the reference program's by a relative error of at most 0.00002.
Values sent between devices are 32-bit elements; how exact they have to be, the bound alone decides.
No kernel may reach another device: no remote copies, remote signals or barrier semaphores. Data moves between devices by JAX's collectives and lax.ppermute only.
A program may use at most 192 MiB of HBM per device.

```python
import math
import jax
import jax.numpy as jnp
from jax import lax

FIELDS = 5
LEVELS = 4
SUBSTEPS = 3
FY = 128
PY = 384
PARENT_ROWS = 192
PARENT_COLS = 3072
NEST_ROWS = 192
NEST_COLS = 3072


def draw_nest_anchor(key, part):
    row_key = jax.random.fold_in(key, 11)
    column_key = jax.random.fold_in(key, 23)
    row_limit = PARENT_ROWS - NEST_ROWS // 3 - 1
    column_start = PARENT_COLS // 2 + 1
    column_limit = PARENT_COLS // 2 + PY - FY
    row_anchor = jax.random.randint(row_key, (1,), 1, row_limit, dtype=jnp.int32)
    column_anchor = jax.random.randint(column_key, (1,), column_start, column_limit, dtype=jnp.int32)
    return jnp.concatenate((row_anchor, column_anchor)).astype(jnp.int32)


def block_scale(rng, shape, shards, least, largest):
    factor_of = 1.0
    for axis_at, blocks in shards:
        draws = jax.random.uniform(jax.random.fold_in(jax.random.fold_in(rng, 6), axis_at), (blocks,), jnp.float32, least / len(shards), largest / len(shards))
        factor_of = factor_of * jnp.repeat(jnp.exp(draws), shape[axis_at] // blocks).reshape((-1,) + (1,) * (len(shape) - 1 - axis_at))
    return factor_of


def gaussian(own_key, shape, spread, most, shards=(), held_as=jnp.bfloat16):
    values = jax.random.normal(own_key, shape, jnp.float32) * spread
    if len(shards) > 0:
        values = block_scale(own_key, shape, shards, -0.22, 0.18) * values
    return jnp.clip(values, min=-most, max=most).astype(held_as)


def setup_inputs(seed: int = 0) -> dict:
    keys = jax.random.split(jax.random.key(seed), 8)
    parent_fields = gaussian(keys[0], (FIELDS, LEVELS, PARENT_ROWS, PARENT_COLS), 1.0, 6.0, ((2, 4), (3, 8)), jnp.float32)
    parent_velocity = jnp.clip(jax.random.uniform(keys[1], (2, LEVELS, PARENT_ROWS, PARENT_COLS), jnp.float32, -0.3, 0.3) * block_scale(keys[1], (2, LEVELS, PARENT_ROWS, PARENT_COLS), ((2, 4), (3, 8)), -0.4, 0.0), -0.3, 0.3)
    parent_mixing = jnp.clip(jnp.exp(math.log(0.1) - 2.3025851 * jax.random.uniform(keys[2], (LEVELS, PARENT_ROWS, PARENT_COLS), jnp.float32) ** block_scale(keys[2], (LEVELS, PARENT_ROWS, PARENT_COLS), ((1, 4), (2, 8)), -0.2, 0.2)), 0.01, 0.1)
    nest_fields = gaussian(keys[3], (FIELDS, LEVELS, NEST_ROWS, NEST_COLS), 1.0, 6.0, ((2, 4), (3, 8)), jnp.float32)
    nest_velocity = jnp.clip(jax.random.uniform(keys[4], (2, LEVELS, NEST_ROWS, NEST_COLS), jnp.float32, -0.3, 0.3) * block_scale(keys[4], (2, LEVELS, NEST_ROWS, NEST_COLS), ((2, 4), (3, 8)), -0.4, 0.0), -0.3, 0.3)
    nest_mixing = jnp.clip(jnp.exp(math.log(0.1) - 2.3025851 * jax.random.uniform(keys[5], (LEVELS, NEST_ROWS, NEST_COLS), jnp.float32) ** block_scale(keys[5], (LEVELS, NEST_ROWS, NEST_COLS), ((1, 4), (2, 8)), -0.2, 0.2)), 0.01, 0.1)
    nest_anchor = draw_nest_anchor(jax.random.fold_in(keys[7], 71), 0)
    return {"parent_fields": parent_fields, "parent_velocity": parent_velocity, "parent_mixing": parent_mixing, "nest_fields": nest_fields, "nest_velocity": nest_velocity, "nest_mixing": nest_mixing, "nest_anchor": nest_anchor}


third = 1.0 / 3.0
two_thirds = 2.0 / 3.0
nudge_floor = 0.1
relax_width = 4.0


def update(values, padded, velocity, mixing):
    western = padded[:, :, :-2, 1:-1]
    eastern = padded[:, :, 2:, 1:-1]
    southern = padded[:, :, 1:-1, :-2]
    northern = padded[:, :, 1:-1, 2:]
    along_rows = velocity[0]
    along_columns = velocity[1]
    upwind = (jnp.maximum(along_rows, 0.0) * (values - western)
              + jnp.minimum(along_rows, 0.0) * (eastern - values)
              + jnp.maximum(along_columns, 0.0) * (values - southern)
              + jnp.minimum(along_columns, 0.0) * (northern - values))
    return values - upwind + mixing * (eastern + western + northern + southern - 4.0 * values)


def advance(values, velocity, mixing):
    padded = jnp.pad(values, ((0, 0), (0, 0), (1, 1), (1, 1)))
    return update(values, padded, velocity, mixing)


def refine_rows(block):
    lower = block[:, :, :-2]
    centre = block[:, :, 1:-1]
    upper = block[:, :, 2:]
    stacked = jnp.stack((third * lower + two_thirds * centre, centre, two_thirds * centre + third * upper), axis=3)
    extent = centre.shape
    return stacked.reshape(extent[0], extent[1], 3 * extent[2], extent[3])


def refine_columns(block):
    lower = block[:, :, :, :-2]
    centre = block[:, :, :, 1:-1]
    upper = block[:, :, :, 2:]
    stacked = jnp.stack((third * lower + two_thirds * centre, centre, two_thirds * centre + third * upper), axis=4)
    extent = centre.shape
    return stacked.reshape(extent[0], extent[1], extent[2], 3 * extent[3])


def block_mean(state):
    extent = state.shape
    grouped = state.reshape(extent[0], extent[1], extent[2] // 3, 3, extent[3] // 3, 3)
    return jnp.sum(grouped, axis=(3, 5)) / 9.0


def relax_weight(row_global, column_global, total_rows, total_columns):
    row_distance = jnp.minimum(row_global, total_rows - 1 - row_global)
    column_distance = jnp.minimum(column_global, total_columns - 1 - column_global)
    distance = jnp.minimum(row_distance[:, None], column_distance[None, :]).astype(jnp.float32)
    return nudge_floor + (1.0 - nudge_floor) * jnp.exp(-distance / relax_width)


def reference(parent_fields, parent_velocity, parent_mixing, nest_fields, nest_velocity, nest_mixing, nest_anchor):
    parent_next = advance(parent_fields, parent_velocity, parent_mixing)
    fields_count = parent_fields.shape[0]
    levels_count = parent_fields.shape[1]
    nest_rows = nest_fields.shape[2]
    nest_columns = nest_fields.shape[3]
    span_rows = nest_rows // 3
    span_columns = nest_columns // 3
    zero_index = jnp.zeros((), jnp.int32)
    row_anchor = nest_anchor[0].astype(jnp.int32)
    column_anchor = nest_anchor[1].astype(jnp.int32)
    relay = lax.dynamic_slice(parent_next, (zero_index, zero_index, (row_anchor - 1).astype(jnp.int32), (column_anchor - 1).astype(jnp.int32)),
                              (fields_count, levels_count, span_rows + 2, span_columns + 2))
    forcing = refine_columns(refine_rows(relay))
    weight = relax_weight(jnp.arange(nest_rows, dtype=jnp.int32), jnp.arange(nest_columns, dtype=jnp.int32), nest_rows, nest_columns)
    state = nest_fields
    for substep in range(SUBSTEPS):
        moved = advance(state, nest_velocity, nest_mixing)
        state = moved + weight * (forcing - moved)
    coarse = block_mean(state)
    parent_result = lax.dynamic_update_slice(parent_next, coarse, (zero_index, zero_index, row_anchor, column_anchor))
    return parent_result, state
```

```python
import functools

import jax
import jax.numpy as jnp
import numpy as np
from jax import lax
from jax.experimental import pallas as pl
from jax.experimental.pallas import tpu as pltpu
from jax.sharding import PartitionSpec as P

SUBSTEPS = 3
F32 = jnp.float32
LANES = 128
VMEM_LIMIT = 56 * 1024 * 1024
nudge_floor = 0.1
relax_width = 4.0


def call(body, outs, ins, smem=0, scratch=()):
    specs = [pl.BlockSpec(memory_space=pltpu.SMEM)] * smem + [
        pl.BlockSpec(memory_space=pltpu.VMEM)
    ] * (len(ins) - smem)
    return pl.pallas_call(
        body,
        out_shape=[jax.ShapeDtypeStruct(shape, F32) for shape in outs],
        in_specs=specs,
        out_specs=[pl.BlockSpec(memory_space=pltpu.VMEM)] * len(outs),
        scratch_shapes=list(scratch),
        compiler_params=pltpu.CompilerParams(vmem_limit_bytes=VMEM_LIMIT),
    )(*ins)


def lane_index(rows, lanes=LANES):
    return lax.broadcasted_iota(jnp.int32, (rows, lanes), 1)


def row_index(rows, lanes=LANES):
    return lax.broadcasted_iota(jnp.int32, (rows, lanes), 0)


def halo_exchange(axis, to_next, to_previous):
    ends = lax.axis_size(axis) - 1
    from_previous = lax.ppermute(to_next, axis, [(i, i + 1) for i in range(ends)])
    from_next = lax.ppermute(to_previous, axis, [(i + 1, i) for i in range(ends)])
    return from_previous, from_next


def pack_kernel(pf, nf, nv, nm, rows_next, rows_prev, cols_next, cols_prev):
    channels, rows, columns = pf.shape
    coefs = nv.shape[0] + nm.shape[0]
    for ch in range(channels):
        for at in range(3):
            here = at * channels + ch
            rows_next[here : here + 1, :] = nf[ch, rows - 3 + at : rows - 2 + at, :]
            rows_prev[here : here + 1, :] = nf[ch, at : at + 1, :]
    base = 3 * channels
    for cc in range(coefs):
        ref, row = (nv, cc) if cc < nv.shape[0] else (nm, cc - nv.shape[0])
        for at in range(2):
            here = base + at * coefs + cc
            rows_next[here : here + 1, :] = ref[row, rows - 2 + at : rows - 1 + at, :]
            rows_prev[here : here + 1, :] = ref[row, at : at + 1, :]
    base = base + 2 * coefs
    for ch in range(channels):
        rows_next[base + ch : base + ch + 1, :] = pf[ch, rows - 1 : rows, :]
        rows_prev[base + ch : base + ch + 1, :] = pf[ch, 0:1, :]
    lanes = lane_index(rows)
    last = jnp.zeros((rows, LANES), F32)
    first = jnp.zeros((rows, LANES), F32)
    for ch in range(channels):
        tail = pltpu.roll(pf[ch, :, columns - LANES :], (ch + 1) % LANES, 1)
        head = pltpu.roll(pf[ch, :, :LANES], ch, 1)
        last = jnp.where(lanes == ch, tail, last)
        first = jnp.where(lanes == ch, head, first)
    cols_next[...] = last
    cols_prev[...] = first


def parent_kernel(anchor, pf, pv, pm, top, bottom, left, right, *rest):
    parent_next, slabs = rest[0], rest[1:]
    channels, rows, columns = pf.shape
    levels = pm.shape[0]
    span = rows // 3
    rank, size_x = lax.axis_index("gx"), lax.axis_size("gx")
    half = lax.axis_size("gy") // 2 * columns
    base = 3 * channels + 2 * 3 * levels
    offset = anchor[1] - half
    shift = lax.rem(2 * columns - offset, columns)
    row_shift = lax.rem((rows - span) * rank + size_x * rows - anchor[0], rows)
    row = row_index(rows, columns)
    column = lane_index(rows, columns)

    def level_body(level, carry):
        u = pv[level]
        v = pv[levels + level]
        k = pm[level]
        a_w = jnp.maximum(u, 0.0) + k
        a_e = k - jnp.minimum(u, 0.0)
        a_s = jnp.maximum(v, 0.0) + k
        a_n = k - jnp.minimum(v, 0.0)
        a_c = 1.0 - (a_w + a_e + a_s + a_n)
        def field_body(field, carry):
            ch = field * levels + level
            q = pf[ch]
            west = jnp.where(row == 0, top[pl.ds(base + ch, 1), :], pltpu.roll(q, 1, 0))
            east = jnp.where(
                row == rows - 1, bottom[pl.ds(base + ch, 1), :], pltpu.roll(q, rows - 1, 0)
            )
            pad = jnp.zeros((rows, columns - LANES), F32)
            at_first = pltpu.roll(left[...], LANES - ch, 1)
            at_last = pltpu.roll(right[...], LANES - 1 - ch, 1)
            south = jnp.where(
                column == 0, jnp.concatenate([at_first, pad], axis=1), pltpu.roll(q, 1, 1)
            )
            north = jnp.where(
                column == columns - 1,
                jnp.concatenate([pad, at_last], axis=1),
                pltpu.roll(q, columns - 1, 1),
            )
            result = a_c * q + a_w * west + a_e * east + a_s * south + a_n * north
            parent_next[ch] = result
            moved = pltpu.roll(pltpu.roll(result, shift, 1), row_shift, 0)
            for tile, slab in enumerate(slabs):
                first = span * tile
                slab[pl.ds(pl.multiple_of(span * ch, 8), span), :] = moved[first : first + span]
                before, after = (first - 1) % rows, (first + span) % rows
                slab[pl.ds(span * channels + ch, 1), :] = moved[before : before + 1]
                slab[pl.ds((span + 1) * channels + ch, 1), :] = moved[after : after + 1]
            return carry

        return lax.fori_loop(0, pf.shape[0] // levels, field_body, carry)

    lax.fori_loop(0, levels, level_body, 0)


def pick(index, choices):
    value = choices[0][1]
    for key, other in choices[1:]:
        value = jnp.where(index == key, other, value)
    return value


def row_select_kernel(shifts, rows, anchor, *refs):
    count = len(shifts)
    slabs, messages = refs[:count], refs[count:]
    span = rows // 3
    total, columns = slabs[0].shape
    channels = total // (span + 2)
    rank = lax.axis_index("gx")
    start = anchor[0] + span * rank
    lowest, highest = lax.div(start, rows), lax.div(start + span - 1, rows)
    above, below = lax.div(start - 1, rows), lax.div(start + span, rows)
    split = jnp.where(highest > lowest, rows * highest - start, span)
    row = row_index(span)
    lanes, rim_lanes = lane_index(span), lane_index(1)

    def views(first, size, tile):
        return [
            (d, ref[first : first + size, LANES * tile : LANES * (tile + 1)])
            for d, ref in zip(shifts, slabs)
        ]

    def edges(rims, tiles, mask, ch):
        for tile in range(3):
            before = pltpu.roll(tiles[(tile + 2) % 3], (2 * ch + 1) % LANES, 1)
            after = pltpu.roll(tiles[(tile + 1) % 3], 2 * ch + 1, 1)
            rim = jnp.where(mask == 2 * ch, before, rims[tile])
            rims[tile] = jnp.where(mask == 2 * ch + 1, after, rim)

    rims = [jnp.zeros((span, LANES), F32) for _ in range(3)]
    for ch in range(channels):
        tiles = []
        for tile in range(3):
            choices = views(span * ch, span, tile)
            low, high = pick(rank - lowest, choices), pick(rank - highest, choices)
            value = jnp.where(row < split, low, high)
            messages[tile][span * ch : span * (ch + 1), :] = value
            tiles.append(value)
        edges(rims, tiles, lanes, ch)
    for side, owner in enumerate((above, below)):
        first = (span + side) * channels
        tiles = [pick(rank - owner, views(first, channels, tile)) for tile in range(3)]
        side_rims = [jnp.zeros((1, LANES), F32) for _ in range(3)]
        for ch in range(channels):
            edges(side_rims, [value[ch : ch + 1] for value in tiles], rim_lanes, ch)
        for tile in range(3):
            messages[tile][first : first + channels, :] = tiles[tile]
            messages[tile][total + span + side : total + span + side + 1, :] = side_rims[tile]
    for tile in range(3):
        messages[tile][total : total + span, :] = rims[tile]
        padding = messages[tile].shape[0] - total - span - 2
        messages[tile][total + span + 2 :, :] = jnp.zeros((padding, LANES), F32)


def nest_columns_kernel(nf, nv, nm, top, bottom, cols_next, cols_prev, block):
    channels, rows, columns = nf.shape
    height = rows + 8
    lanes = lane_index(height)
    coefs = nv.shape[0] + nm.shape[0]
    block[...] = jnp.zeros_like(block)

    def halo(target, ref, source, first_lane):
        block[target : target + 1, :] = ref[source : source + 1, first_lane : first_lane + LANES]

    def packed(first_lane, moved):
        accumulated = jnp.zeros((height, LANES), F32)
        for ch in range(channels):
            block[0:rows, :] = nf[ch, :, first_lane : first_lane + LANES]
            for at in range(3):
                here = at * channels + ch
                halo(rows + at, bottom, here, first_lane)
                halo(height - 3 + at, top, here, first_lane)
            shift = 3 * ch + (3 if moved else 0)
            inside = (lanes >= 3 * ch) & (lanes < 3 * ch + 3)
            accumulated = jnp.where(inside, pltpu.roll(block[...], shift, 1), accumulated)
        base = 3 * channels
        for cc in range(coefs):
            ref, row = (nv, cc) if cc < nv.shape[0] else (nm, cc - nv.shape[0])
            here = base + 2 * cc
            block[0:rows, :] = ref[row, :, first_lane : first_lane + LANES]
            for at in range(2):
                source = base + at * coefs + cc
                halo(rows + at, bottom, source, first_lane)
                halo(height - 2 + at, top, source, first_lane)
            shift = (here + (2 if moved else 0)) % LANES
            inside = (lanes >= here) & (lanes < here + 2)
            accumulated = jnp.where(inside, pltpu.roll(block[...], shift, 1), accumulated)
        return accumulated

    cols_next[...] = packed(columns - LANES, True)
    cols_prev[...] = packed(0, False)


def three_parts(x):
    high = x.astype(jnp.bfloat16)
    rest = x - high.astype(F32)
    middle = rest.astype(jnp.bfloat16)
    low = (rest - middle.astype(F32)).astype(jnp.bfloat16)
    return high, middle, low


def exact_dot(x, matrix):
    parts = three_parts(x)
    total = jnp.dot(parts[2], matrix, preferred_element_type=F32)
    total = total + jnp.dot(parts[1], matrix, preferred_element_type=F32)
    return total + jnp.dot(parts[0], matrix, preferred_element_type=F32)


def nest_kernel(
    ks, anchor, spread, gather, nf, nv, nm, top, bottom, left, right, *refs
):
    count = len(ks)
    received = dict(zip(ks, refs[:count]))
    result, coarse = refs[count : count + 2]
    relay, refined, forcing, weights, coefs, state, sums, final = refs[count + 2 :]
    channels, rows, columns = nf.shape
    levels = nm.shape[0]
    span_rows, span_columns = rows // 3, columns // 3
    height, width = rows + 8, columns + LANES
    tiles = width // LANES
    relay_rows = span_rows + 2
    total = relay_rows * channels
    rank_x, rank_y = lax.axis_index("gx"), lax.axis_index("gy")
    offset = anchor[1] - lax.axis_size("gy") // 2 * columns
    kind = lax.rem(rank_y, 3)
    edge = columns - offset - span_columns * kind

    lower = pick(kind, [(0, received[0][...]), (1, received[1][...]), (2, received[2][...])])
    upper = jnp.where(kind == 1, received[-2][...], received[-1][...])
    lanes = lane_index(lower.shape[0])
    relay[:, 0:LANES] = jnp.where(lanes < edge, lower, upper)
    relay[:, LANES:] = jnp.zeros((relay.shape[0], LANES), F32)
    rim_low, rim_high = lower[total : total + relay_rows], upper[total : total + relay_rows]
    odd = (lane_index(relay_rows) & 1) == 1
    rim = jnp.where(jnp.where(odd, LANES, -1) < edge, rim_low, rim_high)
    for ch in range(channels):
        sides = pltpu.roll(rim, (LANES - 2 * ch) % LANES, 1)
        relay[span_rows * ch : span_rows * (ch + 1), LANES:] = sides[0:span_rows]
        for side in (span_rows, span_rows + 1):
            here = side * channels + ch
            relay[here : here + 1, LANES:] = sides[side : side + 1]
    refined[...] = exact_dot(relay[...], spread[...])

    row = row_index(height, width)
    column = lane_index(height, width)
    local_row = jnp.where(row < rows + 4, row, row - height)
    local_column = jnp.where(column < columns + LANES // 2, column, column - width)
    global_row = rank_x * rows + local_row
    global_column = rank_y * columns + local_column
    row_distance = jnp.minimum(global_row, lax.axis_size("gx") * rows - 1 - global_row)
    column_distance = jnp.minimum(
        global_column, lax.axis_size("gy") * columns - 1 - global_column
    )
    distance = jnp.minimum(row_distance, column_distance)
    weight = nudge_floor + (1.0 - nudge_floor) * jnp.exp(
        jnp.maximum(distance, 0).astype(F32) / -relax_width
    )
    weight = jnp.where(distance < 0, 0.0, weight)
    weights[...] = weight / 9.0
    keep = 1.0 - weight
    state[...] = jnp.zeros_like(state)
    forcing[...] = jnp.zeros_like(forcing)
    edge_lanes = lane_index(height)
    relay_row = row_index(span_rows, width)

    def side_tile(first, size):
        after = pltpu.roll(right[...], lax.rem(2 * LANES - first, LANES), 1)
        before = pltpu.roll(left[...], lax.rem(2 * LANES - first - size, LANES), 1)
        inside = jnp.where(edge_lanes < LANES // 2, after, before)
        outside = (edge_lanes >= size) & (edge_lanes < LANES - size)
        return jnp.where(outside, 0.0, inside)

    def coef_field(slot, cc, ref, at):
        base = 3 * channels + cc
        coefs[slot, 0:rows, 0:columns] = ref[at]
        for step in range(2):
            source = pl.ds(base + 3 * levels * step, 1)
            coefs[slot, rows + step : rows + step + 1, 0:columns] = bottom[source, :]
            target = height - 2 + step
            coefs[slot, target : target + 1, 0:columns] = top[source, :]
        coefs[slot, :, columns:width] = side_tile(3 * channels + 2 * cc, 2)
        return coefs[slot]

    coefs[:, rows : rows + 8, :] = jnp.zeros((5, 8, width), F32)

    def level_body(level, carry):
        u = coef_field(0, level, nv, level)
        v = coef_field(1, levels + level, nv, levels + level)
        k = coef_field(2, 2 * levels + level, nm, level)
        a_w = jnp.maximum(u, 0.0) + k
        a_e = k - jnp.minimum(u, 0.0)
        a_s = jnp.maximum(v, 0.0) + k
        a_n = k - jnp.minimum(v, 0.0)
        a_c = 1.0 - (a_w + a_e + a_s + a_n)
        coefs[0] = keep * a_c
        coefs[1] = keep * a_w
        coefs[2] = keep * a_e
        coefs[3] = keep * a_s
        coefs[4] = keep * a_n

        def field_body(field, carry):
            ch = field * levels + level
            centre = refined[pl.ds(pl.multiple_of(span_rows * ch, 8), span_rows), :]
            above = refined[pl.ds(span_rows * channels + ch, 1), :]
            below = refined[pl.ds((span_rows + 1) * channels + ch, 1), :]
            before = jnp.where(relay_row == 0, above, pltpu.roll(centre, 1, 0))
            after = jnp.where(
                relay_row == span_rows - 1, below, pltpu.roll(centre, span_rows - 1, 0)
            )
            thirds = (before + 2.0 * centre, 3.0 * centre, 2.0 * centre + after)
            rims = (
                (rows, centre[span_rows - 1 :] + 2.0 * below),
                (rows + 1, 3.0 * below),
                (height - 2, 3.0 * above),
                (height - 1, 2.0 * above + centre[0:1]),
            )
            pulls = []
            for tile in range(tiles):
                part = slice(LANES * tile, LANES * (tile + 1))
                for at, value in enumerate(thirds):
                    forcing[tile, pl.ds(at, span_rows, stride=3), :] = value[:, part]
                for at, value in rims:
                    forcing[tile, at : at + 1, :] = value[:, part]
                pulls.append(weights[:, part] * forcing[tile])
            pull = jnp.concatenate(pulls, axis=1)
            state[0:rows, 0:columns] = nf[ch]
            for step in range(3):
                source = pl.ds(channels * step + ch, 1)
                state[rows + step : rows + step + 1, 0:columns] = bottom[source, :]
                target = height - 3 + step
                state[target : target + 1, 0:columns] = top[source, :]
            state[:, columns:width] = side_tile(3 * ch, 3)
            for _ in range(SUBSTEPS):
                q = state[...]
                state[...] = (
                    pull
                    + coefs[0] * q
                    + coefs[1] * pltpu.roll(q, 1, 0)
                    + coefs[2] * pltpu.roll(q, height - 1, 0)
                    + coefs[3] * pltpu.roll(q, 1, 1)
                    + coefs[4] * pltpu.roll(q, width - 1, 1)
                )
            result[ch] = state[0:rows, 0:columns]
            for tile in range(tiles - 1):
                part = slice(LANES * tile, LANES * (tile + 1))
                final[tile] = state[0:rows, part]
                sums[pl.ds(pl.multiple_of(span_rows * ch, 8), span_rows), part] = (
                    final[tile, pl.ds(0, span_rows, stride=3), :]
                    + final[tile, pl.ds(1, span_rows, stride=3), :]
                    + final[tile, pl.ds(2, span_rows, stride=3), :]
                )
            return carry

        return lax.fori_loop(0, channels // levels, field_body, carry)

    lax.fori_loop(0, levels, level_body, 0)
    coarse[...] = exact_dot(sums[...], gather[...]) / 9.0


def column_select_kernel(ks, columns, anchor, *refs):
    received = dict(zip(ks, refs[: len(ks)]))
    placed = refs[-1]
    offset = anchor[1] - lax.axis_size("gy") // 2 * columns
    lanes = lane_index(placed.shape[0])
    placed[:, 0:LANES] = received[0][...]
    for tile in (1, 2):
        own = lanes < columns - offset - LANES * tile
        placed[:, LANES * tile : LANES * (tile + 1)] = jnp.where(
            own, received[tile][...], received[tile - 3][...]
        )


def merge_kernel(shifts, anchor, parent_next, *refs):
    slabs = refs[: len(shifts)]
    merged = refs[len(shifts)]
    channels, rows, columns = parent_next.shape
    span = rows // 3
    rank_x, rank_y = lax.axis_index("gx"), lax.axis_index("gy")
    size_x, size_y = lax.axis_size("gx"), lax.axis_size("gy")
    offset = anchor[1] - size_y // 2 * columns
    shift = lax.rem(offset + columns, columns)
    row = rank_x * rows + row_index(rows, columns) - anchor[0]
    column = rank_y * columns + lane_index(rows, columns) - anchor[1]
    covered = (
        (row >= 0) & (row < size_x * span) & (column >= 0) & (column < size_y * (columns // 3))
    )
    first = anchor[0] - (rows - span) * rank_x
    row_shift = lax.rem(first + size_x * rows, rows)
    slab_row = row_index(span, columns)

    def body(ch, carry):
        tiles = []
        for tile in range(3):
            value = None
            for d, slab in zip(shifts, slabs):
                if d % 3 != tile:
                    continue
                other = slab[pl.ds(pl.multiple_of(span * ch, 8), span), :]
                place = first + span * d + slab_row
                inside = (place >= 0) & (place < rows)
                value = other if value is None else jnp.where(inside, other, value)
            tiles.append(value)
        moved = pltpu.roll(jnp.concatenate(tiles, axis=0), row_shift, 0)
        fed_back = pltpu.roll(moved, shift, 1)
        merged[ch] = jnp.where(covered, fed_back, parent_next[ch])
        return carry

    lax.fori_loop(0, channels, body, 0)


def spread_matrix(columns):
    span = columns // 3
    matrix = np.zeros((2 * LANES, columns + LANES), np.float32)

    def source(m):
        return LANES if m < 0 else (LANES + 1 if m >= span else m)

    for c in range(-2, columns + 2):
        m, j = divmod(c, 3)
        at = c % (columns + LANES)
        if j == 0:
            matrix[source(m - 1), at] += 1.0
            matrix[source(m), at] += 2.0
        elif j == 1:
            matrix[source(m), at] += 3.0
        else:
            matrix[source(m), at] += 2.0
            matrix[source(m + 1), at] += 1.0
    return jnp.asarray(matrix, jnp.bfloat16)


def gather_matrix(columns):
    matrix = np.zeros((columns, columns // 3), np.float32)
    matrix[np.arange(columns), np.arange(columns) // 3] = 1.0
    return jnp.asarray(matrix, jnp.bfloat16)


def row_routes(size, rows):
    span = rows // 3
    routes = {}
    for start in range(size * (rows - span) - 2):
        for nest in range(size):
            for at in (start + span * nest, start + span * nest + span + 1):
                routes.setdefault(nest - at // rows, set()).add((at // rows, nest))
    return {d: sorted(pairs) for d, pairs in sorted(routes.items())}


def column_routes(size):
    routes = {}
    for k in (0, 1, -1, 2, -2):
        pairs = [(size // 2 + p, 3 * p + k) for p in range(size - size // 2)]
        routes[k] = [(s, n) for s, n in pairs if 0 <= n < size]
    return routes


def per_device(
    parent_fields,
    parent_velocity,
    parent_mixing,
    nest_fields,
    nest_velocity,
    nest_mixing,
    nest_anchor,
):
    fields, levels, rows, columns = parent_fields.shape
    channels = fields * levels
    span = rows // 3
    gx, gy = lax.axis_size("gx"), lax.axis_size("gy")
    pf = parent_fields.reshape(channels, rows, columns)
    nf = nest_fields.reshape(channels, rows, columns)
    pv = parent_velocity.reshape(2 * levels, rows, columns)
    nv = nest_velocity.reshape(2 * levels, rows, columns)
    pm, nm = parent_mixing, nest_mixing

    halo_rows = 4 * channels + 6 * levels
    rows_next, rows_prev, cols_next, cols_prev = call(
        pack_kernel,
        [(halo_rows, columns)] * 2 + [(rows, LANES)] * 2,
        [pf, nf, nv, nm],
    )
    top, bottom = halo_exchange("gx", rows_next, rows_prev)
    left, right = halo_exchange("gy", cols_next, cols_prev)

    routes = row_routes(gx, rows)
    shifts = tuple(routes)
    slab_shape = ((span + 2) * channels, columns)
    parent_next, *slabs = call(
        parent_kernel,
        [(channels, rows, columns)] + [slab_shape] * 3,
        [nest_anchor, pf, pv, pm, top, bottom, left, right],
        smem=1,
    )
    slabs = [
        slabs[0] if d == 0 else lax.ppermute(slabs[d % 3], "gx", routes[d]) for d in shifts
    ]
    nest_cols_next, nest_cols_prev = call(
        nest_columns_kernel,
        [(rows + 8, LANES)] * 2,
        [nf, nv, nm, top, bottom],
        scratch=[pltpu.VMEM((rows + 8, LANES), F32)],
    )
    nest_left, nest_right = halo_exchange("gy", nest_cols_next, nest_cols_prev)
    message_rows = -(-(span + 2) * (channels + 1) // 8) * 8
    message_rows = -(-message_rows // 16) * 16
    messages = call(
        functools.partial(row_select_kernel, shifts, rows),
        [(message_rows, LANES)] * 3,
        [nest_anchor, *slabs],
        smem=1,
    )
    columns_of = column_routes(gy)
    ks = tuple(columns_of)
    received = [lax.ppermute(messages[k % 3], "gy", columns_of[k]) for k in ks]
    height, width = rows + 8, columns + LANES
    nest_result, coarse = call(
        functools.partial(nest_kernel, ks),
        [(channels, rows, columns), (span * channels, columns // 3)],
        [
            nest_anchor,
            spread_matrix(columns),
            gather_matrix(columns),
            nf,
            nv,
            nm,
            top,
            bottom,
            nest_left,
            nest_right,
            *received,
        ],
        smem=1,
        scratch=[
            pltpu.VMEM((message_rows, 2 * LANES), F32),
            pltpu.VMEM((message_rows, width), F32),
            pltpu.VMEM((width // LANES, height, LANES), F32),
            pltpu.VMEM((height, width), F32),
            pltpu.VMEM((5, height, width), F32),
            pltpu.VMEM((height, width), F32),
            pltpu.VMEM((span * channels, columns), F32),
            pltpu.VMEM((columns // LANES, rows, LANES), F32),
        ],
    )
    returned = [lax.ppermute(coarse, "gy", [(n, s) for s, n in columns_of[k]]) for k in ks]
    placed = call(
        functools.partial(column_select_kernel, ks, columns),
        [(span * channels, columns)],
        [nest_anchor, *returned],
        smem=1,
    )[0]
    fed_back = [
        placed if d == 0 else lax.ppermute(placed, "gx", [(n, s) for s, n in routes[d]])
        for d in shifts
    ]
    merged = call(
        functools.partial(merge_kernel, shifts),
        [(channels, rows, columns)],
        [nest_anchor, parent_next, *fed_back],
        smem=1,
    )[0]
    shape = parent_fields.shape
    return merged.reshape(shape), nest_result.reshape(shape)


def solution(mesh):
    placed = (
        P(None, None, "gx", "gy"),
        P(None, None, "gx", "gy"),
        P(None, "gx", "gy"),
        P(None, None, "gx", "gy"),
        P(None, None, "gx", "gy"),
        P(None, "gx", "gy"),
        P(),
    )
    return jax.shard_map(
        per_device,
        mesh=mesh,
        in_specs=placed,
        out_specs=(P(None, None, "gx", "gy"), P(None, None, "gx", "gy")),
        check_vma=False,
    )
```

```python
import functools

import jax
import jax.numpy as jnp
import numpy as np
from jax import lax
from jax.experimental import pallas as pl
from jax.experimental.pallas import tpu as pltpu
from jax.sharding import PartitionSpec as P

SUBSTEPS = 3
F32 = jnp.float32
LANES = 128
VMEM_LIMIT = 56 * 1024 * 1024
nudge_floor = 0.1
relax_width = 4.0


def whole(array):
    return pl.BlockSpec(array.shape, lambda level: (0,) * array.ndim)


def block(shape, at):
    return pl.BlockSpec(shape, lambda level: at)


def by_level(shape, dim):
    sizes = tuple(1 if i == dim else n for i, n in enumerate(shape))
    return pl.BlockSpec(sizes, lambda level: tuple(level if i == dim else 0 for i in range(len(shape))))


def call(body, grid, ins, outs, scratch=(), cost=None):
    return pl.pallas_call(
        body,
        grid=(grid,),
        out_shape=[jax.ShapeDtypeStruct(shape, F32) for shape, _ in outs],
        in_specs=[spec for _, spec in ins],
        out_specs=[spec for _, spec in outs],
        scratch_shapes=[pltpu.VMEM(shape, F32) for shape in scratch],
        cost_estimate=cost,
        compiler_params=pltpu.CompilerParams(vmem_limit_bytes=VMEM_LIMIT),
    )(*[array for array, _ in ins])


def lane_index(rows, lanes=LANES):
    return lax.broadcasted_iota(jnp.int32, (rows, lanes), 1)


def row_index(rows, lanes=LANES):
    return lax.broadcasted_iota(jnp.int32, (rows, lanes), 0)


def among(value, numbers):
    found = False
    for number in numbers:
        found = found | (value == number)
    return found


def halo_exchange(axis, to_next, to_previous):
    ends = lax.axis_size(axis) - 1
    from_previous = lax.ppermute(to_next, axis, [(i, i + 1) for i in range(ends)])
    from_next = lax.ppermute(to_previous, axis, [(i + 1, i) for i in range(ends)])
    return from_previous, from_next


def pack_kernel(pf_head, pf_tail, pf_first, pf_last, nf_head, nf_tail, nv_head, nv_tail, nm_head, nm_tail, *outs):
    rows_next, rows_prev, cols_next, cols_prev = outs
    channels, rows = pf_first.shape[:2]
    coefs = nv_head.shape[0] + nm_head.shape[0]
    lanes = lane_index(rows)
    last = jnp.zeros((rows, LANES), F32)
    first = jnp.zeros((rows, LANES), F32)
    for ch in range(channels):
        last = jnp.where(lanes == ch, pltpu.roll(pf_last[ch], (ch + 1) % LANES, 1), last)
        first = jnp.where(lanes == ch, pltpu.roll(pf_first[ch], ch, 1), first)
    cols_next[...] = last
    cols_prev[...] = first
    for ch in range(channels):
        for at in range(3):
            here = at * channels + ch
            rows_next[here : here + 1, :] = nf_tail[ch, 5 + at : 6 + at, :]
            rows_prev[here : here + 1, :] = nf_head[ch, at : at + 1, :]
    base = 3 * channels
    for cc in range(coefs):
        wind = cc < nv_head.shape[0]
        tail, head = (nv_tail, nv_head) if wind else (nm_tail, nm_head)
        row = cc if wind else cc - nv_head.shape[0]
        for at in range(2):
            here = base + at * coefs + cc
            rows_next[here : here + 1, :] = tail[row, 6 + at : 7 + at, :]
            rows_prev[here : here + 1, :] = head[row, at : at + 1, :]
    base = base + 2 * coefs
    for ch in range(channels):
        rows_next[base + ch : base + ch + 1, :] = pf_tail[ch, 7:8, :]
        rows_prev[base + ch : base + ch + 1, :] = pf_head[ch, 0:1, :]


def parent_kernel(cuts, anchor, pf, pv, pm, top, bottom, left, right, parent_next, *rest):
    slabs, rims = rest[:-1], rest[-1]
    fields, _, rows, columns = pf.shape
    level, levels = pl.program_id(0), pl.num_programs(0)
    channels = fields * levels
    span = rows // 3
    rank, size_x = lax.axis_index("gx"), lax.axis_size("gx")
    half = lax.axis_size("gy") // 2 * columns
    base = 3 * channels + 2 * 3 * levels
    shift = lax.rem(2 * columns - anchor[1] + half, columns)
    row_shift = lax.rem((rows - span) * rank + size_x * rows - anchor[0], rows)
    row = row_index(rows, columns)
    column = lane_index(rows, columns)
    lanes = lane_index(rows)
    u, v, k = pv[0, 0], pv[1, 0], pm[0]
    a_w = jnp.maximum(u, 0.0) + k
    a_e = k - jnp.minimum(u, 0.0)
    a_s = jnp.maximum(v, 0.0) + k
    a_n = k - jnp.minimum(v, 0.0)
    a_c = 1.0 - (a_w + a_e + a_s + a_n)
    pad = jnp.zeros((rows, columns - LANES), F32)

    @pl.when(level == 0)
    def _():
        rims[...] = jnp.zeros_like(rims)

    packed = [rims[tile] for tile in range(3)]
    for field in range(fields):
        ch = field * levels + level
        q = pf[field, 0]
        west = jnp.where(row == 0, top[pl.ds(base + ch, 1), :], pltpu.roll(q, 1, 0))
        east = jnp.where(
            row == rows - 1, bottom[pl.ds(base + ch, 1), :], pltpu.roll(q, rows - 1, 0)
        )
        at_first = pltpu.roll(left[...], LANES - ch, 1)
        at_last = pltpu.roll(right[...], LANES - 1 - ch, 1)
        south = jnp.where(
            column == 0, jnp.concatenate([at_first, pad], axis=1), pltpu.roll(q, 1, 1)
        )
        north = jnp.where(
            column == columns - 1,
            jnp.concatenate([pad, at_last], axis=1),
            pltpu.roll(q, columns - 1, 1),
        )
        result = a_c * q + a_w * west + a_e * east + a_s * south + a_n * north
        parent_next[field, 0] = result
        moved = pltpu.roll(pltpu.roll(result, shift, 1), row_shift, 0)
        here = level * fields + field
        tiles = [moved[:, LANES * tile : LANES * (tile + 1)] for tile in range(3)]
        for tile in range(3):
            beside = jnp.where(lanes == LANES - 1, tiles[(tile + 2) % 3], tiles[(tile + 1) % 3])
            inside = (lanes == 2 * here) | (lanes == 2 * here + 1)
            packed[tile] = jnp.where(inside, pltpu.roll(beside, 2 * here + 1, 1), packed[tile])
        for kind in range(3):
            first = span * kind
            before, after = (first - 1) % rows, (first + span) % rows
            for cut, (low, high) in enumerate(cuts):
                slab, part = slabs[3 * cut + kind], slice(LANES * low, LANES * high)
                slab[pl.ds(pl.multiple_of(span * here, 8), span), :] = moved[first : first + span, part]
                slab[pl.ds(span * channels + here, 1), :] = moved[before : before + 1, part]
                slab[pl.ds((span + 1) * channels + here, 1), :] = moved[after : after + 1, part]
    for tile in range(3):
        rims[tile] = packed[tile]

    @pl.when(level == levels - 1)
    def _():
        total = (span + 2) * channels
        for kind in range(3):
            first = span * kind
            before, after = (first - 1) % rows, (first + span) % rows
            for cut, (low, high) in enumerate(cuts):
                slab = slabs[3 * cut + kind]
                for tile in range(low, high):
                    part = slice(LANES * (tile - low), LANES * (tile - low + 1))
                    slab[total : total + span, part] = rims[tile, first : first + span]
                    slab[total + span : total + span + 1, part] = rims[tile, before : before + 1]
                    slab[total + span + 1 : total + span + 2, part] = rims[tile, after : after + 1]
                    padding = slab.shape[0] - total - span - 2
                    slab[total + span + 2 :, part] = jnp.zeros((padding, LANES), F32)


def row_select_kernel(entries, rows, channels, anchor, *refs):
    count = len(entries)
    slabs, messages = refs[:count], refs[count:]
    span = rows // 3
    rank = lax.axis_index("gx")
    start = anchor[0] + span * rank
    lowest, highest = lax.div(start, rows), lax.div(start + span - 1, rows)
    above, below = lax.div(start - 1, rows), lax.div(start + span, rows)
    split = jnp.where(highest > lowest, rows * highest - start, span)

    def pick(owner, first, size, part):
        value = slabs[0][first : first + size, part]
        for (d, ranks), slab in zip(entries[1:], slabs[1:]):
            chosen = (rank - owner == d) & among(rank, ranks)
            value = jnp.where(chosen, slab[first : first + size, part], value)
        return value

    for tile, message in enumerate(messages):
        part = slice(LANES * tile, LANES * (tile + 1))
        cells, total = span * channels, (span + 2) * channels
        for first, size in ((0, cells), (total, span)):
            row = row_index(size) & (span - 1)
            low, high = pick(lowest, first, size, part), pick(highest, first, size, part)
            message[first : first + size, :] = jnp.where(row < split, low, high)
        for first, size in ((cells, channels), (total + span, 1)):
            message[first : first + size, :] = pick(above, first, size, part)
            message[first + size : first + 2 * size, :] = pick(below, first + size, size, part)
        message[total + span + 2 :, :] = jnp.zeros((message.shape[0] - total - span - 2, LANES), F32)


def nest_columns_kernel(nf_first, nf_last, nv_first, nv_last, nm_first, nm_last, top, bottom, cols_next, cols_prev):
    channels, rows = nf_first.shape[:2]
    columns = top.shape[1]
    winds = nv_first.shape[0]
    coefs = winds + nm_first.shape[0]
    height = rows + 8
    lanes, lane = lane_index(rows), lane_index(1)

    def packed(out, nf, nv, nm, part, moved):
        main = jnp.zeros((rows, LANES), F32)
        lines = {at: jnp.zeros((1, LANES), F32) for at in range(-3, 3)}

        def add(first, size, tile, halo_rows):
            nonlocal main
            shift = (first + (size if moved else 0)) % LANES
            inside = (lanes >= first) & (lanes < first + size)
            main = jnp.where(inside, pltpu.roll(tile, shift, 1), main)
            inside = (lane >= first) & (lane < first + size)
            for at, value in halo_rows:
                lines[at] = jnp.where(inside, pltpu.roll(value, shift, 1), lines[at])

        def halos(base, step, size, at):
            pairs = []
            for n in range(size):
                here = base + n * step + at
                pairs.append((n, bottom[here : here + 1, part]))
                pairs.append((n - size, top[here : here + 1, part]))
            return pairs

        for ch in range(channels):
            add(3 * ch, 3, nf[ch], halos(0, channels, 3, ch))
        base = 3 * channels
        for cc in range(coefs):
            tile = nv[cc] if cc < winds else nm[cc - winds]
            add(base + 2 * cc, 2, tile, halos(base, coefs, 2, cc))
        out[0:rows, :] = main
        out[rows:height, :] = jnp.zeros((height - rows, LANES), F32)
        for at, line in lines.items():
            target = rows + at if at >= 0 else height + at
            out[target : target + 1, :] = line

    packed(cols_next, nf_last, nv_last, nm_last, slice(columns - LANES, columns), True)
    packed(cols_prev, nf_first, nv_first, nm_first, slice(0, LANES), False)


def three_parts(x):
    high = x.astype(jnp.bfloat16)
    rest = x - high.astype(F32)
    middle = rest.astype(jnp.bfloat16)
    low = (rest - middle.astype(F32)).astype(jnp.bfloat16)
    return high, middle, low


def exact_dot(x, matrix):
    parts = three_parts(x)
    total = jnp.dot(parts[2], matrix, preferred_element_type=F32)
    total = total + jnp.dot(parts[1], matrix, preferred_element_type=F32)
    return total + jnp.dot(parts[0], matrix, preferred_element_type=F32)


def stencil(q, coefs):
    height, width = q.shape
    return (
        coefs[0] * q
        + coefs[1] * pltpu.roll(q, 1, 0)
        + coefs[2] * pltpu.roll(q, height - 1, 0)
        + coefs[3] * pltpu.roll(q, 1, 1)
        + coefs[4] * pltpu.roll(q, width - 1, 1)
    )


def nest_start_kernel(nf, nv, nm, top, bottom, left, right, coefs, moved, weights, state):
    fields, _, rows, columns = nf.shape
    level, levels = pl.program_id(0), pl.num_programs(0)
    channels = fields * levels
    height, width = rows + 8, columns + LANES
    rank_x, rank_y = lax.axis_index("gx"), lax.axis_index("gy")
    row = row_index(height, width)
    column = lane_index(height, width)
    local_row = jnp.where(row < rows + 4, row, row - height)
    local_column = jnp.where(column < columns + LANES // 2, column, column - width)
    global_row = rank_x * rows + local_row
    global_column = rank_y * columns + local_column
    row_distance = jnp.minimum(global_row, lax.axis_size("gx") * rows - 1 - global_row)
    column_distance = jnp.minimum(
        global_column, lax.axis_size("gy") * columns - 1 - global_column
    )
    distance = jnp.minimum(row_distance, column_distance)
    weight = nudge_floor + (1.0 - nudge_floor) * jnp.exp(
        jnp.maximum(distance, 0).astype(F32) / -relax_width
    )
    weight = jnp.where(distance < 0, 0.0, weight)
    keep = 1.0 - weight
    edge_lanes = lane_index(height)

    @pl.when(level == 0)
    def _():
        weights[...] = weight / 9.0
        state[...] = jnp.zeros_like(state)

    def side_tile(first, size):
        after = pltpu.roll(right[...], lax.rem(2 * LANES - first, LANES), 1)
        before = pltpu.roll(left[...], lax.rem(2 * LANES - first - size, LANES), 1)
        inside = jnp.where(edge_lanes < LANES // 2, after, before)
        outside = (edge_lanes >= size) & (edge_lanes < LANES - size)
        return jnp.where(outside, 0.0, inside)

    def fill(slot, value, base, step, at, size, first):
        state[slot, 0:rows, 0:columns] = value
        for n in range(size):
            source = pl.ds(base + n * step + at, 1)
            state[slot, rows + n : rows + n + 1, 0:columns] = bottom[source, :]
            target = height - size + n
            state[slot, target : target + 1, 0:columns] = top[source, :]
        state[slot, :, columns:width] = side_tile(first, size)

    base = 3 * channels
    for slot, value in enumerate((nv[0, 0], nv[1, 0], nm[0])):
        cc = slot * levels + level
        fill(slot + fields, value, base, 3 * levels, cc, 2, base + 2 * cc)
    for field in range(fields):
        ch = field * levels + level
        fill(field, nf[field, 0], 0, channels, ch, 3, 3 * ch)
    u, v, k = (state[slot + fields] for slot in range(3))
    a_w = jnp.maximum(u, 0.0) + k
    a_e = k - jnp.minimum(u, 0.0)
    a_s = jnp.maximum(v, 0.0) + k
    a_n = k - jnp.minimum(v, 0.0)
    a_c = 1.0 - (a_w + a_e + a_s + a_n)
    for slot, value in enumerate((a_c, a_w, a_e, a_s, a_n)):
        coefs[0, slot] = keep * value
    for field in range(fields):
        moved[0, field] = stencil(state[field], [coefs[0, slot] for slot in range(5)])


def nest_kernel(ks, anchor, spread, gather, coefs, moved, weights, *refs):
    count = len(ks)
    received = dict(zip(ks, refs[:count]))
    result, coarse = refs[count : count + 2]
    relay, refined, forcing, state, sums, final = refs[count + 2 :]
    fields, _, rows, columns = result.shape
    level, levels = pl.program_id(0), pl.num_programs(0)
    channels = fields * levels
    span_rows, span_columns = rows // 3, columns // 3
    height, width = rows + 8, columns + LANES
    tiles = width // LANES
    relay_rows = span_rows + 2
    total = relay_rows * channels
    offset = anchor[1] - lax.axis_size("gy") // 2 * columns
    kind = lax.rem(lax.axis_index("gy"), 3)
    edge = columns - offset - span_columns * kind

    @pl.when(level == 0)
    def _():
        lower = jnp.where(kind == 1, received[1][...], received[2][...])
        lower = jnp.where(kind == 0, received[0][...], lower)
        upper = jnp.where(kind == 1, received[-2][...], received[-1][...])
        lanes = lane_index(lower.shape[0])
        relay[:, 0:LANES] = jnp.where(lanes < edge, lower, upper)
        relay[total:, LANES:] = jnp.zeros((relay.shape[0] - total, LANES), F32)
        rim_low, rim_high = lower[total : total + relay_rows], upper[total : total + relay_rows]
        odd = (lane_index(relay_rows) & 1) == 1
        rim = jnp.where(jnp.where(odd, LANES, -1) < edge, rim_low, rim_high)
        for ch in range(channels):
            sides = pltpu.roll(rim, (LANES - 2 * ch) % LANES, 1)
            relay[span_rows * ch : span_rows * (ch + 1), LANES:] = sides[0:span_rows]
            for side in (span_rows, span_rows + 1):
                here = side * channels + ch
                relay[here : here + 1, LANES:] = sides[side : side + 1]
        refined[...] = exact_dot(relay[...], spread[...])

    relay_row = row_index(span_rows, width)
    for field in range(fields):
        ch = level * fields + field
        centre = refined[pl.ds(pl.multiple_of(span_rows * ch, 8), span_rows), :]
        above = refined[pl.ds(span_rows * channels + ch, 1), :]
        below = refined[pl.ds((span_rows + 1) * channels + ch, 1), :]
        before = jnp.where(relay_row == 0, above, pltpu.roll(centre, 1, 0))
        after = jnp.where(
            relay_row == span_rows - 1, below, pltpu.roll(centre, span_rows - 1, 0)
        )
        thirds = (before + 2.0 * centre, 3.0 * centre, 2.0 * centre + after)
        rims = (
            (rows, centre[span_rows - 1 :] + 2.0 * below),
            (rows + 1, 3.0 * below),
            (height - 2, 3.0 * above),
            (height - 1, 2.0 * above + centre[0:1]),
        )
        for tile in range(tiles):
            part = slice(LANES * tile, LANES * (tile + 1))
            for at, value in enumerate(thirds):
                forcing[field, tile, pl.ds(at, span_rows, stride=3), :] = value[:, part]
            forcing[field, tile, rows + 2 : height - 2, :] = jnp.zeros((4, LANES), F32)
            for at, value in rims:
                forcing[field, tile, at : at + 1, :] = value[:, part]
    for field in range(fields):
        for tile in range(tiles):
            part = slice(LANES * tile, LANES * (tile + 1))
            pull = weights[:, part] * forcing[field, tile]
            forcing[field, tile] = pull
            state[field, :, part] = moved[0, field, :, part] + pull
    for _ in range(SUBSTEPS - 1):
        for field in range(fields):
            pull = jnp.concatenate([forcing[field, tile] for tile in range(tiles)], axis=1)
            state[field] = pull + stencil(state[field], [coefs[0, slot] for slot in range(5)])
    for field in range(fields):
        result[field, 0] = state[field, 0:rows, 0:columns]
        for tile in range(tiles - 1):
            part = slice(LANES * tile, LANES * (tile + 1))
            final[field, tile] = state[field, 0:rows, part]
            sums[span_rows * field : span_rows * (field + 1), part] = (
                final[field, tile, pl.ds(0, span_rows, stride=3), :]
                + final[field, tile, pl.ds(1, span_rows, stride=3), :]
                + final[field, tile, pl.ds(2, span_rows, stride=3), :]
            )
    coarse[...] = exact_dot(sums[...], gather[...]) / 9.0


def column_select_kernel(tile, columns, anchor, own, other, placed):
    offset = anchor[1] - lax.axis_size("gy") // 2 * columns
    inside = lane_index(placed.shape[0]) < columns - offset - LANES * tile
    placed[...] = jnp.where(inside, own[...], other[...])


def merge_kernel(entries, anchor, parent_next, *refs):
    merged = refs[-1]
    fields, _, rows, columns = parent_next.shape
    span = rows // 3
    rank_x, rank_y = lax.axis_index("gx"), lax.axis_index("gy")
    size_x, size_y = lax.axis_size("gx"), lax.axis_size("gy")
    offset = anchor[1] - size_y // 2 * columns
    shift = lax.rem(offset + columns, columns)
    row = rank_x * rows + row_index(rows, columns) - anchor[0]
    column = rank_y * columns + lane_index(rows, columns) - anchor[1]
    covered = (
        (row >= 0) & (row < size_x * span) & (column >= 0) & (column < size_y * (columns // 3))
    )
    first = anchor[0] - (rows - span) * rank_x
    row_shift = lax.rem(first + size_x * rows, rows)
    slab_row = row_index(span)
    choices = [[], [], []]
    for at, (d, ranks) in enumerate(entries):
        place = first + span * d + slab_row
        if ranks is not None:
            place = jnp.where(among(rank_x, ranks), place, -1)
        choices[d % 3].append((at, (place >= 0) & (place < rows)))
    for field in range(fields):
        tiles = []
        for tile in range(3):
            kinds = []
            for options in choices:
                value = jnp.zeros((span, LANES), F32)
                for at, inside in options:
                    slab = refs[tile * len(entries) + at]
                    value = jnp.where(inside, slab[span * field : span * (field + 1), :], value)
                kinds.append(value)
            tiles.append(jnp.concatenate(kinds, axis=0))
        moved = pltpu.roll(jnp.concatenate(tiles, axis=1), row_shift, 0)
        fed_back = pltpu.roll(moved, shift, 1)
        merged[field, 0] = jnp.where(covered, fed_back, parent_next[field, 0])


def spread_matrix(columns):
    span = columns // 3
    matrix = np.zeros((2 * LANES, columns + LANES), np.float32)

    def source(m):
        return LANES if m < 0 else (LANES + 1 if m >= span else m)

    for c in range(-2, columns + 2):
        m, j = divmod(c, 3)
        at = c % (columns + LANES)
        if j == 0:
            matrix[source(m - 1), at] += 1.0
            matrix[source(m), at] += 2.0
        elif j == 1:
            matrix[source(m), at] += 3.0
        else:
            matrix[source(m), at] += 2.0
            matrix[source(m + 1), at] += 1.0
    return jnp.asarray(matrix, jnp.bfloat16)


def gather_matrix(columns):
    matrix = np.zeros((columns, columns // 3), np.float32)
    matrix[np.arange(columns), np.arange(columns) // 3] = 1.0
    return jnp.asarray(matrix, jnp.bfloat16)


def row_routes(size, rows):
    span = rows // 3
    starts = {}
    for start in range(size * (rows - span) - 2):
        for nest in range(size):
            for owner in {(start + span * nest) // rows, (start + span * nest + span + 1) // rows}:
                starts.setdefault((owner, nest), []).append(start)
    usual, rare, limits = {}, {}, [0, size * rows]
    for (owner, nest), needed in sorted(starts.items()):
        if owner == nest:
            continue
        if len(needed) > span:
            usual.setdefault(nest - owner, []).append((owner, nest))
        else:
            rare.setdefault(nest - owner, []).append((owner, nest))
            if needed[0] == 0:
                limits[0] = max(limits[0], needed[-1] + 2)
            else:
                limits[1] = min(limits[1], needed[0] + 1)
    return usual, rare, limits


def column_routes(size):
    routes = {}
    for k in (0, 1, -2, 2, -1):
        pairs = [(size // 2 + p, 3 * p + k) for p in range(size - size // 2)]
        routes[k] = [(s, n) for s, n in pairs if 0 <= n < size]
    return routes


def backward(pairs):
    return [(n, s) for s, n in pairs]


def per_device(
    parent_fields,
    parent_velocity,
    parent_mixing,
    nest_fields,
    nest_velocity,
    nest_mixing,
    nest_anchor,
):
    fields, levels, rows, columns = shape = parent_fields.shape
    channels = fields * levels
    span, last = rows // 3, columns // LANES - 1
    gx, gy = lax.axis_size("gx"), lax.axis_size("gy")
    height, width = rows + 8, columns + LANES
    pf = parent_fields.reshape(channels, rows, columns)
    nf = nest_fields.reshape(channels, rows, columns)
    nv = nest_velocity.reshape(2 * levels, rows, columns)
    nm = nest_mixing
    anchor = (nest_anchor, pl.BlockSpec(memory_space=pltpu.SMEM))

    def row_blocks(array):
        size = (array.shape[0], 8, columns)
        return [(array, block(size, (0, 0, 0))), (array, block(size, (0, rows // 8 - 1, 0)))]

    def column_blocks(array):
        size = (array.shape[0], rows, LANES)
        return [(array, block(size, (0, 0, 0))), (array, block(size, (0, 0, last)))]

    def shaped(*size):
        return size, block(size, (0,) * len(size))

    def whole_of(arrays):
        return [(array, whole(array)) for array in arrays]

    halo_rows = 4 * channels + 6 * levels
    rows_next, rows_prev, cols_next, cols_prev = call(
        pack_kernel,
        1,
        row_blocks(pf) + column_blocks(pf) + row_blocks(nf) + row_blocks(nv) + row_blocks(nm),
        [shaped(halo_rows, columns)] * 2 + [shaped(rows, LANES)] * 2,
    )
    top, bottom = halo_exchange("gx", rows_next, rows_prev)
    left, right = halo_exchange("gy", cols_next, cols_prev)

    usual, rare, limits = row_routes(gx, rows)
    rarely = (nest_anchor[0] < limits[0]) | (nest_anchor[0] >= limits[1])
    cuts = ((0, 3),)
    message_rows = -(-((span + 2) * (channels + 1)) // 16) * 16
    parent_next, *slabs = call(
        functools.partial(parent_kernel, cuts),
        levels,
        [
            anchor,
            (parent_fields, by_level(shape, 1)),
            (parent_velocity, by_level(parent_velocity.shape, 1)),
            (parent_mixing, by_level(parent_mixing.shape, 0)),
        ]
        + whole_of([top, bottom, left, right]),
        [(shape, by_level(shape, 1))]
        + [shaped(message_rows, LANES * (high - low)) for low, high in cuts for _ in range(3)],
        scratch=[(3, rows, LANES)],
    )
    nest_cols_next, nest_cols_prev = call(
        nest_columns_kernel,
        1,
        column_blocks(nf) + column_blocks(nv) + column_blocks(nm) + whole_of([top, bottom]),
        [shaped(height, LANES)] * 2,
    )
    nest_left, nest_right = halo_exchange("gy", nest_cols_next, nest_cols_prev)
    coefs, moved, weights = call(
        nest_start_kernel,
        levels,
        [
            (nest_fields, by_level(shape, 1)),
            (nest_velocity, by_level(nest_velocity.shape, 1)),
            (nest_mixing, by_level(nest_mixing.shape, 0)),
        ]
        + whole_of([top, bottom, nest_left, nest_right]),
        [
            ((levels, 5, height, width), by_level((levels, 5, height, width), 0)),
            ((levels, fields, height, width), by_level((levels, fields, height, width), 0)),
            shaped(height, width),
        ],
        scratch=[(fields + 3, height, width)],
    )

    entries = [(0, None)]
    entries += [(d, [n for _, n in pairs]) for d, pairs in usual.items()]
    entries += [(d, [n for _, n in pairs]) for d, pairs in rare.items()]
    messages = []
    for cut, (low, high) in enumerate(cuts):
        kinds = slabs[3 * cut : 3 * cut + 3]
        common = [lax.ppermute(kinds[d % 3], "gx", pairs) for d, pairs in usual.items()]
        others = lax.cond(
            rarely,
            lambda *kinds: [lax.ppermute(kinds[d % 3], "gx", pairs) for d, pairs in rare.items()],
            lambda *kinds: [kinds[d % 3] for d in rare],
            *kinds,
        )
        messages += call(
            functools.partial(row_select_kernel, entries, rows, channels),
            1,
            [anchor] + whole_of([kinds[0], *common, *others]),
            [shaped(message_rows, LANES)] * (high - low),
        )
    columns_of = column_routes(gy)
    ks = tuple(columns_of)
    received = [lax.ppermute(messages[k % 3], "gy", columns_of[k]) for k in ks]
    nest_result, coarse = call(
        functools.partial(nest_kernel, ks),
        levels,
        [anchor]
        + whole_of([spread_matrix(columns), gather_matrix(columns)])
        + [(coefs, by_level(coefs.shape, 0)), (moved, by_level(moved.shape, 0))]
        + whole_of([weights, *received]),
        [
            (shape, by_level(shape, 1)),
            (
                (span * channels, LANES),
                pl.BlockSpec((span * fields, LANES), lambda level: (level, 0)),
            ),
        ],
        scratch=[
            (message_rows, 2 * LANES),
            (message_rows, width),
            (fields, width // LANES, height, LANES),
            (fields, height, width),
            (span * fields, columns),
            (fields, columns // LANES, rows, LANES),
        ],
    )

    returned = {k: lax.ppermute(coarse, "gy", backward(columns_of[k])) for k in ks}
    placed = [returned[0]]
    for tile in (1, 2):
        own, other = returned[tile], returned[tile - 3]
        placed += call(
            functools.partial(column_select_kernel, tile, columns),
            1,
            [anchor] + whole_of([own, other]),
            [shaped(span * channels, LANES)],
        )
    common = [
        [lax.ppermute(tile, "gx", backward(pairs)) for pairs in usual.values()] for tile in placed
    ]
    others = lax.cond(
        rarely,
        lambda *tiles: [
            [lax.ppermute(tile, "gx", backward(pairs)) for pairs in rare.values()] for tile in tiles
        ],
        lambda *tiles: [[tile for _ in rare] for tile in tiles],
        *placed,
    )
    entries = [(0, None)]
    entries += [(d, [s for s, _ in pairs]) for d, pairs in usual.items()]
    entries += [(d, [s for s, _ in pairs]) for d, pairs in rare.items()]
    slab_block = pl.BlockSpec((span * fields, LANES), lambda level: (level, 0))
    slabs = [
        (array, slab_block)
        for tile in range(3)
        for array in (placed[tile], *common[tile], *others[tile])
    ]
    merged = call(
        functools.partial(merge_kernel, entries),
        levels,
        [anchor, (parent_next, by_level(shape, 1))] + slabs,
        [(shape, by_level(shape, 1))],
    )[0]
    return merged, nest_result


def solution(mesh):
    placed = (
        P(None, None, "gx", "gy"),
        P(None, None, "gx", "gy"),
        P(None, "gx", "gy"),
        P(None, None, "gx", "gy"),
        P(None, None, "gx", "gy"),
        P(None, "gx", "gy"),
        P(),
    )
    return jax.shard_map(
        per_device,
        mesh=mesh,
        in_specs=placed,
        out_specs=(P(None, None, "gx", "gy"), P(None, None, "gx", "gy")),
        check_vma=False,
    )
```

```python
import functools

import jax
import jax.numpy as jnp
import numpy as np
from jax import lax
from jax.experimental import pallas as pl
from jax.experimental.pallas import tpu as pltpu
from jax.sharding import PartitionSpec as P

SUBSTEPS = 3
F32 = jnp.float32
LANES = 128
VMEM_LIMIT = 56 * 1024 * 1024
nudge_floor = 0.1
relax_width = 4.0


def whole(array):
    return pl.BlockSpec(array.shape, lambda level: (0,) * array.ndim)


def block(shape, at):
    return pl.BlockSpec(shape, lambda level: at)


def by_level(shape, dim):
    sizes = tuple(1 if i == dim else n for i, n in enumerate(shape))
    return pl.BlockSpec(sizes, lambda level: tuple(level if i == dim else 0 for i in range(len(shape))))


def call(body, grid, ins, outs, scratch=(), cost=None):
    return pl.pallas_call(
        body,
        grid=(grid,),
        out_shape=[jax.ShapeDtypeStruct(shape, F32) for shape, _ in outs],
        in_specs=[spec for _, spec in ins],
        out_specs=[spec for _, spec in outs],
        scratch_shapes=[pltpu.VMEM(shape, F32) for shape in scratch],
        cost_estimate=cost,
        compiler_params=pltpu.CompilerParams(vmem_limit_bytes=VMEM_LIMIT),
    )(*[array for array, _ in ins])


def lane_index(rows, lanes=LANES):
    return lax.broadcasted_iota(jnp.int32, (rows, lanes), 1)


def row_index(rows, lanes=LANES):
    return lax.broadcasted_iota(jnp.int32, (rows, lanes), 0)


def among(value, numbers):
    found = False
    for number in numbers:
        found = found | (value == number)
    return found


def halo_exchange(axis, to_next, to_previous):
    ends = lax.axis_size(axis) - 1
    from_previous = lax.ppermute(to_next, axis, [(i, i + 1) for i in range(ends)])
    from_next = lax.ppermute(to_previous, axis, [(i + 1, i) for i in range(ends)])
    return from_previous, from_next


def pack_kernel(pf_head, pf_tail, pf_first, pf_last, nf_head, nf_tail, nv_head, nv_tail, nm_head, nm_tail, *outs):
    rows_next, rows_prev, cols_next, cols_prev = outs
    channels, rows = pf_first.shape[:2]
    coefs = nv_head.shape[0] + nm_head.shape[0]
    lanes = lane_index(rows)
    last = jnp.zeros((rows, LANES), F32)
    first = jnp.zeros((rows, LANES), F32)
    for ch in range(channels):
        last = jnp.where(lanes == ch, pltpu.roll(pf_last[ch], (ch + 1) % LANES, 1), last)
        first = jnp.where(lanes == ch, pltpu.roll(pf_first[ch], ch, 1), first)
    cols_next[...] = last
    cols_prev[...] = first
    for ch in range(channels):
        for at in range(3):
            here = at * channels + ch
            rows_next[here : here + 1, :] = nf_tail[ch, 5 + at : 6 + at, :]
            rows_prev[here : here + 1, :] = nf_head[ch, at : at + 1, :]
    base = 3 * channels
    for cc in range(coefs):
        wind = cc < nv_head.shape[0]
        tail, head = (nv_tail, nv_head) if wind else (nm_tail, nm_head)
        row = cc if wind else cc - nv_head.shape[0]
        for at in range(2):
            here = base + at * coefs + cc
            rows_next[here : here + 1, :] = tail[row, 6 + at : 7 + at, :]
            rows_prev[here : here + 1, :] = head[row, at : at + 1, :]
    base = base + 2 * coefs
    for ch in range(channels):
        rows_next[base + ch : base + ch + 1, :] = pf_tail[ch, 7:8, :]
        rows_prev[base + ch : base + ch + 1, :] = pf_head[ch, 0:1, :]


def parent_kernel(cuts, kinds, anchor, pf, pv, pm, top, bottom, left, right, parent_next, *rest):
    slabs, rims = rest[:-1], rest[-1]
    fields, _, rows, columns = pf.shape
    level, levels = pl.program_id(0), pl.num_programs(0)
    channels = fields * levels
    span = rows // 3
    rank, size_x = lax.axis_index("gx"), lax.axis_size("gx")
    half = lax.axis_size("gy") // 2 * columns
    base = 3 * channels + 2 * 3 * levels
    shift = lax.rem(2 * columns - anchor[1] + half, columns)
    row_shift = lax.rem((rows - span) * rank + size_x * rows - anchor[0], rows)
    row = row_index(rows, columns)
    column = lane_index(rows, columns)
    lanes = lane_index(rows)
    u, v, k = pv[0, 0], pv[1, 0], pm[0]
    a_w = jnp.maximum(u, 0.0) + k
    a_e = k - jnp.minimum(u, 0.0)
    a_s = jnp.maximum(v, 0.0) + k
    a_n = k - jnp.minimum(v, 0.0)
    a_c = 1.0 - (a_w + a_e + a_s + a_n)
    pad = jnp.zeros((rows, columns - LANES), F32)

    def rows_by_kind(value):
        third = [
            (
                value[span * kind : span * (kind + 1)],
                value[(span * kind - 1) % rows : (span * kind - 1) % rows + 1],
                value[span * (kind + 1) % rows : span * (kind + 1) % rows + 1],
            )
            for kind in range(3)
        ]
        for ranks_of in kinds:
            (kind, _), *others = ranks_of
            picked = third[kind]
            for kind, ranks in others:
                chosen = among(rank, ranks)
                picked = [jnp.where(chosen, new, old) for new, old in zip(third[kind], picked)]
            yield picked

    @pl.when(level == 0)
    def _():
        rims[...] = jnp.zeros_like(rims)

    packed = [rims[tile] for tile in range(3)]
    for field in range(fields):
        ch = field * levels + level
        q = pf[field, 0]
        west = jnp.where(row == 0, top[pl.ds(base + ch, 1), :], pltpu.roll(q, 1, 0))
        east = jnp.where(
            row == rows - 1, bottom[pl.ds(base + ch, 1), :], pltpu.roll(q, rows - 1, 0)
        )
        at_first = pltpu.roll(left[...], LANES - ch, 1)
        at_last = pltpu.roll(right[...], LANES - 1 - ch, 1)
        south = jnp.where(
            column == 0, jnp.concatenate([at_first, pad], axis=1), pltpu.roll(q, 1, 1)
        )
        north = jnp.where(
            column == columns - 1,
            jnp.concatenate([pad, at_last], axis=1),
            pltpu.roll(q, columns - 1, 1),
        )
        result = a_c * q + a_w * west + a_e * east + a_s * south + a_n * north
        parent_next[field, 0] = result
        moved = pltpu.roll(pltpu.roll(result, shift, 1), row_shift, 0)
        here = level * fields + field
        tiles = [moved[:, LANES * tile : LANES * (tile + 1)] for tile in range(3)]
        for tile in range(3):
            beside = jnp.where(lanes == LANES - 1, tiles[(tile + 2) % 3], tiles[(tile + 1) % 3])
            inside = (lanes == 2 * here) | (lanes == 2 * here + 1)
            packed[tile] = jnp.where(inside, pltpu.roll(beside, 2 * here + 1, 1), packed[tile])
        for at, (cells, before, after) in enumerate(rows_by_kind(moved)):
            for cut, (low, high) in enumerate(cuts):
                slab, part = slabs[len(kinds) * cut + at], slice(LANES * low, LANES * high)
                slab[pl.ds(pl.multiple_of(span * here, 8), span), :] = cells[:, part]
                slab[pl.ds(span * channels + here, 1), :] = before[:, part]
                slab[pl.ds((span + 1) * channels + here, 1), :] = after[:, part]
    for tile in range(3):
        rims[tile] = packed[tile]

    @pl.when(level == levels - 1)
    def _():
        total = (span + 2) * channels
        for tile in range(3):
            for at, (cells, before, after) in enumerate(rows_by_kind(rims[tile])):
                for cut, (low, high) in enumerate(cuts):
                    if not low <= tile < high:
                        continue
                    slab = slabs[len(kinds) * cut + at]
                    part = slice(LANES * (tile - low), LANES * (tile - low + 1))
                    slab[total : total + span, part] = cells
                    slab[total + span : total + span + 1, part] = before
                    slab[total + span + 1 : total + span + 2, part] = after
                    padding = slab.shape[0] - total - span - 2
                    slab[total + span + 2 :, part] = jnp.zeros((padding, LANES), F32)


def row_select_kernel(entries, rows, channels, anchor, *refs):
    count = len(entries)
    slabs, messages = refs[:count], refs[count:]
    span = rows // 3
    rank = lax.axis_index("gx")
    start = anchor[0] + span * rank
    lowest, highest = lax.div(start, rows), lax.div(start + span - 1, rows)
    above, below = lax.div(start - 1, rows), lax.div(start + span, rows)
    split = jnp.where(highest > lowest, rows * highest - start, span)

    def pick(owner, first, size, part):
        value = slabs[0][first : first + size, part]
        for senders, slab in zip(entries[1:], slabs[1:]):
            chosen = False
            for d, ranks in senders:
                chosen = chosen | ((rank - owner == d) & among(rank, ranks))
            value = jnp.where(chosen, slab[first : first + size, part], value)
        return value

    for tile, message in enumerate(messages):
        part = slice(LANES * tile, LANES * (tile + 1))
        cells, total = span * channels, (span + 2) * channels
        for first, size in ((0, cells), (total, span)):
            row = row_index(size) & (span - 1)
            low, high = pick(lowest, first, size, part), pick(highest, first, size, part)
            message[first : first + size, :] = jnp.where(row < split, low, high)
        for first, size in ((cells, channels), (total + span, 1)):
            message[first : first + size, :] = pick(above, first, size, part)
            message[first + size : first + 2 * size, :] = pick(below, first + size, size, part)
        message[total + span + 2 :, :] = jnp.zeros((message.shape[0] - total - span - 2, LANES), F32)


def nest_columns_kernel(nf_first, nf_last, nv_first, nv_last, nm_first, nm_last, top, bottom, cols_next, cols_prev):
    channels, rows = nf_first.shape[:2]
    columns = top.shape[1]
    winds = nv_first.shape[0]
    coefs = winds + nm_first.shape[0]
    height = rows + 8
    lanes, lane = lane_index(rows), lane_index(1)

    def packed(out, nf, nv, nm, part, moved):
        main = jnp.zeros((rows, LANES), F32)
        lines = {at: jnp.zeros((1, LANES), F32) for at in range(-3, 3)}

        def add(first, size, tile, halo_rows):
            nonlocal main
            shift = (first + (size if moved else 0)) % LANES
            inside = (lanes >= first) & (lanes < first + size)
            main = jnp.where(inside, pltpu.roll(tile, shift, 1), main)
            inside = (lane >= first) & (lane < first + size)
            for at, value in halo_rows:
                lines[at] = jnp.where(inside, pltpu.roll(value, shift, 1), lines[at])

        def halos(base, step, size, at):
            pairs = []
            for n in range(size):
                here = base + n * step + at
                pairs.append((n, bottom[here : here + 1, part]))
                pairs.append((n - size, top[here : here + 1, part]))
            return pairs

        for ch in range(channels):
            add(3 * ch, 3, nf[ch], halos(0, channels, 3, ch))
        base = 3 * channels
        for cc in range(coefs):
            tile = nv[cc] if cc < winds else nm[cc - winds]
            add(base + 2 * cc, 2, tile, halos(base, coefs, 2, cc))
        out[0:rows, :] = main
        out[rows:height, :] = jnp.zeros((height - rows, LANES), F32)
        for at, line in lines.items():
            target = rows + at if at >= 0 else height + at
            out[target : target + 1, :] = line

    packed(cols_next, nf_last, nv_last, nm_last, slice(columns - LANES, columns), True)
    packed(cols_prev, nf_first, nv_first, nm_first, slice(0, LANES), False)


def three_parts(x):
    high = x.astype(jnp.bfloat16)
    rest = x - high.astype(F32)
    middle = rest.astype(jnp.bfloat16)
    low = (rest - middle.astype(F32)).astype(jnp.bfloat16)
    return high, middle, low


def exact_dot(x, matrix):
    parts = three_parts(x)
    total = jnp.dot(parts[2], matrix, preferred_element_type=F32)
    total = total + jnp.dot(parts[1], matrix, preferred_element_type=F32)
    return total + jnp.dot(parts[0], matrix, preferred_element_type=F32)


def stencil(q, coefs):
    height, width = q.shape
    return (
        coefs[0] * q
        + coefs[1] * pltpu.roll(q, 1, 0)
        + coefs[2] * pltpu.roll(q, height - 1, 0)
        + coefs[3] * pltpu.roll(q, 1, 1)
        + coefs[4] * pltpu.roll(q, width - 1, 1)
    )


def nest_start_kernel(nf, nv, nm, top, bottom, left, right, coefs, moved, weights, state):
    fields, _, rows, columns = nf.shape
    level, levels = pl.program_id(0), pl.num_programs(0)
    channels = fields * levels
    height, width = rows + 8, columns + LANES
    rank_x, rank_y = lax.axis_index("gx"), lax.axis_index("gy")
    row = row_index(height, width)
    column = lane_index(height, width)
    local_row = jnp.where(row < rows + 4, row, row - height)
    local_column = jnp.where(column < columns + LANES // 2, column, column - width)
    global_row = rank_x * rows + local_row
    global_column = rank_y * columns + local_column
    row_distance = jnp.minimum(global_row, lax.axis_size("gx") * rows - 1 - global_row)
    column_distance = jnp.minimum(
        global_column, lax.axis_size("gy") * columns - 1 - global_column
    )
    distance = jnp.minimum(row_distance, column_distance)
    weight = nudge_floor + (1.0 - nudge_floor) * jnp.exp(
        jnp.maximum(distance, 0).astype(F32) / -relax_width
    )
    weight = jnp.where(distance < 0, 0.0, weight)
    keep = 1.0 - weight
    edge_lanes = lane_index(height)

    @pl.when(level == 0)
    def _():
        weights[...] = weight / 9.0
        state[...] = jnp.zeros_like(state)

    def side_tile(first, size):
        after = pltpu.roll(right[...], lax.rem(2 * LANES - first, LANES), 1)
        before = pltpu.roll(left[...], lax.rem(2 * LANES - first - size, LANES), 1)
        inside = jnp.where(edge_lanes < LANES // 2, after, before)
        outside = (edge_lanes >= size) & (edge_lanes < LANES - size)
        return jnp.where(outside, 0.0, inside)

    def fill(slot, value, base, step, at, size, first):
        state[slot, 0:rows, 0:columns] = value
        for n in range(size):
            source = pl.ds(base + n * step + at, 1)
            state[slot, rows + n : rows + n + 1, 0:columns] = bottom[source, :]
            target = height - size + n
            state[slot, target : target + 1, 0:columns] = top[source, :]
        state[slot, :, columns:width] = side_tile(first, size)

    base = 3 * channels
    for slot, value in enumerate((nv[0, 0], nv[1, 0], nm[0])):
        cc = slot * levels + level
        fill(slot + fields, value, base, 3 * levels, cc, 2, base + 2 * cc)
    for field in range(fields):
        ch = field * levels + level
        fill(field, nf[field, 0], 0, channels, ch, 3, 3 * ch)
    u, v, k = (state[slot + fields] for slot in range(3))
    a_w = jnp.maximum(u, 0.0) + k
    a_e = k - jnp.minimum(u, 0.0)
    a_s = jnp.maximum(v, 0.0) + k
    a_n = k - jnp.minimum(v, 0.0)
    a_c = 1.0 - (a_w + a_e + a_s + a_n)
    for slot, value in enumerate((a_c, a_w, a_e, a_s, a_n)):
        coefs[0, slot] = keep * value
    for field in range(fields):
        moved[0, field] = stencil(state[field], [coefs[0, slot] for slot in range(5)])


def nest_kernel(ks, anchor, spread, gather, coefs, moved, weights, *refs):
    count = len(ks)
    received = dict(zip(ks, refs[:count]))
    result, coarse = refs[count : count + 2]
    relay, refined, forcing, state, sums, final = refs[count + 2 :]
    fields, _, rows, columns = result.shape
    level, levels = pl.program_id(0), pl.num_programs(0)
    channels = fields * levels
    span_rows, span_columns = rows // 3, columns // 3
    height, width = rows + 8, columns + LANES
    tiles = width // LANES
    relay_rows = span_rows + 2
    total = relay_rows * channels
    offset = anchor[1] - lax.axis_size("gy") // 2 * columns
    kind = lax.rem(lax.axis_index("gy"), 3)
    edge = columns - offset - span_columns * kind

    @pl.when(level == 0)
    def _():
        lower = jnp.where(kind == 1, received[1][...], received[2][...])
        lower = jnp.where(kind == 0, received[0][...], lower)
        upper = jnp.where(kind == 1, received[-2][...], received[-1][...])
        lanes = lane_index(lower.shape[0])
        relay[:, 0:LANES] = jnp.where(lanes < edge, lower, upper)
        relay[total:, LANES:] = jnp.zeros((relay.shape[0] - total, LANES), F32)
        rim_low, rim_high = lower[total : total + relay_rows], upper[total : total + relay_rows]
        odd = (lane_index(relay_rows) & 1) == 1
        rim = jnp.where(jnp.where(odd, LANES, -1) < edge, rim_low, rim_high)
        for ch in range(channels):
            sides = pltpu.roll(rim, (LANES - 2 * ch) % LANES, 1)
            relay[span_rows * ch : span_rows * (ch + 1), LANES:] = sides[0:span_rows]
            for side in (span_rows, span_rows + 1):
                here = side * channels + ch
                relay[here : here + 1, LANES:] = sides[side : side + 1]
        refined[...] = exact_dot(relay[...], spread[...])

    relay_row = row_index(span_rows, width)
    for field in range(fields):
        ch = level * fields + field
        centre = refined[pl.ds(pl.multiple_of(span_rows * ch, 8), span_rows), :]
        above = refined[pl.ds(span_rows * channels + ch, 1), :]
        below = refined[pl.ds((span_rows + 1) * channels + ch, 1), :]
        before = jnp.where(relay_row == 0, above, pltpu.roll(centre, 1, 0))
        after = jnp.where(
            relay_row == span_rows - 1, below, pltpu.roll(centre, span_rows - 1, 0)
        )
        thirds = (before + 2.0 * centre, 3.0 * centre, 2.0 * centre + after)
        rims = (
            (rows, centre[span_rows - 1 :] + 2.0 * below),
            (rows + 1, 3.0 * below),
            (height - 2, 3.0 * above),
            (height - 1, 2.0 * above + centre[0:1]),
        )
        for tile in range(tiles):
            part = slice(LANES * tile, LANES * (tile + 1))
            for at, value in enumerate(thirds):
                forcing[field, tile, pl.ds(at, span_rows, stride=3), :] = value[:, part]
            forcing[field, tile, rows + 2 : height - 2, :] = jnp.zeros((4, LANES), F32)
            for at, value in rims:
                forcing[field, tile, at : at + 1, :] = value[:, part]
    for field in range(fields):
        for tile in range(tiles):
            part = slice(LANES * tile, LANES * (tile + 1))
            pull = weights[:, part] * forcing[field, tile]
            forcing[field, tile] = pull
            state[field, :, part] = moved[0, field, :, part] + pull
    for _ in range(SUBSTEPS - 1):
        for field in range(fields):
            pull = jnp.concatenate([forcing[field, tile] for tile in range(tiles)], axis=1)
            state[field] = pull + stencil(state[field], [coefs[0, slot] for slot in range(5)])
    for field in range(fields):
        result[field, 0] = state[field, 0:rows, 0:columns]
        for tile in range(tiles - 1):
            part = slice(LANES * tile, LANES * (tile + 1))
            final[field, tile] = state[field, 0:rows, part]
            sums[span_rows * field : span_rows * (field + 1), part] = (
                final[field, tile, pl.ds(0, span_rows, stride=3), :]
                + final[field, tile, pl.ds(1, span_rows, stride=3), :]
                + final[field, tile, pl.ds(2, span_rows, stride=3), :]
            )
    coarse[...] = exact_dot(sums[...], gather[...]) / 9.0


def column_select_kernel(columns, anchor, *refs):
    placed = refs[-1]
    offset = anchor[1] - lax.axis_size("gy") // 2 * columns
    for tile in (1, 2):
        own, other = refs[2 * tile - 2], refs[2 * tile - 1]
        inside = lane_index(placed.shape[0]) < columns - offset - LANES * tile
        placed[:, LANES * (tile - 1) : LANES * tile] = jnp.where(inside, own[...], other[...])


def merge_kernel(entries, cuts, anchor, parent_next, *refs):
    merged = refs[-1]
    fields, _, rows, columns = parent_next.shape
    span = rows // 3
    rank_x, rank_y = lax.axis_index("gx"), lax.axis_index("gy")
    size_x, size_y = lax.axis_size("gx"), lax.axis_size("gy")
    offset = anchor[1] - size_y // 2 * columns
    shift = lax.rem(offset + columns, columns)
    row = rank_x * rows + row_index(rows, columns) - anchor[0]
    column = rank_y * columns + lane_index(rows, columns) - anchor[1]
    covered = (
        (row >= 0) & (row < size_x * span) & (column >= 0) & (column < size_y * (columns // 3))
    )
    first = anchor[0] - (rows - span) * rank_x
    row_shift = lax.rem(first + size_x * rows, rows)
    slab_row = row_index(span)
    choices = [[], [], []]
    for at, receivers in enumerate(entries):
        for d, ranks in receivers:
            place = first + span * d + slab_row
            if ranks is not None:
                place = jnp.where(among(rank_x, ranks), place, -1)
            choices[d % 3].append((at, (place >= 0) & (place < rows)))
    where = [(cut, tile - low) for cut, (low, high) in enumerate(cuts) for tile in range(low, high)]
    for field in range(fields):
        tiles = []
        for tile in range(3):
            kinds = []
            for options in choices:
                value = jnp.zeros((span, LANES), F32)
                for at, inside in options:
                    cut, lane_tile = where[tile]
                    slab = refs[cut * len(entries) + at]
                    part = slice(LANES * lane_tile, LANES * (lane_tile + 1))
                    cells = slab[span * field : span * (field + 1), part]
                    value = jnp.where(inside, cells, value)
                kinds.append(value)
            tiles.append(jnp.concatenate(kinds, axis=0))
        moved = pltpu.roll(jnp.concatenate(tiles, axis=1), row_shift, 0)
        fed_back = pltpu.roll(moved, shift, 1)
        merged[field, 0] = jnp.where(covered, fed_back, parent_next[field, 0])


def spread_matrix(columns):
    span = columns // 3
    matrix = np.zeros((2 * LANES, columns + LANES), np.float32)

    def source(m):
        return LANES if m < 0 else (LANES + 1 if m >= span else m)

    for c in range(-2, columns + 2):
        m, j = divmod(c, 3)
        at = c % (columns + LANES)
        if j == 0:
            matrix[source(m - 1), at] += 1.0
            matrix[source(m), at] += 2.0
        elif j == 1:
            matrix[source(m), at] += 3.0
        else:
            matrix[source(m), at] += 2.0
            matrix[source(m + 1), at] += 1.0
    return jnp.asarray(matrix, jnp.bfloat16)


def gather_matrix(columns):
    matrix = np.zeros((columns, columns // 3), np.float32)
    matrix[np.arange(columns), np.arange(columns) // 3] = 1.0
    return jnp.asarray(matrix, jnp.bfloat16)


def row_routes(size, rows):
    span = rows // 3
    starts = {}
    for start in range(size * (rows - span) - 2):
        for nest in range(size):
            for owner in {(start + span * nest) // rows, (start + span * nest + span + 1) // rows}:
                starts.setdefault((owner, nest), []).append(start)
    usual, rare, limits = {}, {}, [0, size * rows]
    for (owner, nest), needed in sorted(starts.items()):
        if owner == nest:
            continue
        if len(needed) > span:
            usual.setdefault(nest - owner, []).append((owner, nest))
        else:
            rare.setdefault(nest - owner, []).append((owner, nest))
            if needed[0] == 0:
                limits[0] = max(limits[0], needed[-1] + 2)
            else:
                limits[1] = min(limits[1], needed[0] + 1)
    groups = []
    for d in range(1, size):
        pairs = [usual.get(e, []) + rare.get(e, []) for e in (d, -d)]
        apart = all(not {p[end] for p in pairs[0]} & {p[end] for p in pairs[1]} for end in (0, 1))
        groups += [(d, -d)] if apart else [(d,), (-d,)]
    return groups, usual, rare, limits


def column_routes(size):
    routes = {}
    for k in (0, 1, -2, 2, -1):
        pairs = [(size // 2 + p, 3 * p + k) for p in range(size - size // 2)]
        routes[k] = [(s, n) for s, n in pairs if 0 <= n < size]
    return routes


def per_device(
    parent_fields,
    parent_velocity,
    parent_mixing,
    nest_fields,
    nest_velocity,
    nest_mixing,
    nest_anchor,
):
    fields, levels, rows, columns = shape = parent_fields.shape
    channels = fields * levels
    span, last = rows // 3, columns // LANES - 1
    gx, gy = lax.axis_size("gx"), lax.axis_size("gy")
    height, width = rows + 8, columns + LANES
    pf = parent_fields.reshape(channels, rows, columns)
    nf = nest_fields.reshape(channels, rows, columns)
    nv = nest_velocity.reshape(2 * levels, rows, columns)
    nm = nest_mixing
    anchor = (nest_anchor, pl.BlockSpec(memory_space=pltpu.SMEM))

    def row_blocks(array):
        size = (array.shape[0], 8, columns)
        return [(array, block(size, (0, 0, 0))), (array, block(size, (0, rows // 8 - 1, 0)))]

    def column_blocks(array):
        size = (array.shape[0], rows, LANES)
        return [(array, block(size, (0, 0, 0))), (array, block(size, (0, 0, last)))]

    def shaped(*size):
        return size, block(size, (0,) * len(size))

    def whole_of(arrays):
        return [(array, whole(array)) for array in arrays]

    halo_rows = 4 * channels + 6 * levels
    rows_next, rows_prev, cols_next, cols_prev = call(
        pack_kernel,
        1,
        row_blocks(pf) + column_blocks(pf) + row_blocks(nf) + row_blocks(nv) + row_blocks(nm),
        [shaped(halo_rows, columns)] * 2 + [shaped(rows, LANES)] * 2,
    )
    top, bottom = halo_exchange("gx", rows_next, rows_prev)
    left, right = halo_exchange("gy", cols_next, cols_prev)

    groups, usual, rare, limits = row_routes(gx, rows)
    rarely = (nest_anchor[0] < limits[0]) | (nest_anchor[0] >= limits[1])
    kinds = [[(0, None)], [(1, None)], [(2, None)]]
    kind_of = {}
    for group in groups:
        if len(group) == 1:
            kind_of[group] = group[0] % 3
        else:
            by_rank = [(d % 3, [a for a, _ in usual.get(d, []) + rare.get(d, [])]) for d in group]
            kind_of[group] = len(kinds)
            kinds.append(by_rank)

    def exchange(routes, arrays, turn):
        received, entries = [], []
        for group in groups:
            pairs = [turn(pair) for d in group for pair in routes.get(d, [])]
            if pairs:
                received.append(lax.ppermute(arrays[kind_of[group]], "gx", pairs))
                entries.append([(d, [turn(pair)[1] for pair in routes.get(d, [])]) for d in group])
        return received, entries

    cuts = ((0, 1), (1, 3))
    message_rows = -(-((span + 2) * (channels + 1)) // 16) * 16
    nest_cols_next, nest_cols_prev = call(
        nest_columns_kernel,
        1,
        column_blocks(nf) + column_blocks(nv) + column_blocks(nm) + whole_of([top, bottom]),
        [shaped(height, LANES)] * 2,
    )
    left, right, nest_cols_next, nest_cols_prev = lax.optimization_barrier(
        (left, right, nest_cols_next, nest_cols_prev)
    )
    parent_next, *slabs = call(
        functools.partial(parent_kernel, cuts, kinds),
        levels,
        [
            anchor,
            (parent_fields, by_level(shape, 1)),
            (parent_velocity, by_level(parent_velocity.shape, 1)),
            (parent_mixing, by_level(parent_mixing.shape, 0)),
        ]
        + whole_of([top, bottom, left, right]),
        [(shape, by_level(shape, 1))]
        + [shaped(message_rows, LANES * (high - low)) for low, high in cuts for _ in kinds],
        scratch=[(3, rows, LANES)],
    )
    nest_left, nest_right = halo_exchange("gy", nest_cols_next, nest_cols_prev)
    coefs, moved, weights = call(
        nest_start_kernel,
        levels,
        [
            (nest_fields, by_level(shape, 1)),
            (nest_velocity, by_level(nest_velocity.shape, 1)),
            (nest_mixing, by_level(nest_mixing.shape, 0)),
        ]
        + whole_of([top, bottom, nest_left, nest_right]),
        [
            ((levels, 5, height, width), by_level((levels, 5, height, width), 0)),
            ((levels, fields, height, width), by_level((levels, fields, height, width), 0)),
            shaped(height, width),
        ],
        scratch=[(fields + 3, height, width)],
    )

    def forward(pair):
        return pair

    def backward(pair):
        return pair[::-1]

    def row_select(count, entries, arrays):
        return call(
            functools.partial(row_select_kernel, entries, rows, channels),
            1,
            [anchor] + whole_of(arrays),
            [shaped(message_rows, LANES)] * count,
        )

    messages = []
    travelling = []
    for cut, (low, high) in enumerate(cuts):
        arrays = slabs[len(kinds) * cut : len(kinds) * (cut + 1)]
        travelling.append((high - low, arrays, *exchange(usual, arrays, forward)))
    for count, arrays, received, entries in travelling:
        if messages:
            received, messages = lax.optimization_barrier((received, messages))

        def seldom(arrays, received, count=count, entries=entries):
            others, more = exchange(rare, arrays, forward)
            return row_select(count, [None, *entries, *more], [arrays[0], *received, *others])

        def mostly(arrays, received, count=count, entries=entries):
            return row_select(count, [None, *entries], [arrays[0], *received])

        messages = [*messages, *lax.cond(rarely, seldom, mostly, arrays, received)]
    columns_of = column_routes(gy)
    ks = tuple(columns_of)
    received = [lax.ppermute(messages[k % 3], "gy", columns_of[k]) for k in ks]
    nest_result, coarse = call(
        functools.partial(nest_kernel, ks),
        levels,
        [anchor]
        + whole_of([spread_matrix(columns), gather_matrix(columns)])
        + [(coefs, by_level(coefs.shape, 0)), (moved, by_level(moved.shape, 0))]
        + whole_of([weights, *received]),
        [
            (shape, by_level(shape, 1)),
            (
                (span * channels, LANES),
                pl.BlockSpec((span * fields, LANES), lambda level: (level, 0)),
            ),
        ],
        scratch=[
            (message_rows, 2 * LANES),
            (message_rows, width),
            (fields, width // LANES, height, LANES),
            (fields, height, width),
            (span * fields, columns),
            (fields, columns // LANES, rows, LANES),
        ],
    )

    returned = {
        k: lax.ppermute(coarse, "gy", [backward(pair) for pair in columns_of[k]]) for k in ks
    }
    placed = [returned[0]]
    first_received, entries = exchange(usual, placed * len(kinds), backward)
    placed += call(
        functools.partial(column_select_kernel, columns),
        1,
        [anchor] + whole_of([returned[k] for k in (1, -2, 2, -1)]),
        [shaped(span * channels, 2 * LANES)],
    )
    received = [first_received, exchange(usual, placed[1:] * len(kinds), backward)[0]]

    def merge(entries, parent_next, by_cut):
        slabs = [
            (array, pl.BlockSpec((span * fields, array.shape[1]), lambda level: (level, 0)))
            for arrays in by_cut
            for array in arrays
        ]
        return call(
            functools.partial(merge_kernel, entries, cuts),
            levels,
            [anchor, (parent_next, by_level(shape, 1))] + slabs,
            [(shape, by_level(shape, 1))],
        )[0]

    def seldom(parent_next, placed, received):
        others = [exchange(rare, [array] * len(kinds), backward) for array in placed]
        by_cut = [[own, *some, *rest[0]] for own, some, rest in zip(placed, received, others)]
        return merge([[(0, None)], *entries, *others[0][1]], parent_next, by_cut)

    def mostly(parent_next, placed, received):
        by_cut = [[own, *some] for own, some in zip(placed, received)]
        return merge([[(0, None)], *entries], parent_next, by_cut)

    merged = lax.cond(rarely, seldom, mostly, parent_next, placed, received)
    return merged, nest_result


def solution(mesh):
    placed = (
        P(None, None, "gx", "gy"),
        P(None, None, "gx", "gy"),
        P(None, "gx", "gy"),
        P(None, None, "gx", "gy"),
        P(None, None, "gx", "gy"),
        P(None, "gx", "gy"),
        P(),
    )
    return jax.shard_map(
        per_device,
        mesh=mesh,
        in_specs=placed,
        out_specs=(P(None, None, "gx", "gy"), P(None, None, "gx", "gy")),
        check_vma=False,
    )
```

```python
import functools

import jax
import jax.numpy as jnp
import numpy as np
from jax import lax
from jax.experimental import pallas as pl
from jax.experimental.pallas import tpu as pltpu
from jax.sharding import PartitionSpec as P

SUBSTEPS = 3
F32 = jnp.float32
LANES = 128
VMEM_LIMIT = 56 * 1024 * 1024
nudge_floor = 0.1
relax_width = 4.0


def whole(array):
    return pl.BlockSpec(array.shape, lambda level: (0,) * array.ndim)


def block(shape, at):
    return pl.BlockSpec(shape, lambda level: at)


def by_level(shape, dim):
    sizes = tuple(1 if i == dim else n for i, n in enumerate(shape))
    return pl.BlockSpec(sizes, lambda level: tuple(level if i == dim else 0 for i in range(len(shape))))


def call(body, grid, ins, outs, scratch=(), cost=None):
    return pl.pallas_call(
        body,
        grid=(grid,),
        out_shape=[jax.ShapeDtypeStruct(shape, F32) for shape, _ in outs],
        in_specs=[spec for _, spec in ins],
        out_specs=[spec for _, spec in outs],
        scratch_shapes=[pltpu.VMEM(shape, F32) for shape in scratch],
        cost_estimate=cost,
        compiler_params=pltpu.CompilerParams(vmem_limit_bytes=VMEM_LIMIT),
    )(*[array for array, _ in ins])


def lane_index(rows, lanes=LANES):
    return lax.broadcasted_iota(jnp.int32, (rows, lanes), 1)


def row_index(rows, lanes=LANES):
    return lax.broadcasted_iota(jnp.int32, (rows, lanes), 0)


def among(value, numbers):
    found = False
    for number in numbers:
        found = found | (value == number)
    return found


def halo_exchange(axis, to_next, to_previous):
    ends = lax.axis_size(axis) - 1
    from_previous = lax.ppermute(to_next, axis, [(i, i + 1) for i in range(ends)])
    from_next = lax.ppermute(to_previous, axis, [(i + 1, i) for i in range(ends)])
    return from_previous, from_next


def pack_kernel(pf_head, pf_tail, pf_first, pf_last, nf_head, nf_tail, nv_head, nv_tail, nm_head, nm_tail, *outs):
    rows_next, rows_prev, cols_next, cols_prev = outs
    channels, rows = pf_first.shape[:2]
    coefs = nv_head.shape[0] + nm_head.shape[0]
    lanes = lane_index(rows)
    last = jnp.zeros((rows, LANES), F32)
    first = jnp.zeros((rows, LANES), F32)
    for ch in range(channels):
        last = jnp.where(lanes == ch, pltpu.roll(pf_last[ch], (ch + 1) % LANES, 1), last)
        first = jnp.where(lanes == ch, pltpu.roll(pf_first[ch], ch, 1), first)
    cols_next[...] = last
    cols_prev[...] = first
    for ch in range(channels):
        for at in range(3):
            here = at * channels + ch
            rows_next[here : here + 1, :] = nf_tail[ch, 5 + at : 6 + at, :]
            rows_prev[here : here + 1, :] = nf_head[ch, at : at + 1, :]
    base = 3 * channels
    for cc in range(coefs):
        wind = cc < nv_head.shape[0]
        tail, head = (nv_tail, nv_head) if wind else (nm_tail, nm_head)
        row = cc if wind else cc - nv_head.shape[0]
        for at in range(2):
            here = base + at * coefs + cc
            rows_next[here : here + 1, :] = tail[row, 6 + at : 7 + at, :]
            rows_prev[here : here + 1, :] = head[row, at : at + 1, :]
    base = base + 2 * coefs
    for ch in range(channels):
        rows_next[base + ch : base + ch + 1, :] = pf_tail[ch, 7:8, :]
        rows_prev[base + ch : base + ch + 1, :] = pf_head[ch, 0:1, :]


def parent_kernel(cuts, kinds, anchor, pf, pv, pm, top, bottom, left, right, parent_next, *rest):
    slabs, rims = rest[:-1], rest[-1]
    fields, _, rows, columns = pf.shape
    level, levels = pl.program_id(0), pl.num_programs(0)
    channels = fields * levels
    span = rows // 3
    rank, size_x = lax.axis_index("gx"), lax.axis_size("gx")
    half = lax.axis_size("gy") // 2 * columns
    base = 3 * channels + 2 * 3 * levels
    shift = lax.rem(2 * columns - anchor[1] + half, columns)
    row_shift = lax.rem((rows - span) * rank + size_x * rows - anchor[0], rows)
    row = row_index(rows, columns)
    column = lane_index(rows, columns)
    lanes = lane_index(rows)
    u, v, k = pv[0, 0], pv[1, 0], pm[0]
    a_w = jnp.maximum(u, 0.0) + k
    a_e = k - jnp.minimum(u, 0.0)
    a_s = jnp.maximum(v, 0.0) + k
    a_n = k - jnp.minimum(v, 0.0)
    a_c = 1.0 - (a_w + a_e + a_s + a_n)
    pad = jnp.zeros((rows, columns - LANES), F32)

    def rows_by_kind(value):
        third = [
            (
                value[span * kind : span * (kind + 1)],
                value[(span * kind - 1) % rows : (span * kind - 1) % rows + 1],
                value[span * (kind + 1) % rows : span * (kind + 1) % rows + 1],
            )
            for kind in range(3)
        ]
        for ranks_of in kinds:
            (kind, _), *others = ranks_of
            picked = third[kind]
            for kind, ranks in others:
                chosen = among(rank, ranks)
                picked = [jnp.where(chosen, new, old) for new, old in zip(third[kind], picked)]
            yield picked

    @pl.when(level == 0)
    def _():
        rims[...] = jnp.zeros_like(rims)

    packed = [rims[tile] for tile in range(3)]
    for field in range(fields):
        ch = field * levels + level
        q = pf[field, 0]
        west = jnp.where(row == 0, top[pl.ds(base + ch, 1), :], pltpu.roll(q, 1, 0))
        east = jnp.where(
            row == rows - 1, bottom[pl.ds(base + ch, 1), :], pltpu.roll(q, rows - 1, 0)
        )
        at_first = pltpu.roll(left[...], LANES - ch, 1)
        at_last = pltpu.roll(right[...], LANES - 1 - ch, 1)
        south = jnp.where(
            column == 0, jnp.concatenate([at_first, pad], axis=1), pltpu.roll(q, 1, 1)
        )
        north = jnp.where(
            column == columns - 1,
            jnp.concatenate([pad, at_last], axis=1),
            pltpu.roll(q, columns - 1, 1),
        )
        result = a_c * q + a_w * west + a_e * east + a_s * south + a_n * north
        parent_next[field, 0] = result
        moved = pltpu.roll(pltpu.roll(result, shift, 1), row_shift, 0)
        here = level * fields + field
        tiles = [moved[:, LANES * tile : LANES * (tile + 1)] for tile in range(3)]
        for tile in range(3):
            beside = jnp.where(lanes == LANES - 1, tiles[(tile + 2) % 3], tiles[(tile + 1) % 3])
            inside = (lanes == 2 * here) | (lanes == 2 * here + 1)
            packed[tile] = jnp.where(inside, pltpu.roll(beside, 2 * here + 1, 1), packed[tile])
        for at, (cells, before, after) in enumerate(rows_by_kind(moved)):
            for cut, (low, high) in enumerate(cuts):
                slab, part = slabs[len(kinds) * cut + at], slice(LANES * low, LANES * high)
                slab[pl.ds(pl.multiple_of(span * here, 8), span), :] = cells[:, part]
                slab[pl.ds(span * channels + here, 1), :] = before[:, part]
                slab[pl.ds((span + 1) * channels + here, 1), :] = after[:, part]
    for tile in range(3):
        rims[tile] = packed[tile]

    @pl.when(level == levels - 1)
    def _():
        total = (span + 2) * channels
        for tile in range(3):
            for at, (cells, before, after) in enumerate(rows_by_kind(rims[tile])):
                for cut, (low, high) in enumerate(cuts):
                    if not low <= tile < high:
                        continue
                    slab = slabs[len(kinds) * cut + at]
                    part = slice(LANES * (tile - low), LANES * (tile - low + 1))
                    slab[total : total + span, part] = cells
                    slab[total + span : total + span + 1, part] = before
                    slab[total + span + 1 : total + span + 2, part] = after
                    padding = slab.shape[0] - total - span - 2
                    slab[total + span + 2 :, part] = jnp.zeros((padding, LANES), F32)


def row_select_kernel(entries, rows, channels, anchor, *refs):
    count = len(entries)
    slabs, messages = refs[:count], refs[count:]
    span = rows // 3
    rank = lax.axis_index("gx")
    start = anchor[0] + span * rank
    lowest, highest = lax.div(start, rows), lax.div(start + span - 1, rows)
    above, below = lax.div(start - 1, rows), lax.div(start + span, rows)
    split = jnp.where(highest > lowest, rows * highest - start, span)

    def pick(owner, first, size, part):
        value = slabs[0][first : first + size, part]
        for senders, slab in zip(entries[1:], slabs[1:]):
            chosen = False
            for d, ranks in senders:
                chosen = chosen | ((rank - owner == d) & among(rank, ranks))
            value = jnp.where(chosen, slab[first : first + size, part], value)
        return value

    for tile, message in enumerate(messages):
        part = slice(LANES * tile, LANES * (tile + 1))
        cells, total = span * channels, (span + 2) * channels
        for first, size in ((0, cells), (total, span)):
            row = row_index(size) & (span - 1)
            low, high = pick(lowest, first, size, part), pick(highest, first, size, part)
            message[first : first + size, :] = jnp.where(row < split, low, high)
        for first, size in ((cells, channels), (total + span, 1)):
            message[first : first + size, :] = pick(above, first, size, part)
            message[first + size : first + 2 * size, :] = pick(below, first + size, size, part)
        message[total + span + 2 :, :] = jnp.zeros((message.shape[0] - total - span - 2, LANES), F32)


def nest_columns_kernel(nf_first, nf_last, nv_first, nv_last, nm_first, nm_last, top, bottom, cols_next, cols_prev):
    channels, rows = nf_first.shape[:2]
    columns = top.shape[1]
    winds = nv_first.shape[0]
    coefs = winds + nm_first.shape[0]
    height = rows + 8
    lanes, lane = lane_index(rows), lane_index(1)

    def packed(out, nf, nv, nm, part, moved):
        main = jnp.zeros((rows, LANES), F32)
        lines = {at: jnp.zeros((1, LANES), F32) for at in range(-3, 3)}

        def add(first, size, tile, halo_rows):
            nonlocal main
            shift = (first + (size if moved else 0)) % LANES
            inside = (lanes >= first) & (lanes < first + size)
            main = jnp.where(inside, pltpu.roll(tile, shift, 1), main)
            inside = (lane >= first) & (lane < first + size)
            for at, value in halo_rows:
                lines[at] = jnp.where(inside, pltpu.roll(value, shift, 1), lines[at])

        def halos(base, step, size, at):
            pairs = []
            for n in range(size):
                here = base + n * step + at
                pairs.append((n, bottom[here : here + 1, part]))
                pairs.append((n - size, top[here : here + 1, part]))
            return pairs

        for ch in range(channels):
            add(3 * ch, 3, nf[ch], halos(0, channels, 3, ch))
        base = 3 * channels
        for cc in range(coefs):
            tile = nv[cc] if cc < winds else nm[cc - winds]
            add(base + 2 * cc, 2, tile, halos(base, coefs, 2, cc))
        out[0:rows, :] = main
        out[rows:height, :] = jnp.zeros((height - rows, LANES), F32)
        for at, line in lines.items():
            target = rows + at if at >= 0 else height + at
            out[target : target + 1, :] = line

    packed(cols_next, nf_last, nv_last, nm_last, slice(columns - LANES, columns), True)
    packed(cols_prev, nf_first, nv_first, nm_first, slice(0, LANES), False)


def three_parts(x):
    high = x.astype(jnp.bfloat16)
    rest = x - high.astype(F32)
    middle = rest.astype(jnp.bfloat16)
    low = (rest - middle.astype(F32)).astype(jnp.bfloat16)
    return high, middle, low


def exact_dot(x, matrix):
    parts = three_parts(x)
    total = jnp.dot(parts[2], matrix, preferred_element_type=F32)
    total = total + jnp.dot(parts[1], matrix, preferred_element_type=F32)
    return total + jnp.dot(parts[0], matrix, preferred_element_type=F32)


def stencil(q, coefs):
    height, width = q.shape
    return (
        coefs[0] * q
        + coefs[1] * pltpu.roll(q, 1, 0)
        + coefs[2] * pltpu.roll(q, height - 1, 0)
        + coefs[3] * pltpu.roll(q, 1, 1)
        + coefs[4] * pltpu.roll(q, width - 1, 1)
    )


def nest_start_kernel(nf, nv, nm, top, bottom, left, right, coefs, moved, weights, state):
    fields, _, rows, columns = nf.shape
    level, levels = pl.program_id(0), pl.num_programs(0)
    channels = fields * levels
    height, width = rows + 8, columns + LANES
    rank_x, rank_y = lax.axis_index("gx"), lax.axis_index("gy")
    row = row_index(height, width)
    column = lane_index(height, width)
    local_row = jnp.where(row < rows + 4, row, row - height)
    local_column = jnp.where(column < columns + LANES // 2, column, column - width)
    global_row = rank_x * rows + local_row
    global_column = rank_y * columns + local_column
    row_distance = jnp.minimum(global_row, lax.axis_size("gx") * rows - 1 - global_row)
    column_distance = jnp.minimum(
        global_column, lax.axis_size("gy") * columns - 1 - global_column
    )
    distance = jnp.minimum(row_distance, column_distance)
    weight = nudge_floor + (1.0 - nudge_floor) * jnp.exp(
        jnp.maximum(distance, 0).astype(F32) / -relax_width
    )
    weight = jnp.where(distance < 0, 0.0, weight)
    keep = 1.0 - weight
    edge_lanes = lane_index(height)

    @pl.when(level == 0)
    def _():
        weights[...] = weight / 9.0
        state[...] = jnp.zeros_like(state)

    def side_tile(first, size):
        after = pltpu.roll(right[...], lax.rem(2 * LANES - first, LANES), 1)
        before = pltpu.roll(left[...], lax.rem(2 * LANES - first - size, LANES), 1)
        inside = jnp.where(edge_lanes < LANES // 2, after, before)
        outside = (edge_lanes >= size) & (edge_lanes < LANES - size)
        return jnp.where(outside, 0.0, inside)

    def fill(slot, value, base, step, at, size, first):
        state[slot, 0:rows, 0:columns] = value
        for n in range(size):
            source = pl.ds(base + n * step + at, 1)
            state[slot, rows + n : rows + n + 1, 0:columns] = bottom[source, :]
            target = height - size + n
            state[slot, target : target + 1, 0:columns] = top[source, :]
        state[slot, :, columns:width] = side_tile(first, size)

    base = 3 * channels
    for slot, value in enumerate((nv[0, 0], nv[1, 0], nm[0])):
        cc = slot * levels + level
        fill(slot + fields, value, base, 3 * levels, cc, 2, base + 2 * cc)
    for field in range(fields):
        ch = field * levels + level
        fill(field, nf[field, 0], 0, channels, ch, 3, 3 * ch)
    u, v, k = (state[slot + fields] for slot in range(3))
    a_w = jnp.maximum(u, 0.0) + k
    a_e = k - jnp.minimum(u, 0.0)
    a_s = jnp.maximum(v, 0.0) + k
    a_n = k - jnp.minimum(v, 0.0)
    a_c = 1.0 - (a_w + a_e + a_s + a_n)
    for slot, value in enumerate((a_c, a_w, a_e, a_s, a_n)):
        coefs[0, slot] = keep * value
    for field in range(fields):
        moved[0, field] = stencil(state[field], [coefs[0, slot] for slot in range(5)])


def nest_kernel(ks, anchor, spread, gather, coefs, moved, weights, *refs):
    count = len(ks)
    received = dict(zip(ks, refs[:count]))
    result, coarse = refs[count : count + 2]
    relay, refined, forcing, state, sums, final = refs[count + 2 :]
    fields, _, rows, columns = result.shape
    level, levels = pl.program_id(0), pl.num_programs(0)
    channels = fields * levels
    span_rows, span_columns = rows // 3, columns // 3
    height, width = rows + 8, columns + LANES
    tiles = width // LANES
    relay_rows = span_rows + 2
    total = relay_rows * channels
    offset = anchor[1] - lax.axis_size("gy") // 2 * columns
    kind = lax.rem(lax.axis_index("gy"), 3)
    edge = columns - offset - span_columns * kind

    @pl.when(level == 0)
    def _():
        lower = jnp.where(kind == 1, received[1][...], received[2][...])
        lower = jnp.where(kind == 0, received[0][...], lower)
        upper = jnp.where(kind == 1, received[-2][...], received[-1][...])
        lanes = lane_index(lower.shape[0])
        relay[:, 0:LANES] = jnp.where(lanes < edge, lower, upper)
        relay[total:, LANES:] = jnp.zeros((relay.shape[0] - total, LANES), F32)
        rim_low, rim_high = lower[total : total + relay_rows], upper[total : total + relay_rows]
        odd = (lane_index(relay_rows) & 1) == 1
        rim = jnp.where(jnp.where(odd, LANES, -1) < edge, rim_low, rim_high)
        for ch in range(channels):
            sides = pltpu.roll(rim, (LANES - 2 * ch) % LANES, 1)
            relay[span_rows * ch : span_rows * (ch + 1), LANES:] = sides[0:span_rows]
            for side in (span_rows, span_rows + 1):
                here = side * channels + ch
                relay[here : here + 1, LANES:] = sides[side : side + 1]
        refined[...] = exact_dot(relay[...], spread[...])

    relay_row = row_index(span_rows, width)
    for field in range(fields):
        ch = level * fields + field
        centre = refined[pl.ds(pl.multiple_of(span_rows * ch, 8), span_rows), :]
        above = refined[pl.ds(span_rows * channels + ch, 1), :]
        below = refined[pl.ds((span_rows + 1) * channels + ch, 1), :]
        before = jnp.where(relay_row == 0, above, pltpu.roll(centre, 1, 0))
        after = jnp.where(
            relay_row == span_rows - 1, below, pltpu.roll(centre, span_rows - 1, 0)
        )
        thirds = (before + 2.0 * centre, 3.0 * centre, 2.0 * centre + after)
        rims = (
            (rows, centre[span_rows - 1 :] + 2.0 * below),
            (rows + 1, 3.0 * below),
            (height - 2, 3.0 * above),
            (height - 1, 2.0 * above + centre[0:1]),
        )
        for tile in range(tiles):
            part = slice(LANES * tile, LANES * (tile + 1))
            for at, value in enumerate(thirds):
                forcing[field, tile, pl.ds(at, span_rows, stride=3), :] = value[:, part]
            forcing[field, tile, rows + 2 : height - 2, :] = jnp.zeros((4, LANES), F32)
            for at, value in rims:
                forcing[field, tile, at : at + 1, :] = value[:, part]
    for field in range(fields):
        for tile in range(tiles):
            part = slice(LANES * tile, LANES * (tile + 1))
            pull = weights[:, part] * forcing[field, tile]
            forcing[field, tile] = pull
            state[field, :, part] = moved[0, field, :, part] + pull
    for _ in range(SUBSTEPS - 1):
        for field in range(fields):
            pull = jnp.concatenate([forcing[field, tile] for tile in range(tiles)], axis=1)
            state[field] = pull + stencil(state[field], [coefs[0, slot] for slot in range(5)])
    for field in range(fields):
        result[field, 0] = state[field, 0:rows, 0:columns]
        for tile in range(tiles - 1):
            part = slice(LANES * tile, LANES * (tile + 1))
            final[field, tile] = state[field, 0:rows, part]
            sums[span_rows * field : span_rows * (field + 1), part] = (
                final[field, tile, pl.ds(0, span_rows, stride=3), :]
                + final[field, tile, pl.ds(1, span_rows, stride=3), :]
                + final[field, tile, pl.ds(2, span_rows, stride=3), :]
            )
    coarse[...] = exact_dot(sums[...], gather[...]) / 9.0


def column_select_kernel(ks, columns, anchor, *refs):
    received = dict(zip(ks, refs[: len(ks)]))
    placed = refs[-1]
    offset = anchor[1] - lax.axis_size("gy") // 2 * columns
    placed[:, 0:LANES] = received[0][...]
    for tile in (1, 2):
        inside = lane_index(placed.shape[0]) < columns - offset - LANES * tile
        placed[:, LANES * tile : LANES * (tile + 1)] = jnp.where(
            inside, received[tile][...], received[tile - 3][...]
        )


def merge_kernel(entries, cuts, anchor, parent_next, *refs):
    merged = refs[-1]
    fields, _, rows, columns = parent_next.shape
    span = rows // 3
    rank_x, rank_y = lax.axis_index("gx"), lax.axis_index("gy")
    size_x, size_y = lax.axis_size("gx"), lax.axis_size("gy")
    offset = anchor[1] - size_y // 2 * columns
    shift = lax.rem(offset + columns, columns)
    row = rank_x * rows + row_index(rows, columns) - anchor[0]
    column = rank_y * columns + lane_index(rows, columns) - anchor[1]
    covered = (
        (row >= 0) & (row < size_x * span) & (column >= 0) & (column < size_y * (columns // 3))
    )
    first = anchor[0] - (rows - span) * rank_x
    row_shift = lax.rem(first + size_x * rows, rows)
    slab_row = row_index(span)
    choices = [[], [], []]
    for at, receivers in enumerate(entries):
        for d, ranks in receivers:
            place = first + span * d + slab_row
            if ranks is not None:
                place = jnp.where(among(rank_x, ranks), place, -1)
            choices[d % 3].append((at, (place >= 0) & (place < rows)))
    where = [(cut, tile - low) for cut, (low, high) in enumerate(cuts) for tile in range(low, high)]
    for field in range(fields):
        tiles = []
        for tile in range(3):
            kinds = []
            for options in choices:
                value = jnp.zeros((span, LANES), F32)
                for at, inside in options:
                    cut, lane_tile = where[tile]
                    slab = refs[cut * len(entries) + at]
                    part = slice(LANES * lane_tile, LANES * (lane_tile + 1))
                    cells = slab[span * field : span * (field + 1), part]
                    value = jnp.where(inside, cells, value)
                kinds.append(value)
            tiles.append(jnp.concatenate(kinds, axis=0))
        moved = pltpu.roll(jnp.concatenate(tiles, axis=1), row_shift, 0)
        fed_back = pltpu.roll(moved, shift, 1)
        merged[field, 0] = jnp.where(covered, fed_back, parent_next[field, 0])


def spread_matrix(columns):
    span = columns // 3
    matrix = np.zeros((2 * LANES, columns + LANES), np.float32)

    def source(m):
        return LANES if m < 0 else (LANES + 1 if m >= span else m)

    for c in range(-2, columns + 2):
        m, j = divmod(c, 3)
        at = c % (columns + LANES)
        if j == 0:
            matrix[source(m - 1), at] += 1.0
            matrix[source(m), at] += 2.0
        elif j == 1:
            matrix[source(m), at] += 3.0
        else:
            matrix[source(m), at] += 2.0
            matrix[source(m + 1), at] += 1.0
    return jnp.asarray(matrix, jnp.bfloat16)


def gather_matrix(columns):
    matrix = np.zeros((columns, columns // 3), np.float32)
    matrix[np.arange(columns), np.arange(columns) // 3] = 1.0
    return jnp.asarray(matrix, jnp.bfloat16)


def coloured(pairs):
    degree = max(sum(pair[end] == at for pair in pairs) for end in (0, 1) for at, _ in enumerate(pairs + [0, 0]))
    routes = [[] for _ in range(degree)]

    def free(route, end, at):
        return all(pair[end] != at for pair in routes[route])

    for pair in pairs:
        first = next(route for route in range(degree) if free(route, 0, pair[0]))
        second = next(route for route in range(degree) if free(route, 1, pair[1]))
        if not free(first, 1, pair[1]):
            end, at, route, other = 1, pair[1], first, second
            path = []
            while not free(route, end, at):
                step = next(p for p in routes[route] if p[end] == at)
                path.append((step, route, other))
                end, at, route, other = 1 - end, step[1 - end], other, route
            for step, source, _ in path:
                routes[source].remove(step)
            for step, _, target in path:
                routes[target].append(step)
        routes[first].append(pair)
    return [sorted(route) for route in routes]


def row_routes(size, rows):
    span = rows // 3

    def needed(start):
        pairs = set()
        for nest in range(size):
            for at in (start + span * nest, start + span * nest + span + 1):
                pairs.add((at // rows, nest))
        return {(owner, nest) for owner, nest in pairs if owner != nest}

    def cost(pairs):
        cuts = [
            sum((a < cut <= n) if up else (n < cut <= a) for a, n in pairs)
            for cut in range(2, size, 2)
            for up in (False, True)
        ]
        return 4 * max(cuts) + len(coloured(sorted(pairs)))

    ranges = []
    pending = None
    for first in range(0, size * (rows - span) - 2, span):
        last = min(first + span, size * (rows - span) - 2) - 1
        pairs = set().union(*(needed(start) for start in range(first, last)))
        start, extra = first, needed(last)
        if pending is not None:
            before, more = ranges[-1][1], pending
            if cost(before | more) + cost(pairs) <= cost(before) + cost(pairs | more):
                ranges[-1] = (ranges[-1][0], before | more)
            else:
                start, pairs = first - 1, pairs | more
        ranges.append((start + 1, pairs))
        pending = extra
    ranges[-1] = (ranges[-1][0], ranges[-1][1] | pending)
    return [(first, coloured(sorted(pairs))) for first, pairs in ranges]


def column_routes(size):
    routes = {}
    for k in (0, 1, -2, 2, -1):
        pairs = [(size // 2 + p, 3 * p + k) for p in range(size - size // 2)]
        routes[k] = [(s, n) for s, n in pairs if 0 <= n < size]
    return routes


def per_device(
    parent_fields,
    parent_velocity,
    parent_mixing,
    nest_fields,
    nest_velocity,
    nest_mixing,
    nest_anchor,
):
    fields, levels, rows, columns = shape = parent_fields.shape
    channels = fields * levels
    span, last = rows // 3, columns // LANES - 1
    gx, gy = lax.axis_size("gx"), lax.axis_size("gy")
    height, width = rows + 8, columns + LANES
    pf = parent_fields.reshape(channels, rows, columns)
    nf = nest_fields.reshape(channels, rows, columns)
    nv = nest_velocity.reshape(2 * levels, rows, columns)
    nm = nest_mixing
    def row_blocks(array):
        size = (array.shape[0], 8, columns)
        return [(array, block(size, (0, 0, 0))), (array, block(size, (0, rows // 8 - 1, 0)))]

    def column_blocks(array):
        size = (array.shape[0], rows, LANES)
        return [(array, block(size, (0, 0, 0))), (array, block(size, (0, 0, last)))]

    def shaped(*size):
        return size, block(size, (0,) * len(size))

    def whole_of(arrays):
        return [(array, whole(array)) for array in arrays]

    halo_rows = 4 * channels + 6 * levels
    rows_next, rows_prev, cols_next, cols_prev = call(
        pack_kernel,
        1,
        row_blocks(pf) + column_blocks(pf) + row_blocks(nf) + row_blocks(nv) + row_blocks(nm),
        [shaped(halo_rows, columns)] * 2 + [shaped(rows, LANES)] * 2,
    )
    top, bottom = halo_exchange("gx", rows_next, rows_prev)
    left, right = halo_exchange("gy", cols_next, cols_prev)

    ranges = row_routes(gx, rows)
    cuts = ((0, 3),)
    message_rows = -(-((span + 2) * (channels + 1)) // 16) * 16
    columns_of = column_routes(gy)
    ks = tuple(columns_of)

    def branch(routes):
        return lambda operands: after_halo(routes, *operands)

    def by_shift(pairs):
        shifts = sorted({nest - owner for owner, nest in pairs})
        return [(d, [(a, n) for a, n in pairs if n - a == d]) for d in shifts]

    def after_halo(routes, nest_anchor, pf, pv, pm, nf, nv, nm, top, bottom, left, right):
        anchor = (nest_anchor, pl.BlockSpec(memory_space=pltpu.SMEM))
        kinds = [[(0, None)]]
        for route in routes:
            kinds.append([(d % 3, [a for a, _ in pairs]) for d, pairs in by_shift(route)])
        parent_next, *slabs = call(
            functools.partial(parent_kernel, cuts, kinds),
            levels,
            [
                anchor,
                (pf, by_level(shape, 1)),
                (pv, by_level(pv.shape, 1)),
                (pm, by_level(pm.shape, 0)),
            ]
            + whole_of([top, bottom, left, right]),
            [(shape, by_level(shape, 1))] + [shaped(message_rows, columns)] * len(kinds),
            scratch=[(3, rows, LANES)],
        )
        received = [lax.ppermute(slab, "gx", route) for slab, route in zip(slabs[1:], routes)]
        nf_by_channel = nf.reshape(channels, rows, columns)
        nv_by_channel = nv.reshape(2 * levels, rows, columns)
        nest_cols_next, nest_cols_prev = call(
            nest_columns_kernel,
            1,
            column_blocks(nf_by_channel)
            + column_blocks(nv_by_channel)
            + column_blocks(nm)
            + whole_of([top, bottom]),
            [shaped(height, LANES)] * 2,
        )
        nest_left, nest_right = halo_exchange("gy", nest_cols_next, nest_cols_prev)
        coefs, moved, weights = call(
            nest_start_kernel,
            levels,
            [
                (nf, by_level(shape, 1)),
                (nv, by_level(nv.shape, 1)),
                (nm, by_level(nm.shape, 0)),
            ]
            + whole_of([top, bottom, nest_left, nest_right]),
            [
                ((levels, 5, height, width), by_level((levels, 5, height, width), 0)),
                ((levels, fields, height, width), by_level((levels, fields, height, width), 0)),
                shaped(height, width),
            ],
            scratch=[(fields + 3, height, width)],
        )
        entries = [None]
        for route in routes:
            entries.append([(d, [n for _, n in pairs]) for d, pairs in by_shift(route)])
        messages = call(
            functools.partial(row_select_kernel, entries, rows, channels),
            1,
            [anchor] + whole_of([slabs[0], *received]),
            [shaped(message_rows, LANES)] * 3,
        )
        received = [lax.ppermute(messages[k % 3], "gy", columns_of[k]) for k in ks]
        nest_result, coarse = call(
            functools.partial(nest_kernel, ks),
            levels,
            [anchor]
            + whole_of([spread_matrix(columns), gather_matrix(columns)])
            + [(coefs, by_level(coefs.shape, 0)), (moved, by_level(moved.shape, 0))]
            + whole_of([weights, *received]),
            [
                (shape, by_level(shape, 1)),
                (
                    (span * channels, LANES),
                    pl.BlockSpec((span * fields, LANES), lambda level: (level, 0)),
                ),
            ],
            scratch=[
                (message_rows, 2 * LANES),
                (message_rows, width),
                (fields, width // LANES, height, LANES),
                (fields, height, width),
                (span * fields, columns),
                (fields, columns // LANES, rows, LANES),
            ],
        )
        returned = [
            lax.ppermute(coarse, "gy", [pair[::-1] for pair in columns_of[k]]) for k in ks
        ]
        placed = call(
            functools.partial(column_select_kernel, ks, columns),
            1,
            [anchor] + whole_of(returned),
            [shaped(span * channels, columns)],
        )[0]
        received = [lax.ppermute(placed, "gx", [pair[::-1] for pair in route]) for route in routes]
        entries = [[(0, None)]]
        for route in routes:
            entries.append([(d, [a for a, _ in pairs]) for d, pairs in by_shift(route)])
        slab_block = pl.BlockSpec((span * fields, columns), lambda level: (level, 0))
        merged = call(
            functools.partial(merge_kernel, entries, cuts),
            levels,
            [anchor, (parent_next, by_level(shape, 1))]
            + [(array, slab_block) for array in (placed, *received)],
            [(shape, by_level(shape, 1))],
        )[0]
        return merged, nest_result

    index = sum((nest_anchor[0] >= first).astype(jnp.int32) for first, _ in ranges[1:])
    operands = (
        nest_anchor,
        parent_fields,
        parent_velocity,
        parent_mixing,
        nest_fields,
        nest_velocity,
        nest_mixing,
        top,
        bottom,
        left,
        right,
    )
    return lax.switch(index, [branch(routes) for _, routes in ranges], operands)


def solution(mesh):
    placed = (
        P(None, None, "gx", "gy"),
        P(None, None, "gx", "gy"),
        P(None, "gx", "gy"),
        P(None, None, "gx", "gy"),
        P(None, None, "gx", "gy"),
        P(None, "gx", "gy"),
        P(),
    )
    return jax.shard_map(
        per_device,
        mesh=mesh,
        in_specs=placed,
        out_specs=(P(None, None, "gx", "gy"), P(None, None, "gx", "gy")),
        check_vma=False,
    )
```

```python
import functools

import jax
import jax.numpy as jnp
import numpy as np
from jax import lax
from jax.experimental import pallas as pl
from jax.experimental.pallas import tpu as pltpu
from jax.sharding import PartitionSpec as P

SUBSTEPS = 3
F32 = jnp.float32
LANES = 128
VMEM_LIMIT = 56 * 1024 * 1024
nudge_floor = 0.1
relax_width = 4.0


def whole(array):
    return pl.BlockSpec(array.shape, lambda level: (0,) * array.ndim)


def block(shape, at):
    return pl.BlockSpec(shape, lambda level: at)


def by_level(shape, dim):
    sizes = tuple(1 if i == dim else n for i, n in enumerate(shape))
    return pl.BlockSpec(sizes, lambda level: tuple(level if i == dim else 0 for i in range(len(shape))))


def call(body, grid, ins, outs, scratch=(), cost=None):
    return pl.pallas_call(
        body,
        grid=(grid,),
        out_shape=[jax.ShapeDtypeStruct(shape, F32) for shape, _ in outs],
        in_specs=[spec for _, spec in ins],
        out_specs=[spec for _, spec in outs],
        scratch_shapes=[pltpu.VMEM(shape, F32) for shape in scratch],
        cost_estimate=cost,
        compiler_params=pltpu.CompilerParams(vmem_limit_bytes=VMEM_LIMIT),
    )(*[array for array, _ in ins])


def lane_index(rows, lanes=LANES):
    return lax.broadcasted_iota(jnp.int32, (rows, lanes), 1)


def row_index(rows, lanes=LANES):
    return lax.broadcasted_iota(jnp.int32, (rows, lanes), 0)


def among(value, numbers):
    found = False
    for number in numbers:
        found = found | (value == number)
    return found


def range_index(firsts, row_anchor):
    return sum((row_anchor >= first).astype(jnp.int32) for first in firsts[1:])


def halo_exchange(axis, to_next, to_previous):
    ends = lax.axis_size(axis) - 1
    from_previous = lax.ppermute(to_next, axis, [(i, i + 1) for i in range(ends)])
    from_next = lax.ppermute(to_previous, axis, [(i + 1, i) for i in range(ends)])
    return from_previous, from_next


def pack_kernel(pf_head, pf_tail, pf_first, pf_last, nf_head, nf_tail, nv_head, nv_tail, nm_head, nm_tail, *outs):
    rows_next, rows_prev, cols_next, cols_prev = outs
    channels, rows = pf_first.shape[:2]
    coefs = nv_head.shape[0] + nm_head.shape[0]
    lanes = lane_index(rows)
    last = jnp.zeros((rows, LANES), F32)
    first = jnp.zeros((rows, LANES), F32)
    for ch in range(channels):
        last = jnp.where(lanes == ch, pltpu.roll(pf_last[ch], (ch + 1) % LANES, 1), last)
        first = jnp.where(lanes == ch, pltpu.roll(pf_first[ch], ch, 1), first)
    cols_next[...] = last
    cols_prev[...] = first
    for ch in range(channels):
        for at in range(3):
            here = at * channels + ch
            rows_next[here : here + 1, :] = nf_tail[ch, 5 + at : 6 + at, :]
            rows_prev[here : here + 1, :] = nf_head[ch, at : at + 1, :]
    base = 3 * channels
    for cc in range(coefs):
        wind = cc < nv_head.shape[0]
        tail, head = (nv_tail, nv_head) if wind else (nm_tail, nm_head)
        row = cc if wind else cc - nv_head.shape[0]
        for at in range(2):
            here = base + at * coefs + cc
            rows_next[here : here + 1, :] = tail[row, 6 + at : 7 + at, :]
            rows_prev[here : here + 1, :] = head[row, at : at + 1, :]
    base = base + 2 * coefs
    for ch in range(channels):
        rows_next[base + ch : base + ch + 1, :] = pf_tail[ch, 7:8, :]
        rows_prev[base + ch : base + ch + 1, :] = pf_head[ch, 0:1, :]


def parent_kernel(firsts, size_x, anchor, table, pf, pv, pm, top, bottom, left, right, parent_next, *rest):
    slabs, rims = rest[:-1], rest[-1]
    fields, _, rows, columns = pf.shape
    level, levels = pl.program_id(0), pl.num_programs(0)
    channels = fields * levels
    span = rows // 3
    rank = lax.axis_index("gx")
    half = lax.axis_size("gy") // 2 * columns
    base = 3 * channels + 2 * 3 * levels
    shift = lax.rem(2 * columns - anchor[1] + half, columns)
    row_shift = lax.rem((rows - span) * rank + size_x * rows - anchor[0], rows)
    row = row_index(rows, columns)
    column = lane_index(rows, columns)
    lanes = lane_index(rows)
    place = (range_index(firsts, anchor[0]) * size_x + rank) * (len(slabs) - 1)
    kinds = [table[place + slot] for slot in range(len(slabs) - 1)]
    u, v, k = pv[0, 0], pv[1, 0], pm[0]
    a_w = jnp.maximum(u, 0.0) + k
    a_e = k - jnp.minimum(u, 0.0)
    a_s = jnp.maximum(v, 0.0) + k
    a_n = k - jnp.minimum(v, 0.0)
    a_c = 1.0 - (a_w + a_e + a_s + a_n)
    pad = jnp.zeros((rows, columns - LANES), F32)

    def rows_by_slab(value):
        thirds = [
            (
                value[span * kind : span * (kind + 1)],
                value[(span * kind - 1) % rows : (span * kind - 1) % rows + 1],
                value[span * (kind + 1) % rows : span * (kind + 1) % rows + 1],
            )
            for kind in range(3)
        ]
        yield thirds[0]
        for kind in kinds:
            yield [
                jnp.where(kind == 0, zero, jnp.where(kind == 1, one, two))
                for zero, one, two in zip(*thirds)
            ]

    @pl.when(level == 0)
    def _():
        rims[...] = jnp.zeros_like(rims)

    packed = [rims[tile] for tile in range(3)]
    for field in range(fields):
        ch = field * levels + level
        q = pf[field, 0]
        west = jnp.where(row == 0, top[pl.ds(base + ch, 1), :], pltpu.roll(q, 1, 0))
        east = jnp.where(
            row == rows - 1, bottom[pl.ds(base + ch, 1), :], pltpu.roll(q, rows - 1, 0)
        )
        at_first = pltpu.roll(left[...], LANES - ch, 1)
        at_last = pltpu.roll(right[...], LANES - 1 - ch, 1)
        south = jnp.where(
            column == 0, jnp.concatenate([at_first, pad], axis=1), pltpu.roll(q, 1, 1)
        )
        north = jnp.where(
            column == columns - 1,
            jnp.concatenate([pad, at_last], axis=1),
            pltpu.roll(q, columns - 1, 1),
        )
        result = a_c * q + a_w * west + a_e * east + a_s * south + a_n * north
        parent_next[field, 0] = result
        moved = pltpu.roll(pltpu.roll(result, shift, 1), row_shift, 0)
        here = level * fields + field
        tiles = [moved[:, LANES * tile : LANES * (tile + 1)] for tile in range(3)]
        for tile in range(3):
            beside = jnp.where(lanes == LANES - 1, tiles[(tile + 2) % 3], tiles[(tile + 1) % 3])
            inside = (lanes == 2 * here) | (lanes == 2 * here + 1)
            packed[tile] = jnp.where(inside, pltpu.roll(beside, 2 * here + 1, 1), packed[tile])
        for slab, (cells, before, after) in zip(slabs, rows_by_slab(moved)):
            slab[pl.ds(pl.multiple_of(span * here, 8), span), :] = cells
            slab[pl.ds(span * channels + here, 1), :] = before
            slab[pl.ds((span + 1) * channels + here, 1), :] = after
    for tile in range(3):
        rims[tile] = packed[tile]

    @pl.when(level == levels - 1)
    def _():
        total = (span + 2) * channels
        for tile in range(3):
            part = slice(LANES * tile, LANES * (tile + 1))
            for slab, (cells, before, after) in zip(slabs, rows_by_slab(rims[tile])):
                slab[total : total + span, part] = cells
                slab[total + span : total + span + 1, part] = before
                slab[total + span + 1 : total + span + 2, part] = after
                padding = slab.shape[0] - total - span - 2
                slab[total + span + 2 :, part] = jnp.zeros((padding, LANES), F32)


def row_select_kernel(entries, rows, channels, anchor, *refs):
    count = len(entries)
    slabs, messages = refs[:count], refs[count:]
    span = rows // 3
    rank = lax.axis_index("gx")
    start = anchor[0] + span * rank
    lowest, highest = lax.div(start, rows), lax.div(start + span - 1, rows)
    above, below = lax.div(start - 1, rows), lax.div(start + span, rows)
    split = jnp.where(highest > lowest, rows * highest - start, span)

    def pick(owner, first, size, part):
        value = slabs[0][first : first + size, part]
        for senders, slab in zip(entries[1:], slabs[1:]):
            chosen = False
            for d, ranks in senders:
                chosen = chosen | ((rank - owner == d) & among(rank, ranks))
            value = jnp.where(chosen, slab[first : first + size, part], value)
        return value

    for tile, message in enumerate(messages):
        part = slice(LANES * tile, LANES * (tile + 1))
        cells, total = span * channels, (span + 2) * channels
        for first, size in ((0, cells), (total, span)):
            row = row_index(size) & (span - 1)
            low, high = pick(lowest, first, size, part), pick(highest, first, size, part)
            message[first : first + size, :] = jnp.where(row < split, low, high)
        for first, size in ((cells, channels), (total + span, 1)):
            message[first : first + size, :] = pick(above, first, size, part)
            message[first + size : first + 2 * size, :] = pick(below, first + size, size, part)
        message[total + span + 2 :, :] = jnp.zeros((message.shape[0] - total - span - 2, LANES), F32)


def nest_columns_kernel(nf_first, nf_last, nv_first, nv_last, nm_first, nm_last, top, bottom, cols_next, cols_prev):
    channels, rows = nf_first.shape[:2]
    columns = top.shape[1]
    winds = nv_first.shape[0]
    coefs = winds + nm_first.shape[0]
    height = rows + 8
    lanes, lane = lane_index(rows), lane_index(1)

    def packed(out, nf, nv, nm, part, moved):
        main = jnp.zeros((rows, LANES), F32)
        lines = {at: jnp.zeros((1, LANES), F32) for at in range(-3, 3)}

        def add(first, size, tile, halo_rows):
            nonlocal main
            shift = (first + (size if moved else 0)) % LANES
            inside = (lanes >= first) & (lanes < first + size)
            main = jnp.where(inside, pltpu.roll(tile, shift, 1), main)
            inside = (lane >= first) & (lane < first + size)
            for at, value in halo_rows:
                lines[at] = jnp.where(inside, pltpu.roll(value, shift, 1), lines[at])

        def halos(base, step, size, at):
            pairs = []
            for n in range(size):
                here = base + n * step + at
                pairs.append((n, bottom[here : here + 1, part]))
                pairs.append((n - size, top[here : here + 1, part]))
            return pairs

        for ch in range(channels):
            add(3 * ch, 3, nf[ch], halos(0, channels, 3, ch))
        base = 3 * channels
        for cc in range(coefs):
            tile = nv[cc] if cc < winds else nm[cc - winds]
            add(base + 2 * cc, 2, tile, halos(base, coefs, 2, cc))
        out[0:rows, :] = main
        out[rows:height, :] = jnp.zeros((height - rows, LANES), F32)
        for at, line in lines.items():
            target = rows + at if at >= 0 else height + at
            out[target : target + 1, :] = line

    packed(cols_next, nf_last, nv_last, nm_last, slice(columns - LANES, columns), True)
    packed(cols_prev, nf_first, nv_first, nm_first, slice(0, LANES), False)


def three_parts(x):
    high = x.astype(jnp.bfloat16)
    rest = x - high.astype(F32)
    middle = rest.astype(jnp.bfloat16)
    low = (rest - middle.astype(F32)).astype(jnp.bfloat16)
    return high, middle, low


def exact_dot(x, matrix):
    parts = three_parts(x)
    total = jnp.dot(parts[2], matrix, preferred_element_type=F32)
    total = total + jnp.dot(parts[1], matrix, preferred_element_type=F32)
    return total + jnp.dot(parts[0], matrix, preferred_element_type=F32)


def stencil(q, coefs):
    height, width = q.shape
    return (
        coefs[0] * q
        + coefs[1] * pltpu.roll(q, 1, 0)
        + coefs[2] * pltpu.roll(q, height - 1, 0)
        + coefs[3] * pltpu.roll(q, 1, 1)
        + coefs[4] * pltpu.roll(q, width - 1, 1)
    )


def nest_start_kernel(nf, nv, nm, top, bottom, left, right, coefs, moved, weights, state):
    fields, _, rows, columns = nf.shape
    level, levels = pl.program_id(0), pl.num_programs(0)
    channels = fields * levels
    height, width = rows + 8, columns + LANES
    rank_x, rank_y = lax.axis_index("gx"), lax.axis_index("gy")
    row = row_index(height, width)
    column = lane_index(height, width)
    local_row = jnp.where(row < rows + 4, row, row - height)
    local_column = jnp.where(column < columns + LANES // 2, column, column - width)
    global_row = rank_x * rows + local_row
    global_column = rank_y * columns + local_column
    row_distance = jnp.minimum(global_row, lax.axis_size("gx") * rows - 1 - global_row)
    column_distance = jnp.minimum(
        global_column, lax.axis_size("gy") * columns - 1 - global_column
    )
    distance = jnp.minimum(row_distance, column_distance)
    weight = nudge_floor + (1.0 - nudge_floor) * jnp.exp(
        jnp.maximum(distance, 0).astype(F32) / -relax_width
    )
    weight = jnp.where(distance < 0, 0.0, weight)
    keep = 1.0 - weight
    edge_lanes = lane_index(height)

    @pl.when(level == 0)
    def _():
        weights[...] = weight / 9.0
        state[...] = jnp.zeros_like(state)

    def side_tile(first, size):
        after = pltpu.roll(right[...], lax.rem(2 * LANES - first, LANES), 1)
        before = pltpu.roll(left[...], lax.rem(2 * LANES - first - size, LANES), 1)
        inside = jnp.where(edge_lanes < LANES // 2, after, before)
        outside = (edge_lanes >= size) & (edge_lanes < LANES - size)
        return jnp.where(outside, 0.0, inside)

    def fill(slot, value, base, step, at, size, first):
        state[slot, 0:rows, 0:columns] = value
        for n in range(size):
            source = pl.ds(base + n * step + at, 1)
            state[slot, rows + n : rows + n + 1, 0:columns] = bottom[source, :]
            target = height - size + n
            state[slot, target : target + 1, 0:columns] = top[source, :]
        state[slot, :, columns:width] = side_tile(first, size)

    base = 3 * channels
    for slot, value in enumerate((nv[0, 0], nv[1, 0], nm[0])):
        cc = slot * levels + level
        fill(slot + fields, value, base, 3 * levels, cc, 2, base + 2 * cc)
    for field in range(fields):
        ch = field * levels + level
        fill(field, nf[field, 0], 0, channels, ch, 3, 3 * ch)
    u, v, k = (state[slot + fields] for slot in range(3))
    a_w = jnp.maximum(u, 0.0) + k
    a_e = k - jnp.minimum(u, 0.0)
    a_s = jnp.maximum(v, 0.0) + k
    a_n = k - jnp.minimum(v, 0.0)
    a_c = 1.0 - (a_w + a_e + a_s + a_n)
    for slot, value in enumerate((a_c, a_w, a_e, a_s, a_n)):
        coefs[0, slot] = keep * value
    for field in range(fields):
        moved[0, field] = stencil(state[field], [coefs[0, slot] for slot in range(5)])


def nest_kernel(ks, selves, anchor, spread, gather, coefs, moved, weights, *refs):
    count = len(ks) + 3
    received, messages = dict(zip(ks, refs[: len(ks)])), refs[len(ks) : count]
    result, coarse = refs[count : count + 2]
    relay, refined, forcing, state, sums, final = refs[count + 2 :]
    fields, _, rows, columns = result.shape
    level, levels = pl.program_id(0), pl.num_programs(0)
    channels = fields * levels
    span_rows, span_columns = rows // 3, columns // 3
    height, width = rows + 8, columns + LANES
    tiles = width // LANES
    relay_rows = span_rows + 2
    total = relay_rows * channels
    offset = anchor[1] - lax.axis_size("gy") // 2 * columns
    kind = lax.rem(lax.axis_index("gy"), 3)
    edge = columns - offset - span_columns * kind

    @pl.when(level == 0)
    def _():
        arrived = {k: ref[...] for k, ref in received.items()}
        for k, at in selves.items():
            own = messages[k % 3][...]
            arrived[k] = jnp.where(lax.axis_index("gy") == at, own, arrived[k])
        lower = jnp.where(kind == 1, arrived[1], arrived[2])
        lower = jnp.where(kind == 0, arrived[0], lower)
        upper = jnp.where(kind == 1, arrived[-2], arrived[-1])
        lanes = lane_index(lower.shape[0])
        relay[:, 0:LANES] = jnp.where(lanes < edge, lower, upper)
        relay[total:, LANES:] = jnp.zeros((relay.shape[0] - total, LANES), F32)
        rim_low, rim_high = lower[total : total + relay_rows], upper[total : total + relay_rows]
        odd = (lane_index(relay_rows) & 1) == 1
        rim = jnp.where(jnp.where(odd, LANES, -1) < edge, rim_low, rim_high)
        for ch in range(channels):
            sides = pltpu.roll(rim, (LANES - 2 * ch) % LANES, 1)
            relay[span_rows * ch : span_rows * (ch + 1), LANES:] = sides[0:span_rows]
            for side in (span_rows, span_rows + 1):
                here = side * channels + ch
                relay[here : here + 1, LANES:] = sides[side : side + 1]
        refined[...] = exact_dot(relay[...], spread[...])

    relay_row = row_index(span_rows, width)
    for field in range(fields):
        ch = level * fields + field
        centre = refined[pl.ds(pl.multiple_of(span_rows * ch, 8), span_rows), :]
        above = refined[pl.ds(span_rows * channels + ch, 1), :]
        below = refined[pl.ds((span_rows + 1) * channels + ch, 1), :]
        before = jnp.where(relay_row == 0, above, pltpu.roll(centre, 1, 0))
        after = jnp.where(
            relay_row == span_rows - 1, below, pltpu.roll(centre, span_rows - 1, 0)
        )
        thirds = (before + 2.0 * centre, 3.0 * centre, 2.0 * centre + after)
        rims = (
            (rows, centre[span_rows - 1 :] + 2.0 * below),
            (rows + 1, 3.0 * below),
            (height - 2, 3.0 * above),
            (height - 1, 2.0 * above + centre[0:1]),
        )
        for tile in range(tiles):
            part = slice(LANES * tile, LANES * (tile + 1))
            for at, value in enumerate(thirds):
                forcing[field, tile, pl.ds(at, span_rows, stride=3), :] = value[:, part]
            forcing[field, tile, rows + 2 : height - 2, :] = jnp.zeros((4, LANES), F32)
            for at, value in rims:
                forcing[field, tile, at : at + 1, :] = value[:, part]
    for field in range(fields):
        for tile in range(tiles):
            part = slice(LANES * tile, LANES * (tile + 1))
            pull = weights[:, part] * forcing[field, tile]
            forcing[field, tile] = pull
            state[field, :, part] = moved[0, field, :, part] + pull
    for step in range(SUBSTEPS - 1):
        for field in range(fields):
            pull = jnp.concatenate([forcing[field, tile] for tile in range(tiles)], axis=1)
            value = pull + stencil(state[field], [coefs[0, slot] for slot in range(5)])
            if step < SUBSTEPS - 2:
                state[field] = value
            else:
                result[field, 0] = value[0:rows, 0:columns]
                for tile in range(tiles - 1):
                    final[field, tile] = value[0:rows, LANES * tile : LANES * (tile + 1)]
    for field in range(fields):
        for tile in range(tiles - 1):
            part = slice(LANES * tile, LANES * (tile + 1))
            sums[span_rows * field : span_rows * (field + 1), part] = (
                final[field, tile, pl.ds(0, span_rows, stride=3), :]
                + final[field, tile, pl.ds(1, span_rows, stride=3), :]
                + final[field, tile, pl.ds(2, span_rows, stride=3), :]
            )
    coarse[...] = exact_dot(sums[...], gather[...]) / 9.0


def merge_kernel(entries, anchor, parent_next, *refs):
    merged = refs[-1]
    fields, _, rows, columns = parent_next.shape
    span = rows // 3
    rank_x, rank_y = lax.axis_index("gx"), lax.axis_index("gy")
    size_x, size_y = lax.axis_size("gx"), lax.axis_size("gy")
    offset = anchor[1] - size_y // 2 * columns
    shift = lax.rem(offset + columns, columns)
    row = rank_x * rows + row_index(rows, columns) - anchor[0]
    column = rank_y * columns + lane_index(rows, columns) - anchor[1]
    covered = (
        (row >= 0) & (row < size_x * span) & (column >= 0) & (column < size_y * (columns // 3))
    )
    first = anchor[0] - (rows - span) * rank_x
    row_shift = lax.rem(first + size_x * rows, rows)
    slab_row = row_index(span)
    choices = [[], [], []]
    for at, receivers in enumerate(entries):
        for d, ranks in receivers:
            place = first + span * d + slab_row
            if ranks is not None:
                place = jnp.where(among(rank_x, ranks), place, -1)
            choices[d % 3].append((at, (place >= 0) & (place < rows)))
    for field in range(fields):
        tiles = []
        for tile in range(3):
            kinds = []
            for options in choices:
                value = jnp.zeros((span, LANES), F32)
                for at, inside in options:
                    part = slice(LANES * tile, LANES * (tile + 1))
                    cells = refs[at][span * field : span * (field + 1), part]
                    value = jnp.where(inside, cells, value)
                kinds.append(value)
            tiles.append(jnp.concatenate(kinds, axis=0))
        moved = pltpu.roll(jnp.concatenate(tiles, axis=1), row_shift, 0)
        fed_back = pltpu.roll(moved, shift, 1)
        merged[field, 0] = jnp.where(covered, fed_back, parent_next[field, 0])


def spread_matrix(columns):
    span = columns // 3
    matrix = np.zeros((2 * LANES, columns + LANES), np.float32)

    def source(m):
        return LANES if m < 0 else (LANES + 1 if m >= span else m)

    for c in range(-2, columns + 2):
        m, j = divmod(c, 3)
        at = c % (columns + LANES)
        if j == 0:
            matrix[source(m - 1), at] += 1.0
            matrix[source(m), at] += 2.0
        elif j == 1:
            matrix[source(m), at] += 3.0
        else:
            matrix[source(m), at] += 2.0
            matrix[source(m + 1), at] += 1.0
    return jnp.asarray(matrix, jnp.bfloat16)


def gather_matrix(columns):
    matrix = np.zeros((columns, columns // 3), np.float32)
    matrix[np.arange(columns), np.arange(columns) // 3] = 1.0
    return jnp.asarray(matrix, jnp.bfloat16)


def coloured(pairs):
    degree = max(sum(pair[end] == at for pair in pairs) for end in (0, 1) for at, _ in enumerate(pairs + [0, 0]))
    routes = [[] for _ in range(degree)]

    def free(route, end, at):
        return all(pair[end] != at for pair in routes[route])

    for pair in pairs:
        first = next(route for route in range(degree) if free(route, 0, pair[0]))
        second = next(route for route in range(degree) if free(route, 1, pair[1]))
        if not free(first, 1, pair[1]):
            end, at, route, other = 1, pair[1], first, second
            path = []
            while not free(route, end, at):
                step = next(p for p in routes[route] if p[end] == at)
                path.append((step, route, other))
                end, at, route, other = 1 - end, step[1 - end], other, route
            for step, source, _ in path:
                routes[source].remove(step)
            for step, _, target in path:
                routes[target].append(step)
        routes[first].append(pair)
    return [sorted(route) for route in routes]


def row_routes(size, rows):
    span = rows // 3

    def needed(start):
        pairs = set()
        for nest in range(size):
            for at in (start + span * nest, start + span * nest + span + 1):
                pairs.add((at // rows, nest))
        return {(owner, nest) for owner, nest in pairs if owner != nest}

    def cost(pairs):
        cuts = [
            sum((a < cut <= n) if up else (n < cut <= a) for a, n in pairs)
            for cut in range(2, size, 2)
            for up in (False, True)
        ]
        return 4 * max(cuts) + len(coloured(sorted(pairs)))

    ranges = []
    pending = None
    for first in range(0, size * (rows - span) - 2, span):
        last = min(first + span, size * (rows - span) - 2) - 1
        pairs = set().union(*(needed(start) for start in range(first, last)))
        start, extra = first, needed(last)
        if pending is not None:
            before, more = ranges[-1][1], pending
            if cost(before | more) + cost(pairs) <= cost(before) + cost(pairs | more):
                ranges[-1] = (ranges[-1][0], before | more)
            else:
                start, pairs = first - 1, pairs | more
        ranges.append((start + 1, pairs))
        pending = extra
    ranges[-1] = (ranges[-1][0], ranges[-1][1] | pending)
    return [(first, coloured(sorted(pairs))) for first, pairs in ranges]


def column_routes(size):
    routes, selves = {}, {}
    for k in (0, 1, -2, 2, -1):
        pairs = [(size // 2 + p, 3 * p + k) for p in range(size - size // 2)]
        routes[k] = [(s, n) for s, n in pairs if 0 <= n < size and n != s]
        selves.update({k: s for s, n in pairs if n == s})
    return routes, selves


def per_device(
    parent_fields,
    parent_velocity,
    parent_mixing,
    nest_fields,
    nest_velocity,
    nest_mixing,
    nest_anchor,
):
    fields, levels, rows, columns = shape = parent_fields.shape
    channels = fields * levels
    span, last = rows // 3, columns // LANES - 1
    gx, gy = lax.axis_size("gx"), lax.axis_size("gy")
    height, width = rows + 8, columns + LANES
    pf = parent_fields.reshape(channels, rows, columns)
    nf = nest_fields.reshape(channels, rows, columns)
    nv = nest_velocity.reshape(2 * levels, rows, columns)
    nm = nest_mixing
    def row_blocks(array):
        size = (array.shape[0], 8, columns)
        return [(array, block(size, (0, 0, 0))), (array, block(size, (0, rows // 8 - 1, 0)))]

    def column_blocks(array):
        size = (array.shape[0], rows, LANES)
        return [(array, block(size, (0, 0, 0))), (array, block(size, (0, 0, last)))]

    def shaped(*size):
        return size, block(size, (0,) * len(size))

    def whole_of(arrays):
        return [(array, whole(array)) for array in arrays]

    halo_rows = 4 * channels + 6 * levels
    rows_next, rows_prev, cols_next, cols_prev = call(
        pack_kernel,
        1,
        row_blocks(pf) + column_blocks(pf) + row_blocks(nf) + row_blocks(nv) + row_blocks(nm),
        [shaped(halo_rows, columns)] * 2 + [shaped(rows, LANES)] * 2,
    )
    top, bottom = halo_exchange("gx", rows_next, rows_prev)
    left, right = halo_exchange("gy", cols_next, cols_prev)

    ranges = row_routes(gx, rows)
    firsts = [first for first, _ in ranges]
    index = range_index(firsts, nest_anchor[0])
    slots = max(len(routes) for _, routes in ranges)
    table = np.zeros((len(ranges), gx, slots), np.int32)
    for at, (_, routes) in enumerate(ranges):
        for slot, route in enumerate(routes):
            for owner, nest in route:
                table[at, owner, slot] = (nest - owner) % 3
    message_rows = -(-((span + 2) * (channels + 1)) // 16) * 16
    columns_of, selves = column_routes(gy)
    ks = tuple(columns_of)
    anchor = (nest_anchor, pl.BlockSpec(memory_space=pltpu.SMEM))

    def by_shift(route, receiver):
        shifts = sorted({nest - owner for owner, nest in route})
        return [(d, [pair[receiver] for pair in route if pair[1] - pair[0] == d]) for d in shifts]

    parent_next, *slabs = call(
        functools.partial(parent_kernel, firsts, gx),
        levels,
        [
            anchor,
            (jnp.asarray(table.reshape(-1)), pl.BlockSpec(memory_space=pltpu.SMEM)),
            (parent_fields, by_level(shape, 1)),
            (parent_velocity, by_level(parent_velocity.shape, 1)),
            (parent_mixing, by_level(parent_mixing.shape, 0)),
        ]
        + whole_of([top, bottom, left, right]),
        [(shape, by_level(shape, 1))] + [shaped(message_rows, columns)] * (slots + 1),
        scratch=[(3, rows, LANES)],
    )

    def relay_rows(routes):
        def branch(nest_anchor, slabs, nf, nv, nm, top, bottom):
            received = [lax.ppermute(slab, "gx", route) for slab, route in zip(slabs[1:], routes)]
            to_next, to_previous = call(
                nest_columns_kernel,
                1,
                column_blocks(nf) + column_blocks(nv) + column_blocks(nm) + whole_of([top, bottom]),
                [shaped(height, LANES)] * 2,
            )
            sides = halo_exchange("gy", to_next, to_previous)
            entries = [None] + [by_shift(route, 1) for route in routes]
            messages = call(
                functools.partial(row_select_kernel, entries, rows, channels),
                1,
                [(nest_anchor, pl.BlockSpec(memory_space=pltpu.SMEM))]
                + whole_of([slabs[0], *received]),
                [shaped(message_rows, LANES)] * 3,
            )
            return messages, sides

        return branch

    messages, (nest_left, nest_right) = lax.switch(
        index, [relay_rows(routes) for _, routes in ranges], nest_anchor, slabs, nf, nv, nm, top, bottom
    )
    received = [lax.ppermute(messages[k % 3], "gy", columns_of[k]) for k in ks]
    coefs, moved, weights = call(
        nest_start_kernel,
        levels,
        [
            (nest_fields, by_level(shape, 1)),
            (nest_velocity, by_level(nest_velocity.shape, 1)),
            (nest_mixing, by_level(nest_mixing.shape, 0)),
        ]
        + whole_of([top, bottom, nest_left, nest_right]),
        [
            ((levels, 5, height, width), by_level((levels, 5, height, width), 0)),
            ((levels, fields, height, width), by_level((levels, fields, height, width), 0)),
            shaped(height, width),
        ],
        scratch=[(fields + 3, height, width)],
    )
    nest_result, coarse = call(
        functools.partial(nest_kernel, ks, selves),
        levels,
        [anchor]
        + whole_of([spread_matrix(columns), gather_matrix(columns)])
        + [(coefs, by_level(coefs.shape, 0)), (moved, by_level(moved.shape, 0))]
        + whole_of([weights, *received, *messages]),
        [
            (shape, by_level(shape, 1)),
            (
                (span * channels, LANES),
                pl.BlockSpec((span * fields, LANES), lambda level: (level, 0)),
            ),
        ],
        scratch=[
            (message_rows, 2 * LANES),
            (message_rows, width),
            (fields, width // LANES, height, LANES),
            (fields, height, width),
            (span * fields, columns),
            (fields, columns // LANES, rows, LANES),
        ],
    )

    returned = {k: lax.ppermute(coarse, "gy", [pair[::-1] for pair in columns_of[k]]) for k in ks}
    for k, at in selves.items():
        returned[k] = jnp.where(lax.axis_index("gy") == at, coarse, returned[k])
    inside = jnp.arange(columns, dtype=jnp.int32) < columns - nest_anchor[1] + gy // 2 * columns
    placed = jnp.where(
        inside,
        jnp.concatenate([returned[0], returned[1], returned[2]], axis=1),
        jnp.concatenate([returned[0], returned[-2], returned[-1]], axis=1),
    )

    def feedback_rows(routes):
        def branch(nest_anchor, parent_next, placed):
            received = [
                lax.ppermute(placed, "gx", [pair[::-1] for pair in route]) for route in routes
            ]
            entries = [[(0, None)]] + [by_shift(route, 0) for route in routes]
            slab_block = pl.BlockSpec((span * fields, columns), lambda level: (level, 0))
            return call(
                functools.partial(merge_kernel, entries),
                levels,
                [
                    (nest_anchor, pl.BlockSpec(memory_space=pltpu.SMEM)),
                    (parent_next, by_level(shape, 1)),
                ]
                + [(array, slab_block) for array in (placed, *received)],
                [(shape, by_level(shape, 1))],
            )[0]

        return branch

    merged = lax.switch(
        index, [feedback_rows(routes) for _, routes in ranges], nest_anchor, parent_next, placed
    )
    return merged, nest_result


def solution(mesh):
    placed = (
        P(None, None, "gx", "gy"),
        P(None, None, "gx", "gy"),
        P(None, "gx", "gy"),
        P(None, None, "gx", "gy"),
        P(None, None, "gx", "gy"),
        P(None, "gx", "gy"),
        P(),
    )
    return jax.shard_map(
        per_device,
        mesh=mesh,
        in_specs=placed,
        out_specs=(P(None, None, "gx", "gy"), P(None, None, "gx", "gy")),
        check_vma=False,
    )
```

```python
import functools

import jax
import jax.numpy as jnp
import numpy as np
from jax import lax
from jax.experimental import pallas as pl
from jax.experimental.pallas import tpu as pltpu
from jax.sharding import PartitionSpec as P

SUBSTEPS = 3
F32 = jnp.float32
LANES = 128
VMEM_LIMIT = 56 * 1024 * 1024
nudge_floor = 0.1
relax_width = 4.0


def whole(array):
    return pl.BlockSpec(array.shape, lambda level: (0,) * array.ndim)


def block(shape, at):
    return pl.BlockSpec(shape, lambda level: at)


def by_level(shape, dim):
    sizes = tuple(1 if i == dim else n for i, n in enumerate(shape))
    return pl.BlockSpec(sizes, lambda level: tuple(level if i == dim else 0 for i in range(len(shape))))


def call(body, grid, ins, outs, scratch=(), cost=None):
    return pl.pallas_call(
        body,
        grid=(grid,),
        out_shape=[jax.ShapeDtypeStruct(out[0], *(out[2:] or (F32,))) for out in outs],
        in_specs=[spec for _, spec in ins],
        out_specs=[out[1] for out in outs],
        scratch_shapes=[pltpu.VMEM(shape, F32) for shape in scratch],
        cost_estimate=cost,
        compiler_params=pltpu.CompilerParams(vmem_limit_bytes=VMEM_LIMIT),
    )(*[array for array, _ in ins])


def lane_index(rows, lanes=LANES):
    return lax.broadcasted_iota(jnp.int32, (rows, lanes), 1)


def row_index(rows, lanes=LANES):
    return lax.broadcasted_iota(jnp.int32, (rows, lanes), 0)


def among(value, numbers):
    found = False
    for number in numbers:
        found = found | (value == number)
    return found


def halo_exchange(axis, to_next, to_previous):
    ends = lax.axis_size(axis) - 1
    from_previous = lax.ppermute(to_next, axis, [(i, i + 1) for i in range(ends)])
    from_next = lax.ppermute(to_previous, axis, [(i + 1, i) for i in range(ends)])
    return from_previous, from_next


def pack_kernel(firsts, anchor, pf_head, pf_tail, pf_first, pf_last, nf_head, nf_tail, nv_head, nv_tail, nm_head, nm_tail, *outs):
    rows_next, rows_prev, cols_next, cols_prev, *indices = outs
    channels, rows = pf_first.shape[:2]
    for at, (index, limits) in enumerate(zip(indices, firsts)):
        index[0] = sum((anchor[at] >= first).astype(jnp.int32) for first in limits[1:])
    coefs = nv_head.shape[0] + nm_head.shape[0]
    lanes = lane_index(rows)
    last = jnp.zeros((rows, LANES), F32)
    first = jnp.zeros((rows, LANES), F32)
    for ch in range(channels):
        last = jnp.where(lanes == ch, pltpu.roll(pf_last[ch], (ch + 1) % LANES, 1), last)
        first = jnp.where(lanes == ch, pltpu.roll(pf_first[ch], ch, 1), first)
    cols_next[...] = last
    cols_prev[...] = first
    for ch in range(channels):
        for at in range(3):
            here = at * channels + ch
            rows_next[here : here + 1, :] = nf_tail[ch, 5 + at : 6 + at, :]
            rows_prev[here : here + 1, :] = nf_head[ch, at : at + 1, :]
    base = 3 * channels
    for cc in range(coefs):
        wind = cc < nv_head.shape[0]
        tail, head = (nv_tail, nv_head) if wind else (nm_tail, nm_head)
        row = cc if wind else cc - nv_head.shape[0]
        for at in range(2):
            here = base + at * coefs + cc
            rows_next[here : here + 1, :] = tail[row, 6 + at : 7 + at, :]
            rows_prev[here : here + 1, :] = head[row, at : at + 1, :]
    base = base + 2 * coefs
    for ch in range(channels):
        rows_next[base + ch : base + ch + 1, :] = pf_tail[ch, 7:8, :]
        rows_prev[base + ch : base + ch + 1, :] = pf_head[ch, 0:1, :]


def parent_kernel(size_x, anchor, index, table, pf, pv, pm, top, bottom, left, right, parent_next, *slabs):
    fields, _, rows, columns = pf.shape
    level, levels = pl.program_id(0), pl.num_programs(0)
    channels = fields * levels
    span = rows // 3
    rank = lax.axis_index("gx")
    half = lax.axis_size("gy") // 2 * columns
    base = 3 * channels + 2 * 3 * levels
    shift = lax.rem(2 * columns - anchor[1] + half, columns)
    row_shift = lax.rem((rows - span) * rank + size_x * rows - anchor[0], rows)
    row = row_index(rows, columns)
    column = lane_index(rows, columns)
    place = (index[0] * size_x + rank) * (len(slabs) - 1)
    kinds = [table[place + slot] for slot in range(len(slabs) - 1)]
    u, v, k = pv[0, 0], pv[1, 0], pm[0]
    a_w = jnp.maximum(u, 0.0) + k
    a_e = k - jnp.minimum(u, 0.0)
    a_s = jnp.maximum(v, 0.0) + k
    a_n = k - jnp.minimum(v, 0.0)
    a_c = 1.0 - (a_w + a_e + a_s + a_n)
    pad = jnp.zeros((rows, columns - LANES), F32)

    def rows_by_slab(value):
        thirds = [
            (
                value[span * kind : span * (kind + 1)],
                value[(span * kind - 1) % rows : (span * kind - 1) % rows + 1],
                value[span * (kind + 1) % rows : span * (kind + 1) % rows + 1],
            )
            for kind in range(3)
        ]
        yield thirds[0]
        for kind in kinds:
            yield [
                jnp.where(kind == 0, zero, jnp.where(kind == 1, one, two))
                for zero, one, two in zip(*thirds)
            ]

    for field in range(fields):
        ch = field * levels + level
        q = pf[field, 0]
        west = jnp.where(row == 0, top[pl.ds(base + ch, 1), :], pltpu.roll(q, 1, 0))
        east = jnp.where(
            row == rows - 1, bottom[pl.ds(base + ch, 1), :], pltpu.roll(q, rows - 1, 0)
        )
        at_first = pltpu.roll(left[...], LANES - ch, 1)
        at_last = pltpu.roll(right[...], LANES - 1 - ch, 1)
        south = jnp.where(
            column == 0, jnp.concatenate([at_first, pad], axis=1), pltpu.roll(q, 1, 1)
        )
        north = jnp.where(
            column == columns - 1,
            jnp.concatenate([pad, at_last], axis=1),
            pltpu.roll(q, columns - 1, 1),
        )
        result = a_c * q + a_w * west + a_e * east + a_s * south + a_n * north
        parent_next[field, 0] = result
        moved = pltpu.roll(pltpu.roll(result, shift, 1), row_shift, 0)
        here = level * fields + field
        for slab, (cells, before, after) in zip(slabs, rows_by_slab(moved)):
            slab[pl.ds(pl.multiple_of(span * here, 8), span), :] = cells
            slab[pl.ds(span * channels + here, 1), :] = before
            slab[pl.ds((span + 1) * channels + here, 1), :] = after


def packed_half(value, side):
    rows = value.shape[0] // 2
    first, second = value[:rows], value[rows:]
    left = lane_index(rows) < LANES // 2
    if side == 0:
        return jnp.where(left, first, pltpu.roll(second, LANES // 2, 1))
    return jnp.where(left, pltpu.roll(first, LANES // 2, 1), second)


def unpacked_half(value, side):
    turned = pltpu.roll(value, LANES // 2, 1)
    return jnp.concatenate([value, turned] if side == 0 else [turned, value], axis=0)


def row_select_kernel(entries, rows, channels, anchor, *refs):
    count = len(entries)
    slabs, messages, half = refs[:count], refs[count:-1], refs[-1]
    span = rows // 3
    columns = slabs[0].shape[1]
    rank = lax.axis_index("gx")
    start = anchor[0] + span * rank
    lowest, highest = lax.div(start, rows), lax.div(start + span - 1, rows)
    above, below = lax.div(start - 1, rows), lax.div(start + span, rows)
    split = jnp.where(highest > lowest, rows * highest - start, span)
    cells, total = span * channels, (span + 2) * channels

    def pick(owner, first, size, part):
        value = slabs[0][first : first + size, part]
        for senders, slab in zip(entries[1:], slabs[1:]):
            chosen = False
            for d, ranks in senders:
                chosen = chosen | ((rank - owner == d) & among(rank, ranks))
            value = jnp.where(chosen, slab[first : first + size, part], value)
        return value

    tiles, sides = [], []
    for tile in range(3):
        part = slice(LANES * tile, LANES * (tile + 1))
        row = row_index(cells) & (span - 1)
        low, high = pick(lowest, 0, cells, part), pick(highest, 0, cells, part)
        tiles.append(jnp.where(row < split, low, high))
        sides.append([pick(above, cells, channels, part), pick(below, cells + channels, channels, part)])
    lanes, edge_lanes = lane_index(span), lane_index(channels)
    edge_inside = lax.div(edge_lanes, 2) == row_index(channels)

    def beside(parts, tile, lane):
        return jnp.where(lane == LANES - 1, parts[(tile + 2) % 3], parts[(tile + 1) % 3])

    for tile, message in enumerate(messages):
        message[0:cells, :] = tiles[tile]
        rim = jnp.zeros((span, LANES), F32)
        for ch in range(channels):
            here = [value[span * ch : span * (ch + 1)] for value in tiles]
            turned = pltpu.roll(beside(here, tile, lanes), 2 * ch + 1, 1)
            rim = jnp.where((lanes == 2 * ch) | (lanes == 2 * ch + 1), turned, rim)
        message[total : total + span, :] = rim + pltpu.roll(rim, LANES // 2, 1)
        for side in range(2):
            first = cells + side * channels
            message[first : first + channels, :] = sides[tile][side]
            line = beside([value[side] for value in sides], tile, edge_lanes)
            line = pltpu.roll(line, 1, 1, stride=2, stride_axis=0)
            line = jnp.sum(jnp.where(edge_inside, line, 0.0), axis=0, keepdims=True)
            target = total + span + side
            message[target : target + 1, :] = line + pltpu.roll(line, LANES // 2, 1)
        message[total + span + 2 :, :] = jnp.zeros((message.shape[0] - total - span - 2, LANES), F32)
    offset = anchor[1] - lax.axis_size("gy") // 2 * columns
    split_tile = jnp.where(offset < LANES, messages[2][...], messages[1][...])
    right = ((offset <= LANES // 2) | (offset > LANES)) & (offset <= LANES + LANES // 2)
    half[...] = jnp.where(right, packed_half(split_tile, 1), packed_half(split_tile, 0))


def nest_columns_kernel(nf_first, nf_last, nv_first, nv_last, nm_first, nm_last, top, bottom, cols_next, cols_prev):
    channels, rows = nf_first.shape[:2]
    columns = top.shape[1]
    winds = nv_first.shape[0]
    coefs = winds + nm_first.shape[0]
    height = rows + 8
    lanes, lane = lane_index(rows), lane_index(1)

    def packed(out, nf, nv, nm, part, moved):
        main = jnp.zeros((rows, LANES), F32)
        lines = {at: jnp.zeros((1, LANES), F32) for at in range(-3, 3)}

        def add(first, size, tile, halo_rows):
            nonlocal main
            shift = (first + (size if moved else 0)) % LANES
            inside = (lanes >= first) & (lanes < first + size)
            main = jnp.where(inside, pltpu.roll(tile, shift, 1), main)
            inside = (lane >= first) & (lane < first + size)
            for at, value in halo_rows:
                lines[at] = jnp.where(inside, pltpu.roll(value, shift, 1), lines[at])

        def halos(base, step, size, at):
            pairs = []
            for n in range(size):
                here = base + n * step + at
                pairs.append((n, bottom[here : here + 1, part]))
                pairs.append((n - size, top[here : here + 1, part]))
            return pairs

        for ch in range(channels):
            add(3 * ch, 3, nf[ch], halos(0, channels, 3, ch))
        base = 3 * channels
        for cc in range(coefs):
            tile = nv[cc] if cc < winds else nm[cc - winds]
            add(base + 2 * cc, 2, tile, halos(base, coefs, 2, cc))
        out[0:rows, :] = main
        out[rows:height, :] = jnp.zeros((height - rows, LANES), F32)
        for at, line in lines.items():
            target = rows + at if at >= 0 else height + at
            out[target : target + 1, :] = line

    packed(cols_next, nf_last, nv_last, nm_last, slice(columns - LANES, columns), True)
    packed(cols_prev, nf_first, nv_first, nm_first, slice(0, LANES), False)


def three_parts(x):
    high = x.astype(jnp.bfloat16)
    rest = x - high.astype(F32)
    middle = rest.astype(jnp.bfloat16)
    low = (rest - middle.astype(F32)).astype(jnp.bfloat16)
    return high, middle, low


def exact_dot(x, matrix):
    parts = three_parts(x)
    total = jnp.dot(parts[2], matrix, preferred_element_type=F32)
    total = total + jnp.dot(parts[1], matrix, preferred_element_type=F32)
    return total + jnp.dot(parts[0], matrix, preferred_element_type=F32)


def stencil(q, coefs):
    height, width = q.shape
    return (
        coefs[0] * q
        + coefs[1] * pltpu.roll(q, 1, 0)
        + coefs[2] * pltpu.roll(q, height - 1, 0)
        + coefs[3] * pltpu.roll(q, 1, 1)
        + coefs[4] * pltpu.roll(q, width - 1, 1)
    )


def nest_start_kernel(nf, nv, nm, top, bottom, left, right, coefs, moved, weights, state):
    fields, _, rows, columns = nf.shape
    level, levels = pl.program_id(0), pl.num_programs(0)
    channels = fields * levels
    height, width = rows + 8, columns + LANES
    rank_x, rank_y = lax.axis_index("gx"), lax.axis_index("gy")
    row = row_index(height, width)
    column = lane_index(height, width)
    local_row = jnp.where(row < rows + 4, row, row - height)
    local_column = jnp.where(column < columns + LANES // 2, column, column - width)
    global_row = rank_x * rows + local_row
    global_column = rank_y * columns + local_column
    row_distance = jnp.minimum(global_row, lax.axis_size("gx") * rows - 1 - global_row)
    column_distance = jnp.minimum(
        global_column, lax.axis_size("gy") * columns - 1 - global_column
    )
    distance = jnp.minimum(row_distance, column_distance)
    weight = nudge_floor + (1.0 - nudge_floor) * jnp.exp(
        jnp.maximum(distance, 0).astype(F32) / -relax_width
    )
    weight = jnp.where(distance < 0, 0.0, weight)
    keep = 1.0 - weight
    edge_lanes = lane_index(height)

    @pl.when(level == 0)
    def _():
        weights[...] = weight / 9.0
        state[...] = jnp.zeros_like(state)

    def side_tile(first, size):
        after = pltpu.roll(right[...], lax.rem(2 * LANES - first, LANES), 1)
        before = pltpu.roll(left[...], lax.rem(2 * LANES - first - size, LANES), 1)
        inside = jnp.where(edge_lanes < LANES // 2, after, before)
        outside = (edge_lanes >= size) & (edge_lanes < LANES - size)
        return jnp.where(outside, 0.0, inside)

    def fill(slot, value, base, step, at, size, first):
        state[slot, 0:rows, 0:columns] = value
        for n in range(size):
            source = pl.ds(base + n * step + at, 1)
            state[slot, rows + n : rows + n + 1, 0:columns] = bottom[source, :]
            target = height - size + n
            state[slot, target : target + 1, 0:columns] = top[source, :]
        state[slot, :, columns:width] = side_tile(first, size)

    base = 3 * channels
    for slot, value in enumerate((nv[0, 0], nv[1, 0], nm[0])):
        cc = slot * levels + level
        fill(slot + fields, value, base, 3 * levels, cc, 2, base + 2 * cc)
    for field in range(fields):
        ch = field * levels + level
        fill(field, nf[field, 0], 0, channels, ch, 3, 3 * ch)
    u, v, k = (state[slot + fields] for slot in range(3))
    a_w = jnp.maximum(u, 0.0) + k
    a_e = k - jnp.minimum(u, 0.0)
    a_s = jnp.maximum(v, 0.0) + k
    a_n = k - jnp.minimum(v, 0.0)
    a_c = 1.0 - (a_w + a_e + a_s + a_n)
    for slot, value in enumerate((a_c, a_w, a_e, a_s, a_n)):
        coefs[0, slot] = keep * value
    for field in range(fields):
        moved[0, field] = stencil(state[field], [coefs[0, slot] for slot in range(5)])


def nest_kernel(ks, half, selves, anchor, spread, gather, coefs, moved, weights, *refs):
    count = len(ks) + 3
    received, messages = dict(zip(ks, refs[: len(ks)])), refs[len(ks) : count]
    result, coarse, *coarse_half = refs[count:-6]
    relay, refined, forcing, state, sums, final = refs[-6:]
    fields, _, rows, columns = result.shape
    level, levels = pl.program_id(0), pl.num_programs(0)
    channels = fields * levels
    span_rows, span_columns = rows // 3, columns // 3
    height, width = rows + 8, columns + LANES
    tiles = width // LANES
    relay_rows = span_rows + 2
    total = relay_rows * channels
    offset = anchor[1] - lax.axis_size("gy") // 2 * columns
    kind = lax.rem(lax.axis_index("gy"), 3)
    edge = columns - offset - span_columns * kind

    @pl.when(level == 0)
    def _():
        arrived, rims = {}, {}
        for k in ks:
            value = received[k][...]
            side = half[1] if half and half[0] == k else 0
            if half and half[0] == k:
                value = unpacked_half(value, side)
            rim = value[total : total + relay_rows]
            if side == 1:
                rim = pltpu.roll(rim, LANES // 2, 1)
            if k in selves:
                itself = lax.axis_index("gy") == selves[k]
                own = messages[k % 3][...]
                value = jnp.where(itself, own, value)
                rim = jnp.where(itself, own[total : total + relay_rows], rim)
            arrived[k], rims[k] = value, rim

        def chosen(values):
            low, high = values.get(2, values[0]), values.get(-1, values[0])
            low = jnp.where(kind == 1, values.get(1, values[0]), low)
            low = jnp.where(kind == 0, values[0], low)
            return low, jnp.where(kind == 1, values.get(-2, values[0]), high)

        lower, upper = chosen(arrived)
        rim_low, rim_high = chosen(rims)
        lanes = lane_index(lower.shape[0])
        relay[:, 0:LANES] = jnp.where(lanes < edge, lower, upper)
        relay[total:, LANES:] = jnp.zeros((relay.shape[0] - total, LANES), F32)
        odd = (lane_index(relay_rows) & 1) == 1
        rim = jnp.where(jnp.where(odd, LANES, -1) < edge, rim_low, rim_high)
        for ch in range(channels):
            sides = pltpu.roll(rim, (LANES - 2 * ch) % LANES, 1)
            relay[span_rows * ch : span_rows * (ch + 1), LANES:] = sides[0:span_rows]
            for side in (span_rows, span_rows + 1):
                here = side * channels + ch
                relay[here : here + 1, LANES:] = sides[side : side + 1]
        refined[...] = exact_dot(relay[...], spread[...])

    relay_row = row_index(span_rows, width)
    for field in range(fields):
        ch = level * fields + field
        centre = refined[pl.ds(pl.multiple_of(span_rows * ch, 8), span_rows), :]
        above = refined[pl.ds(span_rows * channels + ch, 1), :]
        below = refined[pl.ds((span_rows + 1) * channels + ch, 1), :]
        before = jnp.where(relay_row == 0, above, pltpu.roll(centre, 1, 0))
        after = jnp.where(
            relay_row == span_rows - 1, below, pltpu.roll(centre, span_rows - 1, 0)
        )
        thirds = (before + 2.0 * centre, 3.0 * centre, 2.0 * centre + after)
        rims = (
            (rows, centre[span_rows - 1 :] + 2.0 * below),
            (rows + 1, 3.0 * below),
            (height - 2, 3.0 * above),
            (height - 1, 2.0 * above + centre[0:1]),
        )
        for tile in range(tiles):
            part = slice(LANES * tile, LANES * (tile + 1))
            for at, value in enumerate(thirds):
                forcing[field, tile, pl.ds(at, span_rows, stride=3), :] = value[:, part]
            forcing[field, tile, rows + 2 : height - 2, :] = jnp.zeros((4, LANES), F32)
            for at, value in rims:
                forcing[field, tile, at : at + 1, :] = value[:, part]
    for field in range(fields):
        for tile in range(tiles):
            part = slice(LANES * tile, LANES * (tile + 1))
            pull = weights[:, part] * forcing[field, tile]
            forcing[field, tile] = pull
            state[field, :, part] = moved[0, field, :, part] + pull
    for step in range(SUBSTEPS - 1):
        for field in range(fields):
            pull = jnp.concatenate([forcing[field, tile] for tile in range(tiles)], axis=1)
            value = pull + stencil(state[field], [coefs[0, slot] for slot in range(5)])
            if step < SUBSTEPS - 2:
                state[field] = value
            else:
                result[field, 0] = value[0:rows, 0:columns]
                for tile in range(tiles - 1):
                    final[field, tile] = value[0:rows, LANES * tile : LANES * (tile + 1)]
    for field in range(fields):
        for tile in range(tiles - 1):
            part = slice(LANES * tile, LANES * (tile + 1))
            sums[span_rows * field : span_rows * (field + 1), part] = (
                final[field, tile, pl.ds(0, span_rows, stride=3), :]
                + final[field, tile, pl.ds(1, span_rows, stride=3), :]
                + final[field, tile, pl.ds(2, span_rows, stride=3), :]
            )
    means = exact_dot(sums[...], gather[...]) / 9.0
    coarse[...] = means
    if half:
        coarse_half[0][...] = packed_half(means, half[1])


def column_select_kernel(ks, half, selves, columns, levels, anchor, coarse, *refs):
    returned, placed = refs[:-1], refs[-1]
    offset = anchor[1] - lax.axis_size("gy") // 2 * columns
    size = placed.shape[0] // levels
    lanes = lane_index(size)
    for level in range(levels):
        rows = slice(size * level, size * (level + 1))
        arrived = {}
        for k, ref in zip(ks, returned):
            if half and half[0] == k:
                value = ref[size // 2 * level : size // 2 * (level + 1), :]
                value = unpacked_half(value, half[1])
            else:
                value = ref[rows, :]
            if k in selves:
                value = jnp.where(lax.axis_index("gy") == selves[k], coarse[rows, :], value)
            arrived[k] = value
        placed[rows, 0:LANES] = arrived[0]
        for tile in (1, 2):
            own = arrived.get(tile, arrived.get(tile - 3))
            other = arrived.get(tile - 3, own)
            inside = lanes < columns - offset - LANES * tile
            placed[rows, LANES * tile : LANES * (tile + 1)] = jnp.where(inside, own, other)


def merge_kernel(entries, anchor, parent_next, *refs):
    merged = refs[-1]
    fields, _, rows, columns = parent_next.shape
    span = rows // 3
    rank_x, rank_y = lax.axis_index("gx"), lax.axis_index("gy")
    size_x, size_y = lax.axis_size("gx"), lax.axis_size("gy")
    offset = anchor[1] - size_y // 2 * columns
    shift = lax.rem(offset + columns, columns)
    row = rank_x * rows + row_index(rows, columns) - anchor[0]
    column = rank_y * columns + lane_index(rows, columns) - anchor[1]
    covered = (
        (row >= 0) & (row < size_x * span) & (column >= 0) & (column < size_y * (columns // 3))
    )
    first = anchor[0] - (rows - span) * rank_x
    row_shift = lax.rem(first + size_x * rows, rows)
    slab_row = row_index(span)
    choices = [[], [], []]
    for at, receivers in enumerate(entries):
        for d, ranks in receivers:
            place = first + span * d + slab_row
            if ranks is not None:
                place = jnp.where(among(rank_x, ranks), place, -1)
            choices[d % 3].append((at, (place >= 0) & (place < rows)))
    for field in range(fields):
        tiles = []
        for tile in range(3):
            kinds = []
            for options in choices:
                value = jnp.zeros((span, LANES), F32)
                for at, inside in options:
                    part = slice(LANES * tile, LANES * (tile + 1))
                    cells = refs[at][span * field : span * (field + 1), part]
                    value = jnp.where(inside, cells, value)
                kinds.append(value)
            tiles.append(jnp.concatenate(kinds, axis=0))
        moved = pltpu.roll(jnp.concatenate(tiles, axis=1), row_shift, 0)
        fed_back = pltpu.roll(moved, shift, 1)
        merged[field, 0] = jnp.where(covered, fed_back, parent_next[field, 0])


def spread_matrix(columns):
    span = columns // 3
    matrix = np.zeros((2 * LANES, columns + LANES), np.float32)

    def source(m):
        return LANES if m < 0 else (LANES + 1 if m >= span else m)

    for c in range(-2, columns + 2):
        m, j = divmod(c, 3)
        at = c % (columns + LANES)
        if j == 0:
            matrix[source(m - 1), at] += 1.0
            matrix[source(m), at] += 2.0
        elif j == 1:
            matrix[source(m), at] += 3.0
        else:
            matrix[source(m), at] += 2.0
            matrix[source(m + 1), at] += 1.0
    return jnp.asarray(matrix, jnp.bfloat16)


def gather_matrix(columns):
    matrix = np.zeros((columns, columns // 3), np.float32)
    matrix[np.arange(columns), np.arange(columns) // 3] = 1.0
    return jnp.asarray(matrix, jnp.bfloat16)


def coloured(pairs):
    degree = max(sum(pair[end] == at for pair in pairs) for end in (0, 1) for at, _ in enumerate(pairs + [0, 0]))
    routes = [[] for _ in range(degree)]

    def free(route, end, at):
        return all(pair[end] != at for pair in routes[route])

    for pair in pairs:
        first = next(route for route in range(degree) if free(route, 0, pair[0]))
        second = next(route for route in range(degree) if free(route, 1, pair[1]))
        if not free(first, 1, pair[1]):
            end, at, route, other = 1, pair[1], first, second
            path = []
            while not free(route, end, at):
                step = next(p for p in routes[route] if p[end] == at)
                path.append((step, route, other))
                end, at, route, other = 1 - end, step[1 - end], other, route
            for step, source, _ in path:
                routes[source].remove(step)
            for step, _, target in path:
                routes[target].append(step)
        routes[first].append(pair)
    return [sorted(route) for route in routes]


def row_routes(size, rows):
    span = rows // 3

    def needed(start):
        pairs = set()
        for nest in range(size):
            for at in (start + span * nest, start + span * nest + span + 1):
                pairs.add((at // rows, nest))
        return {(owner, nest) for owner, nest in pairs if owner != nest}

    def cost(pairs):
        cuts = [
            sum((a < cut <= n) if up else (n < cut <= a) for a, n in pairs)
            for cut in range(2, size, 2)
            for up in (False, True)
        ]
        return 4 * max(cuts) + len(coloured(sorted(pairs)))

    ranges = []
    pending = None
    for first in range(0, size * (rows - span) - 2, span):
        last = min(first + span, size * (rows - span) - 2) - 1
        pairs = set().union(*(needed(start) for start in range(first, last)))
        start, extra = first, needed(last)
        if pending is not None:
            before, more = ranges[-1][1], pending
            if cost(before | more) + cost(pairs) <= cost(before) + cost(pairs | more):
                ranges[-1] = (ranges[-1][0], before | more)
            else:
                start, pairs = first - 1, pairs | more
        ranges.append((start + 1, pairs))
        pending = extra
    ranges[-1] = (ranges[-1][0], ranges[-1][1] | pending)
    return [(first, coloured(sorted(pairs))) for first, pairs in ranges]


def column_routes(size):
    routes, selves = {}, {}
    for k in (0, 1, -2, 2, -1):
        pairs = [(size // 2 + p, 3 * p + k) for p in range(size - size // 2)]
        routes[k] = [(s, n) for s, n in pairs if 0 <= n < size and n != s]
        selves.update({k: s for s, n in pairs if n == s})
    return routes, selves


column_cases = (
    (1, (0, 1, 2, -1), (-1, 1)),
    (65, (0, 1, 2, -1), (2, 0)),
    (128, (0, 1, 2, -1, -2), None),
    (129, (0, 1, -1, -2), (-2, 1)),
    (193, (0, 1, -1, -2), (1, 0)),
)


def per_device(
    parent_fields,
    parent_velocity,
    parent_mixing,
    nest_fields,
    nest_velocity,
    nest_mixing,
    nest_anchor,
):
    fields, levels, rows, columns = shape = parent_fields.shape
    channels = fields * levels
    span, last = rows // 3, columns // LANES - 1
    gx, gy = lax.axis_size("gx"), lax.axis_size("gy")
    height, width = rows + 8, columns + LANES
    pf = parent_fields.reshape(channels, rows, columns)
    nf = nest_fields.reshape(channels, rows, columns)
    nv = nest_velocity.reshape(2 * levels, rows, columns)
    nm = nest_mixing
    def row_blocks(array):
        size = (array.shape[0], 8, columns)
        return [(array, block(size, (0, 0, 0))), (array, block(size, (0, rows // 8 - 1, 0)))]

    def column_blocks(array):
        size = (array.shape[0], rows, LANES)
        return [(array, block(size, (0, 0, 0))), (array, block(size, (0, 0, last)))]

    def shaped(*size):
        return size, block(size, (0,) * len(size))

    def whole_of(arrays):
        return [(array, whole(array)) for array in arrays]

    halo_rows = 4 * channels + 6 * levels
    ranges = row_routes(gx, rows)
    middle = gy // 2 * columns
    firsts = ([first for first, _ in ranges], [middle + first for first, _, _ in column_cases])
    scalar = pl.BlockSpec(memory_space=pltpu.SMEM)
    anchor = (nest_anchor, scalar)
    rows_next, rows_prev, cols_next, cols_prev, row_range, column_case = call(
        functools.partial(pack_kernel, firsts),
        1,
        [anchor] + row_blocks(pf) + column_blocks(pf) + row_blocks(nf) + row_blocks(nv) + row_blocks(nm),
        [shaped(halo_rows, columns)] * 2
        + [shaped(rows, LANES)] * 2
        + [((1,), scalar, jnp.int32)] * 2,
    )
    top, bottom = halo_exchange("gx", rows_next, rows_prev)
    left, right = halo_exchange("gy", cols_next, cols_prev)

    slots = max(len(routes) for _, routes in ranges)
    table = np.zeros((len(ranges), gx, slots), np.int32)
    for at, (_, routes) in enumerate(ranges):
        for slot, route in enumerate(routes):
            for owner, nest in route:
                table[at, owner, slot] = (nest - owner) % 3
    message_rows = -(-((span + 2) * (channels + 1)) // 16) * 16
    columns_of, selves = column_routes(gy)
    cells_rows, relay_height = span * channels, (span + 2) * channels

    def by_shift(route, receiver):
        shifts = sorted({nest - owner for owner, nest in route})
        return [(d, [pair[receiver] for pair in route if pair[1] - pair[0] == d]) for d in shifts]

    parent_next, *slabs = call(
        functools.partial(parent_kernel, gx),
        levels,
        [
            anchor,
            (row_range, scalar),
            (jnp.asarray(table.reshape(-1)), scalar),
            (parent_fields, by_level(shape, 1)),
            (parent_velocity, by_level(parent_velocity.shape, 1)),
            (parent_mixing, by_level(parent_mixing.shape, 0)),
        ]
        + whole_of([top, bottom, left, right]),
        [(shape, by_level(shape, 1))] + [shaped(relay_height, columns)] * (slots + 1),
    )

    def relay_rows(routes):
        def branch(nest_anchor, slabs, nf, nv, nm, top, bottom):
            received = [lax.ppermute(slab, "gx", route) for slab, route in zip(slabs[1:], routes)]
            to_next, to_previous = call(
                nest_columns_kernel,
                1,
                column_blocks(nf) + column_blocks(nv) + column_blocks(nm) + whole_of([top, bottom]),
                [shaped(height, LANES)] * 2,
            )
            sides = halo_exchange("gy", to_next, to_previous)
            entries = [None] + [by_shift(route, 1) for route in routes]
            messages = call(
                functools.partial(row_select_kernel, entries, rows, channels),
                1,
                [(nest_anchor, scalar)] + whole_of([slabs[0], *received]),
                [shaped(message_rows, LANES)] * 3 + [shaped(message_rows // 2, LANES)],
            )
            return messages, sides

        return branch

    messages, sides = lax.switch(
        row_range[0], [relay_rows(routes) for _, routes in ranges], nest_anchor, slabs, nf, nv, nm, top, bottom
    )

    def nest_part(ks, half):
        def branch(nest_anchor, messages, nest_fields, nest_velocity, nest_mixing, edges):
            anchor = (nest_anchor, scalar)
            packed = half[0] if half else None
            received = [
                lax.ppermute(messages[3 if k == packed else k % 3], "gy", columns_of[k]) for k in ks
            ]
            coefs, moved, weights = call(
                nest_start_kernel,
                levels,
                [
                    (nest_fields, by_level(shape, 1)),
                    (nest_velocity, by_level(nest_velocity.shape, 1)),
                    (nest_mixing, by_level(nest_mixing.shape, 0)),
                ]
                + whole_of(edges),
                [
                    ((levels, 5, height, width), by_level((levels, 5, height, width), 0)),
                    ((levels, fields, height, width), by_level((levels, fields, height, width), 0)),
                    shaped(height, width),
                ],
                scratch=[(fields + 3, height, width)],
            )
            size = cells_rows // levels

            def strip(rows):
                return (rows * levels, LANES), pl.BlockSpec((rows, LANES), lambda level: (level, 0))

            nest_result, coarse, *coarse_half = call(
                functools.partial(nest_kernel, ks, half, selves),
                levels,
                [anchor]
                + whole_of([spread_matrix(columns), gather_matrix(columns)])
                + [(coefs, by_level(coefs.shape, 0)), (moved, by_level(moved.shape, 0))]
                + whole_of([weights, *received, *messages[:3]]),
                [(shape, by_level(shape, 1)), strip(size)] + ([strip(size // 2)] if half else []),
                scratch=[
                    (message_rows, 2 * LANES),
                    (message_rows, width),
                    (fields, width // LANES, height, LANES),
                    (fields, height, width),
                    (span * fields, columns),
                    (fields, columns // LANES, rows, LANES),
                ],
            )
            returned = [
                lax.ppermute(
                    coarse_half[0] if k == packed else coarse,
                    "gy",
                    [pair[::-1] for pair in columns_of[k]],
                )
                for k in ks
            ]
            placed = call(
                functools.partial(column_select_kernel, ks, half, selves, columns, levels),
                1,
                [anchor] + whole_of([coarse, *returned]),
                [shaped(cells_rows, columns)],
            )[0]
            return nest_result, placed

        return branch

    nest_result, placed = lax.switch(
        column_case[0],
        [nest_part(ks, half) for _, ks, half in column_cases],
        nest_anchor,
        messages,
        nest_fields,
        nest_velocity,
        nest_mixing,
        [top, bottom, *sides],
    )

    def feedback_rows(routes):
        def branch(nest_anchor, parent_next, placed):
            received = [
                lax.ppermute(placed, "gx", [pair[::-1] for pair in route]) for route in routes
            ]
            entries = [[(0, None)]] + [by_shift(route, 0) for route in routes]
            slab_block = pl.BlockSpec((span * fields, columns), lambda level: (level, 0))
            return call(
                functools.partial(merge_kernel, entries),
                levels,
                [
                    (nest_anchor, pl.BlockSpec(memory_space=pltpu.SMEM)),
                    (parent_next, by_level(shape, 1)),
                ]
                + [(array, slab_block) for array in (placed, *received)],
                [(shape, by_level(shape, 1))],
            )[0]

        return branch

    merged = lax.switch(
        row_range[0], [feedback_rows(routes) for _, routes in ranges], nest_anchor, parent_next, placed
    )
    return merged, nest_result


def solution(mesh):
    placed = (
        P(None, None, "gx", "gy"),
        P(None, None, "gx", "gy"),
        P(None, "gx", "gy"),
        P(None, None, "gx", "gy"),
        P(None, None, "gx", "gy"),
        P(None, "gx", "gy"),
        P(),
    )
    return jax.shard_map(
        per_device,
        mesh=mesh,
        in_specs=placed,
        out_specs=(P(None, None, "gx", "gy"), P(None, None, "gx", "gy")),
        check_vma=False,
    )
```

```python
import functools

import jax
import jax.numpy as jnp
import numpy as np
from jax import lax
from jax.experimental import pallas as pl
from jax.experimental.pallas import tpu as pltpu
from jax.sharding import PartitionSpec as P

SUBSTEPS = 3
F32 = jnp.float32
LANES = 128
VMEM_LIMIT = 56 * 1024 * 1024
nudge_floor = 0.1
relax_width = 4.0


def whole(array):
    return pl.BlockSpec(array.shape, lambda level: (0,) * array.ndim)


def block(shape, at):
    return pl.BlockSpec(shape, lambda level: at)


def by_level(shape, dim):
    sizes = tuple(1 if i == dim else n for i, n in enumerate(shape))
    return pl.BlockSpec(sizes, lambda level: tuple(level if i == dim else 0 for i in range(len(shape))))


def call(body, grid, ins, outs, scratch=(), cost=None):
    return pl.pallas_call(
        body,
        grid=(grid,),
        out_shape=[jax.ShapeDtypeStruct(out[0], *(out[2:] or (F32,))) for out in outs],
        in_specs=[spec for _, spec in ins],
        out_specs=[out[1] for out in outs],
        scratch_shapes=[pltpu.VMEM(shape, F32) for shape in scratch],
        cost_estimate=cost,
        compiler_params=pltpu.CompilerParams(vmem_limit_bytes=VMEM_LIMIT),
    )(*[array for array, _ in ins])


def lane_index(rows, lanes=LANES):
    return lax.broadcasted_iota(jnp.int32, (rows, lanes), 1)


def row_index(rows, lanes=LANES):
    return lax.broadcasted_iota(jnp.int32, (rows, lanes), 0)


def among(value, numbers):
    found = False
    for number in numbers:
        found = found | (value == number)
    return found


def swapped(axis, to_pair, to_other):
    count = lax.axis_size(axis)
    pairs = [(at, at ^ 1) for at in range(count)]
    others = [(at, at + 1 if at % 2 else at - 1) for at in range(1, count - 1)]
    return lax.ppermute(to_pair, axis, pairs), lax.ppermute(to_other, axis, others)


def by_side(axis, from_pair, from_other):
    even = lax.rem(lax.axis_index(axis), 2) == 0
    return jnp.where(even, from_other, from_pair), jnp.where(even, from_pair, from_other)


def row_pack_kernel(firsts, anchor, pf_head, pf_tail, nf_head, nf_tail, nv_head, nv_tail, nm_head, nm_tail, *outs):
    to_pair, to_other, *indices = outs
    channels = pf_head.shape[0]
    for at, (index, limits) in enumerate(zip(indices, firsts)):
        index[0] = sum((anchor[at] >= first).astype(jnp.int32) for first in limits[1:])
    coefs = nv_head.shape[0] + nm_head.shape[0]
    even = lax.rem(lax.axis_index("gx"), 2) == 0

    def put(here, head, tail):
        to_pair[here : here + 1, :] = jnp.where(even, tail, head)
        to_other[here : here + 1, :] = jnp.where(even, head, tail)

    for ch in range(channels):
        for at in range(3):
            put(at * channels + ch, nf_head[ch, at : at + 1, :], nf_tail[ch, 5 + at : 6 + at, :])
    base = 3 * channels
    for cc in range(coefs):
        wind = cc < nv_head.shape[0]
        tail, head = (nv_tail, nv_head) if wind else (nm_tail, nm_head)
        row = cc if wind else cc - nv_head.shape[0]
        for at in range(2):
            put(base + at * coefs + cc, head[row, at : at + 1, :], tail[row, 6 + at : 7 + at, :])
    base = base + 2 * coefs
    for ch in range(channels):
        put(base + ch, pf_head[ch, 0:1, :], pf_tail[ch, 7:8, :])


def column_pack_kernel(
    pf_first, pf_last, nf_first, nf_last, nv_first, nv_last, nm_first, nm_last, pair, other, to_pair, to_other
):
    channels, rows = nf_first.shape[:2]
    columns = pair.shape[1]
    winds = nv_first.shape[0]
    coefs = winds + nm_first.shape[0]
    height = rows + 8
    lanes, lane = lane_index(rows), lane_index(1)

    def packed(pf, nf, nv, nm, part, moved):
        main = jnp.zeros((rows, LANES), F32)
        lines = {at: jnp.zeros((1, LANES), F32) for at in range(-3, 3)}

        def add(first, size, tile, halo_rows):
            nonlocal main
            shift = (first + (size if moved else 0)) % LANES
            inside = (lanes >= first) & (lanes < first + size)
            main = jnp.where(inside, pltpu.roll(tile, shift, 1), main)
            inside = (lane >= first) & (lane < first + size)
            for at, value in halo_rows:
                lines[at] = jnp.where(inside, pltpu.roll(value, shift, 1), lines[at])

        def halos(base, step, size, at):
            lines_of = []
            for n in range(size):
                here = base + n * step + at
                before, after = by_side("gx", pair[here : here + 1, part], other[here : here + 1, part])
                lines_of += [(n, after), (n - size, before)]
            return lines_of

        for ch in range(channels):
            add(3 * ch, 3, nf[ch], halos(0, channels, 3, ch))
        base = 3 * channels
        for cc in range(coefs):
            tile = nv[cc] if cc < winds else nm[cc - winds]
            add(base + 2 * cc, 2, tile, halos(base, coefs, 2, cc))
        base = base + 2 * coefs
        for ch in range(channels):
            add(base + ch, 1, pf[ch], [])
        blank = jnp.zeros((2, LANES), F32)
        return jnp.concatenate([main, lines[0], lines[1], lines[2], blank, lines[-3], lines[-2], lines[-1]], axis=0)

    last = packed(pf_last, nf_last, nv_last, nm_last, slice(columns - LANES, columns), True)
    first = packed(pf_first, nf_first, nv_first, nm_first, slice(0, LANES), False)
    even = lax.rem(lax.axis_index("gy"), 2) == 0
    to_pair[...] = jnp.where(even, last, first)
    to_other[...] = jnp.where(even, first, last)


def parent_kernel(size_x, anchor, index, table, pf, pv, pm, row_pair, row_other, col_pair, col_other, parent_next, *slabs):
    fields, _, rows, columns = pf.shape
    level, levels = pl.program_id(0), pl.num_programs(0)
    channels = fields * levels
    span = rows // 3
    rank = lax.axis_index("gx")
    half = lax.axis_size("gy") // 2 * columns
    base = 3 * channels + 2 * 3 * levels
    shift = lax.rem(2 * columns - anchor[1] + half, columns)
    row_shift = lax.rem((rows - span) * rank + size_x * rows - anchor[0], rows)
    row = row_index(rows, columns)
    column = lane_index(rows, columns)
    place = (index[0] * size_x + rank) * (len(slabs) - 1)
    kinds = [table[place + slot] for slot in range(len(slabs) - 1)]
    u, v, k = pv[0, 0], pv[1, 0], pm[0]
    a_w = jnp.maximum(u, 0.0) + k
    a_e = k - jnp.minimum(u, 0.0)
    a_s = jnp.maximum(v, 0.0) + k
    a_n = k - jnp.minimum(v, 0.0)
    a_c = 1.0 - (a_w + a_e + a_s + a_n)
    pad = jnp.zeros((rows, columns - LANES), F32)
    left, right = by_side("gy", col_pair[0:rows, :], col_other[0:rows, :])

    def rows_by_slab(value):
        thirds = [
            (
                value[span * kind : span * (kind + 1)],
                value[(span * kind - 1) % rows : (span * kind - 1) % rows + 1],
                value[span * (kind + 1) % rows : span * (kind + 1) % rows + 1],
            )
            for kind in range(3)
        ]
        yield thirds[0]
        for kind in kinds:
            yield [
                jnp.where(kind == 0, zero, jnp.where(kind == 1, one, two))
                for zero, one, two in zip(*thirds)
            ]

    for field in range(fields):
        ch = field * levels + level
        q = pf[field, 0]
        source = pl.ds(base + ch, 1)
        above, below = by_side("gx", row_pair[source, :], row_other[source, :])
        west = jnp.where(row == 0, above, pltpu.roll(q, 1, 0))
        east = jnp.where(row == rows - 1, below, pltpu.roll(q, rows - 1, 0))
        at_first = pltpu.roll(left, LANES - base - ch, 1)
        at_last = pltpu.roll(right, LANES - 1 - base - ch, 1)
        south = jnp.where(
            column == 0, jnp.concatenate([at_first, pad], axis=1), pltpu.roll(q, 1, 1)
        )
        north = jnp.where(
            column == columns - 1,
            jnp.concatenate([pad, at_last], axis=1),
            pltpu.roll(q, columns - 1, 1),
        )
        result = a_c * q + a_w * west + a_e * east + a_s * south + a_n * north
        parent_next[field, 0] = result
        moved = pltpu.roll(pltpu.roll(result, shift, 1), row_shift, 0)
        here = level * fields + field
        for slab, (cells, before, after) in zip(slabs, rows_by_slab(moved)):
            slab[pl.ds(pl.multiple_of(span * here, 8), span), :] = cells
            slab[pl.ds(span * channels + here, 1), :] = before
            slab[pl.ds((span + 1) * channels + here, 1), :] = after


def packed_half(value, side):
    rows = value.shape[0] // 2
    first, second = value[:rows], value[rows:]
    left = lane_index(rows) < LANES // 2
    if side == 0:
        return jnp.where(left, first, pltpu.roll(second, LANES // 2, 1))
    return jnp.where(left, pltpu.roll(first, LANES // 2, 1), second)


def unpacked_half(value, side):
    turned = pltpu.roll(value, LANES // 2, 1)
    return jnp.concatenate([value, turned] if side == 0 else [turned, value], axis=0)


def row_select_kernel(entries, rows, channels, anchor, *refs):
    count = len(entries)
    slabs, messages, half = refs[:count], refs[count:-1], refs[-1]
    span = rows // 3
    columns = slabs[0].shape[1]
    rank = lax.axis_index("gx")
    start = anchor[0] + span * rank
    lowest, highest = lax.div(start, rows), lax.div(start + span - 1, rows)
    above, below = lax.div(start - 1, rows), lax.div(start + span, rows)
    split = jnp.where(highest > lowest, rows * highest - start, span)
    cells, total = span * channels, (span + 2) * channels

    def pick(owner, first, size, part):
        value = slabs[0][first : first + size, part]
        for senders, slab in zip(entries[1:], slabs[1:]):
            chosen = False
            for d, ranks in senders:
                chosen = chosen | ((rank - owner == d) & among(rank, ranks))
            value = jnp.where(chosen, slab[first : first + size, part], value)
        return value

    tiles, sides = [], []
    for tile in range(3):
        part = slice(LANES * tile, LANES * (tile + 1))
        row = row_index(cells) & (span - 1)
        low, high = pick(lowest, 0, cells, part), pick(highest, 0, cells, part)
        tiles.append(jnp.where(row < split, low, high))
        sides.append([pick(above, cells, channels, part), pick(below, cells + channels, channels, part)])
    lanes, edge_lanes = lane_index(span), lane_index(channels)
    edge_inside = lax.div(edge_lanes, 2) == row_index(channels)

    def beside(parts, tile, lane):
        return jnp.where(lane == LANES - 1, parts[(tile + 2) % 3], parts[(tile + 1) % 3])

    for tile, message in enumerate(messages):
        message[0:cells, :] = tiles[tile]
        rim = jnp.zeros((span, LANES), F32)
        for ch in range(channels):
            here = [value[span * ch : span * (ch + 1)] for value in tiles]
            turned = pltpu.roll(beside(here, tile, lanes), 2 * ch + 1, 1)
            rim = jnp.where((lanes == 2 * ch) | (lanes == 2 * ch + 1), turned, rim)
        message[total : total + span, :] = rim + pltpu.roll(rim, LANES // 2, 1)
        for side in range(2):
            first = cells + side * channels
            message[first : first + channels, :] = sides[tile][side]
            line = beside([value[side] for value in sides], tile, edge_lanes)
            line = pltpu.roll(line, 1, 1, stride=2, stride_axis=0)
            line = jnp.sum(jnp.where(edge_inside, line, 0.0), axis=0, keepdims=True)
            target = total + span + side
            message[target : target + 1, :] = line + pltpu.roll(line, LANES // 2, 1)
        message[total + span + 2 :, :] = jnp.zeros((message.shape[0] - total - span - 2, LANES), F32)
    offset = anchor[1] - lax.axis_size("gy") // 2 * columns
    split_tile = jnp.where(offset < LANES, messages[2][...], messages[1][...])
    right = ((offset <= LANES // 2) | (offset > LANES)) & (offset <= LANES + LANES // 2)
    half[...] = jnp.where(right, packed_half(split_tile, 1), packed_half(split_tile, 0))


def three_parts(x):
    high = x.astype(jnp.bfloat16)
    rest = x - high.astype(F32)
    middle = rest.astype(jnp.bfloat16)
    low = (rest - middle.astype(F32)).astype(jnp.bfloat16)
    return high, middle, low


def exact_dot(x, matrix):
    parts = three_parts(x)
    total = jnp.dot(parts[2], matrix, preferred_element_type=F32)
    total = total + jnp.dot(parts[1], matrix, preferred_element_type=F32)
    return total + jnp.dot(parts[0], matrix, preferred_element_type=F32)


def stencil(q, coefs):
    height, width = q.shape
    return (
        coefs[0] * q
        + coefs[1] * pltpu.roll(q, 1, 0)
        + coefs[2] * pltpu.roll(q, height - 1, 0)
        + coefs[3] * pltpu.roll(q, 1, 1)
        + coefs[4] * pltpu.roll(q, width - 1, 1)
    )


def nest_start_kernel(nf, nv, nm, row_pair, row_other, col_pair, col_other, coefs, moved, weights, state):
    fields, _, rows, columns = nf.shape
    level, levels = pl.program_id(0), pl.num_programs(0)
    channels = fields * levels
    height, width = rows + 8, columns + LANES
    rank_x, rank_y = lax.axis_index("gx"), lax.axis_index("gy")
    row = row_index(height, width)
    column = lane_index(height, width)
    local_row = jnp.where(row < rows + 4, row, row - height)
    local_column = jnp.where(column < columns + LANES // 2, column, column - width)
    global_row = rank_x * rows + local_row
    global_column = rank_y * columns + local_column
    row_distance = jnp.minimum(global_row, lax.axis_size("gx") * rows - 1 - global_row)
    column_distance = jnp.minimum(
        global_column, lax.axis_size("gy") * columns - 1 - global_column
    )
    distance = jnp.minimum(row_distance, column_distance)
    weight = nudge_floor + (1.0 - nudge_floor) * jnp.exp(
        jnp.maximum(distance, 0).astype(F32) / -relax_width
    )
    weight = jnp.where(distance < 0, 0.0, weight)
    keep = 1.0 - weight
    edge_lanes = lane_index(height)

    @pl.when(level == 0)
    def _():
        weights[...] = weight / 9.0
        state[...] = jnp.zeros_like(state)

    left, right = by_side("gy", col_pair[...], col_other[...])

    def side_tile(first, size):
        after = pltpu.roll(right, lax.rem(2 * LANES - first, LANES), 1)
        before = pltpu.roll(left, lax.rem(2 * LANES - first - size, LANES), 1)
        inside = jnp.where(edge_lanes < LANES // 2, after, before)
        outside = (edge_lanes >= size) & (edge_lanes < LANES - size)
        return jnp.where(outside, 0.0, inside)

    def fill(slot, value, base, step, at, size, first):
        state[slot, 0:rows, 0:columns] = value
        for n in range(size):
            source = pl.ds(base + n * step + at, 1)
            above, below = by_side("gx", row_pair[source, :], row_other[source, :])
            state[slot, rows + n : rows + n + 1, 0:columns] = below
            target = height - size + n
            state[slot, target : target + 1, 0:columns] = above
        state[slot, :, columns:width] = side_tile(first, size)

    base = 3 * channels
    for slot, value in enumerate((nv[0, 0], nv[1, 0], nm[0])):
        cc = slot * levels + level
        fill(slot + fields, value, base, 3 * levels, cc, 2, base + 2 * cc)
    for field in range(fields):
        ch = field * levels + level
        fill(field, nf[field, 0], 0, channels, ch, 3, 3 * ch)
    u, v, k = (state[slot + fields] for slot in range(3))
    a_w = jnp.maximum(u, 0.0) + k
    a_e = k - jnp.minimum(u, 0.0)
    a_s = jnp.maximum(v, 0.0) + k
    a_n = k - jnp.minimum(v, 0.0)
    a_c = 1.0 - (a_w + a_e + a_s + a_n)
    for slot, value in enumerate((a_c, a_w, a_e, a_s, a_n)):
        coefs[0, slot] = keep * value
    for field in range(fields):
        moved[0, field] = stencil(state[field], [coefs[0, slot] for slot in range(5)])


def nest_kernel(ks, half, selves, anchor, spread, gather, coefs, moved, weights, *refs):
    count = len(ks) + 3
    received, messages = dict(zip(ks, refs[: len(ks)])), refs[len(ks) : count]
    result, coarse, *coarse_half = refs[count:-6]
    relay, refined, forcing, state, sums, final = refs[-6:]
    fields, _, rows, columns = result.shape
    level, levels = pl.program_id(0), pl.num_programs(0)
    channels = fields * levels
    span_rows, span_columns = rows // 3, columns // 3
    height, width = rows + 8, columns + LANES
    tiles = width // LANES
    relay_rows = span_rows + 2
    total = relay_rows * channels
    offset = anchor[1] - lax.axis_size("gy") // 2 * columns
    kind = lax.rem(lax.axis_index("gy"), 3)
    edge = columns - offset - span_columns * kind

    @pl.when(level == 0)
    def _():
        arrived, rims = {}, {}
        for k in ks:
            value = received[k][...]
            side = half[1] if half and half[0] == k else 0
            if half and half[0] == k:
                value = unpacked_half(value, side)
            rim = value[total : total + relay_rows]
            if side == 1:
                rim = pltpu.roll(rim, LANES // 2, 1)
            if k in selves:
                itself = lax.axis_index("gy") == selves[k]
                own = messages[k % 3][...]
                value = jnp.where(itself, own, value)
                rim = jnp.where(itself, own[total : total + relay_rows], rim)
            arrived[k], rims[k] = value, rim

        def chosen(values):
            low, high = values.get(2, values[0]), values.get(-1, values[0])
            low = jnp.where(kind == 1, values.get(1, values[0]), low)
            low = jnp.where(kind == 0, values[0], low)
            return low, jnp.where(kind == 1, values.get(-2, values[0]), high)

        lower, upper = chosen(arrived)
        rim_low, rim_high = chosen(rims)
        lanes = lane_index(lower.shape[0])
        relay[:, 0:LANES] = jnp.where(lanes < edge, lower, upper)
        relay[total:, LANES:] = jnp.zeros((relay.shape[0] - total, LANES), F32)
        odd = (lane_index(relay_rows) & 1) == 1
        rim = jnp.where(jnp.where(odd, LANES, -1) < edge, rim_low, rim_high)
        for ch in range(channels):
            sides = pltpu.roll(rim, (LANES - 2 * ch) % LANES, 1)
            relay[span_rows * ch : span_rows * (ch + 1), LANES:] = sides[0:span_rows]
            for side in (span_rows, span_rows + 1):
                here = side * channels + ch
                relay[here : here + 1, LANES:] = sides[side : side + 1]
        refined[...] = exact_dot(relay[...], spread[...])

    relay_row = row_index(span_rows, width)
    for field in range(fields):
        ch = level * fields + field
        centre = refined[pl.ds(pl.multiple_of(span_rows * ch, 8), span_rows), :]
        above = refined[pl.ds(span_rows * channels + ch, 1), :]
        below = refined[pl.ds((span_rows + 1) * channels + ch, 1), :]
        before = jnp.where(relay_row == 0, above, pltpu.roll(centre, 1, 0))
        after = jnp.where(
            relay_row == span_rows - 1, below, pltpu.roll(centre, span_rows - 1, 0)
        )
        thirds = (before + 2.0 * centre, 3.0 * centre, 2.0 * centre + after)
        rims = (
            (rows, centre[span_rows - 1 :] + 2.0 * below),
            (rows + 1, 3.0 * below),
            (height - 2, 3.0 * above),
            (height - 1, 2.0 * above + centre[0:1]),
        )
        for tile in range(tiles):
            part = slice(LANES * tile, LANES * (tile + 1))
            for at, value in enumerate(thirds):
                forcing[field, tile, pl.ds(at, span_rows, stride=3), :] = value[:, part]
            forcing[field, tile, rows + 2 : height - 2, :] = jnp.zeros((4, LANES), F32)
            for at, value in rims:
                forcing[field, tile, at : at + 1, :] = value[:, part]
    for field in range(fields):
        for tile in range(tiles):
            part = slice(LANES * tile, LANES * (tile + 1))
            pull = weights[:, part] * forcing[field, tile]
            forcing[field, tile] = pull
            state[field, :, part] = moved[0, field, :, part] + pull
    for step in range(SUBSTEPS - 1):
        for field in range(fields):
            pull = jnp.concatenate([forcing[field, tile] for tile in range(tiles)], axis=1)
            value = pull + stencil(state[field], [coefs[0, slot] for slot in range(5)])
            if step < SUBSTEPS - 2:
                state[field] = value
            else:
                result[field, 0] = value[0:rows, 0:columns]
                for tile in range(tiles - 1):
                    final[field, tile] = value[0:rows, LANES * tile : LANES * (tile + 1)]
    for field in range(fields):
        for tile in range(tiles - 1):
            part = slice(LANES * tile, LANES * (tile + 1))
            sums[span_rows * field : span_rows * (field + 1), part] = (
                final[field, tile, pl.ds(0, span_rows, stride=3), :]
                + final[field, tile, pl.ds(1, span_rows, stride=3), :]
                + final[field, tile, pl.ds(2, span_rows, stride=3), :]
            )
    means = exact_dot(sums[...], gather[...]) / 9.0
    coarse[...] = means
    if half:
        coarse_half[0][...] = packed_half(means, half[1])


def column_select_kernel(ks, half, selves, columns, levels, anchor, coarse, *refs):
    returned, placed = refs[:-1], refs[-1]
    offset = anchor[1] - lax.axis_size("gy") // 2 * columns
    size = placed.shape[0] // levels
    lanes = lane_index(size)
    for level in range(levels):
        rows = slice(size * level, size * (level + 1))
        arrived = {}
        for k, ref in zip(ks, returned):
            if half and half[0] == k:
                value = ref[size // 2 * level : size // 2 * (level + 1), :]
                value = unpacked_half(value, half[1])
            else:
                value = ref[rows, :]
            if k in selves:
                value = jnp.where(lax.axis_index("gy") == selves[k], coarse[rows, :], value)
            arrived[k] = value
        placed[rows, 0:LANES] = arrived[0]
        for tile in (1, 2):
            own = arrived.get(tile, arrived.get(tile - 3))
            other = arrived.get(tile - 3, own)
            inside = lanes < columns - offset - LANES * tile
            placed[rows, LANES * tile : LANES * (tile + 1)] = jnp.where(inside, own, other)


def merge_kernel(entries, anchor, parent_next, *refs):
    merged = refs[-1]
    fields, _, rows, columns = parent_next.shape
    span = rows // 3
    rank_x, rank_y = lax.axis_index("gx"), lax.axis_index("gy")
    size_x, size_y = lax.axis_size("gx"), lax.axis_size("gy")
    offset = anchor[1] - size_y // 2 * columns
    shift = lax.rem(offset + columns, columns)
    row = rank_x * rows + row_index(rows, columns) - anchor[0]
    column = rank_y * columns + lane_index(rows, columns) - anchor[1]
    covered = (
        (row >= 0) & (row < size_x * span) & (column >= 0) & (column < size_y * (columns // 3))
    )
    first = anchor[0] - (rows - span) * rank_x
    row_shift = lax.rem(first + size_x * rows, rows)
    slab_row = row_index(span)
    choices = [[], [], []]
    for at, receivers in enumerate(entries):
        for d, ranks in receivers:
            place = first + span * d + slab_row
            if ranks is not None:
                place = jnp.where(among(rank_x, ranks), place, -1)
            choices[d % 3].append((at, (place >= 0) & (place < rows)))
    for field in range(fields):
        tiles = []
        for tile in range(3):
            kinds = []
            for options in choices:
                value = jnp.zeros((span, LANES), F32)
                for at, inside in options:
                    part = slice(LANES * tile, LANES * (tile + 1))
                    cells = refs[at][span * field : span * (field + 1), part]
                    value = jnp.where(inside, cells, value)
                kinds.append(value)
            tiles.append(jnp.concatenate(kinds, axis=0))
        moved = pltpu.roll(jnp.concatenate(tiles, axis=1), row_shift, 0)
        fed_back = pltpu.roll(moved, shift, 1)
        merged[field, 0] = jnp.where(covered, fed_back, parent_next[field, 0])


def spread_matrix(columns):
    span = columns // 3
    matrix = np.zeros((2 * LANES, columns + LANES), np.float32)

    def source(m):
        return LANES if m < 0 else (LANES + 1 if m >= span else m)

    for c in range(-2, columns + 2):
        m, j = divmod(c, 3)
        at = c % (columns + LANES)
        if j == 0:
            matrix[source(m - 1), at] += 1.0
            matrix[source(m), at] += 2.0
        elif j == 1:
            matrix[source(m), at] += 3.0
        else:
            matrix[source(m), at] += 2.0
            matrix[source(m + 1), at] += 1.0
    return jnp.asarray(matrix, jnp.bfloat16)


def gather_matrix(columns):
    matrix = np.zeros((columns, columns // 3), np.float32)
    matrix[np.arange(columns), np.arange(columns) // 3] = 1.0
    return jnp.asarray(matrix, jnp.bfloat16)


def coloured(pairs):
    degree = max(sum(pair[end] == at for pair in pairs) for end in (0, 1) for at, _ in enumerate(pairs + [0, 0]))
    routes = [[] for _ in range(degree)]

    def free(route, end, at):
        return all(pair[end] != at for pair in routes[route])

    for pair in pairs:
        first = next(route for route in range(degree) if free(route, 0, pair[0]))
        second = next(route for route in range(degree) if free(route, 1, pair[1]))
        if not free(first, 1, pair[1]):
            end, at, route, other = 1, pair[1], first, second
            path = []
            while not free(route, end, at):
                step = next(p for p in routes[route] if p[end] == at)
                path.append((step, route, other))
                end, at, route, other = 1 - end, step[1 - end], other, route
            for step, source, _ in path:
                routes[source].remove(step)
            for step, _, target in path:
                routes[target].append(step)
        routes[first].append(pair)
    return [sorted(route) for route in routes]


def row_routes(size, rows):
    span = rows // 3

    def needed(start):
        pairs = set()
        for nest in range(size):
            for at in (start + span * nest, start + span * nest + span + 1):
                pairs.add((at // rows, nest))
        return {(owner, nest) for owner, nest in pairs if owner != nest}

    def cost(pairs):
        cuts = [
            sum((a < cut <= n) if up else (n < cut <= a) for a, n in pairs)
            for cut in range(2, size, 2)
            for up in (False, True)
        ]
        return 4 * max(cuts) + len(coloured(sorted(pairs)))

    ranges = []
    pending = None
    for first in range(0, size * (rows - span) - 2, span):
        last = min(first + span, size * (rows - span) - 2) - 1
        pairs = set().union(*(needed(start) for start in range(first, last)))
        start, extra = first, needed(last)
        if pending is not None:
            before, more = ranges[-1][1], pending
            if cost(before | more) + cost(pairs) <= cost(before) + cost(pairs | more):
                ranges[-1] = (ranges[-1][0], before | more)
            else:
                start, pairs = first - 1, pairs | more
        ranges.append((start + 1, pairs))
        pending = extra
    ranges[-1] = (ranges[-1][0], ranges[-1][1] | pending)
    return [(first, coloured(sorted(pairs))) for first, pairs in ranges]


def column_routes(size):
    routes, selves = {}, {}
    for k in (0, 1, -2, 2, -1):
        pairs = [(size // 2 + p, 3 * p + k) for p in range(size - size // 2)]
        routes[k] = [(s, n) for s, n in pairs if 0 <= n < size and n != s]
        selves.update({k: s for s, n in pairs if n == s})
    return routes, selves


column_cases = (
    (1, (0, 1, 2, -1), (-1, 1)),
    (65, (0, 1, 2, -1), (2, 0)),
    (128, (0, 1, 2, -1, -2), None),
    (129, (0, 1, -1, -2), (-2, 1)),
    (193, (0, 1, -1, -2), (1, 0)),
)


def per_device(
    parent_fields,
    parent_velocity,
    parent_mixing,
    nest_fields,
    nest_velocity,
    nest_mixing,
    nest_anchor,
):
    fields, levels, rows, columns = shape = parent_fields.shape
    channels = fields * levels
    span, last = rows // 3, columns // LANES - 1
    gx, gy = lax.axis_size("gx"), lax.axis_size("gy")
    height, width = rows + 8, columns + LANES
    pf = parent_fields.reshape(channels, rows, columns)
    nf = nest_fields.reshape(channels, rows, columns)
    nv = nest_velocity.reshape(2 * levels, rows, columns)
    nm = nest_mixing
    def row_blocks(array):
        size = (array.shape[0], 8, columns)
        return [(array, block(size, (0, 0, 0))), (array, block(size, (0, rows // 8 - 1, 0)))]

    def column_blocks(array):
        size = (array.shape[0], rows, LANES)
        return [(array, block(size, (0, 0, 0))), (array, block(size, (0, 0, last)))]

    def shaped(*size):
        return size, block(size, (0,) * len(size))

    def whole_of(arrays):
        return [(array, whole(array)) for array in arrays]

    halo_rows = 4 * channels + 6 * levels
    ranges = row_routes(gx, rows)
    middle = gy // 2 * columns
    firsts = ([first for first, _ in ranges], [middle + first for first, _, _ in column_cases])
    scalar = pl.BlockSpec(memory_space=pltpu.SMEM)
    anchor = (nest_anchor, scalar)
    to_pair, to_other, row_range, column_case = call(
        functools.partial(row_pack_kernel, firsts),
        1,
        [anchor] + row_blocks(pf) + row_blocks(nf) + row_blocks(nv) + row_blocks(nm),
        [shaped(halo_rows, columns)] * 2 + [((1,), scalar, jnp.int32)] * 2,
    )
    row_halos = swapped("gx", to_pair, to_other)
    to_pair, to_other = call(
        column_pack_kernel,
        1,
        column_blocks(pf)
        + column_blocks(nf)
        + column_blocks(nv)
        + column_blocks(nm)
        + whole_of(row_halos),
        [shaped(height, LANES)] * 2,
    )
    halos = [*row_halos, *swapped("gy", to_pair, to_other)]

    slots = max(len(routes) for _, routes in ranges)
    table = np.zeros((len(ranges), gx, slots), np.int32)
    for at, (_, routes) in enumerate(ranges):
        for slot, route in enumerate(routes):
            for owner, nest in route:
                table[at, owner, slot] = (nest - owner) % 3
    message_rows = -(-((span + 2) * (channels + 1)) // 16) * 16
    columns_of, selves = column_routes(gy)
    cells_rows, relay_height = span * channels, (span + 2) * channels

    def by_shift(route, receiver):
        shifts = sorted({nest - owner for owner, nest in route})
        return [(d, [pair[receiver] for pair in route if pair[1] - pair[0] == d]) for d in shifts]

    parent_next, *slabs = call(
        functools.partial(parent_kernel, gx),
        levels,
        [
            anchor,
            (row_range, scalar),
            (jnp.asarray(table.reshape(-1)), scalar),
            (parent_fields, by_level(shape, 1)),
            (parent_velocity, by_level(parent_velocity.shape, 1)),
            (parent_mixing, by_level(parent_mixing.shape, 0)),
        ]
        + whole_of(halos),
        [(shape, by_level(shape, 1))] + [shaped(relay_height, columns)] * (slots + 1),
    )

    def relay_rows(routes):
        def branch(nest_anchor, slabs, nest_fields, nest_velocity, nest_mixing, halos):
            received = [lax.ppermute(slab, "gx", route) for slab, route in zip(slabs[1:], routes)]
            started = call(
                nest_start_kernel,
                levels,
                [
                    (nest_fields, by_level(shape, 1)),
                    (nest_velocity, by_level(nest_velocity.shape, 1)),
                    (nest_mixing, by_level(nest_mixing.shape, 0)),
                ]
                + whole_of(halos),
                [
                    ((levels, 5, height, width), by_level((levels, 5, height, width), 0)),
                    ((levels, fields, height, width), by_level((levels, fields, height, width), 0)),
                    shaped(height, width),
                ],
                scratch=[(fields + 3, height, width)],
            )
            entries = [None] + [by_shift(route, 1) for route in routes]
            messages = call(
                functools.partial(row_select_kernel, entries, rows, channels),
                1,
                [(nest_anchor, scalar)] + whole_of([slabs[0], *received]),
                [shaped(message_rows, LANES)] * 3 + [shaped(message_rows // 2, LANES)],
            )
            return messages, started

        return branch

    messages, started = lax.switch(
        row_range[0],
        [relay_rows(routes) for _, routes in ranges],
        nest_anchor,
        slabs,
        nest_fields,
        nest_velocity,
        nest_mixing,
        halos,
    )

    def nest_part(ks, half):
        def branch(nest_anchor, messages, coefs, moved, weights):
            anchor = (nest_anchor, scalar)
            packed = half[0] if half else None
            received = [
                lax.ppermute(messages[3 if k == packed else k % 3], "gy", columns_of[k]) for k in ks
            ]
            size = cells_rows // levels

            def strip(rows):
                return (rows * levels, LANES), pl.BlockSpec((rows, LANES), lambda level: (level, 0))

            nest_result, coarse, *coarse_half = call(
                functools.partial(nest_kernel, ks, half, selves),
                levels,
                [anchor]
                + whole_of([spread_matrix(columns), gather_matrix(columns)])
                + [(coefs, by_level(coefs.shape, 0)), (moved, by_level(moved.shape, 0))]
                + whole_of([weights, *received, *messages[:3]]),
                [(shape, by_level(shape, 1)), strip(size)] + ([strip(size // 2)] if half else []),
                scratch=[
                    (message_rows, 2 * LANES),
                    (message_rows, width),
                    (fields, width // LANES, height, LANES),
                    (fields, height, width),
                    (span * fields, columns),
                    (fields, columns // LANES, rows, LANES),
                ],
            )
            returned = [
                lax.ppermute(
                    coarse_half[0] if k == packed else coarse,
                    "gy",
                    [pair[::-1] for pair in columns_of[k]],
                )
                for k in ks
            ]
            placed = call(
                functools.partial(column_select_kernel, ks, half, selves, columns, levels),
                1,
                [anchor] + whole_of([coarse, *returned]),
                [shaped(cells_rows, columns)],
            )[0]
            return nest_result, placed

        return branch

    nest_result, placed = lax.switch(
        column_case[0],
        [nest_part(ks, half) for _, ks, half in column_cases],
        nest_anchor,
        messages,
        *started,
    )

    def feedback_rows(routes):
        def branch(nest_anchor, parent_next, placed):
            received = [
                lax.ppermute(placed, "gx", [pair[::-1] for pair in route]) for route in routes
            ]
            entries = [[(0, None)]] + [by_shift(route, 0) for route in routes]
            slab_block = pl.BlockSpec((span * fields, columns), lambda level: (level, 0))
            return call(
                functools.partial(merge_kernel, entries),
                levels,
                [
                    (nest_anchor, pl.BlockSpec(memory_space=pltpu.SMEM)),
                    (parent_next, by_level(shape, 1)),
                ]
                + [(array, slab_block) for array in (placed, *received)],
                [(shape, by_level(shape, 1))],
            )[0]

        return branch

    merged = lax.switch(
        row_range[0], [feedback_rows(routes) for _, routes in ranges], nest_anchor, parent_next, placed
    )
    return merged, nest_result


def solution(mesh):
    placed = (
        P(None, None, "gx", "gy"),
        P(None, None, "gx", "gy"),
        P(None, "gx", "gy"),
        P(None, None, "gx", "gy"),
        P(None, None, "gx", "gy"),
        P(None, "gx", "gy"),
        P(),
    )
    return jax.shard_map(
        per_device,
        mesh=mesh,
        in_specs=placed,
        out_specs=(P(None, None, "gx", "gy"), P(None, None, "gx", "gy")),
        check_vma=False,
    )
```

```python
import functools

import jax
import jax.numpy as jnp
import numpy as np
from jax import lax
from jax.experimental import pallas as pl
from jax.experimental.pallas import tpu as pltpu
from jax.sharding import PartitionSpec as P

SUBSTEPS = 3
F32 = jnp.float32
LANES = 128
VMEM_LIMIT = 56 * 1024 * 1024
nudge_floor = 0.1
relax_width = 4.0


def whole(array):
    return pl.BlockSpec(array.shape, lambda level: (0,) * array.ndim)


def block(shape, at):
    return pl.BlockSpec(shape, lambda level: at)


def by_level(shape, dim):
    sizes = tuple(1 if i == dim else n for i, n in enumerate(shape))
    return pl.BlockSpec(sizes, lambda level: tuple(level if i == dim else 0 for i in range(len(shape))))


def call(body, grid, ins, outs, scratch=(), cost=None):
    return pl.pallas_call(
        body,
        grid=(grid,),
        out_shape=[jax.ShapeDtypeStruct(out[0], *(out[2:] or (F32,))) for out in outs],
        in_specs=[spec for _, spec in ins],
        out_specs=[out[1] for out in outs],
        scratch_shapes=[pltpu.VMEM(shape, F32) for shape in scratch],
        cost_estimate=cost,
        compiler_params=pltpu.CompilerParams(vmem_limit_bytes=VMEM_LIMIT),
    )(*[array for array, _ in ins])


def lane_index(rows, lanes=LANES):
    return lax.broadcasted_iota(jnp.int32, (rows, lanes), 1)


def row_index(rows, lanes=LANES):
    return lax.broadcasted_iota(jnp.int32, (rows, lanes), 0)


def among(value, numbers):
    found = False
    for number in numbers:
        found = found | (value == number)
    return found


def swapped(axis, to_pair, to_other):
    count = lax.axis_size(axis)
    pairs = [(at, at ^ 1) for at in range(count)]
    others = [(at, at + 1 if at % 2 else at - 1) for at in range(1, count - 1)]
    return lax.ppermute(to_pair, axis, pairs), lax.ppermute(to_other, axis, others)


def by_side(axis, from_pair, from_other):
    even = lax.rem(lax.axis_index(axis), 2) == 0
    return jnp.where(even, from_other, from_pair), jnp.where(even, from_pair, from_other)


def pack_kernel(firsts, anchor, pf_head, pf_tail, pf_first, pf_last, nf_head, nf_tail, nv_head, nv_tail, nm_head, nm_tail, *outs):
    to_pair, to_other, col_to_pair, col_to_other, *indices = outs
    channels, rows = pf_first.shape[:2]
    for at, (index, limits) in enumerate(zip(indices, firsts)):
        index[0] = sum((anchor[at] >= first).astype(jnp.int32) for first in limits[1:])
    coefs = nv_head.shape[0] + nm_head.shape[0]
    even = lax.rem(lax.axis_index("gx"), 2) == 0

    def put(here, head, tail):
        to_pair[here : here + 1, :] = jnp.where(even, tail, head)
        to_other[here : here + 1, :] = jnp.where(even, head, tail)

    for ch in range(channels):
        for at in range(3):
            put(at * channels + ch, nf_head[ch, at : at + 1, :], nf_tail[ch, 5 + at : 6 + at, :])
    base = 3 * channels
    for cc in range(coefs):
        wind = cc < nv_head.shape[0]
        tail, head = (nv_tail, nv_head) if wind else (nm_tail, nm_head)
        row = cc if wind else cc - nv_head.shape[0]
        for at in range(2):
            put(base + at * coefs + cc, head[row, at : at + 1, :], tail[row, 6 + at : 7 + at, :])
    base = base + 2 * coefs
    for ch in range(channels):
        put(base + ch, pf_head[ch, 0:1, :], pf_tail[ch, 7:8, :])
    lanes = lane_index(rows)
    last = jnp.zeros((rows, LANES), F32)
    first = jnp.zeros((rows, LANES), F32)
    for ch in range(channels):
        last = jnp.where(lanes == ch, pltpu.roll(pf_last[ch], (ch + 1) % LANES, 1), last)
        first = jnp.where(lanes == ch, pltpu.roll(pf_first[ch], ch, 1), first)
    even = lax.rem(lax.axis_index("gy"), 2) == 0
    col_to_pair[...] = jnp.where(even, last, first)
    col_to_other[...] = jnp.where(even, first, last)


def column_pack_kernel(
    nf_first, nf_last, nv_first, nv_last, nm_first, nm_last, pair, other, to_pair, to_other
):
    channels, rows = nf_first.shape[:2]
    columns = pair.shape[1]
    winds = nv_first.shape[0]
    coefs = winds + nm_first.shape[0]
    height = rows + 8
    lanes, lane = lane_index(rows), lane_index(1)

    def packed(nf, nv, nm, part, moved):
        main = jnp.zeros((rows, LANES), F32)
        lines = {at: jnp.zeros((1, LANES), F32) for at in range(-3, 3)}

        def add(first, size, tile, halo_rows):
            nonlocal main
            shift = (first + (size if moved else 0)) % LANES
            inside = (lanes >= first) & (lanes < first + size)
            main = jnp.where(inside, pltpu.roll(tile, shift, 1), main)
            inside = (lane >= first) & (lane < first + size)
            for at, value in halo_rows:
                lines[at] = jnp.where(inside, pltpu.roll(value, shift, 1), lines[at])

        def halos(base, step, size, at):
            lines_of = []
            for n in range(size):
                here = base + n * step + at
                before, after = by_side("gx", pair[here : here + 1, part], other[here : here + 1, part])
                lines_of += [(n, after), (n - size, before)]
            return lines_of

        for ch in range(channels):
            add(3 * ch, 3, nf[ch], halos(0, channels, 3, ch))
        base = 3 * channels
        for cc in range(coefs):
            tile = nv[cc] if cc < winds else nm[cc - winds]
            add(base + 2 * cc, 2, tile, halos(base, coefs, 2, cc))
        blank = jnp.zeros((2, LANES), F32)
        return jnp.concatenate([main, lines[0], lines[1], lines[2], blank, lines[-3], lines[-2], lines[-1]], axis=0)

    last = packed(nf_last, nv_last, nm_last, slice(columns - LANES, columns), True)
    first = packed(nf_first, nv_first, nm_first, slice(0, LANES), False)
    even = lax.rem(lax.axis_index("gy"), 2) == 0
    to_pair[...] = jnp.where(even, last, first)
    to_other[...] = jnp.where(even, first, last)


def parent_kernel(size_x, anchor, index, table, pf, pv, pm, row_pair, row_other, col_pair, col_other, parent_next, *slabs):
    fields, _, rows, columns = pf.shape
    level, levels = pl.program_id(0), pl.num_programs(0)
    channels = fields * levels
    span = rows // 3
    rank = lax.axis_index("gx")
    half = lax.axis_size("gy") // 2 * columns
    base = 3 * channels + 2 * 3 * levels
    shift = lax.rem(2 * columns - anchor[1] + half, columns)
    row_shift = lax.rem((rows - span) * rank + size_x * rows - anchor[0], rows)
    row = row_index(rows, columns)
    column = lane_index(rows, columns)
    place = (index[0] * size_x + rank) * (len(slabs) - 1)
    kinds = [table[place + slot] for slot in range(len(slabs) - 1)]
    u, v, k = pv[0, 0], pv[1, 0], pm[0]
    a_w = jnp.maximum(u, 0.0) + k
    a_e = k - jnp.minimum(u, 0.0)
    a_s = jnp.maximum(v, 0.0) + k
    a_n = k - jnp.minimum(v, 0.0)
    a_c = 1.0 - (a_w + a_e + a_s + a_n)
    pad = jnp.zeros((rows, columns - LANES), F32)
    left, right = by_side("gy", col_pair[...], col_other[...])

    def rows_by_slab(value):
        thirds = [
            (
                value[span * kind : span * (kind + 1)],
                value[(span * kind - 1) % rows : (span * kind - 1) % rows + 1],
                value[span * (kind + 1) % rows : span * (kind + 1) % rows + 1],
            )
            for kind in range(3)
        ]
        yield thirds[0]
        for kind in kinds:
            yield [
                jnp.where(kind == 0, zero, jnp.where(kind == 1, one, two))
                for zero, one, two in zip(*thirds)
            ]

    for field in range(fields):
        ch = field * levels + level
        q = pf[field, 0]
        source = pl.ds(base + ch, 1)
        above, below = by_side("gx", row_pair[source, :], row_other[source, :])
        west = jnp.where(row == 0, above, pltpu.roll(q, 1, 0))
        east = jnp.where(row == rows - 1, below, pltpu.roll(q, rows - 1, 0))
        at_first = pltpu.roll(left, LANES - ch, 1)
        at_last = pltpu.roll(right, LANES - 1 - ch, 1)
        south = jnp.where(
            column == 0, jnp.concatenate([at_first, pad], axis=1), pltpu.roll(q, 1, 1)
        )
        north = jnp.where(
            column == columns - 1,
            jnp.concatenate([pad, at_last], axis=1),
            pltpu.roll(q, columns - 1, 1),
        )
        result = a_c * q + a_w * west + a_e * east + a_s * south + a_n * north
        parent_next[field, 0] = result
        moved = pltpu.roll(pltpu.roll(result, shift, 1), row_shift, 0)
        here = level * fields + field
        for slab, (cells, before, after) in zip(slabs, rows_by_slab(moved)):
            slab[pl.ds(pl.multiple_of(span * here, 8), span), :] = cells
            slab[pl.ds(span * channels + here, 1), :] = before
            slab[pl.ds((span + 1) * channels + here, 1), :] = after


def packed_half(value, side):
    rows = value.shape[0] // 2
    first, second = value[:rows], value[rows:]
    left = lane_index(rows) < LANES // 2
    if side == 0:
        return jnp.where(left, first, pltpu.roll(second, LANES // 2, 1))
    return jnp.where(left, pltpu.roll(first, LANES // 2, 1), second)


def unpacked_half(value, side):
    turned = pltpu.roll(value, LANES // 2, 1)
    return jnp.concatenate([value, turned] if side == 0 else [turned, value], axis=0)


def row_select_kernel(entries, rows, channels, anchor, *refs):
    count = len(entries)
    slabs, messages, half = refs[:count], refs[count:-1], refs[-1]
    span = rows // 3
    columns = slabs[0].shape[1]
    rank = lax.axis_index("gx")
    start = anchor[0] + span * rank
    lowest, highest = lax.div(start, rows), lax.div(start + span - 1, rows)
    above, below = lax.div(start - 1, rows), lax.div(start + span, rows)
    split = jnp.where(highest > lowest, rows * highest - start, span)
    cells, total = span * channels, (span + 2) * channels

    def pick(owner, first, size, part):
        value = slabs[0][first : first + size, part]
        for senders, slab in zip(entries[1:], slabs[1:]):
            chosen = False
            for d, ranks in senders:
                chosen = chosen | ((rank - owner == d) & among(rank, ranks))
            value = jnp.where(chosen, slab[first : first + size, part], value)
        return value

    tiles, sides = [], []
    for tile in range(3):
        part = slice(LANES * tile, LANES * (tile + 1))
        row = row_index(cells) & (span - 1)
        low, high = pick(lowest, 0, cells, part), pick(highest, 0, cells, part)
        tiles.append(jnp.where(row < split, low, high))
        sides.append([pick(above, cells, channels, part), pick(below, cells + channels, channels, part)])
    lanes, edge_lanes = lane_index(span), lane_index(channels)
    edge_inside = lax.div(edge_lanes, 2) == row_index(channels)

    def beside(parts, tile, lane):
        return jnp.where(lane == LANES - 1, parts[(tile + 2) % 3], parts[(tile + 1) % 3])

    for tile, message in enumerate(messages):
        message[0:cells, :] = tiles[tile]
        rim = jnp.zeros((span, LANES), F32)
        for ch in range(channels):
            here = [value[span * ch : span * (ch + 1)] for value in tiles]
            turned = pltpu.roll(beside(here, tile, lanes), 2 * ch + 1, 1)
            rim = jnp.where((lanes == 2 * ch) | (lanes == 2 * ch + 1), turned, rim)
        message[total : total + span, :] = rim + pltpu.roll(rim, LANES // 2, 1)
        for side in range(2):
            first = cells + side * channels
            message[first : first + channels, :] = sides[tile][side]
            line = beside([value[side] for value in sides], tile, edge_lanes)
            line = pltpu.roll(line, 1, 1, stride=2, stride_axis=0)
            line = jnp.sum(jnp.where(edge_inside, line, 0.0), axis=0, keepdims=True)
            target = total + span + side
            message[target : target + 1, :] = line + pltpu.roll(line, LANES // 2, 1)
        message[total + span + 2 :, :] = jnp.zeros((message.shape[0] - total - span - 2, LANES), F32)
    offset = anchor[1] - lax.axis_size("gy") // 2 * columns
    split_tile = jnp.where(offset < LANES, messages[2][...], messages[1][...])
    right = ((offset <= LANES // 2) | (offset > LANES)) & (offset <= LANES + LANES // 2)
    half[...] = jnp.where(right, packed_half(split_tile, 1), packed_half(split_tile, 0))


def three_parts(x):
    high = x.astype(jnp.bfloat16)
    rest = x - high.astype(F32)
    middle = rest.astype(jnp.bfloat16)
    low = (rest - middle.astype(F32)).astype(jnp.bfloat16)
    return high, middle, low


def exact_dot(x, matrix):
    parts = three_parts(x)
    total = jnp.dot(parts[2], matrix, preferred_element_type=F32)
    total = total + jnp.dot(parts[1], matrix, preferred_element_type=F32)
    return total + jnp.dot(parts[0], matrix, preferred_element_type=F32)


def stencil(q, coefs):
    height, width = q.shape
    return (
        coefs[0] * q
        + coefs[1] * pltpu.roll(q, 1, 0)
        + coefs[2] * pltpu.roll(q, height - 1, 0)
        + coefs[3] * pltpu.roll(q, 1, 1)
        + coefs[4] * pltpu.roll(q, width - 1, 1)
    )


def nest_start_kernel(nf, nv, nm, row_pair, row_other, col_pair, col_other, coefs, moved, weights, state):
    fields, _, rows, columns = nf.shape
    level, levels = pl.program_id(0), pl.num_programs(0)
    channels = fields * levels
    height, width = rows + 8, columns + LANES
    rank_x, rank_y = lax.axis_index("gx"), lax.axis_index("gy")
    row = row_index(height, width)
    column = lane_index(height, width)
    local_row = jnp.where(row < rows + 4, row, row - height)
    local_column = jnp.where(column < columns + LANES // 2, column, column - width)
    global_row = rank_x * rows + local_row
    global_column = rank_y * columns + local_column
    row_distance = jnp.minimum(global_row, lax.axis_size("gx") * rows - 1 - global_row)
    column_distance = jnp.minimum(
        global_column, lax.axis_size("gy") * columns - 1 - global_column
    )
    distance = jnp.minimum(row_distance, column_distance)
    weight = nudge_floor + (1.0 - nudge_floor) * jnp.exp(
        jnp.maximum(distance, 0).astype(F32) / -relax_width
    )
    weight = jnp.where(distance < 0, 0.0, weight)
    keep = 1.0 - weight
    edge_lanes = lane_index(height)

    @pl.when(level == 0)
    def _():
        weights[...] = weight / 9.0
        state[...] = jnp.zeros_like(state)

    left, right = by_side("gy", col_pair[...], col_other[...])

    def side_tile(first, size):
        after = pltpu.roll(right, lax.rem(2 * LANES - first, LANES), 1)
        before = pltpu.roll(left, lax.rem(2 * LANES - first - size, LANES), 1)
        inside = jnp.where(edge_lanes < LANES // 2, after, before)
        outside = (edge_lanes >= size) & (edge_lanes < LANES - size)
        return jnp.where(outside, 0.0, inside)

    def fill(slot, value, base, step, at, size, first):
        state[slot, 0:rows, 0:columns] = value
        for n in range(size):
            source = pl.ds(base + n * step + at, 1)
            above, below = by_side("gx", row_pair[source, :], row_other[source, :])
            state[slot, rows + n : rows + n + 1, 0:columns] = below
            target = height - size + n
            state[slot, target : target + 1, 0:columns] = above
        state[slot, :, columns:width] = side_tile(first, size)

    base = 3 * channels
    for slot, value in enumerate((nv[0, 0], nv[1, 0], nm[0])):
        cc = slot * levels + level
        fill(slot + fields, value, base, 3 * levels, cc, 2, base + 2 * cc)
    for field in range(fields):
        ch = field * levels + level
        fill(field, nf[field, 0], 0, channels, ch, 3, 3 * ch)
    u, v, k = (state[slot + fields] for slot in range(3))
    a_w = jnp.maximum(u, 0.0) + k
    a_e = k - jnp.minimum(u, 0.0)
    a_s = jnp.maximum(v, 0.0) + k
    a_n = k - jnp.minimum(v, 0.0)
    a_c = 1.0 - (a_w + a_e + a_s + a_n)
    for slot, value in enumerate((a_c, a_w, a_e, a_s, a_n)):
        coefs[0, slot] = keep * value
    for field in range(fields):
        moved[0, field] = stencil(state[field], [coefs[0, slot] for slot in range(5)])


def nest_kernel(ks, half, selves, anchor, spread, gather, coefs, moved, weights, *refs):
    count = len(ks) + 3
    received, messages = dict(zip(ks, refs[: len(ks)])), refs[len(ks) : count]
    result, coarse, *coarse_half = refs[count:-6]
    relay, refined, forcing, state, sums, final = refs[-6:]
    fields, _, rows, columns = result.shape
    level, levels = pl.program_id(0), pl.num_programs(0)
    channels = fields * levels
    span_rows, span_columns = rows // 3, columns // 3
    height, width = rows + 8, columns + LANES
    tiles = width // LANES
    relay_rows = span_rows + 2
    total = relay_rows * channels
    offset = anchor[1] - lax.axis_size("gy") // 2 * columns
    kind = lax.rem(lax.axis_index("gy"), 3)
    edge = columns - offset - span_columns * kind

    @pl.when(level == 0)
    def _():
        arrived, rims = {}, {}
        for k in ks:
            value = received[k][...]
            side = half[1] if half and half[0] == k else 0
            if half and half[0] == k:
                value = unpacked_half(value, side)
            rim = value[total : total + relay_rows]
            if side == 1:
                rim = pltpu.roll(rim, LANES // 2, 1)
            if k in selves:
                itself = lax.axis_index("gy") == selves[k]
                own = messages[k % 3][...]
                value = jnp.where(itself, own, value)
                rim = jnp.where(itself, own[total : total + relay_rows], rim)
            arrived[k], rims[k] = value, rim

        def chosen(values):
            low, high = values.get(2, values[0]), values.get(-1, values[0])
            low = jnp.where(kind == 1, values.get(1, values[0]), low)
            low = jnp.where(kind == 0, values[0], low)
            return low, jnp.where(kind == 1, values.get(-2, values[0]), high)

        lower, upper = chosen(arrived)
        rim_low, rim_high = chosen(rims)
        lanes = lane_index(lower.shape[0])
        relay[:, 0:LANES] = jnp.where(lanes < edge, lower, upper)
        relay[total:, LANES:] = jnp.zeros((relay.shape[0] - total, LANES), F32)
        odd = (lane_index(relay_rows) & 1) == 1
        rim = jnp.where(jnp.where(odd, LANES, -1) < edge, rim_low, rim_high)
        for ch in range(channels):
            sides = pltpu.roll(rim, (LANES - 2 * ch) % LANES, 1)
            relay[span_rows * ch : span_rows * (ch + 1), LANES:] = sides[0:span_rows]
            for side in (span_rows, span_rows + 1):
                here = side * channels + ch
                relay[here : here + 1, LANES:] = sides[side : side + 1]
        refined[...] = exact_dot(relay[...], spread[...])

    relay_row = row_index(span_rows, width)
    for field in range(fields):
        ch = level * fields + field
        centre = refined[pl.ds(pl.multiple_of(span_rows * ch, 8), span_rows), :]
        above = refined[pl.ds(span_rows * channels + ch, 1), :]
        below = refined[pl.ds((span_rows + 1) * channels + ch, 1), :]
        before = jnp.where(relay_row == 0, above, pltpu.roll(centre, 1, 0))
        after = jnp.where(
            relay_row == span_rows - 1, below, pltpu.roll(centre, span_rows - 1, 0)
        )
        thirds = (before + 2.0 * centre, 3.0 * centre, 2.0 * centre + after)
        rims = (
            (rows, centre[span_rows - 1 :] + 2.0 * below),
            (rows + 1, 3.0 * below),
            (height - 2, 3.0 * above),
            (height - 1, 2.0 * above + centre[0:1]),
        )
        for tile in range(tiles):
            part = slice(LANES * tile, LANES * (tile + 1))
            for at, value in enumerate(thirds):
                forcing[field, tile, pl.ds(at, span_rows, stride=3), :] = value[:, part]
            forcing[field, tile, rows + 2 : height - 2, :] = jnp.zeros((4, LANES), F32)
            for at, value in rims:
                forcing[field, tile, at : at + 1, :] = value[:, part]
    for field in range(fields):
        for tile in range(tiles):
            part = slice(LANES * tile, LANES * (tile + 1))
            pull = weights[:, part] * forcing[field, tile]
            forcing[field, tile] = pull
            state[field, :, part] = moved[0, field, :, part] + pull
    for step in range(SUBSTEPS - 1):
        for field in range(fields):
            pull = jnp.concatenate([forcing[field, tile] for tile in range(tiles)], axis=1)
            value = pull + stencil(state[field], [coefs[0, slot] for slot in range(5)])
            if step < SUBSTEPS - 2:
                state[field] = value
            else:
                result[field, 0] = value[0:rows, 0:columns]
                for tile in range(tiles - 1):
                    final[field, tile] = value[0:rows, LANES * tile : LANES * (tile + 1)]
    for field in range(fields):
        for tile in range(tiles - 1):
            part = slice(LANES * tile, LANES * (tile + 1))
            sums[span_rows * field : span_rows * (field + 1), part] = (
                final[field, tile, pl.ds(0, span_rows, stride=3), :]
                + final[field, tile, pl.ds(1, span_rows, stride=3), :]
                + final[field, tile, pl.ds(2, span_rows, stride=3), :]
            )
    means = exact_dot(sums[...], gather[...]) / 9.0
    coarse[...] = means
    if half:
        coarse_half[0][...] = packed_half(means, half[1])


def column_select_kernel(ks, half, selves, columns, levels, anchor, coarse, *refs):
    returned, placed = refs[:-1], refs[-1]
    offset = anchor[1] - lax.axis_size("gy") // 2 * columns
    size = placed.shape[0] // levels
    lanes = lane_index(size)
    for level in range(levels):
        rows = slice(size * level, size * (level + 1))
        arrived = {}
        for k, ref in zip(ks, returned):
            if half and half[0] == k:
                value = ref[size // 2 * level : size // 2 * (level + 1), :]
                value = unpacked_half(value, half[1])
            else:
                value = ref[rows, :]
            if k in selves:
                value = jnp.where(lax.axis_index("gy") == selves[k], coarse[rows, :], value)
            arrived[k] = value
        placed[rows, 0:LANES] = arrived[0]
        for tile in (1, 2):
            own = arrived.get(tile, arrived.get(tile - 3))
            other = arrived.get(tile - 3, own)
            inside = lanes < columns - offset - LANES * tile
            placed[rows, LANES * tile : LANES * (tile + 1)] = jnp.where(inside, own, other)


def merge_kernel(entries, anchor, parent_next, *refs):
    merged = refs[-1]
    fields, _, rows, columns = parent_next.shape
    span = rows // 3
    rank_x, rank_y = lax.axis_index("gx"), lax.axis_index("gy")
    size_x, size_y = lax.axis_size("gx"), lax.axis_size("gy")
    offset = anchor[1] - size_y // 2 * columns
    shift = lax.rem(offset + columns, columns)
    row = rank_x * rows + row_index(rows, columns) - anchor[0]
    column = rank_y * columns + lane_index(rows, columns) - anchor[1]
    covered = (
        (row >= 0) & (row < size_x * span) & (column >= 0) & (column < size_y * (columns // 3))
    )
    first = anchor[0] - (rows - span) * rank_x
    row_shift = lax.rem(first + size_x * rows, rows)
    slab_row = row_index(span)
    choices = [[], [], []]
    for at, receivers in enumerate(entries):
        for d, ranks in receivers:
            place = first + span * d + slab_row
            if ranks is not None:
                place = jnp.where(among(rank_x, ranks), place, -1)
            choices[d % 3].append((at, (place >= 0) & (place < rows)))
    for field in range(fields):
        tiles = []
        for tile in range(3):
            kinds = []
            for options in choices:
                value = jnp.zeros((span, LANES), F32)
                for at, inside in options:
                    part = slice(LANES * tile, LANES * (tile + 1))
                    cells = refs[at][span * field : span * (field + 1), part]
                    value = jnp.where(inside, cells, value)
                kinds.append(value)
            tiles.append(jnp.concatenate(kinds, axis=0))
        moved = pltpu.roll(jnp.concatenate(tiles, axis=1), row_shift, 0)
        fed_back = pltpu.roll(moved, shift, 1)
        merged[field, 0] = jnp.where(covered, fed_back, parent_next[field, 0])


def spread_matrix(columns):
    span = columns // 3
    matrix = np.zeros((2 * LANES, columns + LANES), np.float32)

    def source(m):
        return LANES if m < 0 else (LANES + 1 if m >= span else m)

    for c in range(-2, columns + 2):
        m, j = divmod(c, 3)
        at = c % (columns + LANES)
        if j == 0:
            matrix[source(m - 1), at] += 1.0
            matrix[source(m), at] += 2.0
        elif j == 1:
            matrix[source(m), at] += 3.0
        else:
            matrix[source(m), at] += 2.0
            matrix[source(m + 1), at] += 1.0
    return jnp.asarray(matrix, jnp.bfloat16)


def gather_matrix(columns):
    matrix = np.zeros((columns, columns // 3), np.float32)
    matrix[np.arange(columns), np.arange(columns) // 3] = 1.0
    return jnp.asarray(matrix, jnp.bfloat16)


def coloured(pairs):
    degree = max(sum(pair[end] == at for pair in pairs) for end in (0, 1) for at, _ in enumerate(pairs + [0, 0]))
    routes = [[] for _ in range(degree)]

    def free(route, end, at):
        return all(pair[end] != at for pair in routes[route])

    for pair in pairs:
        first = next(route for route in range(degree) if free(route, 0, pair[0]))
        second = next(route for route in range(degree) if free(route, 1, pair[1]))
        if not free(first, 1, pair[1]):
            end, at, route, other = 1, pair[1], first, second
            path = []
            while not free(route, end, at):
                step = next(p for p in routes[route] if p[end] == at)
                path.append((step, route, other))
                end, at, route, other = 1 - end, step[1 - end], other, route
            for step, source, _ in path:
                routes[source].remove(step)
            for step, _, target in path:
                routes[target].append(step)
        routes[first].append(pair)
    return [sorted(route) for route in routes]


def row_routes(size, rows):
    span = rows // 3

    def needed(start):
        pairs = set()
        for nest in range(size):
            for at in (start + span * nest, start + span * nest + span + 1):
                pairs.add((at // rows, nest))
        return {(owner, nest) for owner, nest in pairs if owner != nest}

    def cost(pairs):
        cuts = [
            sum((a < cut <= n) if up else (n < cut <= a) for a, n in pairs)
            for cut in range(2, size, 2)
            for up in (False, True)
        ]
        return 4 * max(cuts) + len(coloured(sorted(pairs)))

    ranges = []
    pending = None
    for first in range(0, size * (rows - span) - 2, span):
        last = min(first + span, size * (rows - span) - 2) - 1
        pairs = set().union(*(needed(start) for start in range(first, last)))
        start, extra = first, needed(last)
        if pending is not None:
            before, more = ranges[-1][1], pending
            if cost(before | more) + cost(pairs) <= cost(before) + cost(pairs | more):
                ranges[-1] = (ranges[-1][0], before | more)
            else:
                start, pairs = first - 1, pairs | more
        ranges.append((start + 1, pairs))
        pending = extra
    ranges[-1] = (ranges[-1][0], ranges[-1][1] | pending)
    return [(first, coloured(sorted(pairs))) for first, pairs in ranges]


def column_routes(size):
    routes, selves = {}, {}
    for k in (0, 1, -2, 2, -1):
        pairs = [(size // 2 + p, 3 * p + k) for p in range(size - size // 2)]
        routes[k] = [(s, n) for s, n in pairs if 0 <= n < size and n != s]
        selves.update({k: s for s, n in pairs if n == s})
    return routes, selves


column_cases = (
    (1, (0, 1, 2, -1), (-1, 1)),
    (65, (0, 1, 2, -1), (2, 0)),
    (128, (0, 1, 2, -1, -2), None),
    (129, (0, 1, -1, -2), (-2, 1)),
    (193, (0, 1, -1, -2), (1, 0)),
)


def per_device(
    parent_fields,
    parent_velocity,
    parent_mixing,
    nest_fields,
    nest_velocity,
    nest_mixing,
    nest_anchor,
):
    fields, levels, rows, columns = shape = parent_fields.shape
    channels = fields * levels
    span, last = rows // 3, columns // LANES - 1
    gx, gy = lax.axis_size("gx"), lax.axis_size("gy")
    height, width = rows + 8, columns + LANES
    pf = parent_fields.reshape(channels, rows, columns)
    nf = nest_fields.reshape(channels, rows, columns)
    nv = nest_velocity.reshape(2 * levels, rows, columns)
    nm = nest_mixing
    def row_blocks(array):
        size = (array.shape[0], 8, columns)
        return [(array, block(size, (0, 0, 0))), (array, block(size, (0, rows // 8 - 1, 0)))]

    def column_blocks(array):
        size = (array.shape[0], rows, LANES)
        return [(array, block(size, (0, 0, 0))), (array, block(size, (0, 0, last)))]

    def shaped(*size):
        return size, block(size, (0,) * len(size))

    def whole_of(arrays):
        return [(array, whole(array)) for array in arrays]

    halo_rows = 4 * channels + 6 * levels
    ranges = row_routes(gx, rows)
    middle = gy // 2 * columns
    firsts = ([first for first, _ in ranges], [middle + first for first, _, _ in column_cases])
    scalar = pl.BlockSpec(memory_space=pltpu.SMEM)
    anchor = (nest_anchor, scalar)
    row_pair, row_other, col_pair, col_other, row_range, column_case = call(
        functools.partial(pack_kernel, firsts),
        1,
        [anchor]
        + row_blocks(pf)
        + column_blocks(pf)
        + row_blocks(nf)
        + row_blocks(nv)
        + row_blocks(nm),
        [shaped(halo_rows, columns)] * 2
        + [shaped(rows, LANES)] * 2
        + [((1,), scalar, jnp.int32)] * 2,
    )
    row_halos = swapped("gx", row_pair, row_other)
    col_halos = swapped("gy", col_pair, col_other)

    slots = max(len(routes) for _, routes in ranges)
    table = np.zeros((len(ranges), gx, slots), np.int32)
    for at, (_, routes) in enumerate(ranges):
        for slot, route in enumerate(routes):
            for owner, nest in route:
                table[at, owner, slot] = (nest - owner) % 3
    message_rows = -(-((span + 2) * (channels + 1)) // 16) * 16
    columns_of, selves = column_routes(gy)
    cells_rows, relay_height = span * channels, (span + 2) * channels

    def by_shift(route, receiver):
        shifts = sorted({nest - owner for owner, nest in route})
        return [(d, [pair[receiver] for pair in route if pair[1] - pair[0] == d]) for d in shifts]

    parent_next, *slabs = call(
        functools.partial(parent_kernel, gx),
        levels,
        [
            anchor,
            (row_range, scalar),
            (jnp.asarray(table.reshape(-1)), scalar),
            (parent_fields, by_level(shape, 1)),
            (parent_velocity, by_level(parent_velocity.shape, 1)),
            (parent_mixing, by_level(parent_mixing.shape, 0)),
        ]
        + whole_of([*row_halos, *col_halos]),
        [(shape, by_level(shape, 1))] + [shaped(relay_height, columns)] * (slots + 1),
    )

    def relay_rows(routes):
        def branch(nest_anchor, slabs, nf, nv, nm, row_halos):
            received = [lax.ppermute(slab, "gx", route) for slab, route in zip(slabs[1:], routes)]
            to_pair, to_other = call(
                column_pack_kernel,
                1,
                column_blocks(nf) + column_blocks(nv) + column_blocks(nm) + whole_of(row_halos),
                [shaped(height, LANES)] * 2,
            )
            sides = swapped("gy", to_pair, to_other)
            entries = [None] + [by_shift(route, 1) for route in routes]
            messages = call(
                functools.partial(row_select_kernel, entries, rows, channels),
                1,
                [(nest_anchor, scalar)] + whole_of([slabs[0], *received]),
                [shaped(message_rows, LANES)] * 3 + [shaped(message_rows // 2, LANES)],
            )
            return messages, sides

        return branch

    messages, sides = lax.switch(
        row_range[0],
        [relay_rows(routes) for _, routes in ranges],
        nest_anchor,
        slabs,
        nf,
        nv,
        nm,
        row_halos,
    )

    def nest_part(ks, half):
        def branch(nest_anchor, messages, nest_fields, nest_velocity, nest_mixing, halos):
            anchor = (nest_anchor, scalar)
            packed = half[0] if half else None
            received = [
                lax.ppermute(messages[3 if k == packed else k % 3], "gy", columns_of[k]) for k in ks
            ]
            coefs, moved, weights = call(
                nest_start_kernel,
                levels,
                [
                    (nest_fields, by_level(shape, 1)),
                    (nest_velocity, by_level(nest_velocity.shape, 1)),
                    (nest_mixing, by_level(nest_mixing.shape, 0)),
                ]
                + whole_of(halos),
                [
                    ((levels, 5, height, width), by_level((levels, 5, height, width), 0)),
                    ((levels, fields, height, width), by_level((levels, fields, height, width), 0)),
                    shaped(height, width),
                ],
                scratch=[(fields + 3, height, width)],
            )
            size = cells_rows // levels

            def strip(rows):
                return (rows * levels, LANES), pl.BlockSpec((rows, LANES), lambda level: (level, 0))

            nest_result, coarse, *coarse_half = call(
                functools.partial(nest_kernel, ks, half, selves),
                levels,
                [anchor]
                + whole_of([spread_matrix(columns), gather_matrix(columns)])
                + [(coefs, by_level(coefs.shape, 0)), (moved, by_level(moved.shape, 0))]
                + whole_of([weights, *received, *messages[:3]]),
                [(shape, by_level(shape, 1)), strip(size)] + ([strip(size // 2)] if half else []),
                scratch=[
                    (message_rows, 2 * LANES),
                    (message_rows, width),
                    (fields, width // LANES, height, LANES),
                    (fields, height, width),
                    (span * fields, columns),
                    (fields, columns // LANES, rows, LANES),
                ],
            )
            back = [k for k in (-1, 1, -2, 2, 0) if k in ks]
            returned = [
                lax.ppermute(
                    coarse_half[0] if k == packed else coarse,
                    "gy",
                    [pair[::-1] for pair in columns_of[k]],
                )
                for k in back
            ]
            placed = call(
                functools.partial(column_select_kernel, back, half, selves, columns, levels),
                1,
                [anchor] + whole_of([coarse, *returned]),
                [shaped(cells_rows, columns)],
            )[0]
            return nest_result, placed

        return branch

    nest_result, placed = lax.switch(
        column_case[0],
        [nest_part(ks, half) for _, ks, half in column_cases],
        nest_anchor,
        messages,
        nest_fields,
        nest_velocity,
        nest_mixing,
        [*row_halos, *sides],
    )

    def feedback_rows(routes):
        def branch(nest_anchor, parent_next, placed):
            received = [
                lax.ppermute(placed, "gx", [pair[::-1] for pair in route]) for route in routes
            ]
            entries = [[(0, None)]] + [by_shift(route, 0) for route in routes]
            slab_block = pl.BlockSpec((span * fields, columns), lambda level: (level, 0))
            return call(
                functools.partial(merge_kernel, entries),
                levels,
                [
                    (nest_anchor, pl.BlockSpec(memory_space=pltpu.SMEM)),
                    (parent_next, by_level(shape, 1)),
                ]
                + [(array, slab_block) for array in (placed, *received)],
                [(shape, by_level(shape, 1))],
            )[0]

        return branch

    merged = lax.switch(
        row_range[0], [feedback_rows(routes) for _, routes in ranges], nest_anchor, parent_next, placed
    )
    return merged, nest_result


def solution(mesh):
    placed = (
        P(None, None, "gx", "gy"),
        P(None, None, "gx", "gy"),
        P(None, "gx", "gy"),
        P(None, None, "gx", "gy"),
        P(None, None, "gx", "gy"),
        P(None, "gx", "gy"),
        P(),
    )
    return jax.shard_map(
        per_device,
        mesh=mesh,
        in_specs=placed,
        out_specs=(P(None, None, "gx", "gy"), P(None, None, "gx", "gy")),
        check_vma=False,
    )
```

```python
import functools

import jax
import jax.numpy as jnp
import numpy as np
from jax import lax
from jax.experimental import pallas as pl
from jax.experimental.pallas import tpu as pltpu
from jax.sharding import PartitionSpec as P

SUBSTEPS = 3
F32 = jnp.float32
LANES = 128
VMEM_LIMIT = 16 * 1024 * 1024
nudge_floor = 0.1
relax_width = 4.0


def whole(array):
    return pl.BlockSpec(array.shape, lambda level: (0,) * array.ndim)


def block(shape, at):
    return pl.BlockSpec(shape, lambda level: at)


def by_level(shape, dim):
    sizes = tuple(1 if i == dim else n for i, n in enumerate(shape))
    return pl.BlockSpec(sizes, lambda level: tuple(level if i == dim else 0 for i in range(len(shape))))


def call(body, grid, ins, outs, scratch=(), cost=None):
    return pl.pallas_call(
        body,
        grid=(grid,),
        out_shape=[
            pltpu.HBM(out[0], F32) if out[2:] == (pltpu.HBM,) else jax.ShapeDtypeStruct(out[0], *(out[2:] or (F32,)))
            for out in outs
        ],
        in_specs=[spec for _, spec in ins],
        out_specs=[out[1] for out in outs],
        scratch_shapes=[pltpu.VMEM(shape, F32) for shape in scratch],
        cost_estimate=cost,
        compiler_params=pltpu.CompilerParams(vmem_limit_bytes=VMEM_LIMIT),
    )(*[array for array, _ in ins])


def lane_index(rows, lanes=LANES):
    return lax.broadcasted_iota(jnp.int32, (rows, lanes), 1)


def row_index(rows, lanes=LANES):
    return lax.broadcasted_iota(jnp.int32, (rows, lanes), 0)


def among(value, numbers):
    found = False
    for number in numbers:
        found = found | (value == number)
    return found


def swapped(axis, to_pair, to_other):
    count = lax.axis_size(axis)
    pairs = [(at, at ^ 1) for at in range(count)]
    others = [(at, at + 1 if at % 2 else at - 1) for at in range(1, count - 1)]
    return lax.ppermute(to_pair, axis, pairs), lax.ppermute(to_other, axis, others)


def by_side(axis, from_pair, from_other):
    even = lax.rem(lax.axis_index(axis), 2) == 0
    return jnp.where(even, from_other, from_pair), jnp.where(even, from_pair, from_other)


def pack_kernel(firsts, anchor, pf_head, pf_tail, pf_first, pf_last, nf_head, nf_tail, nv_head, nv_tail, nm_head, nm_tail, *outs):
    to_pair, to_other, col_to_pair, col_to_other, *indices = outs
    channels, rows = pf_first.shape[:2]
    for at, (index, limits) in enumerate(zip(indices, firsts)):
        index[0] = sum((anchor[at] >= first).astype(jnp.int32) for first in limits[1:])
    coefs = nv_head.shape[0] + nm_head.shape[0]
    even = lax.rem(lax.axis_index("gx"), 2) == 0

    def lines(out, parent, field, wind, mixing, at_end):
        def put(here, ref, row, count, at):
            line = 8 - count + at if at_end else at
            out[here : here + 1, :] = ref[row, line : line + 1, :]

        for at in range(3):
            for ch in range(channels):
                put(at * channels + ch, field, ch, 3, at)
        for at in range(2):
            for cc in range(coefs):
                here = 3 * channels + at * coefs + cc
                ref, row = (wind, cc) if cc < wind.shape[0] else (mixing, cc - wind.shape[0])
                put(here, ref, row, 2, at)
        for ch in range(channels):
            put(3 * channels + 2 * coefs + ch, parent, ch, 1, 0)

    heads, tails = (pf_head, nf_head, nv_head, nm_head), (pf_tail, nf_tail, nv_tail, nm_tail)

    @pl.when(even)
    def _():
        lines(to_pair, *tails, True)
        lines(to_other, *heads, False)

    @pl.when(jnp.logical_not(even))
    def _():
        lines(to_pair, *heads, False)
        lines(to_other, *tails, True)

    lanes = lane_index(rows)
    last = jnp.zeros((rows, LANES), F32)
    first = jnp.zeros((rows, LANES), F32)
    for ch in range(channels):
        last = jnp.where(lanes == ch, pltpu.roll(pf_last[ch], (ch + 1) % LANES, 1), last)
        first = jnp.where(lanes == ch, pltpu.roll(pf_first[ch], ch, 1), first)
    even = lax.rem(lax.axis_index("gy"), 2) == 0
    col_to_pair[...] = jnp.where(even, last, first)
    col_to_other[...] = jnp.where(even, first, last)


def column_pack_kernel(
    nf_first, nf_last, nv_first, nv_last, nm_first, nm_last, pair, other, to_pair, to_other
):
    channels, rows = nf_first.shape[:2]
    columns = pair.shape[1]
    winds = nv_first.shape[0]
    coefs = winds + nm_first.shape[0]
    height = rows + 8
    lanes, lane = lane_index(rows), lane_index(1)

    def packed(nf, nv, nm, part, moved):
        main = jnp.zeros((rows, LANES), F32)
        lines = {at: jnp.zeros((1, LANES), F32) for at in range(-3, 3)}

        def add(first, size, tile, halo_rows):
            nonlocal main
            shift = (first + (size if moved else 0)) % LANES
            inside = (lanes >= first) & (lanes < first + size)
            main = jnp.where(inside, pltpu.roll(tile, shift, 1), main)
            inside = (lane >= first) & (lane < first + size)
            for at, value in halo_rows:
                lines[at] = jnp.where(inside, pltpu.roll(value, shift, 1), lines[at])

        def halos(base, step, size, at):
            lines_of = []
            for n in range(size):
                here = base + n * step + at
                before, after = by_side("gx", pair[here : here + 1, part], other[here : here + 1, part])
                lines_of += [(n, after), (n - size, before)]
            return lines_of

        for ch in range(channels):
            add(3 * ch, 3, nf[ch], halos(0, channels, 3, ch))
        base = 3 * channels
        for cc in range(coefs):
            tile = nv[cc] if cc < winds else nm[cc - winds]
            add(base + 2 * cc, 2, tile, halos(base, coefs, 2, cc))
        blank = jnp.zeros((2, LANES), F32)
        return jnp.concatenate([main, lines[0], lines[1], lines[2], blank, lines[-3], lines[-2], lines[-1]], axis=0)

    last = packed(nf_last, nv_last, nm_last, slice(columns - LANES, columns), True)
    first = packed(nf_first, nv_first, nm_first, slice(0, LANES), False)
    even = lax.rem(lax.axis_index("gy"), 2) == 0
    to_pair[...] = jnp.where(even, last, first)
    to_other[...] = jnp.where(even, first, last)


def parent_kernel(size_x, anchor, index, table, pf, pv, pm, col_other, row_other, col_pair, row_pair, parent_next, *slabs):
    fields, _, rows, columns = pf.shape
    level, levels = pl.program_id(0), pl.num_programs(0)
    channels = fields * levels
    span = rows // 3
    rank = lax.axis_index("gx")
    half = lax.axis_size("gy") // 2 * columns
    base = 3 * channels + 2 * 3 * levels
    shift = lax.rem(2 * columns - anchor[1] + half, columns)
    row_shift = lax.rem((rows - span) * rank + size_x * rows - anchor[0], rows)
    row = row_index(rows, columns)
    column = lane_index(rows, columns)
    place = (index[0] * size_x + rank) * (len(slabs) - 1)
    kinds = [table[place + slot] for slot in range(len(slabs) - 1)]
    u, v, k = pv[0, 0], pv[1, 0], pm[0]
    a_w = jnp.maximum(u, 0.0) + k
    a_e = k - jnp.minimum(u, 0.0)
    a_s = jnp.maximum(v, 0.0) + k
    a_n = k - jnp.minimum(v, 0.0)
    a_c = 1.0 - (a_w + a_e + a_s + a_n)
    pad = jnp.zeros((rows, columns - LANES), F32)
    left, right = by_side("gy", col_pair[...], col_other[...])

    def rows_by_slab(value):
        thirds = [
            (
                value[span * kind : span * (kind + 1)],
                value[(span * kind - 1) % rows : (span * kind - 1) % rows + 1],
                value[span * (kind + 1) % rows : span * (kind + 1) % rows + 1],
            )
            for kind in range(3)
        ]
        yield thirds[0]
        for kind in kinds:
            yield [
                jnp.where(kind == 0, zero, jnp.where(kind == 1, one, two))
                for zero, one, two in zip(*thirds)
            ]

    for field in range(fields):
        ch = field * levels + level
        q = pf[field, 0]
        source = pl.ds(base + ch, 1)
        above, below = by_side("gx", row_pair[source, :], row_other[source, :])
        west = jnp.where(row == 0, above, pltpu.roll(q, 1, 0))
        east = jnp.where(row == rows - 1, below, pltpu.roll(q, rows - 1, 0))
        at_first = pltpu.roll(left, LANES - ch, 1)
        at_last = pltpu.roll(right, LANES - 1 - ch, 1)
        south = jnp.where(
            column == 0, jnp.concatenate([at_first, pad], axis=1), pltpu.roll(q, 1, 1)
        )
        north = jnp.where(
            column == columns - 1,
            jnp.concatenate([pad, at_last], axis=1),
            pltpu.roll(q, columns - 1, 1),
        )
        result = a_c * q + a_w * west + a_e * east + a_s * south + a_n * north
        parent_next[field, 0] = result
        moved = pltpu.roll(pltpu.roll(result, shift, 1), row_shift, 0)
        here = level * fields + field
        for slab, (cells, before, after) in zip(slabs, rows_by_slab(moved)):
            slab[pl.ds(pl.multiple_of(span * here, 8), span), :] = cells
            slab[pl.ds(span * channels + here, 1), :] = before
            slab[pl.ds((span + 1) * channels + here, 1), :] = after


def packed_half(value, side):
    rows = value.shape[0] // 2
    first, second = value[:rows], value[rows:]
    left = lane_index(rows) < LANES // 2
    if side == 0:
        return jnp.where(left, first, pltpu.roll(second, LANES // 2, 1))
    return jnp.where(left, pltpu.roll(first, LANES // 2, 1), second)


def unpacked_half(value, side):
    turned = pltpu.roll(value, LANES // 2, 1)
    return jnp.concatenate([value, turned] if side == 0 else [turned, value], axis=0)


def row_select_kernel(entries, rows, channels, anchor, *refs):
    count = len(entries)
    slabs, messages, half = refs[:count], refs[count:-1], refs[-1]
    span = rows // 3
    columns = slabs[0].shape[1]
    rank = lax.axis_index("gx")
    start = anchor[0] + span * rank
    lowest, highest = lax.div(start, rows), lax.div(start + span - 1, rows)
    above, below = lax.div(start - 1, rows), lax.div(start + span, rows)
    split = jnp.where(highest > lowest, rows * highest - start, span)
    cells, total = span * channels, (span + 2) * channels

    def pick(owner, first, size, part):
        value = slabs[0][first : first + size, part]
        for senders, slab in zip(entries[1:], slabs[1:]):
            chosen = False
            for d, ranks in senders:
                chosen = chosen | ((rank - owner == d) & among(rank, ranks))
            value = jnp.where(chosen, slab[first : first + size, part], value)
        return value

    tiles, sides = [], []
    for tile in range(3):
        part = slice(LANES * tile, LANES * (tile + 1))
        row = row_index(cells) & (span - 1)
        low, high = pick(lowest, 0, cells, part), pick(highest, 0, cells, part)
        tiles.append(jnp.where(row < split, low, high))
        sides.append([pick(above, cells, channels, part), pick(below, cells + channels, channels, part)])
    lanes, edge_lanes = lane_index(span), lane_index(channels)
    edge_inside = lax.div(edge_lanes, 2) == row_index(channels)

    def beside(parts, tile, lane):
        return jnp.where(lane == LANES - 1, parts[(tile + 2) % 3], parts[(tile + 1) % 3])

    for tile, message in enumerate(messages):
        message[0:cells, :] = tiles[tile]
        rim = jnp.zeros((span, LANES), F32)
        for ch in range(channels):
            here = [value[span * ch : span * (ch + 1)] for value in tiles]
            turned = pltpu.roll(beside(here, tile, lanes), 2 * ch + 1, 1)
            rim = jnp.where((lanes == 2 * ch) | (lanes == 2 * ch + 1), turned, rim)
        message[total : total + span, :] = rim + pltpu.roll(rim, LANES // 2, 1)
        for side in range(2):
            first = cells + side * channels
            message[first : first + channels, :] = sides[tile][side]
            line = beside([value[side] for value in sides], tile, edge_lanes)
            line = pltpu.roll(line, 1, 1, stride=2, stride_axis=0)
            line = jnp.sum(jnp.where(edge_inside, line, 0.0), axis=0, keepdims=True)
            target = total + span + side
            message[target : target + 1, :] = line + pltpu.roll(line, LANES // 2, 1)
        message[total + span + 2 :, :] = jnp.zeros((message.shape[0] - total - span - 2, LANES), F32)
    offset = anchor[1] - lax.axis_size("gy") // 2 * columns
    split_tile = jnp.where(offset < LANES, messages[2][...], messages[1][...])
    right = ((offset <= LANES // 2) | (offset > LANES)) & (offset <= LANES + LANES // 2)
    half[...] = jnp.where(right, packed_half(split_tile, 1), packed_half(split_tile, 0))


def three_parts(x):
    high = x.astype(jnp.bfloat16)
    rest = x - high.astype(F32)
    middle = rest.astype(jnp.bfloat16)
    low = (rest - middle.astype(F32)).astype(jnp.bfloat16)
    return high, middle, low


def exact_dot(x, matrix):
    parts = three_parts(x)
    total = jnp.dot(parts[2], matrix, preferred_element_type=F32)
    total = total + jnp.dot(parts[1], matrix, preferred_element_type=F32)
    return total + jnp.dot(parts[0], matrix, preferred_element_type=F32)


def stencil(q, coefs):
    height, width = q.shape
    return (
        coefs[0] * q
        + coefs[1] * pltpu.roll(q, 1, 0)
        + coefs[2] * pltpu.roll(q, height - 1, 0)
        + coefs[3] * pltpu.roll(q, 1, 1)
        + coefs[4] * pltpu.roll(q, width - 1, 1)
    )


def nest_start_kernel(nf, nv, nm, row_pair, row_other, col_pair, col_other, coefs, moved, weights, state):
    fields, _, rows, columns = nf.shape
    level, levels = pl.program_id(0), pl.num_programs(0)
    channels = fields * levels
    height, width = rows + 8, columns + LANES
    rank_x, rank_y = lax.axis_index("gx"), lax.axis_index("gy")
    row = row_index(height, width)
    column = lane_index(height, width)
    local_row = jnp.where(row < rows + 4, row, row - height)
    local_column = jnp.where(column < columns + LANES // 2, column, column - width)
    global_row = rank_x * rows + local_row
    global_column = rank_y * columns + local_column
    row_distance = jnp.minimum(global_row, lax.axis_size("gx") * rows - 1 - global_row)
    column_distance = jnp.minimum(
        global_column, lax.axis_size("gy") * columns - 1 - global_column
    )
    distance = jnp.minimum(row_distance, column_distance)
    weight = nudge_floor + (1.0 - nudge_floor) * jnp.exp(
        jnp.maximum(distance, 0).astype(F32) / -relax_width
    )
    weight = jnp.where(distance < 0, 0.0, weight)
    keep = 1.0 - weight
    edge_lanes = lane_index(height)

    @pl.when(level == 0)
    def _():
        weights[...] = weight / 9.0
        state[...] = jnp.zeros_like(state)

    left, right = by_side("gy", col_pair[...], col_other[...])

    def side_tile(first, size):
        after = pltpu.roll(right, lax.rem(2 * LANES - first, LANES), 1)
        before = pltpu.roll(left, lax.rem(2 * LANES - first - size, LANES), 1)
        inside = jnp.where(edge_lanes < LANES // 2, after, before)
        outside = (edge_lanes >= size) & (edge_lanes < LANES - size)
        return jnp.where(outside, 0.0, inside)

    def fill(slot, value, base, step, at, size, first):
        state[slot, 0:rows, 0:columns] = value
        for n in range(size):
            source = pl.ds(base + n * step + at, 1)
            above, below = by_side("gx", row_pair[source, :], row_other[source, :])
            state[slot, rows + n : rows + n + 1, 0:columns] = below
            target = height - size + n
            state[slot, target : target + 1, 0:columns] = above
        state[slot, :, columns:width] = side_tile(first, size)

    base = 3 * channels
    for slot, value in enumerate((nv[0, 0], nv[1, 0], nm[0])):
        cc = slot * levels + level
        fill(slot + fields, value, base, 3 * levels, cc, 2, base + 2 * cc)
    for field in range(fields):
        ch = field * levels + level
        fill(field, nf[field, 0], 0, channels, ch, 3, 3 * ch)
    u, v, k = (state[slot + fields] for slot in range(3))
    a_w = jnp.maximum(u, 0.0) + k
    a_e = k - jnp.minimum(u, 0.0)
    a_s = jnp.maximum(v, 0.0) + k
    a_n = k - jnp.minimum(v, 0.0)
    a_c = 1.0 - (a_w + a_e + a_s + a_n)
    for slot, value in enumerate((a_c, a_w, a_e, a_s, a_n)):
        coefs[0, slot] = keep * value
    for field in range(fields):
        moved[0, field] = stencil(state[field], [coefs[0, slot] for slot in range(5)])


def nest_kernel(ks, half, selves, anchor, spread, gather, coefs, moved, weights, *refs):
    count = len(ks) + 3
    received, messages = dict(zip(ks, refs[: len(ks)])), refs[len(ks) : count]
    result, coarse, *coarse_half = refs[count:-6]
    relay, refined, forcing, state, sums, final = refs[-6:]
    fields, _, rows, columns = result.shape
    level, levels = pl.program_id(0), pl.num_programs(0)
    channels = fields * levels
    span_rows, span_columns = rows // 3, columns // 3
    height, width = rows + 8, columns + LANES
    tiles = width // LANES
    relay_rows = span_rows + 2
    total = relay_rows * channels
    offset = anchor[1] - lax.axis_size("gy") // 2 * columns
    kind = lax.rem(lax.axis_index("gy"), 3)
    edge = columns - offset - span_columns * kind

    @pl.when(level == 0)
    def _():
        arrived, rims = {}, {}
        for k in ks:
            value = received[k][...]
            side = half[1] if half and half[0] == k else 0
            if half and half[0] == k:
                value = unpacked_half(value, side)
            rim = value[total : total + relay_rows]
            if side == 1:
                rim = pltpu.roll(rim, LANES // 2, 1)
            if k in selves:
                itself = lax.axis_index("gy") == selves[k]
                own = messages[k % 3][...]
                value = jnp.where(itself, own, value)
                rim = jnp.where(itself, own[total : total + relay_rows], rim)
            arrived[k], rims[k] = value, rim

        def chosen(values):
            low, high = values.get(2, values[0]), values.get(-1, values[0])
            low = jnp.where(kind == 1, values.get(1, values[0]), low)
            low = jnp.where(kind == 0, values[0], low)
            return low, jnp.where(kind == 1, values.get(-2, values[0]), high)

        lower, upper = chosen(arrived)
        rim_low, rim_high = chosen(rims)
        lanes = lane_index(lower.shape[0])
        relay[:, 0:LANES] = jnp.where(lanes < edge, lower, upper)
        relay[total:, LANES:] = jnp.zeros((relay.shape[0] - total, LANES), F32)
        odd = (lane_index(relay_rows) & 1) == 1
        rim = jnp.where(jnp.where(odd, LANES, -1) < edge, rim_low, rim_high)
        for ch in range(channels):
            sides = pltpu.roll(rim, (LANES - 2 * ch) % LANES, 1)
            relay[span_rows * ch : span_rows * (ch + 1), LANES:] = sides[0:span_rows]
            for side in (span_rows, span_rows + 1):
                here = side * channels + ch
                relay[here : here + 1, LANES:] = sides[side : side + 1]
        refined[...] = exact_dot(relay[...], spread[...])

    relay_row = row_index(span_rows, width)
    for field in range(fields):
        ch = level * fields + field
        centre = refined[pl.ds(pl.multiple_of(span_rows * ch, 8), span_rows), :]
        above = refined[pl.ds(span_rows * channels + ch, 1), :]
        below = refined[pl.ds((span_rows + 1) * channels + ch, 1), :]
        before = jnp.where(relay_row == 0, above, pltpu.roll(centre, 1, 0))
        after = jnp.where(
            relay_row == span_rows - 1, below, pltpu.roll(centre, span_rows - 1, 0)
        )
        thirds = (before + 2.0 * centre, 3.0 * centre, 2.0 * centre + after)
        rims = (
            (rows, centre[span_rows - 1 :] + 2.0 * below),
            (rows + 1, 3.0 * below),
            (height - 2, 3.0 * above),
            (height - 1, 2.0 * above + centre[0:1]),
        )
        for tile in range(tiles):
            part = slice(LANES * tile, LANES * (tile + 1))
            for at, value in enumerate(thirds):
                forcing[field, tile, pl.ds(at, span_rows, stride=3), :] = value[:, part]
            forcing[field, tile, rows + 2 : height - 2, :] = jnp.zeros((4, LANES), F32)
            for at, value in rims:
                forcing[field, tile, at : at + 1, :] = value[:, part]
    for field in range(fields):
        for tile in range(tiles):
            part = slice(LANES * tile, LANES * (tile + 1))
            pull = weights[:, part] * forcing[field, tile]
            forcing[field, tile] = pull
            state[field, :, part] = moved[0, field, :, part] + pull
    for step in range(SUBSTEPS - 1):
        for field in range(fields):
            pull = jnp.concatenate([forcing[field, tile] for tile in range(tiles)], axis=1)
            value = pull + stencil(state[field], [coefs[0, slot] for slot in range(5)])
            if step < SUBSTEPS - 2:
                state[field] = value
            else:
                result[field, 0] = value[0:rows, 0:columns]
                for tile in range(tiles - 1):
                    final[field, tile] = value[0:rows, LANES * tile : LANES * (tile + 1)]
    for field in range(fields):
        for tile in range(tiles - 1):
            part = slice(LANES * tile, LANES * (tile + 1))
            sums[span_rows * field : span_rows * (field + 1), part] = (
                final[field, tile, pl.ds(0, span_rows, stride=3), :]
                + final[field, tile, pl.ds(1, span_rows, stride=3), :]
                + final[field, tile, pl.ds(2, span_rows, stride=3), :]
            )
    means = exact_dot(sums[...], gather[...]) / 9.0
    coarse[...] = means
    if half:
        coarse_half[0][...] = packed_half(means, half[1])


def column_select_kernel(ks, half, selves, columns, levels, anchor, coarse, *refs):
    returned, placed = refs[:-1], refs[-1]
    offset = anchor[1] - lax.axis_size("gy") // 2 * columns
    size = placed.shape[0] // levels
    lanes = lane_index(size)
    for level in range(levels):
        rows = slice(size * level, size * (level + 1))
        arrived = {}
        for k, ref in zip(ks, returned):
            if half and half[0] == k:
                value = ref[size // 2 * level : size // 2 * (level + 1), :]
                value = unpacked_half(value, half[1])
            else:
                value = ref[rows, :]
            if k in selves:
                value = jnp.where(lax.axis_index("gy") == selves[k], coarse[rows, :], value)
            arrived[k] = value
        placed[rows, 0:LANES] = arrived[0]
        for tile in (1, 2):
            own = arrived.get(tile, arrived.get(tile - 3))
            other = arrived.get(tile - 3, own)
            inside = lanes < columns - offset - LANES * tile
            placed[rows, LANES * tile : LANES * (tile + 1)] = jnp.where(inside, own, other)


def merge_kernel(entries, anchor, parent_next, *refs):
    merged = refs[-1]
    fields, _, rows, columns = parent_next.shape
    span = rows // 3
    rank_x, rank_y = lax.axis_index("gx"), lax.axis_index("gy")
    size_x, size_y = lax.axis_size("gx"), lax.axis_size("gy")
    offset = anchor[1] - size_y // 2 * columns
    shift = lax.rem(offset + columns, columns)
    row = rank_x * rows + row_index(rows, columns) - anchor[0]
    column = rank_y * columns + lane_index(rows, columns) - anchor[1]
    covered = (
        (row >= 0) & (row < size_x * span) & (column >= 0) & (column < size_y * (columns // 3))
    )
    first = anchor[0] - (rows - span) * rank_x
    row_shift = lax.rem(first + size_x * rows, rows)
    slab_row = row_index(span)
    choices = [[], [], []]
    for at, receivers in enumerate(entries):
        for d, ranks in receivers:
            place = first + span * d + slab_row
            if ranks is not None:
                place = jnp.where(among(rank_x, ranks), place, -1)
            choices[d % 3].append((at, (place >= 0) & (place < rows)))
    for field in range(fields):
        tiles = []
        for tile in range(3):
            kinds = []
            for options in choices:
                value = jnp.zeros((span, LANES), F32)
                for at, inside in options:
                    part = slice(LANES * tile, LANES * (tile + 1))
                    cells = refs[at][span * field : span * (field + 1), part]
                    value = jnp.where(inside, cells, value)
                kinds.append(value)
            tiles.append(jnp.concatenate(kinds, axis=0))
        moved = pltpu.roll(jnp.concatenate(tiles, axis=1), row_shift, 0)
        fed_back = pltpu.roll(moved, shift, 1)
        merged[field, 0] = jnp.where(covered, fed_back, parent_next[field, 0])


def spread_matrix(columns):
    span = columns // 3
    matrix = np.zeros((2 * LANES, columns + LANES), np.float32)

    def source(m):
        return LANES if m < 0 else (LANES + 1 if m >= span else m)

    for c in range(-2, columns + 2):
        m, j = divmod(c, 3)
        at = c % (columns + LANES)
        if j == 0:
            matrix[source(m - 1), at] += 1.0
            matrix[source(m), at] += 2.0
        elif j == 1:
            matrix[source(m), at] += 3.0
        else:
            matrix[source(m), at] += 2.0
            matrix[source(m + 1), at] += 1.0
    return jnp.asarray(matrix, jnp.bfloat16)


def gather_matrix(columns):
    matrix = np.zeros((columns, columns // 3), np.float32)
    matrix[np.arange(columns), np.arange(columns) // 3] = 1.0
    return jnp.asarray(matrix, jnp.bfloat16)


def coloured(pairs):
    degree = max(sum(pair[end] == at for pair in pairs) for end in (0, 1) for at, _ in enumerate(pairs + [0, 0]))
    routes = [[] for _ in range(degree)]

    def free(route, end, at):
        return all(pair[end] != at for pair in routes[route])

    for pair in pairs:
        first = next(route for route in range(degree) if free(route, 0, pair[0]))
        second = next(route for route in range(degree) if free(route, 1, pair[1]))
        if not free(first, 1, pair[1]):
            end, at, route, other = 1, pair[1], first, second
            path = []
            while not free(route, end, at):
                step = next(p for p in routes[route] if p[end] == at)
                path.append((step, route, other))
                end, at, route, other = 1 - end, step[1 - end], other, route
            for step, source, _ in path:
                routes[source].remove(step)
            for step, _, target in path:
                routes[target].append(step)
        routes[first].append(pair)
    return [sorted(route) for route in routes]


def row_routes(size, rows):
    span = rows // 3

    def needed(start):
        pairs = set()
        for nest in range(size):
            for at in (start + span * nest, start + span * nest + span + 1):
                pairs.add((at // rows, nest))
        return {(owner, nest) for owner, nest in pairs if owner != nest}

    def cost(pairs):
        cuts = [
            sum((a < cut <= n) if up else (n < cut <= a) for a, n in pairs)
            for cut in range(2, size, 2)
            for up in (False, True)
        ]
        return 4 * max(cuts) + len(coloured(sorted(pairs)))

    ranges = []
    pending = None
    for first in range(0, size * (rows - span) - 2, span):
        last = min(first + span, size * (rows - span) - 2) - 1
        pairs = set().union(*(needed(start) for start in range(first, last)))
        start, extra = first, needed(last)
        if pending is not None:
            before, more = ranges[-1][1], pending
            if cost(before | more) + cost(pairs) <= cost(before) + cost(pairs | more):
                ranges[-1] = (ranges[-1][0], before | more)
            else:
                start, pairs = first - 1, pairs | more
        ranges.append((start + 1, pairs))
        pending = extra
    ranges[-1] = (ranges[-1][0], ranges[-1][1] | pending)
    return [(first, coloured(sorted(pairs))) for first, pairs in ranges]


def column_routes(size):
    routes, selves = {}, {}
    for k in (0, 1, -2, 2, -1):
        pairs = [(size // 2 + p, 3 * p + k) for p in range(size - size // 2)]
        routes[k] = [(s, n) for s, n in pairs if 0 <= n < size and n != s]
        selves.update({k: s for s, n in pairs if n == s})
    return routes, selves


column_cases = (
    (1, (0, 1, 2, -1), (-1, 1)),
    (65, (0, 1, 2, -1), (2, 0)),
    (128, (0, 1, 2, -1, -2), None),
    (129, (0, 1, -1, -2), (-2, 1)),
    (193, (0, 1, -1, -2), (1, 0)),
)


def per_device(
    parent_fields,
    parent_velocity,
    parent_mixing,
    nest_fields,
    nest_velocity,
    nest_mixing,
    nest_anchor,
):
    fields, levels, rows, columns = shape = parent_fields.shape
    channels = fields * levels
    span, last = rows // 3, columns // LANES - 1
    gx, gy = lax.axis_size("gx"), lax.axis_size("gy")
    height, width = rows + 8, columns + LANES
    pf = parent_fields.reshape(channels, rows, columns)
    nf = nest_fields.reshape(channels, rows, columns)
    nv = nest_velocity.reshape(2 * levels, rows, columns)
    nm = nest_mixing
    def row_blocks(array):
        size = (array.shape[0], 8, columns)
        return [(array, block(size, (0, 0, 0))), (array, block(size, (0, rows // 8 - 1, 0)))]

    def column_blocks(array):
        size = (array.shape[0], rows, LANES)
        return [(array, block(size, (0, 0, 0))), (array, block(size, (0, 0, last)))]

    def shaped(*size):
        return size, block(size, (0,) * len(size))

    def whole_of(arrays):
        return [(array, whole(array)) for array in arrays]

    halo_rows = 4 * channels + 6 * levels
    ranges = row_routes(gx, rows)
    middle = gy // 2 * columns
    firsts = ([first for first, _ in ranges], [middle + first for first, _, _ in column_cases])
    scalar = pl.BlockSpec(memory_space=pltpu.SMEM)
    anchor = (nest_anchor, scalar)
    row_pair, row_other, col_pair, col_other, row_range, column_case = call(
        functools.partial(pack_kernel, firsts),
        1,
        [anchor]
        + row_blocks(pf)
        + column_blocks(pf)
        + row_blocks(nf)
        + row_blocks(nv)
        + row_blocks(nm),
        [shaped(halo_rows, columns)] * 2
        + [shaped(rows, LANES)] * 2
        + [((1,), scalar, jnp.int32)] * 2,
    )
    col_halos = swapped("gy", col_pair, col_other)
    row_halos = swapped("gx", row_pair, row_other)

    slots = max(len(routes) for _, routes in ranges)
    table = np.zeros((len(ranges), gx, slots), np.int32)
    for at, (_, routes) in enumerate(ranges):
        for slot, route in enumerate(routes):
            for owner, nest in route:
                table[at, owner, slot] = (nest - owner) % 3
    message_rows = -(-((span + 2) * (channels + 1)) // 16) * 16
    columns_of, selves = column_routes(gy)
    cells_rows, relay_height = span * channels, (span + 2) * channels

    def by_shift(route, receiver):
        shifts = sorted({nest - owner for owner, nest in route})
        return [(d, [pair[receiver] for pair in route if pair[1] - pair[0] == d]) for d in shifts]

    parent_next, *slabs = call(
        functools.partial(parent_kernel, gx),
        levels,
        [
            anchor,
            (row_range, scalar),
            (jnp.asarray(table.reshape(-1)), scalar),
            (parent_fields, by_level(shape, 1)),
            (parent_velocity, by_level(parent_velocity.shape, 1)),
            (parent_mixing, by_level(parent_mixing.shape, 0)),
        ]
        + whole_of([col_halos[1], row_halos[1], col_halos[0], row_halos[0]]),
        [(shape, by_level(shape, 1))] + [shaped(relay_height, columns)] * (slots + 1),
    )

    def relay_rows(routes):
        def branch(nest_anchor, slabs, nf, nv, nm, row_halos):
            received = [lax.ppermute(slab, "gx", route) for slab, route in zip(slabs[1:], routes)]
            to_pair, to_other = call(
                column_pack_kernel,
                1,
                column_blocks(nf) + column_blocks(nv) + column_blocks(nm) + whole_of(row_halos),
                [shaped(height, LANES)] * 2,
            )
            sides = swapped("gy", to_pair, to_other)
            entries = [None] + [by_shift(route, 1) for route in routes]
            messages = call(
                functools.partial(row_select_kernel, entries, rows, channels),
                1,
                [(nest_anchor, scalar)] + whole_of([slabs[0], *received]),
                [shaped(message_rows, LANES)] * 3 + [shaped(message_rows // 2, LANES)],
            )
            return messages, sides

        return branch

    messages, sides = lax.switch(
        row_range[0],
        [relay_rows(routes) for _, routes in ranges],
        nest_anchor,
        slabs,
        nf,
        nv,
        nm,
        row_halos,
    )

    def nest_part(ks, half):
        def branch(nest_anchor, messages, nest_fields, nest_velocity, nest_mixing, halos):
            anchor = (nest_anchor, scalar)
            packed = half[0] if half else None
            received = [
                lax.ppermute(messages[3 if k == packed else k % 3], "gy", columns_of[k]) for k in ks
            ]
            coefs, moved, weights = call(
                nest_start_kernel,
                levels,
                [
                    (nest_fields, by_level(shape, 1)),
                    (nest_velocity, by_level(nest_velocity.shape, 1)),
                    (nest_mixing, by_level(nest_mixing.shape, 0)),
                ]
                + whole_of(halos),
                [
                    ((levels, 5, height, width), by_level((levels, 5, height, width), 0)),
                    ((levels, fields, height, width), by_level((levels, fields, height, width), 0)),
                    shaped(height, width),
                ],
                scratch=[(fields + 3, height, width)],
            )
            size = cells_rows // levels

            def strip(rows):
                return (rows * levels, LANES), pl.BlockSpec((rows, LANES), lambda level: (level, 0))

            nest_result, coarse, *coarse_half = call(
                functools.partial(nest_kernel, ks, half, selves),
                levels,
                [anchor]
                + whole_of([spread_matrix(columns), gather_matrix(columns)])
                + [(coefs, by_level(coefs.shape, 0)), (moved, by_level(moved.shape, 0))]
                + whole_of([weights, *received, *messages[:3]]),
                [(shape, by_level(shape, 1)), strip(size)] + ([strip(size // 2)] if half else []),
                scratch=[
                    (message_rows, 2 * LANES),
                    (message_rows, width),
                    (fields, width // LANES, height, LANES),
                    (fields, height, width),
                    (span * fields, columns),
                    (fields, columns // LANES, rows, LANES),
                ],
            )
            back = [k for k in (-1, 1, -2, 2, 0) if k in ks]
            returned = [
                lax.ppermute(
                    coarse_half[0] if k == packed else coarse,
                    "gy",
                    [pair[::-1] for pair in columns_of[k]],
                )
                for k in back
            ]
            placed = call(
                functools.partial(column_select_kernel, back, half, selves, columns, levels),
                1,
                [anchor] + whole_of([coarse, *returned]),
                [shaped(cells_rows, columns)],
            )[0]
            return nest_result, placed

        return branch

    nest_result, placed = lax.switch(
        column_case[0],
        [nest_part(ks, half) for _, ks, half in column_cases],
        nest_anchor,
        messages,
        nest_fields,
        nest_velocity,
        nest_mixing,
        [*row_halos, *sides],
    )

    def feedback_rows(routes):
        def branch(nest_anchor, parent_next, placed):
            received = [
                lax.ppermute(placed, "gx", [pair[::-1] for pair in route]) for route in routes
            ]
            entries = [[(0, None)]] + [by_shift(route, 0) for route in routes]
            slab_block = pl.BlockSpec((span * fields, columns), lambda level: (level, 0))
            return call(
                functools.partial(merge_kernel, entries),
                levels,
                [
                    (nest_anchor, pl.BlockSpec(memory_space=pltpu.SMEM)),
                    (parent_next, by_level(shape, 1)),
                ]
                + [(array, slab_block) for array in (placed, *received)],
                [(shape, by_level(shape, 1), pltpu.HBM)],
            )[0]

        return branch

    merged = lax.switch(
        row_range[0], [feedback_rows(routes) for _, routes in ranges], nest_anchor, parent_next, placed
    )
    return merged, nest_result


def solution(mesh):
    placed = (
        P(None, None, "gx", "gy"),
        P(None, None, "gx", "gy"),
        P(None, "gx", "gy"),
        P(None, None, "gx", "gy"),
        P(None, None, "gx", "gy"),
        P(None, "gx", "gy"),
        P(),
    )
    return jax.shard_map(
        per_device,
        mesh=mesh,
        in_specs=placed,
        out_specs=(P(None, None, "gx", "gy"), P(None, None, "gx", "gy")),
        check_vma=False,
    )
```

```python
import functools

import jax
import jax.numpy as jnp
import numpy as np
from jax import lax
from jax.experimental import pallas as pl
from jax.experimental.pallas import tpu as pltpu
from jax.sharding import PartitionSpec as P

SUBSTEPS = 3
F32 = jnp.float32
LANES = 128
VMEM_LIMIT = 16 * 1024 * 1024
nudge_floor = 0.1
relax_width = 4.0


def whole(array):
    return pl.BlockSpec(array.shape, lambda level: (0,) * array.ndim)


def block(shape, at):
    return pl.BlockSpec(shape, lambda level: at)


def by_level(shape, dim):
    sizes = tuple(1 if i == dim else n for i, n in enumerate(shape))
    return pl.BlockSpec(sizes, lambda level: tuple(level if i == dim else 0 for i in range(len(shape))))


def call(body, grid, ins, outs, scratch=(), cost=None):
    return pl.pallas_call(
        body,
        grid=(grid,),
        out_shape=[
            pltpu.HBM(out[0], F32) if out[2:] == (pltpu.HBM,) else jax.ShapeDtypeStruct(out[0], *(out[2:] or (F32,)))
            for out in outs
        ],
        in_specs=[spec for _, spec in ins],
        out_specs=[out[1] for out in outs],
        scratch_shapes=[pltpu.VMEM(shape, F32) for shape in scratch],
        cost_estimate=cost,
        compiler_params=pltpu.CompilerParams(vmem_limit_bytes=VMEM_LIMIT),
    )(*[array for array, _ in ins])


def lane_index(rows, lanes=LANES):
    return lax.broadcasted_iota(jnp.int32, (rows, lanes), 1)


def row_index(rows, lanes=LANES):
    return lax.broadcasted_iota(jnp.int32, (rows, lanes), 0)


def among(value, numbers):
    found = False
    for number in numbers:
        found = found | (value == number)
    return found


def swapped(axis, to_pair, to_other):
    count = lax.axis_size(axis)
    pairs = [(at, at ^ 1) for at in range(count)]
    others = [(at, at + 1 if at % 2 else at - 1) for at in range(1, count - 1)]
    return lax.ppermute(to_pair, axis, pairs), lax.ppermute(to_other, axis, others)


def by_side(axis, from_pair, from_other):
    even = lax.rem(lax.axis_index(axis), 2) == 0
    return jnp.where(even, from_other, from_pair), jnp.where(even, from_pair, from_other)


def pack_kernel(firsts, anchor, pf_head, pf_tail, pf_first, pf_last, nf_head, nf_tail, nv_head, nv_tail, nm_head, nm_tail, *outs):
    to_pair, to_other, col_to_pair, col_to_other, *indices = outs
    channels, rows = pf_first.shape[:2]
    for at, (index, limits) in enumerate(zip(indices, firsts)):
        index[0] = sum((anchor[at] >= first).astype(jnp.int32) for first in limits[1:])
    coefs = nv_head.shape[0] + nm_head.shape[0]
    even = lax.rem(lax.axis_index("gx"), 2) == 0

    def lines(out, parent, field, wind, mixing, at_end):
        def put(here, ref, row, count, at):
            line = 8 - count + at if at_end else at
            out[here : here + 1, :] = ref[row, line : line + 1, :]

        for at in range(3):
            for ch in range(channels):
                put(at * channels + ch, field, ch, 3, at)
        for at in range(2):
            for cc in range(coefs):
                here = 3 * channels + at * coefs + cc
                ref, row = (wind, cc) if cc < wind.shape[0] else (mixing, cc - wind.shape[0])
                put(here, ref, row, 2, at)
        for ch in range(channels):
            put(3 * channels + 2 * coefs + ch, parent, ch, 1, 0)

    heads, tails = (pf_head, nf_head, nv_head, nm_head), (pf_tail, nf_tail, nv_tail, nm_tail)

    @pl.when(even)
    def _():
        lines(to_pair, *tails, True)
        lines(to_other, *heads, False)

    @pl.when(jnp.logical_not(even))
    def _():
        lines(to_pair, *heads, False)
        lines(to_other, *tails, True)

    lanes = lane_index(rows)
    last = jnp.zeros((rows, LANES), F32)
    first = jnp.zeros((rows, LANES), F32)
    for ch in range(channels):
        last = jnp.where(lanes == ch, pltpu.roll(pf_last[ch], (ch + 1) % LANES, 1), last)
        first = jnp.where(lanes == ch, pltpu.roll(pf_first[ch], ch, 1), first)
    even = lax.rem(lax.axis_index("gy"), 2) == 0
    col_to_pair[...] = jnp.where(even, last, first)
    col_to_other[...] = jnp.where(even, first, last)


def column_pack_kernel(
    nf_first, nf_last, nv_first, nv_last, nm_first, nm_last, pair, other, to_pair, to_other
):
    channels, rows = nf_first.shape[:2]
    columns = pair.shape[1]
    winds = nv_first.shape[0]
    coefs = winds + nm_first.shape[0]
    height = rows + 8
    lanes, lane = lane_index(rows), lane_index(1)

    def packed(nf, nv, nm, part, moved):
        main = jnp.zeros((rows, LANES), F32)
        lines = {at: jnp.zeros((1, LANES), F32) for at in range(-3, 3)}

        def add(first, size, tile, halo_rows):
            nonlocal main
            shift = (first + (size if moved else 0)) % LANES
            inside = (lanes >= first) & (lanes < first + size)
            main = jnp.where(inside, pltpu.roll(tile, shift, 1), main)
            inside = (lane >= first) & (lane < first + size)
            for at, value in halo_rows:
                lines[at] = jnp.where(inside, pltpu.roll(value, shift, 1), lines[at])

        def halos(base, step, size, at):
            lines_of = []
            for n in range(size):
                here = base + n * step + at
                before, after = by_side("gx", pair[here : here + 1, part], other[here : here + 1, part])
                lines_of += [(n, after), (n - size, before)]
            return lines_of

        for ch in range(channels):
            add(3 * ch, 3, nf[ch], halos(0, channels, 3, ch))
        base = 3 * channels
        for cc in range(coefs):
            tile = nv[cc] if cc < winds else nm[cc - winds]
            add(base + 2 * cc, 2, tile, halos(base, coefs, 2, cc))
        blank = jnp.zeros((2, LANES), F32)
        return jnp.concatenate([main, lines[0], lines[1], lines[2], blank, lines[-3], lines[-2], lines[-1]], axis=0)

    last = packed(nf_last, nv_last, nm_last, slice(columns - LANES, columns), True)
    first = packed(nf_first, nv_first, nm_first, slice(0, LANES), False)
    even = lax.rem(lax.axis_index("gy"), 2) == 0
    to_pair[...] = jnp.where(even, last, first)
    to_other[...] = jnp.where(even, first, last)


def parent_kernel(size_x, anchor, index, table, pf, pv, pm, col_other, row_other, col_pair, row_pair, parent_next, *slabs):
    fields, _, rows, columns = pf.shape
    level, levels = pl.program_id(0), pl.num_programs(0)
    channels = fields * levels
    span = rows // 3
    rank = lax.axis_index("gx")
    base = 3 * channels + 2 * 3 * levels
    row_shift = lax.rem((rows - span) * rank + size_x * rows - anchor[0], rows)
    row = row_index(rows, columns)
    column = lane_index(rows, columns)
    place = (index[0] * size_x + rank) * (len(slabs) - 1)
    kinds = [table[place + slot] for slot in range(len(slabs) - 1)]
    u, v, k = pv[0, 0], pv[1, 0], pm[0]
    a_w = jnp.maximum(u, 0.0) + k
    a_e = k - jnp.minimum(u, 0.0)
    a_s = jnp.maximum(v, 0.0) + k
    a_n = k - jnp.minimum(v, 0.0)
    a_c = 1.0 - (a_w + a_e + a_s + a_n)
    pad = jnp.zeros((rows, columns - LANES), F32)
    left, right = by_side("gy", col_pair[...], col_other[...])

    def rows_by_slab(value):
        thirds = [
            (
                value[span * kind : span * (kind + 1)],
                value[(span * kind - 1) % rows : (span * kind - 1) % rows + 1],
                value[span * (kind + 1) % rows : span * (kind + 1) % rows + 1],
            )
            for kind in range(3)
        ]
        yield thirds[0]
        for kind in kinds:
            yield [
                jnp.where(kind == 0, zero, jnp.where(kind == 1, one, two))
                for zero, one, two in zip(*thirds)
            ]

    for field in range(fields):
        ch = field * levels + level
        q = pf[field, 0]
        source = pl.ds(base + ch, 1)
        above, below = by_side("gx", row_pair[source, :], row_other[source, :])
        west = jnp.where(row == 0, above, pltpu.roll(q, 1, 0))
        east = jnp.where(row == rows - 1, below, pltpu.roll(q, rows - 1, 0))
        at_first = pltpu.roll(left, LANES - ch, 1)
        at_last = pltpu.roll(right, LANES - 1 - ch, 1)
        south = jnp.where(
            column == 0, jnp.concatenate([at_first, pad], axis=1), pltpu.roll(q, 1, 1)
        )
        north = jnp.where(
            column == columns - 1,
            jnp.concatenate([pad, at_last], axis=1),
            pltpu.roll(q, columns - 1, 1),
        )
        result = a_c * q + a_w * west + a_e * east + a_s * south + a_n * north
        parent_next[field, 0] = result
        moved = pltpu.roll(result, row_shift, 0)
        here = level * fields + field
        for slab, (cells, before, after) in zip(slabs, rows_by_slab(moved)):
            slab[pl.ds(pl.multiple_of(span * here, 8), span), :] = cells
            slab[pl.ds(span * channels + here, 1), :] = before
            slab[pl.ds((span + 1) * channels + here, 1), :] = after


def packed_half(value, side):
    rows = value.shape[0] // 2
    first, second = value[:rows], value[rows:]
    left = lane_index(rows) < LANES // 2
    if side == 0:
        return jnp.where(left, first, pltpu.roll(second, LANES // 2, 1))
    return jnp.where(left, pltpu.roll(first, LANES // 2, 1), second)


def unpacked_half(value, side):
    turned = pltpu.roll(value, LANES // 2, 1)
    return jnp.concatenate([value, turned] if side == 0 else [turned, value], axis=0)


def row_select_kernel(entries, rows, channels, anchor, *refs):
    count = len(entries)
    slabs, messages, half = refs[:count], refs[count:-1], refs[-1]
    span = rows // 3
    columns = slabs[0].shape[1]
    rank = lax.axis_index("gx")
    start = anchor[0] + span * rank
    lowest, highest = lax.div(start, rows), lax.div(start + span - 1, rows)
    above, below = lax.div(start - 1, rows), lax.div(start + span, rows)
    split = jnp.where(highest > lowest, rows * highest - start, span)
    cells, total = span * channels, (span + 2) * channels

    offset = anchor[1] - lax.axis_size("gy") // 2 * columns
    shift = lax.rem(2 * columns - offset, columns)

    def pick(owner, first, size):
        value = slabs[0][first : first + size, :]
        for senders, slab in zip(entries[1:], slabs[1:]):
            chosen = False
            for d, ranks in senders:
                chosen = chosen | ((rank - owner == d) & among(rank, ranks))
            value = jnp.where(chosen, slab[first : first + size, :], value)
        return value

    def turned_tiles(value):
        value = pltpu.roll(value, shift, 1)
        return [value[:, LANES * tile : LANES * (tile + 1)] for tile in range(3)]

    row = row_index(cells, columns) & (span - 1)
    tiles = turned_tiles(jnp.where(row < split, pick(lowest, 0, cells), pick(highest, 0, cells)))
    edges = (turned_tiles(pick(above, cells, channels)), turned_tiles(pick(below, cells + channels, channels)))
    sides = [[edge[tile] for edge in edges] for tile in range(3)]
    lanes, edge_lanes = lane_index(span), lane_index(channels)
    edge_inside = lax.div(edge_lanes, 2) == row_index(channels)

    def beside(parts, tile, lane):
        return jnp.where(lane == LANES - 1, parts[(tile + 2) % 3], parts[(tile + 1) % 3])

    for tile, message in enumerate(messages):
        message[0:cells, :] = tiles[tile]
        rim = jnp.zeros((span, LANES), F32)
        for ch in range(channels):
            here = [value[span * ch : span * (ch + 1)] for value in tiles]
            turned = pltpu.roll(beside(here, tile, lanes), 2 * ch + 1, 1)
            rim = jnp.where((lanes == 2 * ch) | (lanes == 2 * ch + 1), turned, rim)
        message[total : total + span, :] = rim + pltpu.roll(rim, LANES // 2, 1)
        for side in range(2):
            first = cells + side * channels
            message[first : first + channels, :] = sides[tile][side]
            line = beside([value[side] for value in sides], tile, edge_lanes)
            line = pltpu.roll(line, 1, 1, stride=2, stride_axis=0)
            line = jnp.sum(jnp.where(edge_inside, line, 0.0), axis=0, keepdims=True)
            target = total + span + side
            message[target : target + 1, :] = line + pltpu.roll(line, LANES // 2, 1)
        message[total + span + 2 :, :] = jnp.zeros((message.shape[0] - total - span - 2, LANES), F32)
    split_tile = jnp.where(offset < LANES, messages[2][...], messages[1][...])
    right = ((offset <= LANES // 2) | (offset > LANES)) & (offset <= LANES + LANES // 2)
    half[...] = jnp.where(right, packed_half(split_tile, 1), packed_half(split_tile, 0))


def three_parts(x):
    high = x.astype(jnp.bfloat16)
    rest = x - high.astype(F32)
    middle = rest.astype(jnp.bfloat16)
    low = (rest - middle.astype(F32)).astype(jnp.bfloat16)
    return high, middle, low


def exact_dot(x, matrix):
    parts = three_parts(x)
    total = jnp.dot(parts[2], matrix, preferred_element_type=F32)
    total = total + jnp.dot(parts[1], matrix, preferred_element_type=F32)
    return total + jnp.dot(parts[0], matrix, preferred_element_type=F32)


def stencil(q, coefs):
    height, width = q.shape
    return (
        coefs[0] * q
        + coefs[1] * pltpu.roll(q, 1, 0)
        + coefs[2] * pltpu.roll(q, height - 1, 0)
        + coefs[3] * pltpu.roll(q, 1, 1)
        + coefs[4] * pltpu.roll(q, width - 1, 1)
    )


def nest_start_kernel(nf, nv, nm, row_pair, row_other, col_pair, col_other, coefs, moved, weights, state):
    fields, _, rows, columns = nf.shape
    level, levels = pl.program_id(0), pl.num_programs(0)
    channels = fields * levels
    height, width = rows + 8, columns + LANES
    rank_x, rank_y = lax.axis_index("gx"), lax.axis_index("gy")
    row = row_index(height, width)
    column = lane_index(height, width)
    local_row = jnp.where(row < rows + 4, row, row - height)
    local_column = jnp.where(column < columns + LANES // 2, column, column - width)
    global_row = rank_x * rows + local_row
    global_column = rank_y * columns + local_column
    row_distance = jnp.minimum(global_row, lax.axis_size("gx") * rows - 1 - global_row)
    column_distance = jnp.minimum(
        global_column, lax.axis_size("gy") * columns - 1 - global_column
    )
    distance = jnp.minimum(row_distance, column_distance)
    weight = nudge_floor + (1.0 - nudge_floor) * jnp.exp(
        jnp.maximum(distance, 0).astype(F32) / -relax_width
    )
    weight = jnp.where(distance < 0, 0.0, weight)
    keep = 1.0 - weight
    edge_lanes = lane_index(height)

    @pl.when(level == 0)
    def _():
        weights[...] = weight / 9.0
        state[...] = jnp.zeros_like(state)

    left, right = by_side("gy", col_pair[...], col_other[...])

    def side_tile(first, size):
        after = pltpu.roll(right, lax.rem(2 * LANES - first, LANES), 1)
        before = pltpu.roll(left, lax.rem(2 * LANES - first - size, LANES), 1)
        inside = jnp.where(edge_lanes < LANES // 2, after, before)
        outside = (edge_lanes >= size) & (edge_lanes < LANES - size)
        return jnp.where(outside, 0.0, inside)

    def fill(slot, value, base, step, at, size, first):
        state[slot, 0:rows, 0:columns] = value
        for n in range(size):
            source = pl.ds(base + n * step + at, 1)
            above, below = by_side("gx", row_pair[source, :], row_other[source, :])
            state[slot, rows + n : rows + n + 1, 0:columns] = below
            target = height - size + n
            state[slot, target : target + 1, 0:columns] = above
        state[slot, :, columns:width] = side_tile(first, size)

    base = 3 * channels
    for slot, value in enumerate((nv[0, 0], nv[1, 0], nm[0])):
        cc = slot * levels + level
        fill(slot + fields, value, base, 3 * levels, cc, 2, base + 2 * cc)
    for field in range(fields):
        ch = field * levels + level
        fill(field, nf[field, 0], 0, channels, ch, 3, 3 * ch)
    u, v, k = (state[slot + fields] for slot in range(3))
    a_w = jnp.maximum(u, 0.0) + k
    a_e = k - jnp.minimum(u, 0.0)
    a_s = jnp.maximum(v, 0.0) + k
    a_n = k - jnp.minimum(v, 0.0)
    a_c = 1.0 - (a_w + a_e + a_s + a_n)
    for slot, value in enumerate((a_c, a_w, a_e, a_s, a_n)):
        coefs[0, slot] = keep * value
    for field in range(fields):
        moved[0, field] = stencil(state[field], [coefs[0, slot] for slot in range(5)])


def nest_kernel(ks, half, selves, anchor, spread, gather, coefs, moved, weights, *refs):
    count = len(ks) + 3
    received, messages = dict(zip(ks, refs[: len(ks)])), refs[len(ks) : count]
    result, coarse, *coarse_half = refs[count:-6]
    relay, refined, forcing, state, sums, final = refs[-6:]
    fields, _, rows, columns = result.shape
    level, levels = pl.program_id(0), pl.num_programs(0)
    channels = fields * levels
    span_rows, span_columns = rows // 3, columns // 3
    height, width = rows + 8, columns + LANES
    tiles = width // LANES
    relay_rows = span_rows + 2
    total = relay_rows * channels
    offset = anchor[1] - lax.axis_size("gy") // 2 * columns
    kind = lax.rem(lax.axis_index("gy"), 3)
    edge = columns - offset - span_columns * kind

    @pl.when(level == 0)
    def _():
        arrived, rims = {}, {}
        for k in ks:
            value = received[k][...]
            side = half[1] if half and half[0] == k else 0
            if half and half[0] == k:
                value = unpacked_half(value, side)
            rim = value[total : total + relay_rows]
            if side == 1:
                rim = pltpu.roll(rim, LANES // 2, 1)
            if k in selves:
                itself = lax.axis_index("gy") == selves[k]
                own = messages[k % 3][...]
                value = jnp.where(itself, own, value)
                rim = jnp.where(itself, own[total : total + relay_rows], rim)
            arrived[k], rims[k] = value, rim

        def chosen(values):
            low, high = values.get(2, values[0]), values.get(-1, values[0])
            low = jnp.where(kind == 1, values.get(1, values[0]), low)
            low = jnp.where(kind == 0, values[0], low)
            return low, jnp.where(kind == 1, values.get(-2, values[0]), high)

        lower, upper = chosen(arrived)
        rim_low, rim_high = chosen(rims)
        lanes = lane_index(lower.shape[0])
        relay[:, 0:LANES] = jnp.where(lanes < edge, lower, upper)
        relay[total:, LANES:] = jnp.zeros((relay.shape[0] - total, LANES), F32)
        odd = (lane_index(relay_rows) & 1) == 1
        rim = jnp.where(jnp.where(odd, LANES, -1) < edge, rim_low, rim_high)
        for ch in range(channels):
            sides = pltpu.roll(rim, (LANES - 2 * ch) % LANES, 1)
            relay[span_rows * ch : span_rows * (ch + 1), LANES:] = sides[0:span_rows]
            for side in (span_rows, span_rows + 1):
                here = side * channels + ch
                relay[here : here + 1, LANES:] = sides[side : side + 1]
        refined[...] = exact_dot(relay[...], spread[...])

    relay_row = row_index(span_rows, width)
    for field in range(fields):
        ch = level * fields + field
        centre = refined[pl.ds(pl.multiple_of(span_rows * ch, 8), span_rows), :]
        above = refined[pl.ds(span_rows * channels + ch, 1), :]
        below = refined[pl.ds((span_rows + 1) * channels + ch, 1), :]
        before = jnp.where(relay_row == 0, above, pltpu.roll(centre, 1, 0))
        after = jnp.where(
            relay_row == span_rows - 1, below, pltpu.roll(centre, span_rows - 1, 0)
        )
        thirds = (before + 2.0 * centre, 3.0 * centre, 2.0 * centre + after)
        rims = (
            (rows, centre[span_rows - 1 :] + 2.0 * below),
            (rows + 1, 3.0 * below),
            (height - 2, 3.0 * above),
            (height - 1, 2.0 * above + centre[0:1]),
        )
        for tile in range(tiles):
            part = slice(LANES * tile, LANES * (tile + 1))
            for at, value in enumerate(thirds):
                forcing[field, tile, pl.ds(at, span_rows, stride=3), :] = value[:, part]
            forcing[field, tile, rows + 2 : height - 2, :] = jnp.zeros((4, LANES), F32)
            for at, value in rims:
                forcing[field, tile, at : at + 1, :] = value[:, part]
    for field in range(fields):
        for tile in range(tiles):
            part = slice(LANES * tile, LANES * (tile + 1))
            pull = weights[:, part] * forcing[field, tile]
            forcing[field, tile] = pull
            state[field, :, part] = moved[0, field, :, part] + pull
    for step in range(SUBSTEPS - 1):
        for field in range(fields):
            pull = jnp.concatenate([forcing[field, tile] for tile in range(tiles)], axis=1)
            value = pull + stencil(state[field], [coefs[0, slot] for slot in range(5)])
            if step < SUBSTEPS - 2:
                state[field] = value
            else:
                result[field, 0] = value[0:rows, 0:columns]
                for tile in range(tiles - 1):
                    final[field, tile] = value[0:rows, LANES * tile : LANES * (tile + 1)]
    for field in range(fields):
        for tile in range(tiles - 1):
            part = slice(LANES * tile, LANES * (tile + 1))
            sums[span_rows * field : span_rows * (field + 1), part] = (
                final[field, tile, pl.ds(0, span_rows, stride=3), :]
                + final[field, tile, pl.ds(1, span_rows, stride=3), :]
                + final[field, tile, pl.ds(2, span_rows, stride=3), :]
            )
    means = exact_dot(sums[...], gather[...]) / 9.0
    coarse[...] = means
    if half:
        coarse_half[0][...] = packed_half(means, half[1])


def column_select_kernel(ks, half, selves, columns, levels, anchor, coarse, *refs):
    returned, placed = refs[:-1], refs[-1]
    offset = anchor[1] - lax.axis_size("gy") // 2 * columns
    size = placed.shape[0] // levels
    lanes = lane_index(size)
    for level in range(levels):
        rows = slice(size * level, size * (level + 1))
        arrived = {}
        for k, ref in zip(ks, returned):
            if half and half[0] == k:
                value = ref[size // 2 * level : size // 2 * (level + 1), :]
                value = unpacked_half(value, half[1])
            else:
                value = ref[rows, :]
            if k in selves:
                value = jnp.where(lax.axis_index("gy") == selves[k], coarse[rows, :], value)
            arrived[k] = value
        tiles = [arrived[0]]
        for tile in (1, 2):
            own = arrived.get(tile, arrived.get(tile - 3))
            other = arrived.get(tile - 3, own)
            inside = lanes < columns - offset - LANES * tile
            tiles.append(jnp.where(inside, own, other))
        placed[rows, :] = pltpu.roll(jnp.concatenate(tiles, axis=1), offset, 1)


def merge_kernel(entries, anchor, parent_next, *refs):
    merged = refs[-1]
    fields, _, rows, columns = parent_next.shape
    span = rows // 3
    rank_x, rank_y = lax.axis_index("gx"), lax.axis_index("gy")
    size_x, size_y = lax.axis_size("gx"), lax.axis_size("gy")
    row = rank_x * rows + row_index(rows, columns) - anchor[0]
    column = rank_y * columns + lane_index(rows, columns) - anchor[1]
    covered = (
        (row >= 0) & (row < size_x * span) & (column >= 0) & (column < size_y * (columns // 3))
    )
    first = anchor[0] - (rows - span) * rank_x
    row_shift = lax.rem(first + size_x * rows, rows)
    slab_row = row_index(span)
    choices = [[], [], []]
    for at, receivers in enumerate(entries):
        for d, ranks in receivers:
            place = first + span * d + slab_row
            if ranks is not None:
                place = jnp.where(among(rank_x, ranks), place, -1)
            choices[d % 3].append((at, (place >= 0) & (place < rows)))
    for field in range(fields):
        tiles = []
        for tile in range(3):
            kinds = []
            for options in choices:
                value = jnp.zeros((span, LANES), F32)
                for at, inside in options:
                    part = slice(LANES * tile, LANES * (tile + 1))
                    cells = refs[at][span * field : span * (field + 1), part]
                    value = jnp.where(inside, cells, value)
                kinds.append(value)
            tiles.append(jnp.concatenate(kinds, axis=0))
        fed_back = pltpu.roll(jnp.concatenate(tiles, axis=1), row_shift, 0)
        merged[field, 0] = jnp.where(covered, fed_back, parent_next[field, 0])


def spread_matrix(columns):
    span = columns // 3
    matrix = np.zeros((2 * LANES, columns + LANES), np.float32)

    def source(m):
        return LANES if m < 0 else (LANES + 1 if m >= span else m)

    for c in range(-2, columns + 2):
        m, j = divmod(c, 3)
        at = c % (columns + LANES)
        if j == 0:
            matrix[source(m - 1), at] += 1.0
            matrix[source(m), at] += 2.0
        elif j == 1:
            matrix[source(m), at] += 3.0
        else:
            matrix[source(m), at] += 2.0
            matrix[source(m + 1), at] += 1.0
    return jnp.asarray(matrix, jnp.bfloat16)


def gather_matrix(columns):
    matrix = np.zeros((columns, columns // 3), np.float32)
    matrix[np.arange(columns), np.arange(columns) // 3] = 1.0
    return jnp.asarray(matrix, jnp.bfloat16)


def coloured(pairs):
    degree = max(sum(pair[end] == at for pair in pairs) for end in (0, 1) for at, _ in enumerate(pairs + [0, 0]))
    routes = [[] for _ in range(degree)]

    def free(route, end, at):
        return all(pair[end] != at for pair in routes[route])

    for pair in pairs:
        first = next(route for route in range(degree) if free(route, 0, pair[0]))
        second = next(route for route in range(degree) if free(route, 1, pair[1]))
        if not free(first, 1, pair[1]):
            end, at, route, other = 1, pair[1], first, second
            path = []
            while not free(route, end, at):
                step = next(p for p in routes[route] if p[end] == at)
                path.append((step, route, other))
                end, at, route, other = 1 - end, step[1 - end], other, route
            for step, source, _ in path:
                routes[source].remove(step)
            for step, _, target in path:
                routes[target].append(step)
        routes[first].append(pair)
    return [sorted(route) for route in routes]


def row_routes(size, rows):
    span = rows // 3

    def needed(start):
        pairs = set()
        for nest in range(size):
            for at in (start + span * nest, start + span * nest + span + 1):
                pairs.add((at // rows, nest))
        return {(owner, nest) for owner, nest in pairs if owner != nest}

    def cost(pairs):
        cuts = [
            sum((a < cut <= n) if up else (n < cut <= a) for a, n in pairs)
            for cut in range(2, size, 2)
            for up in (False, True)
        ]
        return 4 * max(cuts) + len(coloured(sorted(pairs)))

    ranges = []
    pending = None
    for first in range(0, size * (rows - span) - 2, span):
        last = min(first + span, size * (rows - span) - 2) - 1
        pairs = set().union(*(needed(start) for start in range(first, last)))
        start, extra = first, needed(last)
        if pending is not None:
            before, more = ranges[-1][1], pending
            if cost(before | more) + cost(pairs) <= cost(before) + cost(pairs | more):
                ranges[-1] = (ranges[-1][0], before | more)
            else:
                start, pairs = first - 1, pairs | more
        ranges.append((start + 1, pairs))
        pending = extra
    ranges[-1] = (ranges[-1][0], ranges[-1][1] | pending)

    def crossing(route):
        return -sum(a // 2 != n // 2 for a, n in route)

    return [(first, sorted(coloured(sorted(pairs)), key=crossing)) for first, pairs in ranges]


def column_routes(size):
    routes, selves = {}, {}
    for k in (0, 1, -2, 2, -1):
        pairs = [(size // 2 + p, 3 * p + k) for p in range(size - size // 2)]
        routes[k] = [(s, n) for s, n in pairs if 0 <= n < size and n != s]
        selves.update({k: s for s, n in pairs if n == s})
    return routes, selves


column_cases = (
    (1, (0, 1, 2, -1), (-1, 1)),
    (65, (0, 1, 2, -1), (2, 0)),
    (128, (0, 1, 2, -1, -2), None),
    (129, (0, 1, -1, -2), (-2, 1)),
    (193, (0, 1, -1, -2), (1, 0)),
)


def per_device(
    parent_fields,
    parent_velocity,
    parent_mixing,
    nest_fields,
    nest_velocity,
    nest_mixing,
    nest_anchor,
):
    fields, levels, rows, columns = shape = parent_fields.shape
    channels = fields * levels
    span, last = rows // 3, columns // LANES - 1
    gx, gy = lax.axis_size("gx"), lax.axis_size("gy")
    height, width = rows + 8, columns + LANES
    pf = parent_fields.reshape(channels, rows, columns)
    nf = nest_fields.reshape(channels, rows, columns)
    nv = nest_velocity.reshape(2 * levels, rows, columns)
    nm = nest_mixing
    def row_blocks(array):
        size = (array.shape[0], 8, columns)
        return [(array, block(size, (0, 0, 0))), (array, block(size, (0, rows // 8 - 1, 0)))]

    def column_blocks(array):
        size = (array.shape[0], rows, LANES)
        return [(array, block(size, (0, 0, 0))), (array, block(size, (0, 0, last)))]

    def shaped(*size):
        return size, block(size, (0,) * len(size))

    def whole_of(arrays):
        return [(array, whole(array)) for array in arrays]

    halo_rows = 4 * channels + 6 * levels
    ranges = row_routes(gx, rows)
    middle = gy // 2 * columns
    firsts = ([first for first, _ in ranges], [middle + first for first, _, _ in column_cases])
    scalar = pl.BlockSpec(memory_space=pltpu.SMEM)
    anchor = (nest_anchor, scalar)
    row_pair, row_other, col_pair, col_other, row_range, column_case = call(
        functools.partial(pack_kernel, firsts),
        1,
        [anchor]
        + [
            (pltpu.with_memory_space_constraint(array, pltpu.HBM), spec)
            for array, spec in row_blocks(pf)
            + column_blocks(pf)
            + row_blocks(nf)
            + row_blocks(nv)
            + row_blocks(nm)
        ],
        [shaped(halo_rows, columns)] * 2
        + [shaped(rows, LANES)] * 2
        + [((1,), scalar, jnp.int32)] * 2,
    )
    col_halos = swapped("gy", col_pair, col_other)
    row_halos = swapped("gx", row_pair, row_other)

    slots = max(len(routes) for _, routes in ranges)
    table = np.zeros((len(ranges), gx, slots), np.int32)
    for at, (_, routes) in enumerate(ranges):
        for slot, route in enumerate(routes):
            for owner, nest in route:
                table[at, owner, slot] = (nest - owner) % 3
    message_rows = -(-((span + 2) * (channels + 1)) // 16) * 16
    columns_of, selves = column_routes(gy)
    cells_rows, relay_height = span * channels, (span + 2) * channels

    def by_shift(route, receiver):
        shifts = sorted({nest - owner for owner, nest in route})
        return [(d, [pair[receiver] for pair in route if pair[1] - pair[0] == d]) for d in shifts]

    parent_next, *slabs = call(
        functools.partial(parent_kernel, gx),
        levels,
        [
            anchor,
            (row_range, scalar),
            (jnp.asarray(table.reshape(-1)), scalar),
            (parent_fields, by_level(shape, 1)),
            (parent_velocity, by_level(parent_velocity.shape, 1)),
            (parent_mixing, by_level(parent_mixing.shape, 0)),
        ]
        + whole_of([col_halos[1], row_halos[1], col_halos[0], row_halos[0]]),
        [(shape, by_level(shape, 1))] + [shaped(relay_height, columns)] * (slots + 1),
    )

    def relay_rows(routes):
        def branch(nest_anchor, slabs, nf, nv, nm, row_halos):
            received = [lax.ppermute(slab, "gx", route) for slab, route in zip(slabs[1:], routes)]
            to_pair, to_other = call(
                column_pack_kernel,
                1,
                column_blocks(nf) + column_blocks(nv) + column_blocks(nm) + whole_of(row_halos),
                [shaped(height, LANES)] * 2,
            )
            sides = swapped("gy", to_pair, to_other)
            entries = [None] + [by_shift(route, 1) for route in routes]
            messages = call(
                functools.partial(row_select_kernel, entries, rows, channels),
                1,
                [(nest_anchor, scalar)] + whole_of([slabs[0], *received]),
                [shaped(message_rows, LANES)] * 3 + [shaped(message_rows // 2, LANES)],
            )
            return messages, sides

        return branch

    messages, sides = lax.switch(
        row_range[0],
        [relay_rows(routes) for _, routes in ranges],
        nest_anchor,
        slabs,
        nf,
        nv,
        nm,
        row_halos,
    )

    def nest_part(ks, half):
        def branch(nest_anchor, messages, nest_fields, nest_velocity, nest_mixing, halos):
            anchor = (nest_anchor, scalar)
            packed = half[0] if half else None
            received = [
                lax.ppermute(messages[3 if k == packed else k % 3], "gy", columns_of[k]) for k in ks
            ]
            coefs, moved, weights = call(
                nest_start_kernel,
                levels,
                [
                    (nest_fields, by_level(shape, 1)),
                    (nest_velocity, by_level(nest_velocity.shape, 1)),
                    (nest_mixing, by_level(nest_mixing.shape, 0)),
                ]
                + whole_of(halos),
                [
                    ((levels, 5, height, width), by_level((levels, 5, height, width), 0)),
                    ((levels, fields, height, width), by_level((levels, fields, height, width), 0)),
                    shaped(height, width),
                ],
                scratch=[(fields + 3, height, width)],
            )
            size = cells_rows // levels

            def strip(rows):
                return (rows * levels, LANES), pl.BlockSpec((rows, LANES), lambda level: (level, 0))

            nest_result, coarse, *coarse_half = call(
                functools.partial(nest_kernel, ks, half, selves),
                levels,
                [anchor]
                + whole_of([spread_matrix(columns), gather_matrix(columns)])
                + [(coefs, by_level(coefs.shape, 0)), (moved, by_level(moved.shape, 0))]
                + whole_of([weights, *received, *messages[:3]]),
                [(shape, by_level(shape, 1)), strip(size)] + ([strip(size // 2)] if half else []),
                scratch=[
                    (message_rows, 2 * LANES),
                    (message_rows, width),
                    (fields, width // LANES, height, LANES),
                    (fields, height, width),
                    (span * fields, columns),
                    (fields, columns // LANES, rows, LANES),
                ],
            )
            back = [k for k in (-1, 1, -2, 2, 0) if k in ks]
            returned = [
                lax.ppermute(
                    coarse_half[0] if k == packed else coarse,
                    "gy",
                    [pair[::-1] for pair in columns_of[k]],
                )
                for k in back
            ]
            placed = call(
                functools.partial(column_select_kernel, back, half, selves, columns, levels),
                1,
                [anchor] + whole_of([coarse, *returned]),
                [shaped(cells_rows, columns)],
            )[0]
            return nest_result, placed

        return branch

    nest_result, placed = lax.switch(
        column_case[0],
        [nest_part(ks, half) for _, ks, half in column_cases],
        nest_anchor,
        messages,
        nest_fields,
        nest_velocity,
        nest_mixing,
        [*row_halos, *sides],
    )

    def feedback_rows(routes):
        def branch(nest_anchor, parent_next, placed):
            received = [
                lax.ppermute(placed, "gx", [pair[::-1] for pair in route]) for route in routes[::-1]
            ]
            entries = [[(0, None)]] + [by_shift(route, 0) for route in routes[::-1]]
            slab_block = pl.BlockSpec((span * fields, columns), lambda level: (level, 0))
            return call(
                functools.partial(merge_kernel, entries),
                levels,
                [
                    (nest_anchor, pl.BlockSpec(memory_space=pltpu.SMEM)),
                    (parent_next, by_level(shape, 1)),
                ]
                + [(array, slab_block) for array in (placed, *received)],
                [(shape, by_level(shape, 1), pltpu.HBM)],
            )[0]

        return branch

    merged = lax.switch(
        row_range[0], [feedback_rows(routes) for _, routes in ranges], nest_anchor, parent_next, placed
    )
    return merged, nest_result


def solution(mesh):
    placed = (
        P(None, None, "gx", "gy"),
        P(None, None, "gx", "gy"),
        P(None, "gx", "gy"),
        P(None, None, "gx", "gy"),
        P(None, None, "gx", "gy"),
        P(None, "gx", "gy"),
        P(),
    )
    return jax.shard_map(
        per_device,
        mesh=mesh,
        in_specs=placed,
        out_specs=(P(None, None, "gx", "gy"), P(None, None, "gx", "gy")),
        check_vma=False,
    )
```

```python
import functools

import jax
import jax.numpy as jnp
import numpy as np
from jax import lax
from jax.experimental import pallas as pl
from jax.experimental.pallas import tpu as pltpu
from jax.sharding import PartitionSpec as P

SUBSTEPS = 3
F32 = jnp.float32
LANES = 128
VMEM_LIMIT = 16 * 1024 * 1024
nudge_floor = 0.1
relax_width = 4.0


def whole(array):
    return pl.BlockSpec(array.shape, lambda level: (0,) * array.ndim)


def block(shape, at):
    return pl.BlockSpec(shape, lambda level: at)


def by_level(shape, dim):
    sizes = tuple(1 if i == dim else n for i, n in enumerate(shape))
    return pl.BlockSpec(sizes, lambda level: tuple(level if i == dim else 0 for i in range(len(shape))))


def call(body, grid, ins, outs, scratch=(), cost=None):
    return pl.pallas_call(
        body,
        grid=(grid,),
        out_shape=[
            pltpu.HBM(out[0], F32) if out[2:] == (pltpu.HBM,) else jax.ShapeDtypeStruct(out[0], *(out[2:] or (F32,)))
            for out in outs
        ],
        in_specs=[spec for _, spec in ins],
        out_specs=[out[1] for out in outs],
        scratch_shapes=[pltpu.VMEM(shape, F32) for shape in scratch],
        cost_estimate=cost,
        compiler_params=pltpu.CompilerParams(vmem_limit_bytes=VMEM_LIMIT),
    )(*[array for array, _ in ins])


def call_once(body, scalars, ins, outs, scratch=(), results=0):
    vmem, hbm = pl.BlockSpec(memory_space=pltpu.VMEM), pl.BlockSpec(memory_space=pl.ANY)
    return pl.pallas_call(
        body,
        out_shape=[
            pltpu.HBM(shape, F32) if at < results else jax.ShapeDtypeStruct(shape, F32)
            for at, shape in enumerate(outs)
        ],
        in_specs=[pl.BlockSpec(memory_space=pltpu.SMEM)] * len(scalars) + [vmem] * len(ins),
        out_specs=[hbm] * results + [vmem] * (len(outs) - results),
        scratch_shapes=[
            pltpu.VMEM(shape, F32) if isinstance(shape, tuple) else shape for shape in scratch
        ],
        compiler_params=pltpu.CompilerParams(vmem_limit_bytes=VMEM_LIMIT),
    )(*scalars, *ins)


def lane_index(rows, lanes=LANES):
    return lax.broadcasted_iota(jnp.int32, (rows, lanes), 1)


def row_index(rows, lanes=LANES):
    return lax.broadcasted_iota(jnp.int32, (rows, lanes), 0)


def among(value, numbers):
    found = False
    for number in numbers:
        found = found | (value == number)
    return found


def swapped(axis, to_pair, to_other):
    count = lax.axis_size(axis)
    pairs = [(at, at ^ 1) for at in range(count)]
    others = [(at, at + 1 if at % 2 else at - 1) for at in range(1, count - 1)]
    return lax.ppermute(to_pair, axis, pairs), lax.ppermute(to_other, axis, others)


def by_side(axis, from_pair, from_other):
    even = lax.rem(lax.axis_index(axis), 2) == 0
    return jnp.where(even, from_other, from_pair), jnp.where(even, from_pair, from_other)


def pack_kernel(firsts, anchor, pf_head, pf_tail, pf_first, pf_last, nf_head, nf_tail, nv_head, nv_tail, nm_head, nm_tail, *outs):
    to_pair, to_other, col_to_pair, col_to_other, *indices = outs
    channels, rows = pf_first.shape[:2]
    for at, (index, limits) in enumerate(zip(indices, firsts)):
        index[0] = sum((anchor[at] >= first).astype(jnp.int32) for first in limits[1:])
    coefs = nv_head.shape[0] + nm_head.shape[0]
    even = lax.rem(lax.axis_index("gx"), 2) == 0

    def lines(out, parent, field, wind, mixing, at_end):
        def put(here, ref, row, count, at):
            line = 8 - count + at if at_end else at
            out[here : here + 1, :] = ref[row, line : line + 1, :]

        for at in range(3):
            for ch in range(channels):
                put(at * channels + ch, field, ch, 3, at)
        for at in range(2):
            for cc in range(coefs):
                here = 3 * channels + at * coefs + cc
                ref, row = (wind, cc) if cc < wind.shape[0] else (mixing, cc - wind.shape[0])
                put(here, ref, row, 2, at)
        for ch in range(channels):
            put(3 * channels + 2 * coefs + ch, parent, ch, 1, 0)

    heads, tails = (pf_head, nf_head, nv_head, nm_head), (pf_tail, nf_tail, nv_tail, nm_tail)

    @pl.when(even)
    def _():
        lines(to_pair, *tails, True)
        lines(to_other, *heads, False)

    @pl.when(jnp.logical_not(even))
    def _():
        lines(to_pair, *heads, False)
        lines(to_other, *tails, True)

    lanes = lane_index(rows)
    last = jnp.zeros((rows, LANES), F32)
    first = jnp.zeros((rows, LANES), F32)
    for ch in range(channels):
        last = jnp.where(lanes == ch, pltpu.roll(pf_last[ch], (ch + 1) % LANES, 1), last)
        first = jnp.where(lanes == ch, pltpu.roll(pf_first[ch], ch, 1), first)
    even = lax.rem(lax.axis_index("gy"), 2) == 0
    col_to_pair[...] = jnp.where(even, last, first)
    col_to_other[...] = jnp.where(even, first, last)


def column_pack_kernel(
    nf_first, nf_last, nv_first, nv_last, nm_first, nm_last, pair, other, to_pair, to_other
):
    channels, rows = nf_first.shape[:2]
    columns = pair.shape[1]
    winds = nv_first.shape[0]
    coefs = winds + nm_first.shape[0]
    height = rows + 8
    lanes, lane = lane_index(rows), lane_index(1)

    def packed(nf, nv, nm, part, moved):
        main = jnp.zeros((rows, LANES), F32)
        lines = {at: jnp.zeros((1, LANES), F32) for at in range(-3, 3)}

        def add(first, size, tile, halo_rows):
            nonlocal main
            shift = (first + (size if moved else 0)) % LANES
            inside = (lanes >= first) & (lanes < first + size)
            main = jnp.where(inside, pltpu.roll(tile, shift, 1), main)
            inside = (lane >= first) & (lane < first + size)
            for at, value in halo_rows:
                lines[at] = jnp.where(inside, pltpu.roll(value, shift, 1), lines[at])

        def halos(base, step, size, at):
            lines_of = []
            for n in range(size):
                here = base + n * step + at
                before, after = by_side("gx", pair[here : here + 1, part], other[here : here + 1, part])
                lines_of += [(n, after), (n - size, before)]
            return lines_of

        for ch in range(channels):
            add(3 * ch, 3, nf[ch], halos(0, channels, 3, ch))
        base = 3 * channels
        for cc in range(coefs):
            tile = nv[cc] if cc < winds else nm[cc - winds]
            add(base + 2 * cc, 2, tile, halos(base, coefs, 2, cc))
        blank = jnp.zeros((2, LANES), F32)
        return jnp.concatenate([main, lines[0], lines[1], lines[2], blank, lines[-3], lines[-2], lines[-1]], axis=0)

    last = packed(nf_last, nv_last, nm_last, slice(columns - LANES, columns), True)
    first = packed(nf_first, nv_first, nm_first, slice(0, LANES), False)
    even = lax.rem(lax.axis_index("gy"), 2) == 0
    to_pair[...] = jnp.where(even, last, first)
    to_other[...] = jnp.where(even, first, last)


def parent_kernel(size_x, anchor, index, table, pf, pv, pm, col_other, row_other, col_pair, row_pair, parent_next, *slabs):
    fields, _, rows, columns = pf.shape
    levels = pm.shape[0]
    channels = fields * levels
    span = rows // 3
    rank = lax.axis_index("gx")
    base = 3 * channels + 2 * 3 * levels
    row_shift = lax.rem((rows - span) * rank + size_x * rows - anchor[0], rows)
    row = row_index(rows, columns)
    column = lane_index(rows, columns)
    place = (index[0] * size_x + rank) * (len(slabs) - 1)
    kinds = [table[place + slot] for slot in range(len(slabs) - 1)]
    pad = jnp.zeros((rows, columns - LANES), F32)
    left, right = by_side("gy", col_pair[...], col_other[...])

    def rows_by_slab(value):
        thirds = [
            (
                value[span * kind : span * (kind + 1)],
                value[(span * kind - 1) % rows : (span * kind - 1) % rows + 1],
                value[span * (kind + 1) % rows : span * (kind + 1) % rows + 1],
            )
            for kind in range(3)
        ]
        yield thirds[0]
        for kind in kinds:
            yield [
                jnp.where(kind == 0, zero, jnp.where(kind == 1, one, two))
                for zero, one, two in zip(*thirds)
            ]

    def level_body(level, carry):
        u, v, k = pv[0, level], pv[1, level], pm[level]
        a_w = jnp.maximum(u, 0.0) + k
        a_e = k - jnp.minimum(u, 0.0)
        a_s = jnp.maximum(v, 0.0) + k
        a_n = k - jnp.minimum(v, 0.0)
        a_c = 1.0 - (a_w + a_e + a_s + a_n)
        for field in range(fields):
            ch = field * levels + level
            q = pf[field, level]
            source = pl.ds(base + ch, 1)
            above, below = by_side("gx", row_pair[source, :], row_other[source, :])
            west = jnp.where(row == 0, above, pltpu.roll(q, 1, 0))
            east = jnp.where(row == rows - 1, below, pltpu.roll(q, rows - 1, 0))
            at_first = pltpu.roll(left, LANES - ch, 1)
            at_last = pltpu.roll(right, LANES - 1 - ch, 1)
            south = jnp.where(
                column == 0, jnp.concatenate([at_first, pad], axis=1), pltpu.roll(q, 1, 1)
            )
            north = jnp.where(
                column == columns - 1,
                jnp.concatenate([pad, at_last], axis=1),
                pltpu.roll(q, columns - 1, 1),
            )
            result = a_c * q + a_w * west + a_e * east + a_s * south + a_n * north
            parent_next[field, level] = result
            moved = pltpu.roll(result, row_shift, 0)
            here = level * fields + field
            for slab, (cells, before, after) in zip(slabs, rows_by_slab(moved)):
                slab[pl.ds(pl.multiple_of(span * here, 8), span), :] = cells
                slab[pl.ds(span * channels + here, 1), :] = before
                slab[pl.ds((span + 1) * channels + here, 1), :] = after
        return carry

    lax.fori_loop(0, levels, level_body, 0)


def packed_half(value, side):
    rows = value.shape[0] // 2
    first, second = value[:rows], value[rows:]
    left = lane_index(rows) < LANES // 2
    if side == 0:
        return jnp.where(left, first, pltpu.roll(second, LANES // 2, 1))
    return jnp.where(left, pltpu.roll(first, LANES // 2, 1), second)


def unpacked_half(value, side):
    turned = pltpu.roll(value, LANES // 2, 1)
    return jnp.concatenate([value, turned] if side == 0 else [turned, value], axis=0)


def row_select_kernel(entries, rows, channels, anchor, *refs):
    count = len(entries)
    slabs, messages, half = refs[:count], refs[count:-1], refs[-1]
    span = rows // 3
    columns = slabs[0].shape[1]
    rank = lax.axis_index("gx")
    start = anchor[0] + span * rank
    lowest, highest = lax.div(start, rows), lax.div(start + span - 1, rows)
    above, below = lax.div(start - 1, rows), lax.div(start + span, rows)
    split = jnp.where(highest > lowest, rows * highest - start, span)
    cells, total = span * channels, (span + 2) * channels

    offset = anchor[1] - lax.axis_size("gy") // 2 * columns
    shift = lax.rem(2 * columns - offset, columns)

    def pick(owner, first, size):
        value = slabs[0][first : first + size, :]
        for senders, slab in zip(entries[1:], slabs[1:]):
            chosen = False
            for d, ranks in senders:
                chosen = chosen | ((rank - owner == d) & among(rank, ranks))
            value = jnp.where(chosen, slab[first : first + size, :], value)
        return value

    def turned_tiles(value):
        value = pltpu.roll(value, shift, 1)
        return [value[:, LANES * tile : LANES * (tile + 1)] for tile in range(3)]

    row = row_index(cells, columns) & (span - 1)
    tiles = turned_tiles(jnp.where(row < split, pick(lowest, 0, cells), pick(highest, 0, cells)))
    edges = (turned_tiles(pick(above, cells, channels)), turned_tiles(pick(below, cells + channels, channels)))
    sides = [[edge[tile] for edge in edges] for tile in range(3)]
    lanes, edge_lanes = lane_index(span), lane_index(channels)
    edge_inside = lax.div(edge_lanes, 2) == row_index(channels)

    def beside(parts, tile, lane):
        return jnp.where(lane == LANES - 1, parts[(tile + 2) % 3], parts[(tile + 1) % 3])

    for tile, message in enumerate(messages):
        message[0:cells, :] = tiles[tile]
        rim = jnp.zeros((span, LANES), F32)
        for ch in range(channels):
            here = [value[span * ch : span * (ch + 1)] for value in tiles]
            turned = pltpu.roll(beside(here, tile, lanes), 2 * ch + 1, 1)
            rim = jnp.where((lanes == 2 * ch) | (lanes == 2 * ch + 1), turned, rim)
        message[total : total + span, :] = rim + pltpu.roll(rim, LANES // 2, 1)
        for side in range(2):
            first = cells + side * channels
            message[first : first + channels, :] = sides[tile][side]
            line = beside([value[side] for value in sides], tile, edge_lanes)
            line = pltpu.roll(line, 1, 1, stride=2, stride_axis=0)
            line = jnp.sum(jnp.where(edge_inside, line, 0.0), axis=0, keepdims=True)
            target = total + span + side
            message[target : target + 1, :] = line + pltpu.roll(line, LANES // 2, 1)
        message[total + span + 2 :, :] = jnp.zeros((message.shape[0] - total - span - 2, LANES), F32)
    split_tile = jnp.where(offset < LANES, messages[2][...], messages[1][...])
    right = ((offset <= LANES // 2) | (offset > LANES)) & (offset <= LANES + LANES // 2)
    half[...] = jnp.where(right, packed_half(split_tile, 1), packed_half(split_tile, 0))


def three_parts(x):
    high = x.astype(jnp.bfloat16)
    rest = x - high.astype(F32)
    middle = rest.astype(jnp.bfloat16)
    low = (rest - middle.astype(F32)).astype(jnp.bfloat16)
    return high, middle, low


def exact_dot(x, matrix):
    parts = three_parts(x)
    total = jnp.dot(parts[2], matrix, preferred_element_type=F32)
    total = total + jnp.dot(parts[1], matrix, preferred_element_type=F32)
    return total + jnp.dot(parts[0], matrix, preferred_element_type=F32)


def stencil(q, coefs):
    height, width = q.shape
    return (
        coefs[0] * q
        + coefs[1] * pltpu.roll(q, 1, 0)
        + coefs[2] * pltpu.roll(q, height - 1, 0)
        + coefs[3] * pltpu.roll(q, 1, 1)
        + coefs[4] * pltpu.roll(q, width - 1, 1)
    )


def nest_start_kernel(nf, nv, nm, row_pair, row_other, col_pair, col_other, coefs, moved, weights, state):
    fields, _, rows, columns = nf.shape
    levels = nm.shape[0]
    channels = fields * levels
    height, width = rows + 8, columns + LANES
    rank_x, rank_y = lax.axis_index("gx"), lax.axis_index("gy")
    row = row_index(height, width)
    column = lane_index(height, width)
    local_row = jnp.where(row < rows + 4, row, row - height)
    local_column = jnp.where(column < columns + LANES // 2, column, column - width)
    global_row = rank_x * rows + local_row
    global_column = rank_y * columns + local_column
    row_distance = jnp.minimum(global_row, lax.axis_size("gx") * rows - 1 - global_row)
    column_distance = jnp.minimum(
        global_column, lax.axis_size("gy") * columns - 1 - global_column
    )
    distance = jnp.minimum(row_distance, column_distance)
    weight = nudge_floor + (1.0 - nudge_floor) * jnp.exp(
        jnp.maximum(distance, 0).astype(F32) / -relax_width
    )
    weight = jnp.where(distance < 0, 0.0, weight)
    keep = 1.0 - weight
    edge_lanes = lane_index(height)

    weights[...] = weight / 9.0
    state[...] = jnp.zeros_like(state)

    left, right = by_side("gy", col_pair[...], col_other[...])

    def side_tile(first, size):
        after = pltpu.roll(right, lax.rem(2 * LANES - first, LANES), 1)
        before = pltpu.roll(left, lax.rem(2 * LANES - first - size, LANES), 1)
        inside = jnp.where(edge_lanes < LANES // 2, after, before)
        outside = (edge_lanes >= size) & (edge_lanes < LANES - size)
        return jnp.where(outside, 0.0, inside)

    def fill(slot, value, base, step, at, size, first):
        state[slot, 0:rows, 0:columns] = value
        for n in range(size):
            source = pl.ds(base + n * step + at, 1)
            above, below = by_side("gx", row_pair[source, :], row_other[source, :])
            state[slot, rows + n : rows + n + 1, 0:columns] = below
            target = height - size + n
            state[slot, target : target + 1, 0:columns] = above
        state[slot, :, columns:width] = side_tile(first, size)

    def level_body(level, carry):
        base = 3 * channels
        for slot, value in enumerate((nv[0, level], nv[1, level], nm[level])):
            cc = slot * levels + level
            fill(slot + fields, value, base, 3 * levels, cc, 2, base + 2 * cc)
        for field in range(fields):
            ch = field * levels + level
            fill(field, nf[field, level], 0, channels, ch, 3, 3 * ch)
        u, v, k = (state[slot + fields] for slot in range(3))
        a_w = jnp.maximum(u, 0.0) + k
        a_e = k - jnp.minimum(u, 0.0)
        a_s = jnp.maximum(v, 0.0) + k
        a_n = k - jnp.minimum(v, 0.0)
        a_c = 1.0 - (a_w + a_e + a_s + a_n)
        for slot, value in enumerate((a_c, a_w, a_e, a_s, a_n)):
            coefs[level, slot] = keep * value
        for field in range(fields):
            moved[level, field] = stencil(state[field], [coefs[level, slot] for slot in range(5)])
        return carry

    lax.fori_loop(0, levels, level_body, 0)


def nest_kernel(ks, half, selves, anchor, spread, gather, coefs, moved, weights, *refs):
    count = len(ks) + 3
    received, messages = dict(zip(ks, refs[: len(ks)])), refs[len(ks) : count]
    result, coarse, *coarse_half = refs[count:-8]
    relay, refined, forcing, state, sums, final, held, sems = refs[-8:]
    fields, levels, rows, columns = result.shape
    channels = fields * levels
    span_rows, span_columns = rows // 3, columns // 3
    height, width = rows + 8, columns + LANES
    tiles = width // LANES
    relay_rows = span_rows + 2
    total = relay_rows * channels
    offset = anchor[1] - lax.axis_size("gy") // 2 * columns
    kind = lax.rem(lax.axis_index("gy"), 3)
    edge = columns - offset - span_columns * kind

    arrived, rims = {}, {}
    for k in ks:
        value = received[k][...]
        side = half[1] if half and half[0] == k else 0
        if half and half[0] == k:
            value = unpacked_half(value, side)
        rim = value[total : total + relay_rows]
        if side == 1:
            rim = pltpu.roll(rim, LANES // 2, 1)
        if k in selves:
            itself = lax.axis_index("gy") == selves[k]
            own = messages[k % 3][...]
            value = jnp.where(itself, own, value)
            rim = jnp.where(itself, own[total : total + relay_rows], rim)
        arrived[k], rims[k] = value, rim

    def chosen(values):
        low, high = values.get(2, values[0]), values.get(-1, values[0])
        low = jnp.where(kind == 1, values.get(1, values[0]), low)
        low = jnp.where(kind == 0, values[0], low)
        return low, jnp.where(kind == 1, values.get(-2, values[0]), high)

    lower, upper = chosen(arrived)
    rim_low, rim_high = chosen(rims)
    lanes = lane_index(lower.shape[0])
    relay[:, 0:LANES] = jnp.where(lanes < edge, lower, upper)
    relay[total:, LANES:] = jnp.zeros((relay.shape[0] - total, LANES), F32)
    odd = (lane_index(relay_rows) & 1) == 1
    rim = jnp.where(jnp.where(odd, LANES, -1) < edge, rim_low, rim_high)
    for ch in range(channels):
        sides = pltpu.roll(rim, (LANES - 2 * ch) % LANES, 1)
        relay[span_rows * ch : span_rows * (ch + 1), LANES:] = sides[0:span_rows]
        for side in (span_rows, span_rows + 1):
            here = side * channels + ch
            relay[here : here + 1, LANES:] = sides[side : side + 1]
    refined[...] = exact_dot(relay[...], spread[...])

    relay_row = row_index(span_rows, width)

    def leaving(level):
        return pltpu.make_async_copy(held.at[:, level], result.at[:, level], sems.at[level])

    def level_body(level, carry):
        for field in range(fields):
            ch = level * fields + field
            centre = refined[pl.ds(pl.multiple_of(span_rows * ch, 8), span_rows), :]
            above = refined[pl.ds(span_rows * channels + ch, 1), :]
            below = refined[pl.ds((span_rows + 1) * channels + ch, 1), :]
            before = jnp.where(relay_row == 0, above, pltpu.roll(centre, 1, 0))
            after = jnp.where(
                relay_row == span_rows - 1, below, pltpu.roll(centre, span_rows - 1, 0)
            )
            thirds = (before + 2.0 * centre, 3.0 * centre, 2.0 * centre + after)
            rims = (
                (rows, centre[span_rows - 1 :] + 2.0 * below),
                (rows + 1, 3.0 * below),
                (height - 2, 3.0 * above),
                (height - 1, 2.0 * above + centre[0:1]),
            )
            for tile in range(tiles):
                part = slice(LANES * tile, LANES * (tile + 1))
                for at, value in enumerate(thirds):
                    forcing[field, tile, pl.ds(at, span_rows, stride=3), :] = value[:, part]
                forcing[field, tile, rows + 2 : height - 2, :] = jnp.zeros((4, LANES), F32)
                for at, value in rims:
                    forcing[field, tile, at : at + 1, :] = value[:, part]
        for field in range(fields):
            for tile in range(tiles):
                part = slice(LANES * tile, LANES * (tile + 1))
                pull = weights[:, part] * forcing[field, tile]
                forcing[field, tile] = pull
                state[field, :, part] = moved[level, field, :, part] + pull
        for step in range(SUBSTEPS - 1):
            for field in range(fields):
                pull = jnp.concatenate([forcing[field, tile] for tile in range(tiles)], axis=1)
                value = pull + stencil(state[field], [coefs[level, slot] for slot in range(5)])
                if step < SUBSTEPS - 2:
                    state[field] = value
                else:
                    held[field, level] = value[0:rows, 0:columns]
                    for tile in range(tiles - 1):
                        final[field, tile] = value[0:rows, LANES * tile : LANES * (tile + 1)]
        leaving(level).start()
        for field in range(fields):
            for tile in range(tiles - 1):
                part = slice(LANES * tile, LANES * (tile + 1))
                sums[span_rows * field : span_rows * (field + 1), part] = (
                    final[field, tile, pl.ds(0, span_rows, stride=3), :]
                    + final[field, tile, pl.ds(1, span_rows, stride=3), :]
                    + final[field, tile, pl.ds(2, span_rows, stride=3), :]
                )
        means = exact_dot(sums[...], gather[...]) / 9.0
        size = span_rows * fields
        coarse[pl.ds(pl.multiple_of(size * level, 8), size), :] = means
        if half:
            place = pl.ds(pl.multiple_of(size // 2 * level, 8), size // 2)
            coarse_half[0][place, :] = packed_half(means, half[1])
        return carry

    lax.fori_loop(0, levels, level_body, 0)
    for level in range(levels):
        leaving(level).wait()


def column_select_kernel(ks, half, selves, columns, levels, anchor, coarse, *refs):
    returned, placed = refs[:-1], refs[-1]
    offset = anchor[1] - lax.axis_size("gy") // 2 * columns
    size = placed.shape[0] // levels
    lanes = lane_index(size)
    for level in range(levels):
        rows = slice(size * level, size * (level + 1))
        arrived = {}
        for k, ref in zip(ks, returned):
            if half and half[0] == k:
                value = ref[size // 2 * level : size // 2 * (level + 1), :]
                value = unpacked_half(value, half[1])
            else:
                value = ref[rows, :]
            if k in selves:
                value = jnp.where(lax.axis_index("gy") == selves[k], coarse[rows, :], value)
            arrived[k] = value
        tiles = [arrived[0]]
        for tile in (1, 2):
            own = arrived.get(tile, arrived.get(tile - 3))
            other = arrived.get(tile - 3, own)
            inside = lanes < columns - offset - LANES * tile
            tiles.append(jnp.where(inside, own, other))
        placed[rows, :] = pltpu.roll(jnp.concatenate(tiles, axis=1), offset, 1)


def merge_kernel(entries, anchor, parent_next, *refs):
    slabs, (merged, held, sems) = refs[:-3], refs[-3:]
    fields, levels, rows, columns = parent_next.shape
    span = rows // 3
    rank_x, rank_y = lax.axis_index("gx"), lax.axis_index("gy")
    size_x, size_y = lax.axis_size("gx"), lax.axis_size("gy")
    row = rank_x * rows + row_index(rows, columns) - anchor[0]
    column = rank_y * columns + lane_index(rows, columns) - anchor[1]
    covered = (
        (row >= 0) & (row < size_x * span) & (column >= 0) & (column < size_y * (columns // 3))
    )
    first = anchor[0] - (rows - span) * rank_x
    row_shift = lax.rem(first + size_x * rows, rows)
    slab_row = row_index(span)
    choices = [[], [], []]
    for at, receivers in enumerate(entries):
        for d, ranks in receivers:
            place = first + span * d + slab_row
            if ranks is not None:
                place = jnp.where(among(rank_x, ranks), place, -1)
            choices[d % 3].append((at, (place >= 0) & (place < rows)))
    def leaving(level):
        return pltpu.make_async_copy(held.at[:, level], merged.at[:, level], sems.at[level])

    def level_body(level, carry):
        for field in range(fields):
            here = pl.ds(pl.multiple_of(span * (fields * level + field), 8), span)
            tiles = []
            for tile in range(3):
                kinds = []
                for options in choices:
                    value = jnp.zeros((span, LANES), F32)
                    for at, inside in options:
                        part = slice(LANES * tile, LANES * (tile + 1))
                        cells = slabs[at][here, part]
                        value = jnp.where(inside, cells, value)
                    kinds.append(value)
                tiles.append(jnp.concatenate(kinds, axis=0))
            fed_back = pltpu.roll(jnp.concatenate(tiles, axis=1), row_shift, 0)
            held[field, level] = jnp.where(covered, fed_back, parent_next[field, level])
        leaving(level).start()
        return carry

    lax.fori_loop(0, levels, level_body, 0)
    for level in range(levels):
        leaving(level).wait()


def spread_matrix(columns):
    span = columns // 3
    matrix = np.zeros((2 * LANES, columns + LANES), np.float32)

    def source(m):
        return LANES if m < 0 else (LANES + 1 if m >= span else m)

    for c in range(-2, columns + 2):
        m, j = divmod(c, 3)
        at = c % (columns + LANES)
        if j == 0:
            matrix[source(m - 1), at] += 1.0
            matrix[source(m), at] += 2.0
        elif j == 1:
            matrix[source(m), at] += 3.0
        else:
            matrix[source(m), at] += 2.0
            matrix[source(m + 1), at] += 1.0
    return jnp.asarray(matrix, jnp.bfloat16)


def gather_matrix(columns):
    matrix = np.zeros((columns, columns // 3), np.float32)
    matrix[np.arange(columns), np.arange(columns) // 3] = 1.0
    return jnp.asarray(matrix, jnp.bfloat16)


def coloured(pairs):
    degree = max(sum(pair[end] == at for pair in pairs) for end in (0, 1) for at, _ in enumerate(pairs + [0, 0]))
    routes = [[] for _ in range(degree)]

    def free(route, end, at):
        return all(pair[end] != at for pair in routes[route])

    for pair in pairs:
        first = next(route for route in range(degree) if free(route, 0, pair[0]))
        second = next(route for route in range(degree) if free(route, 1, pair[1]))
        if not free(first, 1, pair[1]):
            end, at, route, other = 1, pair[1], first, second
            path = []
            while not free(route, end, at):
                step = next(p for p in routes[route] if p[end] == at)
                path.append((step, route, other))
                end, at, route, other = 1 - end, step[1 - end], other, route
            for step, source, _ in path:
                routes[source].remove(step)
            for step, _, target in path:
                routes[target].append(step)
        routes[first].append(pair)
    return [sorted(route) for route in routes]


def row_routes(size, rows):
    span = rows // 3

    def needed(start):
        pairs = set()
        for nest in range(size):
            for at in (start + span * nest, start + span * nest + span + 1):
                pairs.add((at // rows, nest))
        return {(owner, nest) for owner, nest in pairs if owner != nest}

    def cost(pairs):
        cuts = [
            sum((a < cut <= n) if up else (n < cut <= a) for a, n in pairs)
            for cut in range(2, size, 2)
            for up in (False, True)
        ]
        return 4 * max(cuts) + len(coloured(sorted(pairs)))

    ranges = []
    pending = None
    for first in range(0, size * (rows - span) - 2, span):
        last = min(first + span, size * (rows - span) - 2) - 1
        pairs = set().union(*(needed(start) for start in range(first, last)))
        start, extra = first, needed(last)
        if pending is not None:
            before, more = ranges[-1][1], pending
            if cost(before | more) + cost(pairs) <= cost(before) + cost(pairs | more):
                ranges[-1] = (ranges[-1][0], before | more)
            else:
                start, pairs = first - 1, pairs | more
        ranges.append((start + 1, pairs))
        pending = extra
    ranges[-1] = (ranges[-1][0], ranges[-1][1] | pending)

    def crossing(route):
        return -sum(a // 2 != n // 2 for a, n in route)

    return [(first, sorted(coloured(sorted(pairs)), key=crossing)) for first, pairs in ranges]


def column_routes(size):
    routes, selves = {}, {}
    for k in (0, 1, -2, 2, -1):
        pairs = [(size // 2 + p, 3 * p + k) for p in range(size - size // 2)]
        routes[k] = [(s, n) for s, n in pairs if 0 <= n < size and n != s]
        selves.update({k: s for s, n in pairs if n == s})
    return routes, selves


column_cases = (
    (1, (0, 1, 2, -1), (-1, 1)),
    (65, (0, 1, 2, -1), (2, 0)),
    (128, (0, 1, 2, -1, -2), None),
    (129, (0, 1, -1, -2), (-2, 1)),
    (193, (0, 1, -1, -2), (1, 0)),
)


def per_device(
    parent_fields,
    parent_velocity,
    parent_mixing,
    nest_fields,
    nest_velocity,
    nest_mixing,
    nest_anchor,
):
    fields, levels, rows, columns = shape = parent_fields.shape
    channels = fields * levels
    span, last = rows // 3, columns // LANES - 1
    gx, gy = lax.axis_size("gx"), lax.axis_size("gy")
    height, width = rows + 8, columns + LANES
    pf = parent_fields.reshape(channels, rows, columns)
    nf = nest_fields.reshape(channels, rows, columns)
    nv = nest_velocity.reshape(2 * levels, rows, columns)
    nm = nest_mixing
    def row_blocks(array):
        size = (array.shape[0], 8, columns)
        return [(array, block(size, (0, 0, 0))), (array, block(size, (0, rows // 8 - 1, 0)))]

    def column_blocks(array):
        size = (array.shape[0], rows, LANES)
        return [(array, block(size, (0, 0, 0))), (array, block(size, (0, 0, last)))]

    def shaped(*size):
        return size, block(size, (0,) * len(size))

    def whole_of(arrays):
        return [(array, whole(array)) for array in arrays]

    halo_rows = 4 * channels + 6 * levels
    ranges = row_routes(gx, rows)
    middle = gy // 2 * columns
    firsts = ([first for first, _ in ranges], [middle + first for first, _, _ in column_cases])
    scalar = pl.BlockSpec(memory_space=pltpu.SMEM)
    anchor = (nest_anchor, scalar)
    row_pair, row_other, col_pair, col_other, row_range, column_case = call(
        functools.partial(pack_kernel, firsts),
        1,
        [anchor]
        + [
            (pltpu.with_memory_space_constraint(array, pltpu.HBM), spec)
            for array, spec in row_blocks(pf)
            + column_blocks(pf)
            + row_blocks(nf)
            + row_blocks(nv)
            + row_blocks(nm)
        ],
        [shaped(halo_rows, columns)] * 2
        + [shaped(rows, LANES)] * 2
        + [((1,), scalar, jnp.int32)] * 2,
    )
    col_halos = swapped("gy", col_pair, col_other)
    row_halos = swapped("gx", row_pair, row_other)

    slots = max(len(routes) for _, routes in ranges)
    table = np.zeros((len(ranges), gx, slots), np.int32)
    for at, (_, routes) in enumerate(ranges):
        for slot, route in enumerate(routes):
            for owner, nest in route:
                table[at, owner, slot] = (nest - owner) % 3
    message_rows = -(-((span + 2) * (channels + 1)) // 16) * 16
    columns_of, selves = column_routes(gy)
    cells_rows, relay_height = span * channels, (span + 2) * channels

    def by_shift(route, receiver):
        shifts = sorted({nest - owner for owner, nest in route})
        return [(d, [pair[receiver] for pair in route if pair[1] - pair[0] == d]) for d in shifts]

    parent_next, *slabs = call_once(
        functools.partial(parent_kernel, gx),
        [nest_anchor, row_range, jnp.asarray(table.reshape(-1))],
        [
            parent_fields,
            parent_velocity,
            parent_mixing,
            col_halos[1],
            row_halos[1],
            col_halos[0],
            row_halos[0],
        ],
        [shape] + [(relay_height, columns)] * (slots + 1),
    )

    def relay_rows(routes):
        def branch(nest_anchor, slabs, nf, nv, nm, row_halos):
            received = [lax.ppermute(slab, "gx", route) for slab, route in zip(slabs[1:], routes)]
            to_pair, to_other = call(
                column_pack_kernel,
                1,
                column_blocks(nf) + column_blocks(nv) + column_blocks(nm) + whole_of(row_halos),
                [shaped(height, LANES)] * 2,
            )
            sides = swapped("gy", to_pair, to_other)
            entries = [None] + [by_shift(route, 1) for route in routes]
            messages = call(
                functools.partial(row_select_kernel, entries, rows, channels),
                1,
                [(nest_anchor, scalar)] + whole_of([slabs[0], *received]),
                [shaped(message_rows, LANES)] * 3 + [shaped(message_rows // 2, LANES)],
            )
            return messages, sides

        return branch

    messages, sides = lax.switch(
        row_range[0],
        [relay_rows(routes) for _, routes in ranges],
        nest_anchor,
        slabs,
        nf,
        nv,
        nm,
        row_halos,
    )

    def nest_part(ks, half):
        def branch(nest_anchor, messages, nest_fields, nest_velocity, nest_mixing, halos):
            anchor = (nest_anchor, scalar)
            packed = half[0] if half else None
            received = [
                lax.ppermute(messages[3 if k == packed else k % 3], "gy", columns_of[k]) for k in ks
            ]
            coefs, moved, weights = call_once(
                nest_start_kernel,
                [],
                [nest_fields, nest_velocity, nest_mixing, *halos],
                [
                    (levels, 5, height, width),
                    (levels, fields, height, width),
                    (height, width),
                ],
                scratch=[(fields + 3, height, width)],
            )
            nest_result, coarse, *coarse_half = call_once(
                functools.partial(nest_kernel, ks, half, selves),
                [nest_anchor],
                [
                    spread_matrix(columns),
                    gather_matrix(columns),
                    coefs,
                    moved,
                    weights,
                    *received,
                    *messages[:3],
                ],
                [shape, (cells_rows, LANES)] + ([(cells_rows // 2, LANES)] if half else []),
                scratch=[
                    (message_rows, 2 * LANES),
                    (message_rows, width),
                    (fields, width // LANES, height, LANES),
                    (fields, height, width),
                    (span * fields, columns),
                    (fields, columns // LANES, rows, LANES),
                    shape,
                    pltpu.SemaphoreType.DMA((levels,)),
                ],
                results=1,
            )
            back = [k for k in (-1, 1, -2, 2, 0) if k in ks]
            returned = [
                lax.ppermute(
                    coarse_half[0] if k == packed else coarse,
                    "gy",
                    [pair[::-1] for pair in columns_of[k]],
                )
                for k in back
            ]
            placed = call(
                functools.partial(column_select_kernel, back, half, selves, columns, levels),
                1,
                [anchor] + whole_of([coarse, *returned]),
                [shaped(cells_rows, columns)],
            )[0]
            return nest_result, placed

        return branch

    nest_result, placed = lax.switch(
        column_case[0],
        [nest_part(ks, half) for _, ks, half in column_cases],
        nest_anchor,
        messages,
        nest_fields,
        nest_velocity,
        nest_mixing,
        [*row_halos, *sides],
    )

    def feedback_rows(routes):
        def branch(nest_anchor, parent_next, placed):
            received = [
                lax.ppermute(placed, "gx", [pair[::-1] for pair in route]) for route in routes[::-1]
            ]
            entries = [[(0, None)]] + [by_shift(route, 0) for route in routes[::-1]]
            return call_once(
                functools.partial(merge_kernel, entries),
                [nest_anchor],
                [parent_next, placed, *received],
                [shape],
                scratch=[shape, pltpu.SemaphoreType.DMA((levels,))],
                results=1,
            )[0]

        return branch

    merged = lax.switch(
        row_range[0], [feedback_rows(routes) for _, routes in ranges], nest_anchor, parent_next, placed
    )
    return merged, nest_result


def solution(mesh):
    placed = (
        P(None, None, "gx", "gy"),
        P(None, None, "gx", "gy"),
        P(None, "gx", "gy"),
        P(None, None, "gx", "gy"),
        P(None, None, "gx", "gy"),
        P(None, "gx", "gy"),
        P(),
    )
    return jax.shard_map(
        per_device,
        mesh=mesh,
        in_specs=placed,
        out_specs=(P(None, None, "gx", "gy"), P(None, None, "gx", "gy")),
        check_vma=False,
    )
```

```python
import functools

import jax
import jax.numpy as jnp
import numpy as np
from jax import lax
from jax.experimental import pallas as pl
from jax.experimental.pallas import tpu as pltpu
from jax.sharding import PartitionSpec as P

SUBSTEPS = 3
F32 = jnp.float32
LANES = 128
VMEM_LIMIT = 16 * 1024 * 1024
nudge_floor = 0.1
relax_width = 4.0


def whole(array):
    return pl.BlockSpec(array.shape, lambda level: (0,) * array.ndim)


def block(shape, at):
    return pl.BlockSpec(shape, lambda level: at)


def by_level(shape, dim):
    sizes = tuple(1 if i == dim else n for i, n in enumerate(shape))
    return pl.BlockSpec(sizes, lambda level: tuple(level if i == dim else 0 for i in range(len(shape))))


def call(body, grid, ins, outs, scratch=(), cost=None):
    return pl.pallas_call(
        body,
        grid=(grid,),
        out_shape=[
            pltpu.HBM(out[0], F32) if out[2:] == (pltpu.HBM,) else jax.ShapeDtypeStruct(out[0], *(out[2:] or (F32,)))
            for out in outs
        ],
        in_specs=[spec for _, spec in ins],
        out_specs=[out[1] for out in outs],
        scratch_shapes=[pltpu.VMEM(shape, F32) for shape in scratch],
        cost_estimate=cost,
        compiler_params=pltpu.CompilerParams(vmem_limit_bytes=VMEM_LIMIT),
    )(*[array for array, _ in ins])


def call_once(body, scalars, ins, outs, scratch=(), results=0):
    vmem, hbm = pl.BlockSpec(memory_space=pltpu.VMEM), pl.BlockSpec(memory_space=pl.ANY)
    return pl.pallas_call(
        body,
        out_shape=[
            pltpu.HBM(shape, F32) if at < results else jax.ShapeDtypeStruct(shape, F32)
            for at, shape in enumerate(outs)
        ],
        in_specs=[pl.BlockSpec(memory_space=pltpu.SMEM)] * len(scalars) + [vmem] * len(ins),
        out_specs=[hbm] * results + [vmem] * (len(outs) - results),
        scratch_shapes=[
            pltpu.VMEM(shape, F32) if isinstance(shape, tuple) else shape for shape in scratch
        ],
        compiler_params=pltpu.CompilerParams(vmem_limit_bytes=VMEM_LIMIT),
    )(*scalars, *ins)


def lane_index(rows, lanes=LANES):
    return lax.broadcasted_iota(jnp.int32, (rows, lanes), 1)


def row_index(rows, lanes=LANES):
    return lax.broadcasted_iota(jnp.int32, (rows, lanes), 0)


def among(value, numbers):
    found = False
    for number in numbers:
        found = found | (value == number)
    return found


def swapped(axis, to_pair, to_other):
    count = lax.axis_size(axis)
    pairs = [(at, at ^ 1) for at in range(count)]
    others = [(at, at + 1 if at % 2 else at - 1) for at in range(1, count - 1)]
    return lax.ppermute(to_pair, axis, pairs), lax.ppermute(to_other, axis, others)


def by_side(axis, from_pair, from_other):
    even = lax.rem(lax.axis_index(axis), 2) == 0
    return jnp.where(even, from_other, from_pair), jnp.where(even, from_pair, from_other)


def pack_kernel(firsts, anchor, pf_head, pf_tail, pf_first, pf_last, nf_head, nf_tail, nv_head, nv_tail, nm_head, nm_tail, *outs):
    to_pair, to_other, col_to_pair, col_to_other, *indices = outs
    channels, rows = pf_first.shape[:2]
    for at, (index, limits) in enumerate(zip(indices, firsts)):
        index[0] = sum((anchor[at] >= first).astype(jnp.int32) for first in limits[1:])
    coefs = nv_head.shape[0] + nm_head.shape[0]
    even = lax.rem(lax.axis_index("gx"), 2) == 0

    def lines(out, parent, field, wind, mixing, at_end):
        def put(here, ref, row, count, at):
            line = 8 - count + at if at_end else at
            out[here : here + 1, :] = ref[row, line : line + 1, :]

        for at in range(3):
            for ch in range(channels):
                put(at * channels + ch, field, ch, 3, at)
        for at in range(2):
            for cc in range(coefs):
                here = 3 * channels + at * coefs + cc
                ref, row = (wind, cc) if cc < wind.shape[0] else (mixing, cc - wind.shape[0])
                put(here, ref, row, 2, at)
        for ch in range(channels):
            put(3 * channels + 2 * coefs + ch, parent, ch, 1, 0)

    heads, tails = (pf_head, nf_head, nv_head, nm_head), (pf_tail, nf_tail, nv_tail, nm_tail)

    @pl.when(even)
    def _():
        lines(to_pair, *tails, True)
        lines(to_other, *heads, False)

    @pl.when(jnp.logical_not(even))
    def _():
        lines(to_pair, *heads, False)
        lines(to_other, *tails, True)

    lanes = lane_index(rows)
    last = jnp.zeros((rows, LANES), F32)
    first = jnp.zeros((rows, LANES), F32)
    for ch in range(channels):
        last = jnp.where(lanes == ch, pltpu.roll(pf_last[ch], (ch + 1) % LANES, 1), last)
        first = jnp.where(lanes == ch, pltpu.roll(pf_first[ch], ch, 1), first)
    even = lax.rem(lax.axis_index("gy"), 2) == 0
    col_to_pair[...] = jnp.where(even, last, first)
    col_to_other[...] = jnp.where(even, first, last)


def column_pack_kernel(
    nf_first, nf_last, nv_first, nv_last, nm_first, nm_last, pair, other, to_pair, to_other
):
    channels, rows = nf_first.shape[:2]
    columns = pair.shape[1]
    winds = nv_first.shape[0]
    coefs = winds + nm_first.shape[0]
    height = rows + 8
    lanes, lane = lane_index(rows), lane_index(1)

    def packed(nf, nv, nm, part, moved):
        main = jnp.zeros((rows, LANES), F32)
        lines = {at: jnp.zeros((1, LANES), F32) for at in range(-3, 3)}

        def add(first, size, tile, halo_rows):
            nonlocal main
            shift = (first + (size if moved else 0)) % LANES
            inside = (lanes >= first) & (lanes < first + size)
            main = jnp.where(inside, pltpu.roll(tile, shift, 1), main)
            inside = (lane >= first) & (lane < first + size)
            for at, value in halo_rows:
                lines[at] = jnp.where(inside, pltpu.roll(value, shift, 1), lines[at])

        def halos(base, step, size, at):
            lines_of = []
            for n in range(size):
                here = base + n * step + at
                before, after = by_side("gx", pair[here : here + 1, part], other[here : here + 1, part])
                lines_of += [(n, after), (n - size, before)]
            return lines_of

        for ch in range(channels):
            add(3 * ch, 3, nf[ch], halos(0, channels, 3, ch))
        base = 3 * channels
        for cc in range(coefs):
            tile = nv[cc] if cc < winds else nm[cc - winds]
            add(base + 2 * cc, 2, tile, halos(base, coefs, 2, cc))
        blank = jnp.zeros((2, LANES), F32)
        return jnp.concatenate([main, lines[0], lines[1], lines[2], blank, lines[-3], lines[-2], lines[-1]], axis=0)

    last = packed(nf_last, nv_last, nm_last, slice(columns - LANES, columns), True)
    first = packed(nf_first, nv_first, nm_first, slice(0, LANES), False)
    even = lax.rem(lax.axis_index("gy"), 2) == 0
    to_pair[...] = jnp.where(even, last, first)
    to_other[...] = jnp.where(even, first, last)


def parent_kernel(size_x, anchor, index, table, half_table, pf, pv, pm, col_other, row_other, col_pair, row_pair, parent_next, half_slab, *slabs):
    fields, _, rows, columns = pf.shape
    levels = pm.shape[0]
    channels = fields * levels
    span = rows // 3
    rank = lax.axis_index("gx")
    base = 3 * channels + 2 * 3 * levels
    row_shift = lax.rem((rows - span) * rank + size_x * rows - anchor[0], rows)
    row = row_index(rows, columns)
    column = lane_index(rows, columns)
    place = (index[0] * size_x + rank) * (len(slabs) - 1)
    kinds = [table[place + slot] for slot in range(len(slabs) - 1)]
    of_half = half_table[index[0] * size_x + rank]
    half_kind, half_side = lax.div(of_half, 2), lax.rem(of_half, 2)
    pad = jnp.zeros((rows, columns - LANES), F32)
    left, right = by_side("gy", col_pair[...], col_other[...])

    def rows_by_slab(value):
        thirds = [
            (
                value[span * kind : span * (kind + 1)],
                value[(span * kind - 1) % rows : (span * kind - 1) % rows + 1],
                value[span * (kind + 1) % rows : span * (kind + 1) % rows + 1],
            )
            for kind in range(3)
        ]
        yield thirds[0]
        for kind in [*kinds, half_kind]:
            yield [
                jnp.where(kind == 0, zero, jnp.where(kind == 1, one, two))
                for zero, one, two in zip(*thirds)
            ]

    def level_body(level, carry):
        u, v, k = pv[0, level], pv[1, level], pm[level]
        a_w = jnp.maximum(u, 0.0) + k
        a_e = k - jnp.minimum(u, 0.0)
        a_s = jnp.maximum(v, 0.0) + k
        a_n = k - jnp.minimum(v, 0.0)
        a_c = 1.0 - (a_w + a_e + a_s + a_n)
        for field in range(fields):
            ch = field * levels + level
            q = pf[field, level]
            source = pl.ds(base + ch, 1)
            above, below = by_side("gx", row_pair[source, :], row_other[source, :])
            west = jnp.where(row == 0, above, pltpu.roll(q, 1, 0))
            east = jnp.where(row == rows - 1, below, pltpu.roll(q, rows - 1, 0))
            at_first = pltpu.roll(left, LANES - ch, 1)
            at_last = pltpu.roll(right, LANES - 1 - ch, 1)
            south = jnp.where(
                column == 0, jnp.concatenate([at_first, pad], axis=1), pltpu.roll(q, 1, 1)
            )
            north = jnp.where(
                column == columns - 1,
                jnp.concatenate([pad, at_last], axis=1),
                pltpu.roll(q, columns - 1, 1),
            )
            result = a_c * q + a_w * west + a_e * east + a_s * south + a_n * north
            parent_next[field, level] = result
            moved = pltpu.roll(result, row_shift, 0)
            here = level * fields + field
            *by_slab, (cells, before, after) = rows_by_slab(moved)
            upper = half_side == 0
            size = span // 2
            half_slab[pl.ds(pl.multiple_of(size * here, 8), size), :] = jnp.where(
                upper, cells[:size], cells[size:]
            )
            half_slab[pl.ds(size * channels + here, 1), :] = jnp.where(upper, before, after)
            for slab, (cells, before, after) in zip(slabs, by_slab):
                slab[pl.ds(pl.multiple_of(span * here, 8), span), :] = cells
                slab[pl.ds(span * channels + here, 1), :] = before
                slab[pl.ds((span + 1) * channels + here, 1), :] = after
        return carry

    lax.fori_loop(0, levels, level_body, 0)


def packed_half(value, side):
    rows = value.shape[0] // 2
    first, second = value[:rows], value[rows:]
    left = lane_index(rows) < LANES // 2
    if side == 0:
        return jnp.where(left, first, pltpu.roll(second, LANES // 2, 1))
    return jnp.where(left, pltpu.roll(first, LANES // 2, 1), second)


def unpacked_half(value, side):
    turned = pltpu.roll(value, LANES // 2, 1)
    return jnp.concatenate([value, turned] if side == 0 else [turned, value], axis=0)


def row_select_kernel(entries, halved, rows, channels, anchor, *refs):
    count = len(entries)
    slabs, messages, half = refs[:count], refs[count:-1], refs[-1]
    span = rows // 3
    columns = slabs[0].shape[1]
    rank = lax.axis_index("gx")
    start = anchor[0] + span * rank
    lowest, highest = lax.div(start, rows), lax.div(start + span - 1, rows)
    above, below = lax.div(start - 1, rows), lax.div(start + span, rows)
    split = jnp.where(highest > lowest, rows * highest - start, span)
    cells, total = span * channels, (span + 2) * channels

    offset = anchor[1] - lax.axis_size("gy") // 2 * columns
    shift = lax.rem(2 * columns - offset, columns)

    def rows_of(slab, first, size):
        if slab is not slabs[-1] or not halved:
            return slab[first : first + size, :]
        if first >= cells:
            return slab[cells // 2 : cells // 2 + size, :]
        parts = [slab[at : at + span // 2, :] for at in range(0, cells // 2, span // 2)]
        return jnp.concatenate([part for part in parts for _ in range(2)], axis=0)

    def pick(owner, first, size):
        value = rows_of(slabs[0], first, size)
        for senders, slab in zip(entries[1:], slabs[1:]):
            chosen = False
            for d, ranks in senders:
                chosen = chosen | ((rank - owner == d) & among(rank, ranks))
            value = jnp.where(chosen, rows_of(slab, first, size), value)
        return value

    def turned_tiles(value):
        value = pltpu.roll(value, shift, 1)
        return [value[:, LANES * tile : LANES * (tile + 1)] for tile in range(3)]

    row = row_index(cells, columns) & (span - 1)
    tiles = turned_tiles(jnp.where(row < split, pick(lowest, 0, cells), pick(highest, 0, cells)))
    edges = (turned_tiles(pick(above, cells, channels)), turned_tiles(pick(below, cells + channels, channels)))
    sides = [[edge[tile] for edge in edges] for tile in range(3)]
    lanes, edge_lanes = lane_index(span), lane_index(channels)
    edge_inside = lax.div(edge_lanes, 2) == row_index(channels)

    def beside(parts, tile, lane):
        return jnp.where(lane == LANES - 1, parts[(tile + 2) % 3], parts[(tile + 1) % 3])

    for tile, message in enumerate(messages):
        message[0:cells, :] = tiles[tile]
        rim = jnp.zeros((span, LANES), F32)
        for ch in range(channels):
            here = [value[span * ch : span * (ch + 1)] for value in tiles]
            turned = pltpu.roll(beside(here, tile, lanes), 2 * ch + 1, 1)
            rim = jnp.where((lanes == 2 * ch) | (lanes == 2 * ch + 1), turned, rim)
        message[total : total + span, :] = rim + pltpu.roll(rim, LANES // 2, 1)
        for side in range(2):
            first = cells + side * channels
            message[first : first + channels, :] = sides[tile][side]
            line = beside([value[side] for value in sides], tile, edge_lanes)
            line = pltpu.roll(line, 1, 1, stride=2, stride_axis=0)
            line = jnp.sum(jnp.where(edge_inside, line, 0.0), axis=0, keepdims=True)
            target = total + span + side
            message[target : target + 1, :] = line + pltpu.roll(line, LANES // 2, 1)
        message[total + span + 2 :, :] = jnp.zeros((message.shape[0] - total - span - 2, LANES), F32)
    split_tile = jnp.where(offset < LANES, messages[2][...], messages[1][...])
    right = ((offset <= LANES // 2) | (offset > LANES)) & (offset <= LANES + LANES // 2)
    half[...] = jnp.where(right, packed_half(split_tile, 1), packed_half(split_tile, 0))


def three_parts(x):
    high = x.astype(jnp.bfloat16)
    rest = x - high.astype(F32)
    middle = rest.astype(jnp.bfloat16)
    low = (rest - middle.astype(F32)).astype(jnp.bfloat16)
    return high, middle, low


def exact_dot(x, matrix):
    parts = three_parts(x)
    total = jnp.dot(parts[2], matrix, preferred_element_type=F32)
    total = total + jnp.dot(parts[1], matrix, preferred_element_type=F32)
    return total + jnp.dot(parts[0], matrix, preferred_element_type=F32)


def stencil(q, coefs):
    height, width = q.shape
    return (
        coefs[0] * q
        + coefs[1] * pltpu.roll(q, 1, 0)
        + coefs[2] * pltpu.roll(q, height - 1, 0)
        + coefs[3] * pltpu.roll(q, 1, 1)
        + coefs[4] * pltpu.roll(q, width - 1, 1)
    )


def nest_start_kernel(nf, nv, nm, row_pair, row_other, col_pair, col_other, coefs, moved, weights, state):
    fields, _, rows, columns = nf.shape
    levels = nm.shape[0]
    channels = fields * levels
    height, width = rows + 8, columns + LANES
    rank_x, rank_y = lax.axis_index("gx"), lax.axis_index("gy")
    row = row_index(height, width)
    column = lane_index(height, width)
    local_row = jnp.where(row < rows + 4, row, row - height)
    local_column = jnp.where(column < columns + LANES // 2, column, column - width)
    global_row = rank_x * rows + local_row
    global_column = rank_y * columns + local_column
    row_distance = jnp.minimum(global_row, lax.axis_size("gx") * rows - 1 - global_row)
    column_distance = jnp.minimum(
        global_column, lax.axis_size("gy") * columns - 1 - global_column
    )
    distance = jnp.minimum(row_distance, column_distance)
    weight = nudge_floor + (1.0 - nudge_floor) * jnp.exp(
        jnp.maximum(distance, 0).astype(F32) / -relax_width
    )
    weight = jnp.where(distance < 0, 0.0, weight)
    keep = 1.0 - weight
    edge_lanes = lane_index(height)

    weights[...] = weight / 9.0
    state[...] = jnp.zeros_like(state)

    left, right = by_side("gy", col_pair[...], col_other[...])

    def side_tile(first, size):
        after = pltpu.roll(right, lax.rem(2 * LANES - first, LANES), 1)
        before = pltpu.roll(left, lax.rem(2 * LANES - first - size, LANES), 1)
        inside = jnp.where(edge_lanes < LANES // 2, after, before)
        outside = (edge_lanes >= size) & (edge_lanes < LANES - size)
        return jnp.where(outside, 0.0, inside)

    def fill(slot, value, base, step, at, size, first):
        state[slot, 0:rows, 0:columns] = value
        for n in range(size):
            source = pl.ds(base + n * step + at, 1)
            above, below = by_side("gx", row_pair[source, :], row_other[source, :])
            state[slot, rows + n : rows + n + 1, 0:columns] = below
            target = height - size + n
            state[slot, target : target + 1, 0:columns] = above
        state[slot, :, columns:width] = side_tile(first, size)

    def level_body(level, carry):
        base = 3 * channels
        for slot, value in enumerate((nv[0, level], nv[1, level], nm[level])):
            cc = slot * levels + level
            fill(slot + fields, value, base, 3 * levels, cc, 2, base + 2 * cc)
        for field in range(fields):
            ch = field * levels + level
            fill(field, nf[field, level], 0, channels, ch, 3, 3 * ch)
        u, v, k = (state[slot + fields] for slot in range(3))
        a_w = jnp.maximum(u, 0.0) + k
        a_e = k - jnp.minimum(u, 0.0)
        a_s = jnp.maximum(v, 0.0) + k
        a_n = k - jnp.minimum(v, 0.0)
        a_c = 1.0 - (a_w + a_e + a_s + a_n)
        for slot, value in enumerate((a_c, a_w, a_e, a_s, a_n)):
            coefs[level, slot] = keep * value
        for field in range(fields):
            moved[level, field] = stencil(state[field], [coefs[level, slot] for slot in range(5)])
        return carry

    lax.fori_loop(0, levels, level_body, 0)


def nest_kernel(ks, half, selves, anchor, spread, gather, coefs, moved, weights, *refs):
    count = len(ks) + 3
    received, messages = dict(zip(ks, refs[: len(ks)])), refs[len(ks) : count]
    result, coarse, *coarse_half = refs[count:-8]
    relay, refined, forcing, state, sums, final, held, sems = refs[-8:]
    fields, levels, rows, columns = result.shape
    channels = fields * levels
    span_rows, span_columns = rows // 3, columns // 3
    height, width = rows + 8, columns + LANES
    tiles = width // LANES
    relay_rows = span_rows + 2
    total = relay_rows * channels
    offset = anchor[1] - lax.axis_size("gy") // 2 * columns
    kind = lax.rem(lax.axis_index("gy"), 3)
    edge = columns - offset - span_columns * kind

    arrived, rims = {}, {}
    for k in ks:
        value = received[k][...]
        side = half[1] if half and half[0] == k else 0
        if half and half[0] == k:
            value = unpacked_half(value, side)
        rim = value[total : total + relay_rows]
        if side == 1:
            rim = pltpu.roll(rim, LANES // 2, 1)
        if k in selves:
            itself = lax.axis_index("gy") == selves[k]
            own = messages[k % 3][...]
            value = jnp.where(itself, own, value)
            rim = jnp.where(itself, own[total : total + relay_rows], rim)
        arrived[k], rims[k] = value, rim

    def chosen(values):
        low, high = values.get(2, values[0]), values.get(-1, values[0])
        low = jnp.where(kind == 1, values.get(1, values[0]), low)
        low = jnp.where(kind == 0, values[0], low)
        return low, jnp.where(kind == 1, values.get(-2, values[0]), high)

    lower, upper = chosen(arrived)
    rim_low, rim_high = chosen(rims)
    lanes = lane_index(lower.shape[0])
    relay[:, 0:LANES] = jnp.where(lanes < edge, lower, upper)
    relay[total:, LANES:] = jnp.zeros((relay.shape[0] - total, LANES), F32)
    odd = (lane_index(relay_rows) & 1) == 1
    rim = jnp.where(jnp.where(odd, LANES, -1) < edge, rim_low, rim_high)
    for ch in range(channels):
        sides = pltpu.roll(rim, (LANES - 2 * ch) % LANES, 1)
        relay[span_rows * ch : span_rows * (ch + 1), LANES:] = sides[0:span_rows]
        for side in (span_rows, span_rows + 1):
            here = side * channels + ch
            relay[here : here + 1, LANES:] = sides[side : side + 1]
    refined[...] = exact_dot(relay[...], spread[...])

    relay_row = row_index(span_rows, width)

    def leaving(level):
        return pltpu.make_async_copy(held.at[:, level], result.at[:, level], sems.at[level])

    def level_body(level, carry):
        for field in range(fields):
            ch = level * fields + field
            centre = refined[pl.ds(pl.multiple_of(span_rows * ch, 8), span_rows), :]
            above = refined[pl.ds(span_rows * channels + ch, 1), :]
            below = refined[pl.ds((span_rows + 1) * channels + ch, 1), :]
            before = jnp.where(relay_row == 0, above, pltpu.roll(centre, 1, 0))
            after = jnp.where(
                relay_row == span_rows - 1, below, pltpu.roll(centre, span_rows - 1, 0)
            )
            thirds = (before + 2.0 * centre, 3.0 * centre, 2.0 * centre + after)
            rims = (
                (rows, centre[span_rows - 1 :] + 2.0 * below),
                (rows + 1, 3.0 * below),
                (height - 2, 3.0 * above),
                (height - 1, 2.0 * above + centre[0:1]),
            )
            for tile in range(tiles):
                part = slice(LANES * tile, LANES * (tile + 1))
                for at, value in enumerate(thirds):
                    forcing[field, tile, pl.ds(at, span_rows, stride=3), :] = value[:, part]
                forcing[field, tile, rows + 2 : height - 2, :] = jnp.zeros((4, LANES), F32)
                for at, value in rims:
                    forcing[field, tile, at : at + 1, :] = value[:, part]
        for field in range(fields):
            for tile in range(tiles):
                part = slice(LANES * tile, LANES * (tile + 1))
                pull = weights[:, part] * forcing[field, tile]
                forcing[field, tile] = pull
                state[field, :, part] = moved[level, field, :, part] + pull
        for step in range(SUBSTEPS - 1):
            for field in range(fields):
                pull = jnp.concatenate([forcing[field, tile] for tile in range(tiles)], axis=1)
                value = pull + stencil(state[field], [coefs[level, slot] for slot in range(5)])
                if step < SUBSTEPS - 2:
                    state[field] = value
                else:
                    held[field, level] = value[0:rows, 0:columns]
                    for tile in range(tiles - 1):
                        final[field, tile] = value[0:rows, LANES * tile : LANES * (tile + 1)]
        leaving(level).start()
        for field in range(fields):
            for tile in range(tiles - 1):
                part = slice(LANES * tile, LANES * (tile + 1))
                sums[span_rows * field : span_rows * (field + 1), part] = (
                    final[field, tile, pl.ds(0, span_rows, stride=3), :]
                    + final[field, tile, pl.ds(1, span_rows, stride=3), :]
                    + final[field, tile, pl.ds(2, span_rows, stride=3), :]
                )
        means = exact_dot(sums[...], gather[...]) / 9.0
        size = span_rows * fields
        coarse[pl.ds(pl.multiple_of(size * level, 8), size), :] = means
        if half:
            place = pl.ds(pl.multiple_of(size // 2 * level, 8), size // 2)
            coarse_half[0][place, :] = packed_half(means, half[1])
        return carry

    lax.fori_loop(0, levels, level_body, 0)
    for level in range(levels):
        leaving(level).wait()


def column_select_kernel(ks, half, selves, span, columns, levels, size_x, anchor, index, side_table, coarse, *refs):
    returned, (placed, placed_half) = refs[:-2], refs[-2:]
    upper = side_table[index[0] * size_x + lax.axis_index("gx")] == 0
    offset = anchor[1] - lax.axis_size("gy") // 2 * columns
    size, part = placed.shape[0] // levels, span // 2
    lanes = lane_index(size)
    for level in range(levels):
        rows = slice(size * level, size * (level + 1))
        arrived = {}
        for k, ref in zip(ks, returned):
            if half and half[0] == k:
                value = ref[size // 2 * level : size // 2 * (level + 1), :]
                value = unpacked_half(value, half[1])
            else:
                value = ref[rows, :]
            if k in selves:
                value = jnp.where(lax.axis_index("gy") == selves[k], coarse[rows, :], value)
            arrived[k] = value
        tiles = [arrived[0]]
        for tile in (1, 2):
            own = arrived.get(tile, arrived.get(tile - 3))
            other = arrived.get(tile - 3, own)
            inside = lanes < columns - offset - LANES * tile
            tiles.append(jnp.where(inside, own, other))
        value = pltpu.roll(jnp.concatenate(tiles, axis=1), offset, 1)
        placed[rows, :] = value
        for at in range(0, size, 2 * part):
            here = (size * level + at) // 2
            first, second = value[at : at + part], value[at + part : at + 2 * part]
            placed_half[here : here + part, :] = jnp.where(upper, first, second)


def merge_kernel(entries, halved, anchor, parent_next, *refs):
    slabs, (merged, held, sems) = refs[:-3], refs[-3:]
    fields, levels, rows, columns = parent_next.shape
    span = rows // 3
    rank_x, rank_y = lax.axis_index("gx"), lax.axis_index("gy")
    size_x, size_y = lax.axis_size("gx"), lax.axis_size("gy")
    row = rank_x * rows + row_index(rows, columns) - anchor[0]
    column = rank_y * columns + lane_index(rows, columns) - anchor[1]
    covered = (
        (row >= 0) & (row < size_x * span) & (column >= 0) & (column < size_y * (columns // 3))
    )
    first = anchor[0] - (rows - span) * rank_x
    row_shift = lax.rem(first + size_x * rows, rows)
    slab_row = row_index(span)
    choices = [[], [], []]
    for at, receivers in enumerate(entries):
        for d, ranks in receivers:
            place = first + span * d + slab_row
            if ranks is not None:
                place = jnp.where(among(rank_x, ranks), place, -1)
            choices[d % 3].append((at, (place >= 0) & (place < rows)))

    def leaving(level):
        return pltpu.make_async_copy(held.at[:, level], merged.at[:, level], sems.at[level])

    def level_body(level, carry):
        for field in range(fields):
            here = pl.ds(pl.multiple_of(span * (fields * level + field), 8), span)
            tiles = []
            for tile in range(3):
                kinds = []
                for options in choices:
                    value = jnp.zeros((span, LANES), F32)
                    for at, inside in options:
                        part = slice(LANES * tile, LANES * (tile + 1))
                        if halved and at == len(entries) - 1:
                            size = span // 2
                            start = pl.multiple_of(size * (fields * level + field), 8)
                            cells = slabs[at][pl.ds(start, size), part]
                            cells = jnp.concatenate([cells, cells], axis=0)
                        else:
                            cells = slabs[at][here, part]
                        value = jnp.where(inside, cells, value)
                    kinds.append(value)
                tiles.append(jnp.concatenate(kinds, axis=0))
            fed_back = pltpu.roll(jnp.concatenate(tiles, axis=1), row_shift, 0)
            held[field, level] = jnp.where(covered, fed_back, parent_next[field, level])
        leaving(level).start()
        return carry

    lax.fori_loop(0, levels, level_body, 0)
    for level in range(levels):
        leaving(level).wait()


def spread_matrix(columns):
    span = columns // 3
    matrix = np.zeros((2 * LANES, columns + LANES), np.float32)

    def source(m):
        return LANES if m < 0 else (LANES + 1 if m >= span else m)

    for c in range(-2, columns + 2):
        m, j = divmod(c, 3)
        at = c % (columns + LANES)
        if j == 0:
            matrix[source(m - 1), at] += 1.0
            matrix[source(m), at] += 2.0
        elif j == 1:
            matrix[source(m), at] += 3.0
        else:
            matrix[source(m), at] += 2.0
            matrix[source(m + 1), at] += 1.0
    return jnp.asarray(matrix, jnp.bfloat16)


def gather_matrix(columns):
    matrix = np.zeros((columns, columns // 3), np.float32)
    matrix[np.arange(columns), np.arange(columns) // 3] = 1.0
    return jnp.asarray(matrix, jnp.bfloat16)


def coloured(pairs):
    degree = max(sum(pair[end] == at for pair in pairs) for end in (0, 1) for at, _ in enumerate(pairs + [0, 0]))
    routes = [[] for _ in range(degree)]

    def free(route, end, at):
        return all(pair[end] != at for pair in routes[route])

    for pair in pairs:
        first = next(route for route in range(degree) if free(route, 0, pair[0]))
        second = next(route for route in range(degree) if free(route, 1, pair[1]))
        if not free(first, 1, pair[1]):
            end, at, route, other = 1, pair[1], first, second
            path = []
            while not free(route, end, at):
                step = next(p for p in routes[route] if p[end] == at)
                path.append((step, route, other))
                end, at, route, other = 1 - end, step[1 - end], other, route
            for step, source, _ in path:
                routes[source].remove(step)
            for step, _, target in path:
                routes[target].append(step)
        routes[first].append(pair)
    return [sorted(route) for route in routes]


def row_routes(size, rows):
    span = rows // 3

    def needed(start):
        pairs = {}
        for nest in range(size):
            for at in range(span + 2):
                owner = (start + span * nest + at) // rows
                if owner != nest:
                    low, high = pairs.get((owner, nest), (at, at))
                    pairs[owner, nest] = (min(low, at), max(high, at))
        return pairs

    def union(*many):
        pairs = {}
        for some in many:
            for pair, (low, high) in some.items():
                least, most = pairs.get(pair, (low, high))
                pairs[pair] = (min(low, least), max(high, most))
        return pairs

    def divided(pairs):
        whole, half = [], []
        for (owner, nest), (low, high) in sorted(pairs.items()):
            side = 0 if high <= span // 2 else 1 if low > span // 2 else None
            taken = any(owner == a or nest == n for a, n, _ in half)
            if owner // 2 == nest // 2 or side is None or taken:
                whole.append((owner, nest))
            else:
                half.append((owner, nest, side))
        return whole, half

    def cost(pairs):
        whole, half = divided(pairs)
        weighed = [(a, n, 2) for a, n in whole] + [(a, n, 1) for a, n, _ in half]
        cuts = [
            sum(weight for a, n, weight in weighed if ((a < cut <= n) if up else (n < cut <= a)))
            for cut in range(2, size, 2)
            for up in (False, True)
        ]
        return 2 * max(cuts) + len(coloured(whole)) + bool(half)

    ranges = []
    pending = None
    step, count = span // 2, size * (rows - span) - 2
    for first in range(0, count, step):
        last = min(first + step, count) - 1
        pairs = union(*(needed(start) for start in range(first, last)))
        start, extra = first, needed(last)
        if pending is not None:
            before, more = ranges[-1][1], pending
            if cost(union(before, more)) + cost(pairs) <= cost(before) + cost(union(pairs, more)):
                ranges[-1] = (ranges[-1][0], union(before, more))
            else:
                start, pairs = first - 1, union(pairs, more)
        ranges.append((start + 1, pairs))
        pending = extra
    ranges[-1] = (ranges[-1][0], union(ranges[-1][1], pending))

    def crossing(route):
        return -sum(a // 2 != n // 2 for a, n in route)

    merged = []
    for first, pairs in ranges:
        whole, half = divided(pairs)
        found = sorted(coloured(whole), key=crossing), half
        if not merged or merged[-1][1:] != found:
            merged.append((first, *found))
    return merged


def column_routes(size):
    routes, selves = {}, {}
    for k in (0, 1, -2, 2, -1):
        pairs = [(size // 2 + p, 3 * p + k) for p in range(size - size // 2)]
        routes[k] = [(s, n) for s, n in pairs if 0 <= n < size and n != s]
        selves.update({k: s for s, n in pairs if n == s})
    return routes, selves


column_cases = (
    (1, (0, 1, 2, -1), (-1, 1)),
    (65, (0, 1, 2, -1), (2, 0)),
    (128, (0, 1, 2, -1, -2), None),
    (129, (0, 1, -1, -2), (-2, 1)),
    (193, (0, 1, -1, -2), (1, 0)),
)


def per_device(
    parent_fields,
    parent_velocity,
    parent_mixing,
    nest_fields,
    nest_velocity,
    nest_mixing,
    nest_anchor,
):
    fields, levels, rows, columns = shape = parent_fields.shape
    channels = fields * levels
    span, last = rows // 3, columns // LANES - 1
    gx, gy = lax.axis_size("gx"), lax.axis_size("gy")
    height, width = rows + 8, columns + LANES
    pf = parent_fields.reshape(channels, rows, columns)
    nf = nest_fields.reshape(channels, rows, columns)
    nv = nest_velocity.reshape(2 * levels, rows, columns)
    nm = nest_mixing
    def row_blocks(array):
        size = (array.shape[0], 8, columns)
        return [(array, block(size, (0, 0, 0))), (array, block(size, (0, rows // 8 - 1, 0)))]

    def column_blocks(array):
        size = (array.shape[0], rows, LANES)
        return [(array, block(size, (0, 0, 0))), (array, block(size, (0, 0, last)))]

    def shaped(*size):
        return size, block(size, (0,) * len(size))

    def whole_of(arrays):
        return [(array, whole(array)) for array in arrays]

    halo_rows = 4 * channels + 6 * levels
    ranges = row_routes(gx, rows)
    middle = gy // 2 * columns
    firsts = ([first for first, _, _ in ranges], [middle + first for first, _, _ in column_cases])
    scalar = pl.BlockSpec(memory_space=pltpu.SMEM)
    anchor = (nest_anchor, scalar)
    row_pair, row_other, col_pair, col_other, row_range, column_case = call(
        functools.partial(pack_kernel, firsts),
        1,
        [anchor]
        + [
            (pltpu.with_memory_space_constraint(array, pltpu.HBM), spec)
            for array, spec in row_blocks(pf)
            + column_blocks(pf)
            + row_blocks(nf)
            + row_blocks(nv)
            + row_blocks(nm)
        ],
        [shaped(halo_rows, columns)] * 2
        + [shaped(rows, LANES)] * 2
        + [((1,), scalar, jnp.int32)] * 2,
    )
    col_halos = swapped("gy", col_pair, col_other)
    row_halos = swapped("gx", row_pair, row_other)

    slots = max(len(routes) for _, routes, _ in ranges)
    table = np.zeros((len(ranges), gx, slots), np.int32)
    half_table = np.zeros((len(ranges), gx), np.int32)
    side_table = np.zeros((len(ranges), gx), np.int32)
    for at, (_, routes, half) in enumerate(ranges):
        for slot, route in enumerate(routes):
            for owner, nest in route:
                table[at, owner, slot] = (nest - owner) % 3
        for owner, nest, side in half:
            half_table[at, owner] = (nest - owner) % 3 * 2 + side
            side_table[at, nest] = side
    table, half_table, side_table = (jnp.asarray(t.reshape(-1)) for t in (table, half_table, side_table))
    half_height = -(-(span // 2 + 1) * channels // 8) * 8
    message_rows = -(-((span + 2) * (channels + 1)) // 16) * 16
    columns_of, selves = column_routes(gy)
    cells_rows, relay_height = span * channels, (span + 2) * channels

    def by_shift(route, receiver):
        shifts = sorted({nest - owner for owner, nest in route})
        return [(d, [pair[receiver] for pair in route if pair[1] - pair[0] == d]) for d in shifts]

    parent_next, half_slab, *slabs = call_once(
        functools.partial(parent_kernel, gx),
        [nest_anchor, row_range, table, half_table],
        [
            parent_fields,
            parent_velocity,
            parent_mixing,
            col_halos[1],
            row_halos[1],
            col_halos[0],
            row_halos[0],
        ],
        [shape, (half_height, columns)] + [(relay_height, columns)] * (slots + 1),
    )

    def relay_rows(routes, half):
        halves = [[pair[:2] for pair in half]] if half else []

        def branch(nest_anchor, slabs, half_slab, nf, nv, nm, row_halos):
            received = [lax.ppermute(slab, "gx", route) for slab, route in zip(slabs[1:], routes)]
            received += [lax.ppermute(half_slab, "gx", route) for route in halves]
            to_pair, to_other = call(
                column_pack_kernel,
                1,
                column_blocks(nf) + column_blocks(nv) + column_blocks(nm) + whole_of(row_halos),
                [shaped(height, LANES)] * 2,
            )
            sides = swapped("gy", to_pair, to_other)
            entries = [None] + [by_shift(route, 1) for route in routes + halves]
            messages = call(
                functools.partial(row_select_kernel, entries, bool(half), rows, channels),
                1,
                [(nest_anchor, scalar)] + whole_of([slabs[0], *received]),
                [shaped(message_rows, LANES)] * 3 + [shaped(message_rows // 2, LANES)],
            )
            return messages, sides

        return branch

    messages, sides = lax.switch(
        row_range[0],
        [relay_rows(routes, half) for _, routes, half in ranges],
        nest_anchor,
        slabs,
        half_slab,
        nf,
        nv,
        nm,
        row_halos,
    )

    def nest_part(ks, half):
        def branch(nest_anchor, row_range, messages, nest_fields, nest_velocity, nest_mixing, halos):
            packed = half[0] if half else None
            received = [
                lax.ppermute(messages[3 if k == packed else k % 3], "gy", columns_of[k]) for k in ks
            ]
            coefs, moved, weights = call_once(
                nest_start_kernel,
                [],
                [nest_fields, nest_velocity, nest_mixing, *halos],
                [
                    (levels, 5, height, width),
                    (levels, fields, height, width),
                    (height, width),
                ],
                scratch=[(fields + 3, height, width)],
            )
            nest_result, coarse, *coarse_half = call_once(
                functools.partial(nest_kernel, ks, half, selves),
                [nest_anchor],
                [
                    spread_matrix(columns),
                    gather_matrix(columns),
                    coefs,
                    moved,
                    weights,
                    *received,
                    *messages[:3],
                ],
                [shape, (cells_rows, LANES)] + ([(cells_rows // 2, LANES)] if half else []),
                scratch=[
                    (message_rows, 2 * LANES),
                    (message_rows, width),
                    (fields, width // LANES, height, LANES),
                    (fields, height, width),
                    (span * fields, columns),
                    (fields, columns // LANES, rows, LANES),
                    shape,
                    pltpu.SemaphoreType.DMA((levels,)),
                ],
                results=1,
            )
            back = [k for k in (-1, 1, -2, 2, 0) if k in ks]
            returned = [
                lax.ppermute(
                    coarse_half[0] if k == packed else coarse,
                    "gy",
                    [pair[::-1] for pair in columns_of[k]],
                )
                for k in back
            ]
            placed = call_once(
                functools.partial(column_select_kernel, back, half, selves, span, columns, levels, gx),
                [nest_anchor, row_range, side_table],
                [coarse, *returned],
                [(cells_rows, columns), (cells_rows // 2, columns)],
            )
            return nest_result, placed

        return branch

    nest_result, placed = lax.switch(
        column_case[0],
        [nest_part(ks, half) for _, ks, half in column_cases],
        nest_anchor,
        row_range,
        messages,
        nest_fields,
        nest_velocity,
        nest_mixing,
        [*row_halos, *sides],
    )

    def feedback_rows(routes, half):
        halves = [[pair[:2] for pair in half]] if half else []

        def branch(nest_anchor, parent_next, placed):
            placed, placed_half = placed
            received = [
                lax.ppermute(placed, "gx", [pair[::-1] for pair in route]) for route in routes[::-1]
            ]
            received += [
                lax.ppermute(placed_half, "gx", [pair[::-1] for pair in route]) for route in halves
            ]
            entries = [[(0, None)]] + [by_shift(route, 0) for route in routes[::-1] + halves]
            return call_once(
                functools.partial(merge_kernel, entries, bool(half)),
                [nest_anchor],
                [parent_next, placed, *received],
                [shape],
                scratch=[shape, pltpu.SemaphoreType.DMA((levels,))],
                results=1,
            )[0]

        return branch

    merged = lax.switch(
        row_range[0], [feedback_rows(routes, half) for _, routes, half in ranges], nest_anchor, parent_next, placed
    )
    return merged, nest_result


def solution(mesh):
    placed = (
        P(None, None, "gx", "gy"),
        P(None, None, "gx", "gy"),
        P(None, "gx", "gy"),
        P(None, None, "gx", "gy"),
        P(None, None, "gx", "gy"),
        P(None, "gx", "gy"),
        P(),
    )
    return jax.shard_map(
        per_device,
        mesh=mesh,
        in_specs=placed,
        out_specs=(P(None, None, "gx", "gy"), P(None, None, "gx", "gy")),
        check_vma=False,
    )
```

```python
import functools

import jax
import jax.numpy as jnp
import numpy as np
from jax import lax
from jax.experimental import pallas as pl
from jax.experimental.pallas import tpu as pltpu
from jax.sharding import PartitionSpec as P

SUBSTEPS = 3
F32 = jnp.float32
LANES = 128
VMEM_LIMIT = 16 * 1024 * 1024
nudge_floor = 0.1
relax_width = 4.0


def whole(array):
    return pl.BlockSpec(array.shape, lambda level: (0,) * array.ndim)


def block(shape, at):
    return pl.BlockSpec(shape, lambda level: at)


def by_level(shape, dim):
    sizes = tuple(1 if i == dim else n for i, n in enumerate(shape))
    return pl.BlockSpec(sizes, lambda level: tuple(level if i == dim else 0 for i in range(len(shape))))


def call(body, grid, ins, outs, scratch=(), cost=None):
    return pl.pallas_call(
        body,
        grid=(grid,),
        out_shape=[
            pltpu.HBM(out[0], F32) if out[2:] == (pltpu.HBM,) else jax.ShapeDtypeStruct(out[0], *(out[2:] or (F32,)))
            for out in outs
        ],
        in_specs=[spec for _, spec in ins],
        out_specs=[out[1] for out in outs],
        scratch_shapes=[pltpu.VMEM(shape, F32) for shape in scratch],
        cost_estimate=cost,
        compiler_params=pltpu.CompilerParams(vmem_limit_bytes=VMEM_LIMIT),
    )(*[array for array, _ in ins])


def call_once(body, scalars, ins, outs, scratch=(), results=0):
    vmem, hbm = pl.BlockSpec(memory_space=pltpu.VMEM), pl.BlockSpec(memory_space=pl.ANY)
    return pl.pallas_call(
        body,
        out_shape=[
            pltpu.HBM(shape, F32) if at < results else jax.ShapeDtypeStruct(shape, F32)
            for at, shape in enumerate(outs)
        ],
        in_specs=[pl.BlockSpec(memory_space=pltpu.SMEM)] * len(scalars) + [vmem] * len(ins),
        out_specs=[hbm] * results + [vmem] * (len(outs) - results),
        scratch_shapes=[
            pltpu.VMEM(shape, F32) if isinstance(shape, tuple) else shape for shape in scratch
        ],
        compiler_params=pltpu.CompilerParams(vmem_limit_bytes=VMEM_LIMIT),
    )(*scalars, *ins)


def lane_index(rows, lanes=LANES):
    return lax.broadcasted_iota(jnp.int32, (rows, lanes), 1)


def row_index(rows, lanes=LANES):
    return lax.broadcasted_iota(jnp.int32, (rows, lanes), 0)


def among(value, numbers):
    found = False
    for number in numbers:
        found = found | (value == number)
    return found


def swapped(axis, to_pair, to_other):
    count = lax.axis_size(axis)
    pairs = [(at, at ^ 1) for at in range(count)]
    others = [(at, at + 1 if at % 2 else at - 1) for at in range(1, count - 1)]
    return lax.ppermute(to_pair, axis, pairs), lax.ppermute(to_other, axis, others)


def by_side(axis, from_pair, from_other):
    even = lax.rem(lax.axis_index(axis), 2) == 0
    return jnp.where(even, from_other, from_pair), jnp.where(even, from_pair, from_other)


def pack_kernel(firsts, anchor, pf_head, pf_tail, pf_first, pf_last, nf_head, nf_tail, nv_head, nv_tail, nm_head, nm_tail, *outs):
    to_pair, to_other, col_to_pair, col_to_other, *indices = outs
    channels, rows = pf_first.shape[:2]
    for at, (index, limits) in enumerate(zip(indices, firsts)):
        index[0] = sum((anchor[at] >= first).astype(jnp.int32) for first in limits[1:])
    coefs = nv_head.shape[0] + nm_head.shape[0]
    even = lax.rem(lax.axis_index("gx"), 2) == 0

    def lines(out, parent, field, wind, mixing, at_end):
        def put(here, ref, row, count, at):
            line = 8 - count + at if at_end else at
            out[here : here + 1, :] = ref[row, line : line + 1, :]

        for at in range(3):
            for ch in range(channels):
                put(at * channels + ch, field, ch, 3, at)
        for at in range(2):
            for cc in range(coefs):
                here = 3 * channels + at * coefs + cc
                ref, row = (wind, cc) if cc < wind.shape[0] else (mixing, cc - wind.shape[0])
                put(here, ref, row, 2, at)
        for ch in range(channels):
            put(3 * channels + 2 * coefs + ch, parent, ch, 1, 0)

    heads, tails = (pf_head, nf_head, nv_head, nm_head), (pf_tail, nf_tail, nv_tail, nm_tail)

    @pl.when(even)
    def _():
        lines(to_pair, *tails, True)
        lines(to_other, *heads, False)

    @pl.when(jnp.logical_not(even))
    def _():
        lines(to_pair, *heads, False)
        lines(to_other, *tails, True)

    lanes = lane_index(rows)
    last = jnp.zeros((rows, LANES), F32)
    first = jnp.zeros((rows, LANES), F32)
    for ch in range(channels):
        last = jnp.where(lanes == ch, pltpu.roll(pf_last[ch], (ch + 1) % LANES, 1), last)
        first = jnp.where(lanes == ch, pltpu.roll(pf_first[ch], ch, 1), first)
    even = lax.rem(lax.axis_index("gy"), 2) == 0
    col_to_pair[...] = jnp.where(even, last, first)
    col_to_other[...] = jnp.where(even, first, last)


def column_pack_kernel(
    nf_first, nf_last, nv_first, nv_last, nm_first, nm_last, pair, other, to_pair, to_other
):
    channels, rows = nf_first.shape[:2]
    columns = pair.shape[1]
    winds = nv_first.shape[0]
    coefs = winds + nm_first.shape[0]
    height = rows + 8
    lanes, lane = lane_index(rows), lane_index(1)

    def packed(nf, nv, nm, part, moved):
        main = jnp.zeros((rows, LANES), F32)
        lines = {at: jnp.zeros((1, LANES), F32) for at in range(-3, 3)}

        def add(first, size, tile, halo_rows):
            nonlocal main
            shift = (first + (size if moved else 0)) % LANES
            inside = (lanes >= first) & (lanes < first + size)
            main = jnp.where(inside, pltpu.roll(tile, shift, 1), main)
            inside = (lane >= first) & (lane < first + size)
            for at, value in halo_rows:
                lines[at] = jnp.where(inside, pltpu.roll(value, shift, 1), lines[at])

        def halos(base, step, size, at):
            lines_of = []
            for n in range(size):
                here = base + n * step + at
                before, after = by_side("gx", pair[here : here + 1, part], other[here : here + 1, part])
                lines_of += [(n, after), (n - size, before)]
            return lines_of

        for ch in range(channels):
            add(3 * ch, 3, nf[ch], halos(0, channels, 3, ch))
        base = 3 * channels
        for cc in range(coefs):
            tile = nv[cc] if cc < winds else nm[cc - winds]
            add(base + 2 * cc, 2, tile, halos(base, coefs, 2, cc))
        blank = jnp.zeros((2, LANES), F32)
        return jnp.concatenate([main, lines[0], lines[1], lines[2], blank, lines[-3], lines[-2], lines[-1]], axis=0)

    last = packed(nf_last, nv_last, nm_last, slice(columns - LANES, columns), True)
    first = packed(nf_first, nv_first, nm_first, slice(0, LANES), False)
    even = lax.rem(lax.axis_index("gy"), 2) == 0
    to_pair[...] = jnp.where(even, last, first)
    to_other[...] = jnp.where(even, first, last)


def parent_kernel(size_x, anchor, index, table, pf, pv, pm, col_other, row_other, col_pair, row_pair, parent_next, *slabs):
    fields, _, rows, columns = pf.shape
    levels = pm.shape[0]
    channels = fields * levels
    span = rows // 3
    rank = lax.axis_index("gx")
    base = 3 * channels + 2 * 3 * levels
    row_shift = lax.rem((rows - span) * rank + size_x * rows - anchor[0], rows)
    row = row_index(rows, columns)
    column = lane_index(rows, columns)
    place = (index[0] * size_x + rank) * (len(slabs) - 1)
    kinds = [table[place + slot] for slot in range(len(slabs) - 1)]
    pad = jnp.zeros((rows, columns - LANES), F32)
    left, right = by_side("gy", col_pair[...], col_other[...])

    def rows_by_slab(value):
        thirds = [
            (
                value[span * kind : span * (kind + 1)],
                value[(span * kind - 1) % rows : (span * kind - 1) % rows + 1],
                value[span * (kind + 1) % rows : span * (kind + 1) % rows + 1],
            )
            for kind in range(3)
        ]
        yield thirds[0]
        for kind in kinds:
            yield [
                jnp.where(kind == 0, zero, jnp.where(kind == 1, one, two))
                for zero, one, two in zip(*thirds)
            ]

    def level_body(level, carry):
        u, v, k = pv[0, level], pv[1, level], pm[level]
        a_w = jnp.maximum(u, 0.0) + k
        a_e = k - jnp.minimum(u, 0.0)
        a_s = jnp.maximum(v, 0.0) + k
        a_n = k - jnp.minimum(v, 0.0)
        a_c = 1.0 - (a_w + a_e + a_s + a_n)
        for field in range(fields):
            ch = field * levels + level
            q = pf[field, level]
            source = pl.ds(base + ch, 1)
            above, below = by_side("gx", row_pair[source, :], row_other[source, :])
            west = jnp.where(row == 0, above, pltpu.roll(q, 1, 0))
            east = jnp.where(row == rows - 1, below, pltpu.roll(q, rows - 1, 0))
            at_first = pltpu.roll(left, LANES - ch, 1)
            at_last = pltpu.roll(right, LANES - 1 - ch, 1)
            south = jnp.where(
                column == 0, jnp.concatenate([at_first, pad], axis=1), pltpu.roll(q, 1, 1)
            )
            north = jnp.where(
                column == columns - 1,
                jnp.concatenate([pad, at_last], axis=1),
                pltpu.roll(q, columns - 1, 1),
            )
            result = a_c * q + a_w * west + a_e * east + a_s * south + a_n * north
            parent_next[field, level] = result
            moved = pltpu.roll(result, row_shift, 0)
            here = level * fields + field
            for slab, (cells, before, after) in zip(slabs, rows_by_slab(moved)):
                slab[pl.ds(pl.multiple_of(span * here, 8), span), :] = cells
                slab[pl.ds(span * channels + here, 1), :] = before
                slab[pl.ds((span + 1) * channels + here, 1), :] = after
        return carry

    lax.fori_loop(0, levels, level_body, 0)


def packed_half(value, side):
    rows = value.shape[0] // 2
    first, second = value[:rows], value[rows:]
    left = lane_index(rows) < LANES // 2
    if side == 0:
        return jnp.where(left, first, pltpu.roll(second, LANES // 2, 1))
    return jnp.where(left, pltpu.roll(first, LANES // 2, 1), second)


def unpacked_half(value, side):
    turned = pltpu.roll(value, LANES // 2, 1)
    return jnp.concatenate([value, turned] if side == 0 else [turned, value], axis=0)


def row_select_kernel(entries, rows, channels, anchor, *refs):
    count = len(entries)
    slabs, messages, half = refs[:count], refs[count:-1], refs[-1]
    span = rows // 3
    columns = slabs[0].shape[1]
    rank = lax.axis_index("gx")
    start = anchor[0] + span * rank
    lowest, highest = lax.div(start, rows), lax.div(start + span - 1, rows)
    above, below = lax.div(start - 1, rows), lax.div(start + span, rows)
    split = jnp.where(highest > lowest, rows * highest - start, span)
    cells, total = span * channels, (span + 2) * channels

    offset = anchor[1] - lax.axis_size("gy") // 2 * columns
    shift = lax.rem(2 * columns - offset, columns)

    def pick(owner, first, size):
        value = slabs[0][first : first + size, :]
        for senders, slab in zip(entries[1:], slabs[1:]):
            chosen = False
            for d, ranks in senders:
                chosen = chosen | ((rank - owner == d) & among(rank, ranks))
            value = jnp.where(chosen, slab[first : first + size, :], value)
        return value

    def turned_tiles(value):
        value = pltpu.roll(value, shift, 1)
        return [value[:, LANES * tile : LANES * (tile + 1)] for tile in range(3)]

    row = row_index(cells, columns) & (span - 1)
    tiles = turned_tiles(jnp.where(row < split, pick(lowest, 0, cells), pick(highest, 0, cells)))
    edges = (turned_tiles(pick(above, cells, channels)), turned_tiles(pick(below, cells + channels, channels)))
    sides = [[edge[tile] for edge in edges] for tile in range(3)]
    lanes, edge_lanes = lane_index(span), lane_index(channels)
    edge_inside = lax.div(edge_lanes, 2) == row_index(channels)

    def beside(parts, tile, lane):
        return jnp.where(lane == LANES - 1, parts[(tile + 2) % 3], parts[(tile + 1) % 3])

    for tile, message in enumerate(messages):
        message[0:cells, :] = tiles[tile]
        rim = jnp.zeros((span, LANES), F32)
        for ch in range(channels):
            here = [value[span * ch : span * (ch + 1)] for value in tiles]
            turned = pltpu.roll(beside(here, tile, lanes), 2 * ch + 1, 1)
            rim = jnp.where((lanes == 2 * ch) | (lanes == 2 * ch + 1), turned, rim)
        message[total : total + span, :] = rim + pltpu.roll(rim, LANES // 2, 1)
        for side in range(2):
            first = cells + side * channels
            message[first : first + channels, :] = sides[tile][side]
            line = beside([value[side] for value in sides], tile, edge_lanes)
            line = pltpu.roll(line, 1, 1, stride=2, stride_axis=0)
            line = jnp.sum(jnp.where(edge_inside, line, 0.0), axis=0, keepdims=True)
            target = total + span + side
            message[target : target + 1, :] = line + pltpu.roll(line, LANES // 2, 1)
        message[total + span + 2 :, :] = jnp.zeros((message.shape[0] - total - span - 2, LANES), F32)
    split_tile = jnp.where(offset < LANES, messages[2][...], messages[1][...])
    right = ((offset <= LANES // 2) | (offset > LANES)) & (offset <= LANES + LANES // 2)
    half[...] = jnp.where(right, packed_half(split_tile, 1), packed_half(split_tile, 0))


def three_parts(x):
    high = x.astype(jnp.bfloat16)
    rest = x - high.astype(F32)
    middle = rest.astype(jnp.bfloat16)
    low = (rest - middle.astype(F32)).astype(jnp.bfloat16)
    return high, middle, low


def exact_dot(x, matrix):
    parts = three_parts(x)
    total = jnp.dot(parts[2], matrix, preferred_element_type=F32)
    total = total + jnp.dot(parts[1], matrix, preferred_element_type=F32)
    return total + jnp.dot(parts[0], matrix, preferred_element_type=F32)


def stencil(q, coefs):
    height, width = q.shape
    return (
        coefs[0] * q
        + coefs[1] * pltpu.roll(q, 1, 0)
        + coefs[2] * pltpu.roll(q, height - 1, 0)
        + coefs[3] * pltpu.roll(q, 1, 1)
        + coefs[4] * pltpu.roll(q, width - 1, 1)
    )


def nest_start_kernel(nf, nv, nm, row_pair, row_other, col_pair, col_other, coefs, moved, weights, state):
    fields, _, rows, columns = nf.shape
    levels = nm.shape[0]
    channels = fields * levels
    height, width = rows + 8, columns + LANES
    rank_x, rank_y = lax.axis_index("gx"), lax.axis_index("gy")
    row = row_index(height, width)
    column = lane_index(height, width)
    local_row = jnp.where(row < rows + 4, row, row - height)
    local_column = jnp.where(column < columns + LANES // 2, column, column - width)
    global_row = rank_x * rows + local_row
    global_column = rank_y * columns + local_column
    row_distance = jnp.minimum(global_row, lax.axis_size("gx") * rows - 1 - global_row)
    column_distance = jnp.minimum(
        global_column, lax.axis_size("gy") * columns - 1 - global_column
    )
    distance = jnp.minimum(row_distance, column_distance)
    weight = nudge_floor + (1.0 - nudge_floor) * jnp.exp(
        jnp.maximum(distance, 0).astype(F32) / -relax_width
    )
    weight = jnp.where(distance < 0, 0.0, weight)
    keep = 1.0 - weight
    edge_lanes = lane_index(height)

    weights[...] = weight / 9.0
    state[...] = jnp.zeros_like(state)

    left, right = by_side("gy", col_pair[...], col_other[...])

    def side_tile(first, size):
        after = pltpu.roll(right, lax.rem(2 * LANES - first, LANES), 1)
        before = pltpu.roll(left, lax.rem(2 * LANES - first - size, LANES), 1)
        inside = jnp.where(edge_lanes < LANES // 2, after, before)
        outside = (edge_lanes >= size) & (edge_lanes < LANES - size)
        return jnp.where(outside, 0.0, inside)

    def fill(slot, value, base, step, at, size, first):
        state[slot, 0:rows, 0:columns] = value
        for n in range(size):
            source = pl.ds(base + n * step + at, 1)
            above, below = by_side("gx", row_pair[source, :], row_other[source, :])
            state[slot, rows + n : rows + n + 1, 0:columns] = below
            target = height - size + n
            state[slot, target : target + 1, 0:columns] = above
        state[slot, :, columns:width] = side_tile(first, size)

    def level_body(level, carry):
        base = 3 * channels
        for slot, value in enumerate((nv[0, level], nv[1, level], nm[level])):
            cc = slot * levels + level
            fill(slot + fields, value, base, 3 * levels, cc, 2, base + 2 * cc)
        for field in range(fields):
            ch = field * levels + level
            fill(field, nf[field, level], 0, channels, ch, 3, 3 * ch)
        u, v, k = (state[slot + fields] for slot in range(3))
        a_w = jnp.maximum(u, 0.0) + k
        a_e = k - jnp.minimum(u, 0.0)
        a_s = jnp.maximum(v, 0.0) + k
        a_n = k - jnp.minimum(v, 0.0)
        a_c = 1.0 - (a_w + a_e + a_s + a_n)
        for slot, value in enumerate((a_c, a_w, a_e, a_s, a_n)):
            coefs[level, slot] = keep * value
        for field in range(fields):
            moved[level, field] = stencil(state[field], [coefs[level, slot] for slot in range(5)])
        return carry

    lax.fori_loop(0, levels, level_body, 0)


def nest_kernel(ks, half, selves, anchor, spread, gather, coefs, moved, weights, *refs):
    count = len(ks) + 3
    received, messages = dict(zip(ks, refs[: len(ks)])), refs[len(ks) : count]
    result, coarse, *coarse_half = refs[count:-8]
    relay, refined, forcing, state, sums, final, held, sems = refs[-8:]
    fields, levels, rows, columns = result.shape
    channels = fields * levels
    span_rows, span_columns = rows // 3, columns // 3
    height, width = rows + 8, columns + LANES
    tiles = width // LANES
    relay_rows = span_rows + 2
    total = relay_rows * channels
    offset = anchor[1] - lax.axis_size("gy") // 2 * columns
    kind = lax.rem(lax.axis_index("gy"), 3)
    edge = columns - offset - span_columns * kind

    arrived, rims = {}, {}
    for k in ks:
        value = received[k][...]
        side = half[1] if half and half[0] == k else 0
        if half and half[0] == k:
            value = unpacked_half(value, side)
        rim = value[total : total + relay_rows]
        if side == 1:
            rim = pltpu.roll(rim, LANES // 2, 1)
        if k in selves:
            itself = lax.axis_index("gy") == selves[k]
            own = messages[k % 3][...]
            value = jnp.where(itself, own, value)
            rim = jnp.where(itself, own[total : total + relay_rows], rim)
        arrived[k], rims[k] = value, rim

    def chosen(values):
        low, high = values.get(2, values[0]), values.get(-1, values[0])
        low = jnp.where(kind == 1, values.get(1, values[0]), low)
        low = jnp.where(kind == 0, values[0], low)
        return low, jnp.where(kind == 1, values.get(-2, values[0]), high)

    lower, upper = chosen(arrived)
    rim_low, rim_high = chosen(rims)
    lanes = lane_index(lower.shape[0])
    relay[:, 0:LANES] = jnp.where(lanes < edge, lower, upper)
    relay[total:, LANES:] = jnp.zeros((relay.shape[0] - total, LANES), F32)
    odd = (lane_index(relay_rows) & 1) == 1
    rim = jnp.where(jnp.where(odd, LANES, -1) < edge, rim_low, rim_high)
    for ch in range(channels):
        sides = pltpu.roll(rim, (LANES - 2 * ch) % LANES, 1)
        relay[span_rows * ch : span_rows * (ch + 1), LANES:] = sides[0:span_rows]
        for side in (span_rows, span_rows + 1):
            here = side * channels + ch
            relay[here : here + 1, LANES:] = sides[side : side + 1]
    refined[...] = exact_dot(relay[...], spread[...])

    relay_row = row_index(span_rows, width)

    def leaving(level):
        return pltpu.make_async_copy(held.at[:, level], result.at[:, level], sems.at[level])

    def level_body(level, carry):
        for field in range(fields):
            ch = level * fields + field
            centre = refined[pl.ds(pl.multiple_of(span_rows * ch, 8), span_rows), :]
            above = refined[pl.ds(span_rows * channels + ch, 1), :]
            below = refined[pl.ds((span_rows + 1) * channels + ch, 1), :]
            before = jnp.where(relay_row == 0, above, pltpu.roll(centre, 1, 0))
            after = jnp.where(
                relay_row == span_rows - 1, below, pltpu.roll(centre, span_rows - 1, 0)
            )
            thirds = (before + 2.0 * centre, 3.0 * centre, 2.0 * centre + after)
            rims = (
                (rows, centre[span_rows - 1 :] + 2.0 * below),
                (rows + 1, 3.0 * below),
                (height - 2, 3.0 * above),
                (height - 1, 2.0 * above + centre[0:1]),
            )
            for tile in range(tiles):
                part = slice(LANES * tile, LANES * (tile + 1))
                for at, value in enumerate(thirds):
                    forcing[field, tile, pl.ds(at, span_rows, stride=3), :] = value[:, part]
                forcing[field, tile, rows + 2 : height - 2, :] = jnp.zeros((4, LANES), F32)
                for at, value in rims:
                    forcing[field, tile, at : at + 1, :] = value[:, part]
        def put(field, tile, value):
            state[field, tile, 8 : height + 8, :] = value
            state[field, tile, 7:8, :] = value[height - 1 :]
            state[field, tile, height + 8 : height + 9, :] = value[0:1]

        for field in range(fields):
            for tile in range(tiles):
                part = slice(LANES * tile, LANES * (tile + 1))
                pull = weights[:, part] * forcing[field, tile]
                forcing[field, tile] = pull
                put(field, tile, moved[level, field, :, part] + pull)
        for step in range(SUBSTEPS - 1):
            size = height if step < SUBSTEPS - 2 else rows
            lane = lane_index(size)
            for field in range(fields):
                cells = [state[field, tile, 8 : size + 8, :] for tile in range(tiles)]
                up = [pltpu.roll(value, 1, 1) for value in cells]
                down = [pltpu.roll(value, LANES - 1, 1) for value in cells]
                values = []
                for tile in range(tiles if step < SUBSTEPS - 2 else tiles - 1):
                    part = slice(LANES * tile, LANES * (tile + 1))
                    south = jnp.where(lane == 0, up[(tile - 1) % tiles], up[tile])
                    north = jnp.where(lane == LANES - 1, down[(tile + 1) % tiles], down[tile])
                    values.append(
                        forcing[field, tile, 0:size, :]
                        + coefs[level, 0, 0:size, part] * cells[tile]
                        + coefs[level, 1, 0:size, part] * state[field, tile, 7 : size + 7, :]
                        + coefs[level, 2, 0:size, part] * state[field, tile, 9 : size + 9, :]
                        + coefs[level, 3, 0:size, part] * south
                        + coefs[level, 4, 0:size, part] * north
                    )
                for tile, value in enumerate(values):
                    if step < SUBSTEPS - 2:
                        put(field, tile, value)
                    else:
                        held[field, level, :, LANES * tile : LANES * (tile + 1)] = value
                        final[field, tile] = value
        leaving(level).start()
        for field in range(fields):
            for tile in range(tiles - 1):
                part = slice(LANES * tile, LANES * (tile + 1))
                sums[span_rows * field : span_rows * (field + 1), part] = (
                    final[field, tile, pl.ds(0, span_rows, stride=3), :]
                    + final[field, tile, pl.ds(1, span_rows, stride=3), :]
                    + final[field, tile, pl.ds(2, span_rows, stride=3), :]
                )
        means = exact_dot(sums[...], gather[...]) / 9.0
        size = span_rows * fields
        coarse[pl.ds(pl.multiple_of(size * level, 8), size), :] = means
        if half:
            place = pl.ds(pl.multiple_of(size // 2 * level, 8), size // 2)
            coarse_half[0][place, :] = packed_half(means, half[1])
        return carry

    lax.fori_loop(0, levels, level_body, 0)
    for level in range(levels):
        leaving(level).wait()


def column_select_kernel(ks, half, selves, columns, levels, anchor, coarse, *refs):
    returned, placed = refs[:-1], refs[-1]
    offset = anchor[1] - lax.axis_size("gy") // 2 * columns
    size = placed.shape[0] // levels
    lanes = lane_index(size)
    for level in range(levels):
        rows = slice(size * level, size * (level + 1))
        arrived = {}
        for k, ref in zip(ks, returned):
            if half and half[0] == k:
                value = ref[size // 2 * level : size // 2 * (level + 1), :]
                value = unpacked_half(value, half[1])
            else:
                value = ref[rows, :]
            if k in selves:
                value = jnp.where(lax.axis_index("gy") == selves[k], coarse[rows, :], value)
            arrived[k] = value
        tiles = [arrived[0]]
        for tile in (1, 2):
            own = arrived.get(tile, arrived.get(tile - 3))
            other = arrived.get(tile - 3, own)
            inside = lanes < columns - offset - LANES * tile
            tiles.append(jnp.where(inside, own, other))
        placed[rows, :] = pltpu.roll(jnp.concatenate(tiles, axis=1), offset, 1)


def merge_kernel(entries, anchor, parent_next, *refs):
    slabs, (merged, held, sems) = refs[:-3], refs[-3:]
    fields, levels, rows, columns = parent_next.shape
    span = rows // 3
    rank_x, rank_y = lax.axis_index("gx"), lax.axis_index("gy")
    size_x, size_y = lax.axis_size("gx"), lax.axis_size("gy")
    row = rank_x * rows + row_index(rows, columns) - anchor[0]
    column = rank_y * columns + lane_index(rows, columns) - anchor[1]
    covered = (
        (row >= 0) & (row < size_x * span) & (column >= 0) & (column < size_y * (columns // 3))
    )
    first = anchor[0] - (rows - span) * rank_x
    row_shift = lax.rem(first + size_x * rows, rows)
    slab_row = row_index(span)
    choices = [[], [], []]
    for at, receivers in enumerate(entries):
        for d, ranks in receivers:
            place = first + span * d + slab_row
            if ranks is not None:
                place = jnp.where(among(rank_x, ranks), place, -1)
            choices[d % 3].append((at, (place >= 0) & (place < rows)))
    def leaving(level):
        return pltpu.make_async_copy(held.at[:, level], merged.at[:, level], sems.at[level])

    def level_body(level, carry):
        for field in range(fields):
            here = pl.ds(pl.multiple_of(span * (fields * level + field), 8), span)
            tiles = []
            for tile in range(3):
                kinds = []
                for options in choices:
                    value = jnp.zeros((span, LANES), F32)
                    for at, inside in options:
                        part = slice(LANES * tile, LANES * (tile + 1))
                        cells = slabs[at][here, part]
                        value = jnp.where(inside, cells, value)
                    kinds.append(value)
                tiles.append(jnp.concatenate(kinds, axis=0))
            fed_back = pltpu.roll(jnp.concatenate(tiles, axis=1), row_shift, 0)
            held[field, level] = jnp.where(covered, fed_back, parent_next[field, level])
        leaving(level).start()
        return carry

    lax.fori_loop(0, levels, level_body, 0)
    for level in range(levels):
        leaving(level).wait()


def spread_matrix(columns):
    span = columns // 3
    matrix = np.zeros((2 * LANES, columns + LANES), np.float32)

    def source(m):
        return LANES if m < 0 else (LANES + 1 if m >= span else m)

    for c in range(-2, columns + 2):
        m, j = divmod(c, 3)
        at = c % (columns + LANES)
        if j == 0:
            matrix[source(m - 1), at] += 1.0
            matrix[source(m), at] += 2.0
        elif j == 1:
            matrix[source(m), at] += 3.0
        else:
            matrix[source(m), at] += 2.0
            matrix[source(m + 1), at] += 1.0
    return jnp.asarray(matrix, jnp.bfloat16)


def gather_matrix(columns):
    matrix = np.zeros((columns, columns // 3), np.float32)
    matrix[np.arange(columns), np.arange(columns) // 3] = 1.0
    return jnp.asarray(matrix, jnp.bfloat16)


def coloured(pairs):
    degree = max(sum(pair[end] == at for pair in pairs) for end in (0, 1) for at, _ in enumerate(pairs + [0, 0]))
    routes = [[] for _ in range(degree)]

    def free(route, end, at):
        return all(pair[end] != at for pair in routes[route])

    for pair in pairs:
        first = next(route for route in range(degree) if free(route, 0, pair[0]))
        second = next(route for route in range(degree) if free(route, 1, pair[1]))
        if not free(first, 1, pair[1]):
            end, at, route, other = 1, pair[1], first, second
            path = []
            while not free(route, end, at):
                step = next(p for p in routes[route] if p[end] == at)
                path.append((step, route, other))
                end, at, route, other = 1 - end, step[1 - end], other, route
            for step, source, _ in path:
                routes[source].remove(step)
            for step, _, target in path:
                routes[target].append(step)
        routes[first].append(pair)
    return [sorted(route) for route in routes]


def row_routes(size, rows):
    span = rows // 3

    def needed(start):
        pairs = set()
        for nest in range(size):
            for at in (start + span * nest, start + span * nest + span + 1):
                pairs.add((at // rows, nest))
        return {(owner, nest) for owner, nest in pairs if owner != nest}

    def cost(pairs):
        cuts = [
            sum((a < cut <= n) if up else (n < cut <= a) for a, n in pairs)
            for cut in range(2, size, 2)
            for up in (False, True)
        ]
        return 4 * max(cuts) + len(coloured(sorted(pairs)))

    ranges = []
    pending = None
    for first in range(0, size * (rows - span) - 2, span):
        last = min(first + span, size * (rows - span) - 2) - 1
        pairs = set().union(*(needed(start) for start in range(first, last)))
        start, extra = first, needed(last)
        if pending is not None:
            before, more = ranges[-1][1], pending
            if cost(before | more) + cost(pairs) <= cost(before) + cost(pairs | more):
                ranges[-1] = (ranges[-1][0], before | more)
            else:
                start, pairs = first - 1, pairs | more
        ranges.append((start + 1, pairs))
        pending = extra
    ranges[-1] = (ranges[-1][0], ranges[-1][1] | pending)

    def crossing(route):
        return -sum(a // 2 != n // 2 for a, n in route)

    return [(first, sorted(coloured(sorted(pairs)), key=crossing)) for first, pairs in ranges]


def column_routes(size):
    routes, selves = {}, {}
    for k in (0, 1, -2, 2, -1):
        pairs = [(size // 2 + p, 3 * p + k) for p in range(size - size // 2)]
        routes[k] = [(s, n) for s, n in pairs if 0 <= n < size and n != s]
        selves.update({k: s for s, n in pairs if n == s})
    return routes, selves


column_cases = (
    (1, (0, 1, 2, -1), (-1, 1)),
    (65, (0, 1, 2, -1), (2, 0)),
    (128, (0, 1, 2, -1, -2), None),
    (129, (0, 1, -1, -2), (-2, 1)),
    (193, (0, 1, -1, -2), (1, 0)),
)


def per_device(
    parent_fields,
    parent_velocity,
    parent_mixing,
    nest_fields,
    nest_velocity,
    nest_mixing,
    nest_anchor,
):
    fields, levels, rows, columns = shape = parent_fields.shape
    channels = fields * levels
    span, last = rows // 3, columns // LANES - 1
    gx, gy = lax.axis_size("gx"), lax.axis_size("gy")
    height, width = rows + 8, columns + LANES
    pf = parent_fields.reshape(channels, rows, columns)
    nf = nest_fields.reshape(channels, rows, columns)
    nv = nest_velocity.reshape(2 * levels, rows, columns)
    nm = nest_mixing
    def row_blocks(array):
        size = (array.shape[0], 8, columns)
        return [(array, block(size, (0, 0, 0))), (array, block(size, (0, rows // 8 - 1, 0)))]

    def column_blocks(array):
        size = (array.shape[0], rows, LANES)
        return [(array, block(size, (0, 0, 0))), (array, block(size, (0, 0, last)))]

    def shaped(*size):
        return size, block(size, (0,) * len(size))

    def whole_of(arrays):
        return [(array, whole(array)) for array in arrays]

    halo_rows = 4 * channels + 6 * levels
    ranges = row_routes(gx, rows)
    middle = gy // 2 * columns
    firsts = ([first for first, _ in ranges], [middle + first for first, _, _ in column_cases])
    scalar = pl.BlockSpec(memory_space=pltpu.SMEM)
    anchor = (nest_anchor, scalar)
    row_pair, row_other, col_pair, col_other, row_range, column_case = call(
        functools.partial(pack_kernel, firsts),
        1,
        [anchor]
        + [
            (pltpu.with_memory_space_constraint(array, pltpu.HBM), spec)
            for array, spec in row_blocks(pf)
            + column_blocks(pf)
            + row_blocks(nf)
            + row_blocks(nv)
            + row_blocks(nm)
        ],
        [shaped(halo_rows, columns)] * 2
        + [shaped(rows, LANES)] * 2
        + [((1,), scalar, jnp.int32)] * 2,
    )
    col_halos = swapped("gy", col_pair, col_other)
    row_halos = swapped("gx", row_pair, row_other)

    slots = max(len(routes) for _, routes in ranges)
    table = np.zeros((len(ranges), gx, slots), np.int32)
    for at, (_, routes) in enumerate(ranges):
        for slot, route in enumerate(routes):
            for owner, nest in route:
                table[at, owner, slot] = (nest - owner) % 3
    message_rows = -(-((span + 2) * (channels + 1)) // 16) * 16
    columns_of, selves = column_routes(gy)
    cells_rows, relay_height = span * channels, (span + 2) * channels

    def by_shift(route, receiver):
        shifts = sorted({nest - owner for owner, nest in route})
        return [(d, [pair[receiver] for pair in route if pair[1] - pair[0] == d]) for d in shifts]

    parent_next, *slabs = call_once(
        functools.partial(parent_kernel, gx),
        [nest_anchor, row_range, jnp.asarray(table.reshape(-1))],
        [
            parent_fields,
            parent_velocity,
            parent_mixing,
            col_halos[1],
            row_halos[1],
            col_halos[0],
            row_halos[0],
        ],
        [shape] + [(relay_height, columns)] * (slots + 1),
    )

    def relay_rows(routes):
        def branch(nest_anchor, slabs, nf, nv, nm, row_halos):
            received = [lax.ppermute(slab, "gx", route) for slab, route in zip(slabs[1:], routes)]
            to_pair, to_other = call(
                column_pack_kernel,
                1,
                column_blocks(nf) + column_blocks(nv) + column_blocks(nm) + whole_of(row_halos),
                [shaped(height, LANES)] * 2,
            )
            sides = swapped("gy", to_pair, to_other)
            entries = [None] + [by_shift(route, 1) for route in routes]
            messages = call(
                functools.partial(row_select_kernel, entries, rows, channels),
                1,
                [(nest_anchor, scalar)] + whole_of([slabs[0], *received]),
                [shaped(message_rows, LANES)] * 3 + [shaped(message_rows // 2, LANES)],
            )
            return messages, sides

        return branch

    messages, sides = lax.switch(
        row_range[0],
        [relay_rows(routes) for _, routes in ranges],
        nest_anchor,
        slabs,
        nf,
        nv,
        nm,
        row_halos,
    )

    def nest_part(ks, half):
        def branch(nest_anchor, messages, nest_fields, nest_velocity, nest_mixing, halos):
            anchor = (nest_anchor, scalar)
            packed = half[0] if half else None
            received = [
                lax.ppermute(messages[3 if k == packed else k % 3], "gy", columns_of[k]) for k in ks
            ]
            coefs, moved, weights = call_once(
                nest_start_kernel,
                [],
                [nest_fields, nest_velocity, nest_mixing, *halos],
                [
                    (levels, 5, height, width),
                    (levels, fields, height, width),
                    (height, width),
                ],
                scratch=[(fields + 3, height, width)],
            )
            nest_result, coarse, *coarse_half = call_once(
                functools.partial(nest_kernel, ks, half, selves),
                [nest_anchor],
                [
                    spread_matrix(columns),
                    gather_matrix(columns),
                    coefs,
                    moved,
                    weights,
                    *received,
                    *messages[:3],
                ],
                [shape, (cells_rows, LANES)] + ([(cells_rows // 2, LANES)] if half else []),
                scratch=[
                    (message_rows, 2 * LANES),
                    (message_rows, width),
                    (fields, width // LANES, height, LANES),
                    (fields, width // LANES, height + 16, LANES),
                    (span * fields, columns),
                    (fields, columns // LANES, rows, LANES),
                    shape,
                    pltpu.SemaphoreType.DMA((levels,)),
                ],
                results=1,
            )
            back = [k for k in (-1, 1, -2, 2, 0) if k in ks]
            returned = [
                lax.ppermute(
                    coarse_half[0] if k == packed else coarse,
                    "gy",
                    [pair[::-1] for pair in columns_of[k]],
                )
                for k in back
            ]
            placed = call(
                functools.partial(column_select_kernel, back, half, selves, columns, levels),
                1,
                [anchor] + whole_of([coarse, *returned]),
                [shaped(cells_rows, columns)],
            )[0]
            return nest_result, placed

        return branch

    nest_result, placed = lax.switch(
        column_case[0],
        [nest_part(ks, half) for _, ks, half in column_cases],
        nest_anchor,
        messages,
        nest_fields,
        nest_velocity,
        nest_mixing,
        [*row_halos, *sides],
    )

    def feedback_rows(routes):
        def branch(nest_anchor, parent_next, placed):
            received = [
                lax.ppermute(placed, "gx", [pair[::-1] for pair in route]) for route in routes[::-1]
            ]
            entries = [[(0, None)]] + [by_shift(route, 0) for route in routes[::-1]]
            return call_once(
                functools.partial(merge_kernel, entries),
                [nest_anchor],
                [parent_next, placed, *received],
                [shape],
                scratch=[shape, pltpu.SemaphoreType.DMA((levels,))],
                results=1,
            )[0]

        return branch

    merged = lax.switch(
        row_range[0], [feedback_rows(routes) for _, routes in ranges], nest_anchor, parent_next, placed
    )
    return merged, nest_result


def solution(mesh):
    placed = (
        P(None, None, "gx", "gy"),
        P(None, None, "gx", "gy"),
        P(None, "gx", "gy"),
        P(None, None, "gx", "gy"),
        P(None, None, "gx", "gy"),
        P(None, "gx", "gy"),
        P(),
    )
    return jax.shard_map(
        per_device,
        mesh=mesh,
        in_specs=placed,
        out_specs=(P(None, None, "gx", "gy"), P(None, None, "gx", "gy")),
        check_vma=False,
    )
```

```python
import functools

import jax
import jax.numpy as jnp
import numpy as np
from jax import lax
from jax.experimental import pallas as pl
from jax.experimental.pallas import tpu as pltpu
from jax.sharding import PartitionSpec as P

SUBSTEPS = 3
F32 = jnp.float32
LANES = 128
VMEM_LIMIT = 16 * 1024 * 1024
nudge_floor = 0.1
relax_width = 4.0


def whole(array):
    return pl.BlockSpec(array.shape, lambda level: (0,) * array.ndim)


def block(shape, at):
    return pl.BlockSpec(shape, lambda level: at)


def by_level(shape, dim):
    sizes = tuple(1 if i == dim else n for i, n in enumerate(shape))
    return pl.BlockSpec(sizes, lambda level: tuple(level if i == dim else 0 for i in range(len(shape))))


def call(body, grid, ins, outs, scratch=(), cost=None):
    return pl.pallas_call(
        body,
        grid=(grid,),
        out_shape=[
            pltpu.HBM(out[0], F32) if out[2:] == (pltpu.HBM,) else jax.ShapeDtypeStruct(out[0], *(out[2:] or (F32,)))
            for out in outs
        ],
        in_specs=[spec for _, spec in ins],
        out_specs=[out[1] for out in outs],
        scratch_shapes=[pltpu.VMEM(shape, F32) for shape in scratch],
        cost_estimate=cost,
        compiler_params=pltpu.CompilerParams(vmem_limit_bytes=VMEM_LIMIT),
    )(*[array for array, _ in ins])


def call_once(body, scalars, ins, outs, scratch=(), results=0):
    vmem, hbm = pl.BlockSpec(memory_space=pltpu.VMEM), pl.BlockSpec(memory_space=pl.ANY)
    return pl.pallas_call(
        body,
        out_shape=[
            pltpu.HBM(shape, F32) if at < results else jax.ShapeDtypeStruct(shape, F32)
            for at, shape in enumerate(outs)
        ],
        in_specs=[pl.BlockSpec(memory_space=pltpu.SMEM)] * len(scalars) + [vmem] * len(ins),
        out_specs=[hbm] * results + [vmem] * (len(outs) - results),
        scratch_shapes=[
            pltpu.VMEM(shape, F32) if isinstance(shape, tuple) else shape for shape in scratch
        ],
        compiler_params=pltpu.CompilerParams(vmem_limit_bytes=VMEM_LIMIT),
    )(*scalars, *ins)


def lane_index(rows, lanes=LANES):
    return lax.broadcasted_iota(jnp.int32, (rows, lanes), 1)


def row_index(rows, lanes=LANES):
    return lax.broadcasted_iota(jnp.int32, (rows, lanes), 0)


def among(value, numbers):
    found = False
    for number in numbers:
        found = found | (value == number)
    return found


def swapped(axis, to_pair, to_other):
    count = lax.axis_size(axis)
    pairs = [(at, at ^ 1) for at in range(count)]
    others = [(at, at + 1 if at % 2 else at - 1) for at in range(1, count - 1)]
    return lax.ppermute(to_pair, axis, pairs), lax.ppermute(to_other, axis, others)


def by_side(axis, from_pair, from_other):
    even = lax.rem(lax.axis_index(axis), 2) == 0
    return jnp.where(even, from_other, from_pair), jnp.where(even, from_pair, from_other)


def pack_kernel(firsts, anchor, pf_head, pf_tail, pf_first, pf_last, nf_head, nf_tail, nv_head, nv_tail, nm_head, nm_tail, *outs):
    to_pair, to_other, col_to_pair, col_to_other, *indices = outs
    channels, rows = pf_first.shape[:2]
    for at, (index, limits) in enumerate(zip(indices, firsts)):
        index[0] = sum((anchor[at] >= first).astype(jnp.int32) for first in limits[1:])
    coefs = nv_head.shape[0] + nm_head.shape[0]
    even = lax.rem(lax.axis_index("gx"), 2) == 0

    def lines(out, parent, field, wind, mixing, at_end):
        def put(here, ref, row, count, at):
            line = 8 - count + at if at_end else at
            out[here : here + 1, :] = ref[row, line : line + 1, :]

        for at in range(3):
            for ch in range(channels):
                put(at * channels + ch, field, ch, 3, at)
        for at in range(2):
            for cc in range(coefs):
                here = 3 * channels + at * coefs + cc
                ref, row = (wind, cc) if cc < wind.shape[0] else (mixing, cc - wind.shape[0])
                put(here, ref, row, 2, at)
        for ch in range(channels):
            put(3 * channels + 2 * coefs + ch, parent, ch, 1, 0)

    heads, tails = (pf_head, nf_head, nv_head, nm_head), (pf_tail, nf_tail, nv_tail, nm_tail)

    @pl.when(even)
    def _():
        lines(to_pair, *tails, True)
        lines(to_other, *heads, False)

    @pl.when(jnp.logical_not(even))
    def _():
        lines(to_pair, *heads, False)
        lines(to_other, *tails, True)

    lanes = lane_index(rows)
    last = jnp.zeros((rows, LANES), F32)
    first = jnp.zeros((rows, LANES), F32)
    for ch in range(channels):
        last = jnp.where(lanes == ch, pltpu.roll(pf_last[ch], (ch + 1) % LANES, 1), last)
        first = jnp.where(lanes == ch, pltpu.roll(pf_first[ch], ch, 1), first)
    even = lax.rem(lax.axis_index("gy"), 2) == 0
    col_to_pair[...] = jnp.where(even, last, first)
    col_to_other[...] = jnp.where(even, first, last)


def column_pack_kernel(
    nf_first, nf_last, nv_first, nv_last, nm_first, nm_last, pair, other, to_pair, to_other
):
    channels, rows = nf_first.shape[:2]
    columns = pair.shape[1]
    winds = nv_first.shape[0]
    coefs = winds + nm_first.shape[0]
    height = rows + 8
    lanes, lane = lane_index(rows), lane_index(1)

    def packed(nf, nv, nm, part, moved):
        main = jnp.zeros((rows, LANES), F32)
        lines = {at: jnp.zeros((1, LANES), F32) for at in range(-3, 3)}

        def add(first, size, tile, halo_rows):
            nonlocal main
            shift = (first + (size if moved else 0)) % LANES
            inside = (lanes >= first) & (lanes < first + size)
            main = jnp.where(inside, pltpu.roll(tile, shift, 1), main)
            inside = (lane >= first) & (lane < first + size)
            for at, value in halo_rows:
                lines[at] = jnp.where(inside, pltpu.roll(value, shift, 1), lines[at])

        def halos(base, step, size, at):
            lines_of = []
            for n in range(size):
                here = base + n * step + at
                before, after = by_side("gx", pair[here : here + 1, part], other[here : here + 1, part])
                lines_of += [(n, after), (n - size, before)]
            return lines_of

        for ch in range(channels):
            add(3 * ch, 3, nf[ch], halos(0, channels, 3, ch))
        base = 3 * channels
        for cc in range(coefs):
            tile = nv[cc] if cc < winds else nm[cc - winds]
            add(base + 2 * cc, 2, tile, halos(base, coefs, 2, cc))
        blank = jnp.zeros((2, LANES), F32)
        return jnp.concatenate([main, lines[0], lines[1], lines[2], blank, lines[-3], lines[-2], lines[-1]], axis=0)

    last = packed(nf_last, nv_last, nm_last, slice(columns - LANES, columns), True)
    first = packed(nf_first, nv_first, nm_first, slice(0, LANES), False)
    even = lax.rem(lax.axis_index("gy"), 2) == 0
    to_pair[...] = jnp.where(even, last, first)
    to_other[...] = jnp.where(even, first, last)


def parent_kernel(size_x, anchor, index, table, pf, pv, pm, col_other, row_other, col_pair, row_pair, parent_next, *slabs):
    fields, _, rows, columns = pf.shape
    levels = pm.shape[0]
    channels = fields * levels
    span = rows // 3
    rank = lax.axis_index("gx")
    base = 3 * channels + 2 * 3 * levels
    row_shift = lax.rem((rows - span) * rank + size_x * rows - anchor[0], rows)
    row, lane = row_index(8, columns), lane_index(rows)
    place = (index[0] * size_x + rank) * (len(slabs) - 1)
    kinds = [table[place + slot] for slot in range(len(slabs) - 1)]
    left, right = by_side("gy", col_pair[...], col_other[...])

    def rows_by_slab(value):
        thirds = [
            (
                value[span * kind : span * (kind + 1)],
                value[(span * kind - 1) % rows : (span * kind - 1) % rows + 1],
                value[span * (kind + 1) % rows : span * (kind + 1) % rows + 1],
            )
            for kind in range(3)
        ]
        yield thirds[0]
        for kind in kinds:
            yield [
                jnp.where(kind == 0, zero, jnp.where(kind == 1, one, two))
                for zero, one, two in zip(*thirds)
            ]

    def level_body(level, carry):
        u, v, k = pv[0, level], pv[1, level], pm[level]
        a_w = jnp.maximum(u, 0.0) + k
        a_e = k - jnp.minimum(u, 0.0)
        a_s = jnp.maximum(v, 0.0) + k
        a_n = k - jnp.minimum(v, 0.0)
        a_c = 1.0 - (a_w + a_e + a_s + a_n)
        for field in range(fields):
            ch = field * levels + level
            q = pf[field, level]
            source = pl.ds(base + ch, 1)
            above, below = by_side("gx", row_pair[source, :], row_other[source, :])
            at_first = pltpu.roll(left, LANES - ch, 1)
            at_last = pltpu.roll(right, LANES - 1 - ch, 1)
            west, east = pltpu.roll(q, 1, 0), pltpu.roll(q, rows - 1, 0)
            west = jnp.concatenate([jnp.where(row == 0, above, west[:8]), west[8:]], axis=0)
            east = jnp.concatenate(
                [east[: rows - 8], jnp.where(row == 7, below, east[rows - 8 :])], axis=0
            )
            south, north = pltpu.roll(q, 1, 1), pltpu.roll(q, columns - 1, 1)
            south = jnp.concatenate(
                [jnp.where(lane == 0, at_first, south[:, :LANES]), south[:, LANES:]], axis=1
            )
            outer = columns - LANES
            north = jnp.concatenate(
                [north[:, :outer], jnp.where(lane == LANES - 1, at_last, north[:, outer:])], axis=1
            )
            result = a_c * q + a_w * west + a_e * east + a_s * south + a_n * north
            parent_next[field, level] = result
            moved = pltpu.roll(result, row_shift, 0)
            here = level * fields + field
            for slab, (cells, before, after) in zip(slabs, rows_by_slab(moved)):
                slab[pl.ds(pl.multiple_of(span * here, 8), span), :] = cells
                slab[pl.ds(span * channels + here, 1), :] = before
                slab[pl.ds((span + 1) * channels + here, 1), :] = after
        return carry

    lax.fori_loop(0, levels, level_body, 0)


def packed_half(value, side):
    rows = value.shape[0] // 2
    first, second = value[:rows], value[rows:]
    left = lane_index(rows) < LANES // 2
    if side == 0:
        return jnp.where(left, first, pltpu.roll(second, LANES // 2, 1))
    return jnp.where(left, pltpu.roll(first, LANES // 2, 1), second)


def unpacked_half(value, side):
    turned = pltpu.roll(value, LANES // 2, 1)
    return jnp.concatenate([value, turned] if side == 0 else [turned, value], axis=0)


def row_select_kernel(entries, rows, channels, anchor, *refs):
    count = len(entries)
    slabs, messages, half = refs[:count], refs[count:-1], refs[-1]
    span = rows // 3
    columns = slabs[0].shape[1]
    rank = lax.axis_index("gx")
    start = anchor[0] + span * rank
    lowest, highest = lax.div(start, rows), lax.div(start + span - 1, rows)
    above, below = lax.div(start - 1, rows), lax.div(start + span, rows)
    split = jnp.where(highest > lowest, rows * highest - start, span)
    cells, total = span * channels, (span + 2) * channels

    offset = anchor[1] - lax.axis_size("gy") // 2 * columns
    shift = lax.rem(2 * columns - offset, columns)

    def pick(owner, first, size):
        value = slabs[0][first : first + size, :]
        for senders, slab in zip(entries[1:], slabs[1:]):
            chosen = False
            for d, ranks in senders:
                chosen = chosen | ((rank - owner == d) & among(rank, ranks))
            value = jnp.where(chosen, slab[first : first + size, :], value)
        return value

    def turned_tiles(value):
        value = pltpu.roll(value, shift, 1)
        return [value[:, LANES * tile : LANES * (tile + 1)] for tile in range(3)]

    row = row_index(cells, columns) & (span - 1)
    tiles = turned_tiles(jnp.where(row < split, pick(lowest, 0, cells), pick(highest, 0, cells)))
    edges = (turned_tiles(pick(above, cells, channels)), turned_tiles(pick(below, cells + channels, channels)))
    sides = [[edge[tile] for edge in edges] for tile in range(3)]
    lanes, edge_lanes = lane_index(span), lane_index(channels)
    edge_inside = lax.div(edge_lanes, 2) == row_index(channels)

    def beside(parts, tile, lane):
        return jnp.where(lane == LANES - 1, parts[(tile + 2) % 3], parts[(tile + 1) % 3])

    for tile, message in enumerate(messages):
        message[0:cells, :] = tiles[tile]
        rim = jnp.zeros((span, LANES), F32)
        for ch in range(channels):
            here = [value[span * ch : span * (ch + 1)] for value in tiles]
            turned = pltpu.roll(beside(here, tile, lanes), 2 * ch + 1, 1)
            rim = jnp.where((lanes == 2 * ch) | (lanes == 2 * ch + 1), turned, rim)
        message[total : total + span, :] = rim + pltpu.roll(rim, LANES // 2, 1)
        for side in range(2):
            first = cells + side * channels
            message[first : first + channels, :] = sides[tile][side]
            line = beside([value[side] for value in sides], tile, edge_lanes)
            line = pltpu.roll(line, 1, 1, stride=2, stride_axis=0)
            line = jnp.sum(jnp.where(edge_inside, line, 0.0), axis=0, keepdims=True)
            target = total + span + side
            message[target : target + 1, :] = line + pltpu.roll(line, LANES // 2, 1)
        message[total + span + 2 :, :] = jnp.zeros((message.shape[0] - total - span - 2, LANES), F32)
    split_tile = jnp.where(offset < LANES, messages[2][...], messages[1][...])
    right = ((offset <= LANES // 2) | (offset > LANES)) & (offset <= LANES + LANES // 2)
    half[...] = jnp.where(right, packed_half(split_tile, 1), packed_half(split_tile, 0))


def three_parts(x):
    high = x.astype(jnp.bfloat16)
    rest = x - high.astype(F32)
    middle = rest.astype(jnp.bfloat16)
    low = (rest - middle.astype(F32)).astype(jnp.bfloat16)
    return high, middle, low


def exact_dot(x, matrix):
    parts = three_parts(x)
    total = jnp.dot(parts[2], matrix, preferred_element_type=F32)
    total = total + jnp.dot(parts[1], matrix, preferred_element_type=F32)
    return total + jnp.dot(parts[0], matrix, preferred_element_type=F32)


def stencil(q, coefs):
    height, width = q.shape
    return (
        coefs[0] * q
        + coefs[1] * pltpu.roll(q, 1, 0)
        + coefs[2] * pltpu.roll(q, height - 1, 0)
        + coefs[3] * pltpu.roll(q, 1, 1)
        + coefs[4] * pltpu.roll(q, width - 1, 1)
    )


def nest_start_kernel(nf, nv, nm, row_pair, row_other, col_pair, col_other, coefs, moved, weights, state):
    fields, _, rows, columns = nf.shape
    levels = nm.shape[0]
    channels = fields * levels
    height, width = rows + 8, columns + LANES
    rank_x, rank_y = lax.axis_index("gx"), lax.axis_index("gy")
    row = row_index(height, width)
    column = lane_index(height, width)
    local_row = jnp.where(row < rows + 4, row, row - height)
    local_column = jnp.where(column < columns + LANES // 2, column, column - width)
    global_row = rank_x * rows + local_row
    global_column = rank_y * columns + local_column
    row_distance = jnp.minimum(global_row, lax.axis_size("gx") * rows - 1 - global_row)
    column_distance = jnp.minimum(
        global_column, lax.axis_size("gy") * columns - 1 - global_column
    )
    distance = jnp.minimum(row_distance, column_distance)
    weight = nudge_floor + (1.0 - nudge_floor) * jnp.exp(
        jnp.maximum(distance, 0).astype(F32) / -relax_width
    )
    weight = jnp.where(distance < 0, 0.0, weight)
    keep = 1.0 - weight
    edge_lanes = lane_index(height)

    weights[...] = weight / 9.0
    state[...] = jnp.zeros_like(state)

    left, right = by_side("gy", col_pair[...], col_other[...])

    def side_tile(first, size):
        after = pltpu.roll(right, lax.rem(2 * LANES - first, LANES), 1)
        before = pltpu.roll(left, lax.rem(2 * LANES - first - size, LANES), 1)
        inside = jnp.where(edge_lanes < LANES // 2, after, before)
        outside = (edge_lanes >= size) & (edge_lanes < LANES - size)
        return jnp.where(outside, 0.0, inside)

    def fill(slot, value, base, step, at, size, first):
        state[slot, 0:rows, 0:columns] = value
        for n in range(size):
            source = pl.ds(base + n * step + at, 1)
            above, below = by_side("gx", row_pair[source, :], row_other[source, :])
            state[slot, rows + n : rows + n + 1, 0:columns] = below
            target = height - size + n
            state[slot, target : target + 1, 0:columns] = above
        state[slot, :, columns:width] = side_tile(first, size)

    def level_body(level, carry):
        base = 3 * channels
        for slot, value in enumerate((nv[0, level], nv[1, level], nm[level])):
            cc = slot * levels + level
            fill(slot + fields, value, base, 3 * levels, cc, 2, base + 2 * cc)
        for field in range(fields):
            ch = field * levels + level
            fill(field, nf[field, level], 0, channels, ch, 3, 3 * ch)
        u, v, k = (state[slot + fields] for slot in range(3))
        a_w = jnp.maximum(u, 0.0) + k
        a_e = k - jnp.minimum(u, 0.0)
        a_s = jnp.maximum(v, 0.0) + k
        a_n = k - jnp.minimum(v, 0.0)
        a_c = 1.0 - (a_w + a_e + a_s + a_n)
        for slot, value in enumerate((a_c, a_w, a_e, a_s, a_n)):
            coefs[level, slot] = keep * value
        for field in range(fields):
            moved[level, field] = stencil(state[field], [coefs[level, slot] for slot in range(5)])
        return carry

    lax.fori_loop(0, levels, level_body, 0)


def nest_kernel(ks, half, selves, anchor, spread, gather, coefs, moved, weights, *refs):
    count = len(ks) + 3
    received, messages = dict(zip(ks, refs[: len(ks)])), refs[len(ks) : count]
    result, coarse, *coarse_half = refs[count:-8]
    relay, refined, forcing, state, sums, final, held, sems = refs[-8:]
    fields, levels, rows, columns = result.shape
    channels = fields * levels
    span_rows, span_columns = rows // 3, columns // 3
    height, width = rows + 8, columns + LANES
    tiles = width // LANES
    relay_rows = span_rows + 2
    total = relay_rows * channels
    offset = anchor[1] - lax.axis_size("gy") // 2 * columns
    kind = lax.rem(lax.axis_index("gy"), 3)
    edge = columns - offset - span_columns * kind

    arrived, rims = {}, {}
    for k in ks:
        value = received[k][...]
        side = half[1] if half and half[0] == k else 0
        if half and half[0] == k:
            value = unpacked_half(value, side)
        rim = value[total : total + relay_rows]
        if side == 1:
            rim = pltpu.roll(rim, LANES // 2, 1)
        if k in selves:
            itself = lax.axis_index("gy") == selves[k]
            own = messages[k % 3][...]
            value = jnp.where(itself, own, value)
            rim = jnp.where(itself, own[total : total + relay_rows], rim)
        arrived[k], rims[k] = value, rim

    def chosen(values):
        low, high = values.get(2, values[0]), values.get(-1, values[0])
        low = jnp.where(kind == 1, values.get(1, values[0]), low)
        low = jnp.where(kind == 0, values[0], low)
        return low, jnp.where(kind == 1, values.get(-2, values[0]), high)

    lower, upper = chosen(arrived)
    rim_low, rim_high = chosen(rims)
    lanes = lane_index(lower.shape[0])
    relay[:, 0:LANES] = jnp.where(lanes < edge, lower, upper)
    relay[total:, LANES:] = jnp.zeros((relay.shape[0] - total, LANES), F32)
    odd = (lane_index(relay_rows) & 1) == 1
    rim = jnp.where(jnp.where(odd, LANES, -1) < edge, rim_low, rim_high)
    for ch in range(channels):
        sides = pltpu.roll(rim, (LANES - 2 * ch) % LANES, 1)
        relay[span_rows * ch : span_rows * (ch + 1), LANES:] = sides[0:span_rows]
        for side in (span_rows, span_rows + 1):
            here = side * channels + ch
            relay[here : here + 1, LANES:] = sides[side : side + 1]
    refined[...] = exact_dot(relay[...], spread[...])

    relay_row = row_index(span_rows, width)

    def leaving(level):
        return pltpu.make_async_copy(held.at[:, level], result.at[:, level], sems.at[level])

    def level_body(level, carry):
        for field in range(fields):
            ch = level * fields + field
            centre = refined[pl.ds(pl.multiple_of(span_rows * ch, 8), span_rows), :]
            above = refined[pl.ds(span_rows * channels + ch, 1), :]
            below = refined[pl.ds((span_rows + 1) * channels + ch, 1), :]
            before = jnp.where(relay_row == 0, above, pltpu.roll(centre, 1, 0))
            after = jnp.where(
                relay_row == span_rows - 1, below, pltpu.roll(centre, span_rows - 1, 0)
            )
            thirds = (before + 2.0 * centre, 3.0 * centre, 2.0 * centre + after)
            rims = (
                (rows, centre[span_rows - 1 :] + 2.0 * below),
                (rows + 1, 3.0 * below),
                (height - 2, 3.0 * above),
                (height - 1, 2.0 * above + centre[0:1]),
            )
            for tile in range(tiles):
                part = slice(LANES * tile, LANES * (tile + 1))
                for at, value in enumerate(thirds):
                    forcing[field, tile, pl.ds(at, span_rows, stride=3), :] = value[:, part]
                forcing[field, tile, rows + 2 : height - 2, :] = jnp.zeros((4, LANES), F32)
                for at, value in rims:
                    forcing[field, tile, at : at + 1, :] = value[:, part]
        for field in range(fields):
            for tile in range(tiles):
                part = slice(LANES * tile, LANES * (tile + 1))
                pull = weights[:, part] * forcing[field, tile]
                forcing[field, tile] = pull
                state[field, :, part] = moved[level, field, :, part] + pull
        for step in range(SUBSTEPS - 1):
            for field in range(fields):
                pull = jnp.concatenate([forcing[field, tile] for tile in range(tiles)], axis=1)
                value = pull + stencil(state[field], [coefs[level, slot] for slot in range(5)])
                if step < SUBSTEPS - 2:
                    state[field] = value
                else:
                    held[field, level] = value[0:rows, 0:columns]
                    for tile in range(tiles - 1):
                        final[field, tile] = value[0:rows, LANES * tile : LANES * (tile + 1)]
        leaving(level).start()
        for field in range(fields):
            for tile in range(tiles - 1):
                part = slice(LANES * tile, LANES * (tile + 1))
                sums[span_rows * field : span_rows * (field + 1), part] = (
                    final[field, tile, pl.ds(0, span_rows, stride=3), :]
                    + final[field, tile, pl.ds(1, span_rows, stride=3), :]
                    + final[field, tile, pl.ds(2, span_rows, stride=3), :]
                )
        means = exact_dot(sums[...], gather[...]) / 9.0
        size = span_rows * fields
        coarse[pl.ds(pl.multiple_of(size * level, 8), size), :] = means
        if half:
            place = pl.ds(pl.multiple_of(size // 2 * level, 8), size // 2)
            coarse_half[0][place, :] = packed_half(means, half[1])
        return carry

    lax.fori_loop(0, levels, level_body, 0)
    for level in range(levels):
        leaving(level).wait()


def column_select_kernel(ks, half, selves, columns, levels, anchor, coarse, *refs):
    returned, placed = refs[:-1], refs[-1]
    offset = anchor[1] - lax.axis_size("gy") // 2 * columns
    size = placed.shape[0] // levels
    lanes = lane_index(size)
    for level in range(levels):
        rows = slice(size * level, size * (level + 1))
        arrived = {}
        for k, ref in zip(ks, returned):
            if half and half[0] == k:
                value = ref[size // 2 * level : size // 2 * (level + 1), :]
                value = unpacked_half(value, half[1])
            else:
                value = ref[rows, :]
            if k in selves:
                value = jnp.where(lax.axis_index("gy") == selves[k], coarse[rows, :], value)
            arrived[k] = value
        tiles = [arrived[0]]
        for tile in (1, 2):
            own = arrived.get(tile, arrived.get(tile - 3))
            other = arrived.get(tile - 3, own)
            inside = lanes < columns - offset - LANES * tile
            tiles.append(jnp.where(inside, own, other))
        placed[rows, :] = pltpu.roll(jnp.concatenate(tiles, axis=1), offset, 1)


def merge_kernel(entries, anchor, parent_next, *refs):
    slabs, (merged, held, sems) = refs[:-3], refs[-3:]
    fields, levels, rows, columns = parent_next.shape
    span = rows // 3
    rank_x, rank_y = lax.axis_index("gx"), lax.axis_index("gy")
    size_x, size_y = lax.axis_size("gx"), lax.axis_size("gy")
    row = rank_x * rows + row_index(rows, columns) - anchor[0]
    column = rank_y * columns + lane_index(rows, columns) - anchor[1]
    covered = (
        (row >= 0) & (row < size_x * span) & (column >= 0) & (column < size_y * (columns // 3))
    )
    first = anchor[0] - (rows - span) * rank_x
    row_shift = lax.rem(first + size_x * rows, rows)
    slab_row = row_index(span)
    choices = [[], [], []]
    for at, receivers in enumerate(entries):
        for d, ranks in receivers:
            place = first + span * d + slab_row
            if ranks is not None:
                place = jnp.where(among(rank_x, ranks), place, -1)
            choices[d % 3].append((at, (place >= 0) & (place < rows)))
    def leaving(level):
        return pltpu.make_async_copy(held.at[:, level], merged.at[:, level], sems.at[level])

    def level_body(level, carry):
        for field in range(fields):
            here = pl.ds(pl.multiple_of(span * (fields * level + field), 8), span)
            tiles = []
            for tile in range(3):
                kinds = []
                for options in choices:
                    value = jnp.zeros((span, LANES), F32)
                    for at, inside in options:
                        part = slice(LANES * tile, LANES * (tile + 1))
                        cells = slabs[at][here, part]
                        value = jnp.where(inside, cells, value)
                    kinds.append(value)
                tiles.append(jnp.concatenate(kinds, axis=0))
            fed_back = pltpu.roll(jnp.concatenate(tiles, axis=1), row_shift, 0)
            held[field, level] = jnp.where(covered, fed_back, parent_next[field, level])
        leaving(level).start()
        return carry

    lax.fori_loop(0, levels, level_body, 0)
    for level in range(levels):
        leaving(level).wait()


def spread_matrix(columns):
    span = columns // 3
    matrix = np.zeros((2 * LANES, columns + LANES), np.float32)

    def source(m):
        return LANES if m < 0 else (LANES + 1 if m >= span else m)

    for c in range(-2, columns + 2):
        m, j = divmod(c, 3)
        at = c % (columns + LANES)
        if j == 0:
            matrix[source(m - 1), at] += 1.0
            matrix[source(m), at] += 2.0
        elif j == 1:
            matrix[source(m), at] += 3.0
        else:
            matrix[source(m), at] += 2.0
            matrix[source(m + 1), at] += 1.0
    return jnp.asarray(matrix, jnp.bfloat16)


def gather_matrix(columns):
    matrix = np.zeros((columns, columns // 3), np.float32)
    matrix[np.arange(columns), np.arange(columns) // 3] = 1.0
    return jnp.asarray(matrix, jnp.bfloat16)


def coloured(pairs):
    degree = max(sum(pair[end] == at for pair in pairs) for end in (0, 1) for at, _ in enumerate(pairs + [0, 0]))
    routes = [[] for _ in range(degree)]

    def free(route, end, at):
        return all(pair[end] != at for pair in routes[route])

    for pair in pairs:
        first = next(route for route in range(degree) if free(route, 0, pair[0]))
        second = next(route for route in range(degree) if free(route, 1, pair[1]))
        if not free(first, 1, pair[1]):
            end, at, route, other = 1, pair[1], first, second
            path = []
            while not free(route, end, at):
                step = next(p for p in routes[route] if p[end] == at)
                path.append((step, route, other))
                end, at, route, other = 1 - end, step[1 - end], other, route
            for step, source, _ in path:
                routes[source].remove(step)
            for step, _, target in path:
                routes[target].append(step)
        routes[first].append(pair)
    return [sorted(route) for route in routes]


def row_routes(size, rows):
    span = rows // 3

    def needed(start):
        pairs = set()
        for nest in range(size):
            for at in (start + span * nest, start + span * nest + span + 1):
                pairs.add((at // rows, nest))
        return {(owner, nest) for owner, nest in pairs if owner != nest}

    def cost(pairs):
        cuts = [
            sum((a < cut <= n) if up else (n < cut <= a) for a, n in pairs)
            for cut in range(2, size, 2)
            for up in (False, True)
        ]
        return 4 * max(cuts) + len(coloured(sorted(pairs)))

    ranges = []
    pending = None
    for first in range(0, size * (rows - span) - 2, span):
        last = min(first + span, size * (rows - span) - 2) - 1
        pairs = set().union(*(needed(start) for start in range(first, last)))
        start, extra = first, needed(last)
        if pending is not None:
            before, more = ranges[-1][1], pending
            if cost(before | more) + cost(pairs) <= cost(before) + cost(pairs | more):
                ranges[-1] = (ranges[-1][0], before | more)
            else:
                start, pairs = first - 1, pairs | more
        ranges.append((start + 1, pairs))
        pending = extra
    ranges[-1] = (ranges[-1][0], ranges[-1][1] | pending)

    def crossing(route):
        return -sum(a // 2 != n // 2 for a, n in route)

    def ordered(routes):
        routes = sorted(routes, key=crossing)
        if len(routes) > 2 and crossing(routes[1]) and not crossing(routes[-1]):
            routes.insert(1, routes.pop())
        return routes

    return [(first, ordered(coloured(sorted(pairs)))) for first, pairs in ranges]


def column_routes(size):
    routes, selves = {}, {}
    for k in (0, 1, -2, 2, -1):
        pairs = [(size // 2 + p, 3 * p + k) for p in range(size - size // 2)]
        routes[k] = [(s, n) for s, n in pairs if 0 <= n < size and n != s]
        selves.update({k: s for s, n in pairs if n == s})
    return routes, selves


column_cases = (
    (1, (0, 1, 2, -1), (-1, 1)),
    (65, (0, 1, 2, -1), (2, 0)),
    (128, (0, 1, 2, -1, -2), None),
    (129, (0, 1, -1, -2), (-2, 1)),
    (193, (0, 1, -1, -2), (1, 0)),
)


def per_device(
    parent_fields,
    parent_velocity,
    parent_mixing,
    nest_fields,
    nest_velocity,
    nest_mixing,
    nest_anchor,
):
    fields, levels, rows, columns = shape = parent_fields.shape
    channels = fields * levels
    span, last = rows // 3, columns // LANES - 1
    gx, gy = lax.axis_size("gx"), lax.axis_size("gy")
    height, width = rows + 8, columns + LANES
    pf = parent_fields.reshape(channels, rows, columns)
    nf = nest_fields.reshape(channels, rows, columns)
    nv = nest_velocity.reshape(2 * levels, rows, columns)
    nm = nest_mixing
    def row_blocks(array):
        size = (array.shape[0], 8, columns)
        return [(array, block(size, (0, 0, 0))), (array, block(size, (0, rows // 8 - 1, 0)))]

    def column_blocks(array):
        size = (array.shape[0], rows, LANES)
        return [(array, block(size, (0, 0, 0))), (array, block(size, (0, 0, last)))]

    def shaped(*size):
        return size, block(size, (0,) * len(size))

    def whole_of(arrays):
        return [(array, whole(array)) for array in arrays]

    halo_rows = 4 * channels + 6 * levels
    ranges = row_routes(gx, rows)
    middle = gy // 2 * columns
    firsts = ([first for first, _ in ranges], [middle + first for first, _, _ in column_cases])
    scalar = pl.BlockSpec(memory_space=pltpu.SMEM)
    anchor = (nest_anchor, scalar)
    row_pair, row_other, col_pair, col_other, row_range, column_case = call(
        functools.partial(pack_kernel, firsts),
        1,
        [anchor]
        + [
            (pltpu.with_memory_space_constraint(array, pltpu.HBM), spec)
            for array, spec in row_blocks(pf)
            + column_blocks(pf)
            + row_blocks(nf)
            + row_blocks(nv)
            + row_blocks(nm)
        ],
        [shaped(halo_rows, columns)] * 2
        + [shaped(rows, LANES)] * 2
        + [((1,), scalar, jnp.int32)] * 2,
    )
    col_halos = swapped("gy", col_pair, col_other)
    row_halos = swapped("gx", row_pair, row_other)

    slots = max(len(routes) for _, routes in ranges)
    table = np.zeros((len(ranges), gx, slots), np.int32)
    for at, (_, routes) in enumerate(ranges):
        for slot, route in enumerate(routes):
            for owner, nest in route:
                table[at, owner, slot] = (nest - owner) % 3
    message_rows = -(-((span + 2) * (channels + 1)) // 16) * 16
    columns_of, selves = column_routes(gy)
    cells_rows, relay_height = span * channels, (span + 2) * channels

    def by_shift(route, receiver):
        shifts = sorted({nest - owner for owner, nest in route})
        return [(d, [pair[receiver] for pair in route if pair[1] - pair[0] == d]) for d in shifts]

    parent_next, *slabs = call_once(
        functools.partial(parent_kernel, gx),
        [nest_anchor, row_range, jnp.asarray(table.reshape(-1))],
        [
            parent_fields,
            parent_velocity,
            parent_mixing,
            col_halos[1],
            row_halos[1],
            col_halos[0],
            row_halos[0],
        ],
        [shape] + [(relay_height, columns)] * (slots + 1),
    )

    def relay_rows(routes):
        def branch(nest_anchor, slabs, nf, nv, nm, row_halos):
            received = [lax.ppermute(slab, "gx", route) for slab, route in zip(slabs[1:], routes)]
            to_pair, to_other = call(
                column_pack_kernel,
                1,
                column_blocks(nf) + column_blocks(nv) + column_blocks(nm) + whole_of(row_halos),
                [shaped(height, LANES)] * 2,
            )
            sides = swapped("gy", to_pair, to_other)
            entries = [None] + [by_shift(route, 1) for route in routes]
            messages = call(
                functools.partial(row_select_kernel, entries, rows, channels),
                1,
                [(nest_anchor, scalar)] + whole_of([slabs[0], *received]),
                [shaped(message_rows, LANES)] * 3 + [shaped(message_rows // 2, LANES)],
            )
            return messages, sides

        return branch

    messages, sides = lax.switch(
        row_range[0],
        [relay_rows(routes) for _, routes in ranges],
        nest_anchor,
        slabs,
        nf,
        nv,
        nm,
        row_halos,
    )

    def nest_part(ks, half):
        def branch(nest_anchor, messages, nest_fields, nest_velocity, nest_mixing, halos):
            anchor = (nest_anchor, scalar)
            packed = half[0] if half else None
            received = [
                lax.ppermute(messages[3 if k == packed else k % 3], "gy", columns_of[k]) for k in ks
            ]
            coefs, moved, weights = call_once(
                nest_start_kernel,
                [],
                [nest_fields, nest_velocity, nest_mixing, *halos],
                [
                    (levels, 5, height, width),
                    (levels, fields, height, width),
                    (height, width),
                ],
                scratch=[(fields + 3, height, width)],
            )
            nest_result, coarse, *coarse_half = call_once(
                functools.partial(nest_kernel, ks, half, selves),
                [nest_anchor],
                [
                    spread_matrix(columns),
                    gather_matrix(columns),
                    coefs,
                    moved,
                    weights,
                    *received,
                    *messages[:3],
                ],
                [shape, (cells_rows, LANES)] + ([(cells_rows // 2, LANES)] if half else []),
                scratch=[
                    (message_rows, 2 * LANES),
                    (message_rows, width),
                    (fields, width // LANES, height, LANES),
                    (fields, height, width),
                    (span * fields, columns),
                    (fields, columns // LANES, rows, LANES),
                    shape,
                    pltpu.SemaphoreType.DMA((levels,)),
                ],
                results=1,
            )
            back = [k for k in (-1, 1, -2, 2, 0) if k in ks]
            returned = [
                lax.ppermute(
                    coarse_half[0] if k == packed else coarse,
                    "gy",
                    [pair[::-1] for pair in columns_of[k]],
                )
                for k in back
            ]
            placed = call(
                functools.partial(column_select_kernel, back, half, selves, columns, levels),
                1,
                [anchor] + whole_of([coarse, *returned]),
                [shaped(cells_rows, columns)],
            )[0]
            return nest_result, placed

        return branch

    nest_result, placed = lax.switch(
        column_case[0],
        [nest_part(ks, half) for _, ks, half in column_cases],
        nest_anchor,
        messages,
        nest_fields,
        nest_velocity,
        nest_mixing,
        [*row_halos, *sides],
    )

    def feedback_rows(routes):
        def branch(nest_anchor, parent_next, placed):
            received = [
                lax.ppermute(placed, "gx", [pair[::-1] for pair in route]) for route in routes[::-1]
            ]
            entries = [[(0, None)]] + [by_shift(route, 0) for route in routes[::-1]]
            return call_once(
                functools.partial(merge_kernel, entries),
                [nest_anchor],
                [parent_next, placed, *received],
                [shape],
                scratch=[shape, pltpu.SemaphoreType.DMA((levels,))],
                results=1,
            )[0]

        return branch

    merged = lax.switch(
        row_range[0], [feedback_rows(routes) for _, routes in ranges], nest_anchor, parent_next, placed
    )
    return merged, nest_result


def solution(mesh):
    placed = (
        P(None, None, "gx", "gy"),
        P(None, None, "gx", "gy"),
        P(None, "gx", "gy"),
        P(None, None, "gx", "gy"),
        P(None, None, "gx", "gy"),
        P(None, "gx", "gy"),
        P(),
    )
    return jax.shard_map(
        per_device,
        mesh=mesh,
        in_specs=placed,
        out_specs=(P(None, None, "gx", "gy"), P(None, None, "gx", "gy")),
        check_vma=False,
    )
```
